32 devices in a mesh: section: 2 (over core), tensor: 4 (over y, x), seq: 4 (over z).
Axes of the slice: x: 2, y: 2, z: 4, core: 2. Of those that a mesh axis runs over, the one named last changes fastest.
Arguments:
- tokens: bfloat16 [2, 4096, 768], P(None, 'seq'), may hold values from -6 to 6
- cotangent: bfloat16 [2, 4096, 768], P(None, 'seq'), may hold values from -6 to 6
- lengths: int32 [2, 3], replicated, may hold values from 1 to 3584, 4096 in all within a row
- selected: int32 [2, 2, 12, 64], P('section', None, 'tensor'), may hold values from -1 to 46, as said below
- input_weight: bfloat16 [2, 768, 3, 768], P('section', None, None, 'tensor'), may hold values from -0.21875 to 0.21875
- input_bias: bfloat16 [2, 2, 768], P('section', None, 'tensor'), may hold values from -3 to 3
- score_weight: bfloat16 [2, 768, 12], P('section', None, 'tensor'), may hold values from -0.21875 to 0.21875
- output_weight: bfloat16 [2, 768, 768], P('section', 'tensor'), may hold values from -0.625 to 0.625
- output_bias: bfloat16 [2, 768], P('section'), may hold values from -3 to 3
- up_weight: bfloat16 [2, 768, 3072], P('section', None, 'tensor'), may hold values from -0.21875 to 0.21875
- up_bias: bfloat16 [2, 3072], P('section', 'tensor'), may hold values from -3 to 3
- down_weight: bfloat16 [2, 3072, 768], P('section', 'tensor'), may hold values from -0.15625 to 0.15625
- down_bias: bfloat16 [2, 768], P('section'), may hold values from -3 to 3
- norm_gain: bfloat16 [2, 2, 768], P('section'), may hold values from 0.5 to 1.5
- norm_bias: bfloat16 [2, 2, 768], P('section'), may hold values from -2 to 2
Outputs:
- layer_out: bfloat16 [2, 2, 4096, 768], P('section', None, 'seq')
- input_grad: bfloat16 [2, 2, 4096, 768], P('section', None, 'seq')
- input_weight_grad: float32 [2, 768, 3, 768], P('section', 'seq', None, 'tensor')
- input_bias_grad: float32 [2, 2, 768], P('section', None, ('tensor', 'seq'))
- score_weight_grad: float32 [2, 768, 12], P('section', 'seq', 'tensor')
- output_weight_grad: float32 [2, 768, 768], P('section', 'tensor', 'seq')
- output_bias_grad: float32 [2, 768], P('section', 'seq')
- up_weight_grad: float32 [2, 768, 3072], P('section', 'seq', 'tensor')
- up_bias_grad: float32 [2, 3072], P('section', ('tensor', 'seq'))
- down_weight_grad: float32 [2, 3072, 768], P('section', 'tensor', 'seq')
- down_bias_grad: float32 [2, 768], P('section', 'seq')
- norm_gain_grad: float32 [2, 2, 768], P('section', None, 'seq')
- norm_bias_grad: float32 [2, 2, 768], P('section', None, 'seq')
The draws below stay inside these ranges and needn't reach their ends.
Inputs may be any that keep to these rules, and one draw needn't show every extreme that they name: The lengths of the 3 documents packed into each micro-batch, in order; they sum to 4096. `selected`: entry [l, m, h, t] is -1 (no tile) or a key tile that lies on an earlier device along seq than query tile t (tile // 16 < t // 16), and is never the last tile of its device. Among the entries of one layer and micro-batch, of the 3 heads of one tensor index and of the 16 query tiles of one device, at most 16 name tiles of the same device.
All inputs are finite; a program needn't handle non-finite values.
Results may differ from the reference program's by a relative error of at most 0.033.
Values may be sent and summed in bfloat16 or wider, within the bound.
A program may use at most 192 MiB of HBM per device.

```python
import math
from functools import partial
import jax
import jax.numpy as jnp
import numpy as np
from jax import lax

D = 768
H = 12
HEAD = 64
FF = 3072
TILE = 64
DOCS = 3
MICRO = 2
TOK_DEV = 1024
LAYERS = 2
LENGTH = 4096
TILES = 64
TILES_DEV = 16
HEADS_DEV = 3
REACH = 3
N_TENSOR = 4
N_SEQ = 4


def draw_selected(key, part):
    order_key, keep_key, inner_key = jax.random.split(key, 3)
    slot_count = HEADS_DEV * TILES_DEV
    shape_all = (LAYERS, MICRO, N_TENSOR, N_SEQ, slot_count)
    noise_ints = jax.random.randint(order_key, shape_all, 0, 1 << 20)
    ranked = noise_ints * slot_count + lax.broadcasted_iota(jnp.int32, shape_all, 4)
    slot_order = jnp.argsort(ranked, axis=-1, stable=True).astype(jnp.int32)
    distance = slot_order % REACH + 1
    kept_slot = (distance == 1) | (jax.random.randint(keep_key, shape_all, 0, 8) > 0)
    device = lax.broadcasted_iota(jnp.int32, shape_all, 3)
    inner_tile = jax.random.randint(inner_key, shape_all, 0, TILES_DEV - 1)
    inner_tile = jnp.where(slot_order == 0, TILES_DEV - 2, inner_tile)
    tile_number = (device - distance) * TILES_DEV + inner_tile
    picked = jnp.where(kept_slot & (distance <= device), tile_number, -1)
    shaped = picked.reshape(LAYERS, MICRO, N_TENSOR, N_SEQ, HEADS_DEV, TILES_DEV)
    return shaped.transpose(0, 1, 2, 4, 3, 5).reshape(LAYERS, MICRO, H, TILES).astype(jnp.int32)


def steps_of(stream_key, extent, cuts, low, largest):
    def one(axis_at, shards_of):
        steps = jax.random.uniform(jax.random.fold_in(jax.random.fold_in(stream_key, 6), axis_at), (shards_of,), jnp.float32, low / len(cuts), largest / len(cuts))
        return jnp.repeat(jnp.exp(steps), extent[axis_at] // shards_of).reshape((-1,) + (1,) * (len(extent) - axis_at - 1))

    gain = one(*cuts[0])
    for cut in cuts[1:]:
        gain = gain * one(*cut)
    return gain


def profile(count, total, reach, lean):
    portions = [(1 << 20) // math.isqrt(grade ** lean) + 1 for grade in range(2, count + 1)]
    rest, counts = total - reach - (count - 1), [1] * (count - 1)
    while rest > 0:
        movable = [i for i in range(count - 1) if counts[i] < reach]
        mass, budget = sum([portions[i] for i in movable]), rest
        for i in movable:
            more = min(reach - counts[i], max(1, budget * portions[i] // mass), rest)
            counts[i] = counts[i] + more
            rest = rest - more
    return np.array([reach] + counts)


def uneven_parts(own_key, count, total, most, slope):
    if count == 2:
        one = jax.random.randint(own_key, (), max(1, total - most), min(most, total - 1) + 1)
        return jnp.stack([one, total - one])
    tallies = jnp.asarray(profile(count, total, most, slope), jnp.int32)
    twos = (count - 1) // 2
    donor, sink = tallies[1:1 + 2 * twos:2], tallies[2:2 + 2 * twos:2]
    margin = jnp.minimum(donor - 1, most - sink)
    shifted = jax.random.randint(jax.random.fold_in(own_key, 1), (twos,), 0, 1 << 20) % (margin + 1)
    tallies = tallies.at[1:1 + 2 * twos:2].set(donor - shifted).at[2:2 + 2 * twos:2].set(sink + shifted)
    return tallies[jax.random.permutation(jax.random.fold_in(own_key, 2), count)]


def gaussian(stream_key, extent, deviation, reach, pieces=(), kind=jnp.bfloat16):
    entries = deviation * jax.random.normal(stream_key, extent, jnp.float32)
    if pieces:
        entries = entries * steps_of(stream_key, extent, pieces, -0.22, 0.18)
    return jnp.clip(entries, -reach, reach).astype(kind)


def setup_inputs(seed: int = 0) -> dict:
    arg_keys = jax.random.split(jax.random.key(seed), 16)
    return {
        "tokens": gaussian(arg_keys[0], (MICRO, LENGTH, D), 1.0, 6.0, ((1, 4),)),
        "cotangent": gaussian(arg_keys[1], (MICRO, LENGTH, D), 1.0, 6.0, ((1, 4),)),
        "lengths": jax.vmap(lambda own: uneven_parts(own, DOCS, LENGTH, LENGTH - TOK_DEV // 2, 0))(jax.random.split(arg_keys[2], MICRO)).reshape((MICRO, DOCS)).astype(jnp.int32),
        "selected": draw_selected(jax.random.fold_in(arg_keys[15], 71), 0),
        "input_weight": gaussian(arg_keys[4], (LAYERS, D, 3, D), D ** -0.5, 0.21875, ((0, 2), (3, 4))),
        "input_bias": gaussian(arg_keys[5], (LAYERS, 2, D), 0.5, 3.0, ((0, 2), (2, 4))),
        "score_weight": gaussian(arg_keys[6], (LAYERS, D, H), D ** -0.5, 0.21875, ((0, 2), (2, 4))),
        "output_weight": gaussian(arg_keys[7], (LAYERS, D, D), (D // 8) ** -0.5, 0.625, ((0, 2), (1, 4))),
        "output_bias": gaussian(arg_keys[8], (LAYERS, D), 0.5, 3.0, ((0, 2),)),
        "up_weight": gaussian(arg_keys[9], (LAYERS, D, FF), D ** -0.5, 0.21875, ((0, 2), (2, 4))),
        "up_bias": gaussian(arg_keys[10], (LAYERS, FF), 0.5, 3.0, ((0, 2), (1, 4))),
        "down_weight": gaussian(arg_keys[11], (LAYERS, FF, D), (FF // 2) ** -0.5, 0.15625, ((0, 2), (1, 4))),
        "down_bias": gaussian(arg_keys[12], (LAYERS, D), 0.5, 3.0, ((0, 2),)),
        "norm_gain": jnp.clip(1.0 + 0.1 * jax.random.normal(arg_keys[13], (LAYERS, 2, D), jnp.float32), 0.5, 1.5).astype(jnp.bfloat16),
        "norm_bias": gaussian(arg_keys[14], (LAYERS, 2, D), 0.3, 2.0, ((0, 2),)),
    }


MASKED = -1e+30
EPSILON = 1e-05

@jax.custom_vjp
def low(v):
    return lax.optimization_barrier(v.astype(jnp.bfloat16)).astype(jnp.float32)

@jax.custom_vjp
def low_back(v):
    return v

def low_keep(v):
    return (low(v), None)

def low_pass(kept, grad):
    return (grad,)

def back_keep(v):
    return (v, None)

def back_low(kept, grad):
    return (low(grad),)
low.defvjp(low_keep, low_pass)
low_back.defvjp(back_keep, back_low)

def highest(left_side, right_side):
    return jnp.dot(left_side, right_side, precision=lax.Precision.HIGHEST)

def layer_norm(vector, norm_gain, norm_shift):
    average = lax.optimization_barrier(jnp.mean(vector, axis=-1, keepdims=True))
    centred = vector - average
    spread = lax.optimization_barrier(jnp.mean(centred * centred, axis=-1, keepdims=True))
    return centred * lax.rsqrt(spread + EPSILON) * norm_gain + norm_shift

def doc_index(position, doc_ends):
    return lax.optimization_barrier(jnp.sum((position[..., None] >= doc_ends).astype(jnp.int32), axis=-1)).astype(jnp.int32)

def head_attention(inputs, doc_ids):
    query_rows, key_rows, value_rows, gate_row, chosen = inputs
    scale_factor = HEAD ** (-0.5)
    tile_ids = jnp.arange(TILES, dtype=jnp.int32)
    earlier = jnp.maximum(tile_ids - 1, 0)
    picked = jnp.maximum(chosen, 0).astype(jnp.int32)
    tile_index = jnp.stack([tile_ids, earlier, picked], axis=1)
    offsets = jnp.arange(TILE, dtype=jnp.int32)
    key_pos = (tile_index[:, :, None] * TILE + offsets).reshape(TILES, 3 * TILE)
    query_pos = tile_ids[:, None] * TILE + offsets
    key_tiles = key_rows.reshape(TILES, TILE, HEAD)[tile_index].reshape(TILES, 3 * TILE, HEAD)
    value_tiles = value_rows.reshape(TILES, TILE, HEAD)[tile_index].reshape(TILES, 3 * TILE, HEAD)
    gate_tiles = gate_row.reshape(TILES, TILE)[tile_index].reshape(TILES, 3 * TILE)
    same_doc = doc_ids[query_pos][:, :, None] == doc_ids[key_pos][:, None, :]
    distance = query_pos[:, :, None] - key_pos[:, None, :]
    window = (distance >= 0) & (distance < TILE)
    key_kind = jnp.arange(3 * TILE, dtype=jnp.int32) // TILE
    live_key = jnp.where(key_kind[None, :] == 2, chosen[:, None] >= 0, jnp.where(key_kind[None, :] == 1, tile_ids[:, None] > 0, True))
    windowed = jnp.where(key_kind[None, None, :] < 2, window, True)
    allowed = same_doc & windowed & live_key[:, None, :]
    scores = scale_factor * jnp.einsum('tad,tkd->tak', query_rows.reshape(TILES, TILE, HEAD), key_tiles, precision=lax.Precision.HIGHEST) + gate_tiles[:, None, :]
    scores = low_back(scores)
    scores = jnp.where(allowed, scores, MASKED)
    row_top = lax.optimization_barrier(jnp.max(scores, axis=-1, keepdims=True))
    exponent = jnp.exp(scores - row_top)
    probability = exponent / lax.optimization_barrier(jnp.sum(exponent, axis=-1, keepdims=True))
    attended = jnp.einsum('tak,tkd->tad', low(probability), value_tiles, precision=lax.Precision.HIGHEST)
    return attended.reshape(LENGTH, HEAD)

def by_heads(matrix):
    return matrix.reshape(LENGTH, H, HEAD).transpose(1, 0, 2)

def layer(params, residual, chosen, doc_ids):
    input_weight, input_bias, score_weight, output_weight, output_bias, up_weight, up_bias, down_weight, down_bias, norm_gain, norm_bias = params
    normed = low(layer_norm(residual, norm_gain[0], norm_bias[0]))
    projected = jnp.einsum('td,dcf->tcf', normed, input_weight, precision=lax.Precision.HIGHEST)
    queries = low(low_back(projected[:, 0] + input_bias[0]))
    key_proj = low(low_back(projected[:, 1]))
    value_proj = low(low_back(projected[:, 2] + input_bias[1]))
    key_score = low_back(highest(normed, score_weight))
    key_gate = low(jax.nn.log_sigmoid(key_score))
    per_head = lax.map(jax.checkpoint(partial(head_attention, doc_ids=doc_ids)), (by_heads(queries), by_heads(key_proj), by_heads(value_proj), key_gate.T, chosen))
    mixed_out = low(low_back(per_head.transpose(1, 0, 2).reshape(LENGTH, D)))
    middle = residual + low_back(highest(mixed_out, output_weight)) + output_bias
    normed_two = low(layer_norm(middle, norm_gain[1], norm_bias[1]))
    up_proj = low_back(highest(normed_two, up_weight) + up_bias)
    active = low(jax.nn.gelu(up_proj, approximate=True))
    return middle + low_back(highest(active, down_weight)) + down_bias

def reference(tokens, cotangent, lengths, selected, input_weight, input_bias, score_weight, output_weight, output_bias, up_weight, up_bias, down_weight, down_bias, norm_gain, norm_bias):
    weights = (input_weight.astype(jnp.float32), input_bias.astype(jnp.float32), score_weight.astype(jnp.float32), output_weight.astype(jnp.float32), output_bias.astype(jnp.float32), up_weight.astype(jnp.float32), up_bias.astype(jnp.float32), down_weight.astype(jnp.float32), down_bias.astype(jnp.float32), norm_gain.astype(jnp.float32), norm_bias.astype(jnp.float32))

    def one_micro(running, inputs):
        micro_tokens, micro_cotan, micro_lengths, micro_chosen = inputs
        doc_ends = jnp.cumsum(micro_lengths).astype(jnp.int32)[:-1]
        doc_ids = doc_index(jnp.arange(LENGTH, dtype=jnp.int32), doc_ends)

        def forward(params, first_in, offset_in):
            layer_zero = tuple((weight_arg[0] for weight_arg in params))
            layer_one = tuple((weight_arg[1] for weight_arg in params))
            hidden = low(low_back(layer(layer_zero, first_in, micro_chosen[0], doc_ids)))
            final_out = layer(layer_one, hidden + offset_in, micro_chosen[1], doc_ids)
            return (hidden, final_out)
        start_in = micro_tokens.astype(jnp.float32)
        zero_in = jnp.zeros_like(start_in)
        (hidden, final_out), pullback = jax.vjp(forward, weights, start_in, zero_in)
        grad_params, grad_start, grad_hidden = pullback((jnp.zeros_like(hidden), micro_cotan.astype(jnp.float32)))
        running = jax.tree.map(jnp.add, running, grad_params)
        return (running, (hidden.astype(jnp.bfloat16), final_out.astype(jnp.bfloat16), grad_start.astype(jnp.bfloat16), grad_hidden.astype(jnp.bfloat16)))
    initial = tuple((jnp.zeros_like(weight_arg) for weight_arg in weights))
    totals, stacked = lax.scan(one_micro, initial, (tokens, cotangent, lengths, jnp.transpose(selected, (1, 0, 2, 3))))
    hidden_all, final_all, grad_start_all, grad_hidden_all = stacked
    layer_out = jnp.stack([hidden_all, final_all], axis=0)
    input_grad = jnp.stack([grad_start_all, grad_hidden_all], axis=0)
    return (layer_out, input_grad, totals[0], totals[1], totals[2], totals[3], totals[4], totals[5], totals[6], totals[7], totals[8], totals[9], totals[10])
```

```python
import functools
import math

import jax
import jax.numpy as jnp
from jax import lax
from jax.experimental import pallas as pl
from jax.experimental.pallas import tpu as pltpu
from jax.sharding import PartitionSpec as P

TILE = 64
LANES = 128
MASKED = -1e30
EPSILON = 1e-05
FAR = -(1 << 20)
MESH = pl.DeviceIdType.MESH
BF = jnp.bfloat16
F32 = jnp.float32
GELU_A = 0.044715
GELU_K = math.sqrt(2.0 / math.pi)
LIMIT = 60 * 1024 * 1024


class Sizes:
    def __init__(self, mesh_tensor, mesh_seq, rows, width, heads, hidden):
        self.T, self.S = mesh_tensor, mesh_seq
        self.rows, self.width, self.heads, self.hidden = rows, width, heads, hidden
        self.tiles = rows // TILE
        self.slots = heads * self.tiles
        self.cap = -(-self.slots // (mesh_seq - 1))
        self.capg = -(-self.cap // 8) * 8
        self.n = mesh_seq * self.cap
        self.block = rows // mesh_tensor
        self.pad = heads * LANES
        self.SEND, self.INV, self.ORD, self.CONT = 0, self.n, 2 * self.n, 3 * self.n
        self.ARR = 4 * self.n
        self.POS = self.ARR + self.slots
        self.LAST = self.POS + self.slots
        self.ENDS = self.LAST + self.slots
        self.route = self.ENDS + 2


def nn(a, b):
    return jnp.dot(a, b, preferred_element_type=F32)


def nt(a, b):
    return lax.dot_general(a, b, (((1,), (1,)), ((), ())), preferred_element_type=F32)


def tn(a, b):
    return lax.dot_general(a, b, (((0,), (0,)), ((), ())), preferred_element_type=F32)


def normed(x):
    centred = x - jnp.mean(x, axis=-1, keepdims=True)
    spread = lax.rsqrt(jnp.mean(centred * centred, axis=-1, keepdims=True) + EPSILON)
    return centred * spread, spread


def norm_back(grad, gain, y, spread):
    scaled = grad * gain
    return spread * (
        scaled
        - jnp.mean(scaled, axis=-1, keepdims=True)
        - y * jnp.mean(scaled * y, axis=-1, keepdims=True)
    )


def partner(me, step):
    return (me // 2 + step // 2) % 2 * 2 + (me % 2 + step % 2) % 2


def column_sum(x):
    return jnp.sum(x, axis=0, keepdims=True)


def routing_kernel(z, sel_ref, ends_ref, rt0_ref, rt1_ref, key_ref, count_ref):
    me = lax.axis_index("seq")
    for layer, rt in enumerate((rt0_ref, rt1_ref)):

        def clear(i, _):
            rt[z.SEND + i] = 1
            rt[z.INV + i] = 0
            key_ref[i] = z.slots
            return 0

        lax.fori_loop(0, z.n, clear, 0)

        def zero(i, _):
            count_ref[i] = 0
            return 0

        lax.fori_loop(0, z.S, zero, 0)

        def source(d, _):
            def slot(u, count):
                h, t = u // z.tiles, u % z.tiles
                v = sel_ref[layer, h, d * z.tiles + t]
                mine = lax.shift_right_arithmetic(v, z.tiles.bit_length() - 1) == me

                @pl.when(mine)
                def _():
                    inner = v - me * z.tiles
                    rt[z.SEND + d * z.cap + count] = h * (z.tiles + 1) + inner + 1
                    key_ref[d * z.cap + count] = h * z.tiles + inner

                return count + mine.astype(jnp.int32)

            lax.fori_loop(0, z.slots, slot, jnp.int32(0))
            return 0

        lax.fori_loop(me + 1, z.S, source, 0)

        def arrival(u, _):
            h, t = u // z.tiles, u % z.tiles
            v = sel_ref[layer, h, me * z.tiles + t]
            live = v >= 0
            owner = jnp.where(live, v // z.tiles, 0)
            place = count_ref[owner]
            rt[z.ARR + u] = jnp.where(live, owner * z.cap + place, me * z.cap)
            rt[z.POS + u] = jnp.where(live, v * TILE, FAR)

            @pl.when(live)
            def _():
                rt[z.INV + owner * z.cap + place] = u
                count_ref[owner] = place + 1

            return 0

        lax.fori_loop(0, z.slots, arrival, 0)
        lax.fori_loop(0, z.slots + 1, zero, 0)

        def tally(i, _):
            count_ref[key_ref[i]] = count_ref[key_ref[i]] + 1
            return 0

        lax.fori_loop(0, z.n, tally, 0)

        def prefix(tile, begin):
            count = count_ref[tile]
            count_ref[tile] = begin

            @pl.when(tile < z.slots)
            def _():
                rt[z.LAST + tile] = jnp.where(count > 0, begin + count - 1, z.n)

            return begin + count

        lax.fori_loop(0, z.slots + 1, prefix, jnp.int32(0))

        def place_in(i, _):
            tile = key_ref[i]
            at = count_ref[tile]
            rt[z.ORD + at] = i
            count_ref[tile] = at + 1
            return 0

        lax.fori_loop(0, z.n, place_in, 0)

        def follow(k, before):
            tile = key_ref[rt[z.ORD + k]]
            rt[z.CONT + k] = (tile == before).astype(jnp.int32)
            return tile

        lax.fori_loop(0, z.n, follow, jnp.int32(-1))
        rt[z.ENDS] = ends_ref[0]
        rt[z.ENDS + 1] = ends_ref[1]


def smem():
    return pl.BlockSpec(memory_space=pltpu.SMEM)


def vmem():
    return pl.BlockSpec(memory_space=pltpu.VMEM)


def routing(z, sel, ends):
    shape = jax.ShapeDtypeStruct((z.route,), jnp.int32)
    return pl.pallas_call(
        functools.partial(routing_kernel, z),
        out_shape=(shape, shape),
        in_specs=[smem(), smem()],
        out_specs=(smem(), smem()),
        scratch_shapes=[
            pltpu.SMEM((z.n,), jnp.int32),
            pltpu.SMEM((max(z.slots + 1, z.S),), jnp.int32),
        ],
        name="routing",
    )(sel, ends)


def to_tensor(step, me):
    return {"tensor": partner(me, step)}


def remote(src, dst, send, recv, target):
    return pltpu.make_async_remote_copy(
        src_ref=src, dst_ref=dst, send_sem=send, recv_sem=recv, device_id=target, device_id_type=MESH
    )


def forward_kernel(
    z,
    rt,
    r_ref,
    vec_ref,
    w1_ref,
    swt_ref,
    wo_ref,
    wup_ref,
    wdn_ref,
    n1_ref,
    q_ref,
    kvt_ref,
    st_ref,
    p_ref,
    ckv_ref,
    o_ref,
    mid_ref,
    n2_ref,
    u_ref,
    act_ref,
    res_ref,
    gt_ref,
    gate_ref,
    edge_ref,
    edge_gate_ref,
    send_kv,
    send_gate,
    got_gate,
    far_gate_ref,
    wo_all,
    o_all,
    part_send,
    part_got,
    own_part,
    kv_ss,
    kv_rs,
    gate_ss,
    gate_rs,
    edge_ss,
    edge_rs,
    wo_ss,
    wo_rs,
    o_ss,
    o_rs,
    part_ss,
    part_rs,
    res_ss,
    res_rs,
):
    me, at = lax.axis_index("tensor"), lax.axis_index("seq")
    last = z.S - 1
    first_row = at * z.rows
    barrier = pltpu.get_barrier_semaphore()
    ckv_ref[at * z.cap] = jnp.zeros((TILE, LANES), BF)
    for step in range(1, z.T):
        pl.semaphore_signal(barrier, inc=1, device_id=to_tensor(step, me), device_id_type=MESH)

    def greet(d, _):
        pl.semaphore_signal(barrier, inc=1, device_id={"seq": d}, device_id_type=MESH)
        return 0

    lax.fori_loop(0, at, greet, 0)
    pl.semaphore_wait(barrier, z.T - 1 + last - at)

    def wo_copy(step):
        return remote(
            wo_ref, wo_all.at[me], wo_ss.at[step], wo_rs.at[step], to_tensor(step, me)
        )

    for step in range(1, z.T):
        wo_copy(step).start()
    wo_all[me] = wo_ref[...]

    per_block = z.block // TILE

    def project(b, _):
        rows = pl.ds(b * z.block, z.block)
        y, _ = normed(r_ref[rows, :].astype(F32))
        n1 = (y * vec_ref[0:1, :] + vec_ref[1:2, :]).astype(BF)
        n1_ref[rows, :] = n1
        qkv = (nn(n1, w1_ref[...]) + vec_ref[2:3, :]).astype(BF)
        q_ref[rows, :] = qkv[:, : z.pad]
        for h in range(z.heads):
            pairs = qkv[:, z.pad + h * LANES : z.pad + (h + 1) * LANES]
            kvt_ref[pl.ds(h * (z.tiles + 1) + 1 + b * per_block, per_block)] = pairs.reshape(
                per_block, TILE, LANES
            )
        return 0

    lax.fori_loop(0, z.T, project, 0)
    score = nt(swt_ref[...], n1_ref[...])[0:8]
    st_ref[...] = score
    gate = jnp.minimum(score, 0.0) - jnp.log1p(jnp.exp(-jnp.abs(score)))
    gt_ref[:, 0:LANES] = jnp.zeros((8, LANES), F32)
    gt_ref[:, LANES : LANES + z.rows] = gate.astype(BF).astype(F32)
    gt_ref[:, LANES + z.rows :] = jnp.zeros((8, LANES), F32)
    for t in range(z.tiles + 1):
        for h in range(z.heads):
            gate_ref[h * (z.tiles + 1) + t, 0:1, :] = gt_ref[
                h : h + 1, TILE + t * TILE : TILE + t * TILE + LANES
            ]

    def edge_copies():
        after = {"seq": jnp.minimum(at + 1, last)}
        return [
            remote(
                kvt_ref.at[h * (z.tiles + 1) + z.tiles],
                edge_ref.at[h],
                edge_ss.at[h],
                edge_rs.at[h],
                after,
            )
            for h in range(z.heads)
        ] + [
            remote(
                gt_ref.at[:, pl.ds(z.rows, LANES)],
                edge_gate_ref,
                edge_ss.at[z.heads],
                edge_rs.at[z.heads],
                after,
            )
        ]

    @pl.when(at < last)
    def _():
        for copy in edge_copies():
            copy.start()

    def tile_copies(d, source):
        return (
            remote(
                send_kv.at[d],
                ckv_ref.at[pl.ds(source * z.cap, z.cap)],
                kv_ss.at[d],
                kv_rs.at[source],
                {"seq": d},
            ),
            remote(send_gate.at[d], got_gate.at[source], gate_ss.at[d], gate_rs.at[source], {"seq": d}),
        )

    def pack(d, _):
        def slot(s, _):
            u = rt[z.SEND + d * z.cap + s]
            send_kv[d, s] = kvt_ref[u]
            send_gate[d, pl.ds(s, 1), :] = gate_ref[u][0:1]
            return 0

        lax.fori_loop(0, z.cap, slot, 0)
        for copy in tile_copies(d, at):
            copy.start()
        return 0

    lax.fori_loop(at + 1, z.S, pack, 0)

    def landed(source, _):
        for copy in tile_copies(last, source):
            copy.wait_recv()
        for s in range(z.cap):
            far_gate_ref[source * z.cap + s, 0:1, :] = got_gate[source, s : s + 1, :]
        return 0

    lax.fori_loop(0, at, landed, 0)
    lane = lax.broadcasted_iota(jnp.int32, (TILE, LANES), 1)
    row = lax.broadcasted_iota(jnp.int32, (TILE, LANES), 0)

    for h in range(z.heads):
        kvt_ref[h * (z.tiles + 1)] = jnp.zeros((TILE, LANES), BF)

    @pl.when(at > 0)
    def _():
        for copy in edge_copies():
            copy.wait_recv()
        for h in range(z.heads):
            kvt_ref[h * (z.tiles + 1)] = edge_ref[h]
            gate_ref[h * (z.tiles + 1), 0:1, :] = jnp.where(
                lane[0:1] < TILE,
                pltpu.roll(edge_gate_ref[...], TILE, 1)[h : h + 1],
                gate_ref[h * (z.tiles + 1), 0:1, :],
            )

    def attend(t):
        base = pl.multiple_of(t * TILE, TILE)
        query = first_row + base + row
        begin = jnp.where(
            query >= rt[z.ENDS + 1],
            rt[z.ENDS + 1],
            jnp.where(query >= rt[z.ENDS], rt[z.ENDS], 0),
        )
        key = first_row + base - TILE + lane
        near_ok = (key <= query) & (key > query - TILE) & (key >= begin)
        mixed = []
        for h in range(z.heads):
            cols = slice(h * LANES, (h + 1) * LANES)
            u = h * z.tiles + t
            arrived = rt[z.ARR + u]
            query_tile = q_ref[pl.ds(base, TILE), cols]
            near = kvt_ref[pl.ds(h * (z.tiles + 1) + t, 2)].reshape(2 * TILE, LANES)
            far = ckv_ref[arrived]
            near_score = nt(query_tile, near) + gate_ref[h * (z.tiles + 1) + t, 0:1, :]
            far_score = nt(query_tile, jnp.concatenate([far, far], axis=0)) + far_gate_ref[arrived][0:1]
            far_ok = (rt[z.POS + u] + lane >= begin) & (lane < TILE)
            near_score = jnp.where(near_ok, near_score, MASKED)
            far_score = jnp.where(far_ok, far_score, MASKED)
            top = jnp.max(jnp.maximum(near_score, far_score), axis=-1, keepdims=True)
            near_exp = jnp.exp(near_score - top)
            far_exp = jnp.exp(far_score - top)
            scale = 1.0 / jnp.sum(near_exp + far_exp, axis=-1, keepdims=True)
            near_p = (near_exp * scale).astype(BF)
            far_p = (far_exp * scale).astype(BF)
            p_ref[t * z.heads + h, :, 0:LANES] = near_p
            p_ref[t * z.heads + h, :, LANES:] = far_p
            mixed.append(nn(near_p, near) + nn(far_p[:, :TILE], far))
        pair = jnp.where(lane < TILE, pltpu.roll(mixed[0], TILE, 1), mixed[1]).astype(BF)
        single = pltpu.roll(mixed[2], TILE, 1).astype(BF)
        o_ref[pl.ds(base, TILE), 0:LANES] = pair
        o_ref[pl.ds(base, TILE), LANES:] = single

    def o_copy(step, b):
        rows = pl.ds(b * z.block, z.block)
        return remote(
            o_ref.at[rows, :],
            o_all.at[me, rows, :],
            o_ss.at[step * z.T + b],
            o_rs.at[step * z.T + b],
            to_tensor(step, me),
        )

    def attend_block(b, _):
        def pair(i, _):
            attend(b * per_block + 2 * i)
            attend(b * per_block + 2 * i + 1)
            return 0

        lax.fori_loop(0, per_block // 2, pair, 0)
        for step in range(1, z.T):
            o_copy(step, b).start()
        rows = pl.ds(b * z.block, z.block)
        o_all[me, rows, :] = o_ref[rows, :]
        return 0

    lax.fori_loop(0, z.T, attend_block, 0)
    for step in range(1, z.T):
        wo_copy(step).wait()

    def part_copy(step):
        return remote(
            part_send.at[step - 1],
            part_got.at[step - 1],
            part_ss.at[step - 1],
            part_rs.at[step - 1],
            to_tensor(step, me),
        )

    def feed(k, _):
        step = (k + 1) % z.T
        block = partner(me, step)
        rows = pl.ds(pl.multiple_of(block * z.block, z.block), z.block)
        for other in range(1, z.T):
            o_copy(other, block).wait_recv()
        mixed = nn(o_all[0, rows, :], wo_all[0])
        for other in range(1, z.T):
            mixed += nn(o_all[other, rows, :], wo_all[other])
        middle = r_ref[rows, :].astype(F32) + mixed + vec_ref[3:4, :]
        mid_ref[...] = middle
        y, _ = normed(middle)
        n2 = (y * vec_ref[4:5, :] + vec_ref[5:6, :]).astype(BF)
        n2_ref[rows, :] = n2
        u = nn(n2, wup_ref[...]) + vec_ref[6:7, :]
        u_ref[rows, :] = u.astype(BF)
        act = (0.5 * u * (1.0 + jnp.tanh(GELU_K * (u + GELU_A * u * u * u)))).astype(BF)
        act_ref[rows, :] = act
        own_part[...] = nn(act, wdn_ref[...])

        @pl.when(step > 0)
        def _():
            part_send[step - 1] = own_part[...].astype(BF)
            part_copy(step).start()

        return 0

    lax.fori_loop(0, z.T, feed, 0)
    total = mid_ref[...] + own_part[...] + vec_ref[7:8, :]
    for step in range(1, z.T):
        part_copy(step).wait_recv()
        total += part_got[step - 1].astype(F32)
    own_rows = pl.ds(pl.multiple_of(me * z.block, z.block), z.block)
    res_ref[own_rows, :] = total.astype(BF)

    def res_copy(step):
        return remote(
            res_ref.at[own_rows, :],
            res_ref.at[own_rows, :],
            res_ss.at[step],
            res_rs.at[step],
            to_tensor(step, me),
        )

    for step in range(1, z.T):
        res_copy(step).start()
    for step in range(1, z.T):
        part_copy(step).wait_send()
        for b in range(z.T):
            o_copy(step, b).wait_send()

    def sent(d, _):
        for copy in tile_copies(d, at):
            copy.wait_send()
        return 0

    lax.fori_loop(at + 1, z.S, sent, 0)

    @pl.when(at < last)
    def _():
        for copy in edge_copies():
            copy.wait_send()

    for step in range(1, z.T):
        res_copy(step).wait()


def forward(z, ident, route, r, w):
    rows, width, heads = z.rows, z.width, z.heads
    shapes = dict(
        n1=((rows, width), BF),
        q=((rows, z.pad), BF),
        kvt=((heads * (z.tiles + 1), TILE, LANES), BF),
        st=((8, rows), F32),
        p=((z.slots, TILE, 2 * LANES), BF),
        ckv=((z.n, TILE, LANES), BF),
        o=((rows, 2 * LANES), BF),
        mid=((z.block, width), F32),
        n2=((rows, width), BF),
        u=((rows, z.hidden), BF),
        act=((rows, z.hidden), BF),
        res=((rows, width), BF),
    )
    dma = pltpu.SemaphoreType.DMA
    outs = pl.pallas_call(
        functools.partial(forward_kernel, z),
        out_shape=tuple(jax.ShapeDtypeStruct(*s) for s in shapes.values()),
        in_specs=[smem()] + [vmem()] * 7,
        out_specs=tuple(vmem() for _ in shapes),
        scratch_shapes=[
            pltpu.VMEM((8, rows + 2 * LANES), F32),
            pltpu.VMEM((heads * (z.tiles + 1), 8, LANES), F32),
            pltpu.VMEM((heads, TILE, LANES), BF),
            pltpu.VMEM((8, LANES), F32),
            pltpu.VMEM((z.S, z.cap, TILE, LANES), BF),
            pltpu.VMEM((z.S, z.capg, LANES), F32),
            pltpu.VMEM((z.S, z.capg, LANES), F32),
            pltpu.VMEM((z.n, 8, LANES), F32),
            pltpu.VMEM((z.T, 2 * LANES, width), BF),
            pltpu.VMEM((z.T, rows, 2 * LANES), BF),
            pltpu.VMEM((z.T - 1, z.block, width), BF),
            pltpu.VMEM((z.T - 1, z.block, width), BF),
            pltpu.VMEM((z.block, width), F32),
            dma((z.S,)),
            dma((z.S,)),
            dma((z.S,)),
            dma((z.S,)),
            dma((heads + 1,)),
            dma((heads + 1,)),
            dma((z.T,)),
            dma((z.T,)),
            dma((z.T * z.T,)),
            dma((z.T * z.T,)),
            dma((z.T,)),
            dma((z.T,)),
            dma((z.T,)),
            dma((z.T,)),
        ],
        compiler_params=pltpu.CompilerParams(
            collective_id=ident, has_side_effects=True, vmem_limit_bytes=LIMIT
        ),
        name=f"forward{ident}",
    )(route, r, w["vec"], w["w1"], w["swt"], w["wo"], w["wup"], w["wdn"])
    return dict(zip(shapes, outs))


def backward_kernel(
    z,
    rt,
    c_ref,
    r_ref,
    vec_ref,
    w1_ref,
    swt_ref,
    wop_ref,
    wup_ref,
    wdn_ref,
    n1_ref,
    q_ref,
    kvt_ref,
    st_ref,
    p_ref,
    ckv_ref,
    o_ref,
    mid_ref,
    n2_ref,
    u_ref,
    act_ref,
    grad_ref,
    g_ref,
    ib_ref,
    du_ref,
    part_send,
    part_got,
    own_part,
    dr2_ref,
    ob_ref,
    dout_ref,
    dqkv_ref,
    dkvx_ref,
    dgate_ref,
    far_ref,
    far_gate_ref,
    send_kv,
    send_gate,
    got_kv,
    got_gate,
    got_gate_ref,
    edge_send,
    edge_got,
    edge_gate_got,
    sum_ref,
    gate_sum_ref,
    tile_gate_ref,
    ds_ref,
    stat_ref,
    stat_got,
    kv_ss,
    kv_rs,
    gate_ss,
    gate_rs,
    edge_ss,
    edge_rs,
    part_ss,
    part_rs,
    ob_ss,
    ob_rs,
    grad_ss,
    grad_rs,
    stat_ss,
    stat_rs,
):
    me, at = lax.axis_index("tensor"), lax.axis_index("seq")
    last = z.S - 1
    barrier = pltpu.get_barrier_semaphore()
    for step in range(1, z.T):
        pl.semaphore_signal(barrier, inc=1, device_id=to_tensor(step, me), device_id_type=MESH)

    def greet(d, _):
        pl.semaphore_signal(barrier, inc=1, device_id={"seq": d}, device_id_type=MESH)
        return 0

    lax.fori_loop(at + 1, z.S, greet, 0)
    pl.semaphore_wait(barrier, z.T - 1 + at)
    own_rows = pl.ds(pl.multiple_of(me * z.block, z.block), z.block)
    W, FFD = z.width, z.hidden
    C_O = 2 * z.pad
    C_U = C_O + 2 * LANES
    C_D = C_U + FFD
    C_S = C_D + FFD

    def part_copy(step, phase):
        return remote(
            part_send.at[phase, step - 1],
            part_got.at[phase, step - 1],
            part_ss.at[phase, step],
            part_rs.at[phase, step],
            to_tensor(step, me),
        )

    def ff_back(k, _):
        step = (k + 1) % z.T
        rows = pl.ds(pl.multiple_of(partner(me, step) * z.block, z.block), z.block)
        u = u_ref[rows, :].astype(F32)
        squared = u * u
        bent = jnp.tanh(GELU_K * (u + GELU_A * squared * u))
        slope = 0.5 * (1.0 + bent) + 0.5 * u * (1.0 - bent * bent) * (
            GELU_K * (1.0 + 3.0 * GELU_A * squared)
        )
        du = (nt(c_ref[rows, :], wdn_ref[...]) * slope).astype(BF)
        du_ref[rows, :] = du
        own_part[...] = nt(du, wup_ref[...])

        @pl.when(step > 0)
        def _():
            part_send[0, step - 1] = own_part[...].astype(BF)
            part_copy(step, 0).start()

        return 0

    lax.fori_loop(0, z.T, ff_back, 0)
    ones = jnp.ones((16, z.rows), BF)
    stat_ref[...] = jnp.zeros((24, W), F32)
    g_ref[:, C_D:C_S] = tn(c_ref[...], act_ref[...]).astype(BF)
    g_ref[:, C_U:C_D] = tn(n2_ref[...], du_ref[...]).astype(BF)
    stat_ref[8:9, :] = nn(ones, du_ref[...])[0:1]
    stat_ref[9:10, :] = nn(ones, c_ref[...])[0:1]
    grad = own_part[...]
    for step in range(1, z.T):
        part_copy(step, 0).wait_recv()
        grad += part_got[0, step - 1].astype(F32)
    y, spread = normed(mid_ref[...])
    dr2 = c_ref[own_rows, :].astype(F32) + norm_back(grad, vec_ref[4:5, :], y, spread)
    dr2_ref[...] = dr2
    stat_ref[0:1, :] = column_sum(dr2)
    stat_ref[1:2, :] = column_sum(grad * y)
    stat_ref[2:3, :] = column_sum(grad)
    ob_ref[own_rows, :] = dr2.astype(BF)

    def rows_copy(ref, sends, recvs, step):
        return remote(
            ref.at[own_rows, :], ref.at[own_rows, :], sends.at[step], recvs.at[step], to_tensor(step, me)
        )

    for step in range(1, z.T):
        rows_copy(ob_ref, ob_ss, ob_rs, step).start()
    dkvx_ref[...] = jnp.zeros((z.rows + TILE, z.pad), F32)

    def out_back(step, _):
        @pl.when(step > 0)
        def _():
            rows_copy(ob_ref, ob_ss, ob_rs, step).wait_recv()

        rows = pl.ds(pl.multiple_of(partner(me, step) * z.block, z.block), z.block)
        dout_ref[rows, :] = nt(ob_ref[rows, :], wop_ref[...]).astype(BF)
        return 0

    lax.fori_loop(0, z.T, out_back, 0)

    def attend_back(t):
        base = pl.multiple_of(t * TILE, TILE)
        for h in range(z.heads):
            cols = slice(h * LANES, (h + 1) * LANES)
            u = h * z.tiles + t
            arrived = rt[z.ARR + u]
            near = kvt_ref[pl.ds(h * (z.tiles + 1) + t, 2)].reshape(2 * TILE, LANES)
            far = ckv_ref[arrived]
            query = q_ref[pl.ds(base, TILE), cols]
            dout = dout_ref[pl.ds(base, TILE), cols]
            near_p = p_ref[t * z.heads + h, :, 0:LANES]
            far_p = p_ref[t * z.heads + h, :, LANES : LANES + TILE]
            near_pf, far_pf = near_p.astype(F32), far_p.astype(F32)
            near_dp, far_dp = nt(dout, near), nt(dout, far)
            total = jnp.sum(near_pf * near_dp, axis=-1, keepdims=True) + jnp.sum(
                far_pf * far_dp, axis=-1, keepdims=True
            )
            near_dz = (near_pf * (near_dp - total)).astype(BF)
            far_dz = (far_pf * (far_dp - total)).astype(BF)
            dqkv_ref[pl.ds(base, TILE), cols] = (nn(near_dz, near) + nn(far_dz, far)).astype(BF)
            dkvx_ref[pl.ds(base, 2 * TILE), cols] += tn(near_dz, query) + tn(near_p, dout)
            far_ref[u] = (tn(far_dz, query) + tn(far_p, dout)).astype(BF)
            dgate_ref[t, h : h + 1, :] = column_sum(near_dz.astype(F32))
            far_gate_ref[u, 0:1, 0:TILE] = column_sum(far_dz.astype(F32))

    def attend_back_pair(i, _):
        attend_back(2 * i)
        attend_back(2 * i + 1)
        return 0

    lax.fori_loop(0, z.tiles // 2, attend_back_pair, 0)
    dgate_ref[z.tiles] = jnp.zeros((8, LANES), F32)

    def edge_copies():
        return (
            remote(
                edge_send, edge_got, edge_ss.at[0], edge_rs.at[0], {"seq": jnp.maximum(at - 1, 0)}
            ),
            remote(
                dgate_ref.at[0],
                edge_gate_got,
                edge_ss.at[1],
                edge_rs.at[1],
                {"seq": jnp.maximum(at - 1, 0)},
            ),
        )

    @pl.when(at > 0)
    def _():
        edge_send[...] = dkvx_ref[0:TILE, :].astype(BF)
        for copy in edge_copies():
            copy.start()

    def tile_copies(d, source):
        return (
            remote(send_kv.at[d], got_kv.at[pl.ds(source * z.cap, z.cap)], kv_ss.at[d], kv_rs.at[source], {"seq": d}),
            remote(send_gate.at[d], got_gate.at[source], gate_ss.at[d], gate_rs.at[source], {"seq": d}),
        )

    def pack(d, _):
        def slot(s, _):
            u = rt[z.INV + d * z.cap + s]
            send_kv[d, s] = far_ref[u]
            send_gate[d, pl.ds(s, 1), :] = far_gate_ref[u][0:1]
            return 0

        lax.fori_loop(0, z.cap, slot, 0)
        for copy in tile_copies(d, at):
            copy.start()
        return 0

    lax.fori_loop(0, at, pack, 0)
    g_ref[:, C_O:C_U] = tn(ob_ref[...], o_ref[...]).astype(BF)
    sum_ref[z.n] = jnp.zeros((TILE, LANES), F32)
    gate_sum_ref[z.n] = jnp.zeros((8, LANES), F32)

    @pl.when(at < last)
    def _():
        for copy in edge_copies():
            copy.wait_recv()
        dkvx_ref[pl.ds(z.rows, TILE), :] += edge_got[...].astype(F32)
        dgate_ref[z.tiles] = edge_gate_got[...]

    def landed(source, _):
        for copy in tile_copies(0, source):
            copy.wait_recv()
        for s in range(z.cap):
            got_gate_ref[source * z.cap + s, 0:1, :] = got_gate[source, s : s + 1, :]
        return 0

    lax.fori_loop(at + 1, z.S, landed, 0)

    def gather(k, carry):
        running, gates = carry
        index = rt[z.ORD + k]
        joined = rt[z.CONT + k].astype(F32)
        running = running * joined + got_kv[index].astype(F32)
        gates = gates * joined + got_gate_ref[index]
        sum_ref[k] = running
        gate_sum_ref[k] = gates
        return running, gates

    lax.fori_loop(0, z.n, gather, (jnp.zeros((TILE, LANES), F32), jnp.zeros((8, LANES), F32)))

    def settle(t, _):
        base = pl.multiple_of((t + 1) * TILE, TILE)
        for h in range(z.heads):
            cols = slice(h * LANES, (h + 1) * LANES)
            index = rt[z.LAST + h * z.tiles + t]
            dqkv_ref[pl.ds(pl.multiple_of(t * TILE, TILE), TILE), slice(z.pad + h * LANES, z.pad + (h + 1) * LANES)] = (
                dkvx_ref[pl.ds(base, TILE), cols] + sum_ref[index]
            ).astype(BF)
            tile_gate_ref[t, h : h + 1, :] = gate_sum_ref[index][0:1]
        return 0

    lax.fori_loop(0, z.tiles, settle, 0)
    lane = lax.broadcasted_iota(jnp.int32, (8, LANES), 1)
    head_row = lax.broadcasted_iota(jnp.int32, (8, LANES), 0)
    for k in range(z.tiles // 2):
        halves = []
        for t in (2 * k, 2 * k + 1):
            halves.append(pltpu.roll(dgate_ref[t], TILE, 1) + dgate_ref[t + 1] + tile_gate_ref[t])
        both = jnp.where(lane < TILE, halves[0], pltpu.roll(halves[1], TILE, 1))
        score = st_ref[:, k * LANES : (k + 1) * LANES]
        grads = jnp.where(head_row < z.heads, both / (1.0 + jnp.exp(score)), 0.0)
        ds_ref[0:8, k * LANES : (k + 1) * LANES] = grads
        ds_ref[8:16, k * LANES : (k + 1) * LANES] = jnp.zeros((8, LANES), F32)

    def in_back(k, _):
        step = (k + 1) % z.T
        begin = pl.multiple_of(partner(me, step) * z.block, z.block)
        rows = pl.ds(begin, z.block)
        own_part[...] = nt(dqkv_ref[rows, :], w1_ref[...]) + tn(
            ds_ref[:, rows].astype(BF), swt_ref[...]
        )

        @pl.when(step > 0)
        def _():
            part_send[1, step - 1] = own_part[...].astype(BF)
            part_copy(step, 1).start()

        return 0

    lax.fori_loop(0, z.T, in_back, 0)
    g_ref[:, 0:C_O] = tn(n1_ref[...], dqkv_ref[...]).astype(BF)
    stat_ref[10:13, :] = nn(ds_ref[...].astype(BF), n1_ref[...])[0:3]
    ib_ref[...] = nn(ones, dqkv_ref[...])[0:8]
    grad = own_part[...]
    for step in range(1, z.T):
        part_copy(step, 1).wait_recv()
        grad += part_got[1, step - 1].astype(F32)
    y, spread = normed(r_ref[own_rows, :].astype(F32))
    dr = dr2_ref[...] + norm_back(grad, vec_ref[0:1, :], y, spread)
    grad_ref[own_rows, :] = dr.astype(BF)
    for step in range(1, z.T):
        rows_copy(grad_ref, grad_ss, grad_rs, step).start()
    stat_ref[3:4, :] = column_sum(grad * y)
    stat_ref[4:5, :] = column_sum(grad)

    def stat_copy(step):
        return remote(
            stat_ref.at[pl.ds(0, 8), :],
            stat_got.at[step - 1],
            stat_ss.at[step],
            stat_rs.at[step],
            to_tensor(step, me),
        )

    for step in range(1, z.T):
        stat_copy(step).start()
    shared = stat_ref[0:8, :]
    for step in range(1, z.T):
        stat_copy(step).wait()
        shared += stat_got[step - 1]
    stats = jnp.concatenate([shared, stat_ref[8:16, :]], axis=0).astype(BF)
    unit = (
        lax.broadcasted_iota(jnp.int32, (16, LANES), 0)
        == lax.broadcasted_iota(jnp.int32, (16, LANES), 1)
    ).astype(F32).astype(BF)
    g_ref[:, C_S:] = tn(stats, unit).astype(BF)
    for step in range(1, z.T):
        for phase in range(2):
            part_copy(step, phase).wait_send()
        rows_copy(ob_ref, ob_ss, ob_rs, step).wait_send()

    def sent(d, _):
        for copy in tile_copies(d, at):
            copy.wait_send()
        return 0

    lax.fori_loop(0, at, sent, 0)

    @pl.when(at > 0)
    def _():
        for copy in edge_copies():
            copy.wait_send()

    for step in range(1, z.T):
        rows_copy(grad_ref, grad_ss, grad_rs, step).wait()


def backward(z, ident, route, c, r, w, kept):
    rows, width = z.rows, z.width
    columns = 2 * z.pad + 2 * LANES + 2 * z.hidden + LANES
    dma = pltpu.SemaphoreType.DMA
    names = ("n1", "q", "kvt", "st", "p", "ckv", "o", "mid", "n2", "u", "act")
    return pl.pallas_call(
        functools.partial(backward_kernel, z),
        out_shape=(
            jax.ShapeDtypeStruct((rows, width), BF),
            jax.ShapeDtypeStruct((width, columns), BF),
            jax.ShapeDtypeStruct((8, 2 * z.pad), F32),
        ),
        in_specs=[smem()] + [vmem()] * 19,
        out_specs=(vmem(), vmem(), vmem()),
        scratch_shapes=[
            pltpu.VMEM((rows, z.hidden), BF),
            pltpu.VMEM((2, z.T - 1, z.block, width), BF),
            pltpu.VMEM((2, z.T - 1, z.block, width), BF),
            pltpu.VMEM((z.block, width), F32),
            pltpu.VMEM((z.block, width), F32),
            pltpu.VMEM((rows, width), BF),
            pltpu.VMEM((rows, z.pad), BF),
            pltpu.VMEM((rows, 2 * z.pad), BF),
            pltpu.VMEM((rows + TILE, z.pad), F32),
            pltpu.VMEM((z.tiles + 1, 8, LANES), F32),
            pltpu.VMEM((z.slots, TILE, LANES), BF),
            pltpu.VMEM((z.slots, 8, LANES), F32),
            pltpu.VMEM((z.S, z.cap, TILE, LANES), BF),
            pltpu.VMEM((z.S, z.capg, LANES), F32),
            pltpu.VMEM((z.n, TILE, LANES), BF),
            pltpu.VMEM((z.S, z.capg, LANES), F32),
            pltpu.VMEM((z.n, 8, LANES), F32),
            pltpu.VMEM((TILE, z.pad), BF),
            pltpu.VMEM((TILE, z.pad), BF),
            pltpu.VMEM((8, LANES), F32),
            pltpu.VMEM((z.n + 1, TILE, LANES), F32),
            pltpu.VMEM((z.n + 1, 8, LANES), F32),
            pltpu.VMEM((z.tiles, 8, LANES), F32),
            pltpu.VMEM((16, rows), F32),
            pltpu.VMEM((24, width), F32),
            pltpu.VMEM((z.T - 1, 8, width), F32),
            dma((z.S,)),
            dma((z.S,)),
            dma((z.S,)),
            dma((z.S,)),
            dma((2,)),
            dma((2,)),
            dma((2, z.T)),
            dma((2, z.T)),
            dma((z.T,)),
            dma((z.T,)),
            dma((z.T,)),
            dma((z.T,)),
            dma((z.T,)),
            dma((z.T,)),
        ],
        compiler_params=pltpu.CompilerParams(
            collective_id=ident, has_side_effects=True, vmem_limit_bytes=LIMIT
        ),
        name=f"backward{ident}",
    )(
        route,
        c,
        r,
        w["vec"],
        w["w1"],
        w["swt"],
        w["wop"],
        w["wup"],
        w["wdn"],
        *(kept[name] for name in names),
    )


def swapped(value):
    return lax.ppermute(value, "section", [(0, 1), (1, 0)])


def body(
    tokens,
    cotangent,
    lengths,
    selected,
    input_weight,
    input_bias,
    score_weight,
    output_weight,
    output_bias,
    up_weight,
    up_bias,
    down_weight,
    down_bias,
    norm_gain,
    norm_bias,
):
    core = lax.axis_index("section")
    _, rows, width = tokens.shape
    heads, hidden = score_weight.shape[2], up_weight.shape[2]
    head = input_weight.shape[3] // heads
    inner = heads * head
    z = Sizes(lax.axis_size("tensor"), lax.axis_size("seq"), rows, width, heads, hidden)
    scale = head**-0.5
    split = input_weight[0].reshape(width, 3, heads, head)
    w1 = jnp.concatenate(
        [
            jnp.concatenate([split[:, 0] * BF(scale), jnp.zeros_like(split[:, 0])], axis=-1).reshape(
                width, z.pad
            ),
            jnp.concatenate([split[:, 1], split[:, 2]], axis=-1).reshape(width, z.pad),
        ],
        axis=1,
    )
    shift = input_bias[0].astype(F32).reshape(2, heads, head)
    nothing = jnp.zeros((heads, head), F32)
    b1 = jnp.concatenate(
        [
            jnp.concatenate([shift[0] * scale, nothing], axis=-1).reshape(1, z.pad),
            jnp.concatenate([nothing, shift[1]], axis=-1).reshape(1, z.pad),
        ],
        axis=1,
    )
    vec = jnp.concatenate(
        [
            norm_gain[0, 0:1].astype(F32),
            norm_bias[0, 0:1].astype(F32),
            b1,
            output_bias.astype(F32),
            norm_gain[0, 1:2].astype(F32),
            norm_bias[0, 1:2].astype(F32),
            up_bias.astype(F32),
            down_bias.astype(F32),
        ],
        axis=0,
    )
    swt = jnp.pad(score_weight[0].T, ((0, 16 - heads), (0, 0)))
    wo = jnp.pad(output_weight[0], ((0, 2 * LANES - inner), (0, 0)))
    wop = jnp.pad(output_weight[0].reshape(heads, head, width), ((0, 0), (LANES - head, 0), (0, 0))).reshape(
        z.pad, width
    )
    mine = dict(vec=vec, w1=w1, swt=swt, wo=wo, wop=wop, wup=up_weight[0], wdn=down_weight[0])
    theirs = {name: swapped(value) for name, value in mine.items()}
    layers = [
        {name: jnp.where(core == layer, mine[name], theirs[name]) for name in mine} for layer in range(2)
    ]
    given = lax.dynamic_index_in_dim(selected[0], 1 - core, 0, keepdims=False)
    kept_choice = lax.dynamic_index_in_dim(selected[0], core, 0, keepdims=False)
    got_choice = swapped(given)
    choice = jnp.where(
        core == 0, jnp.stack([kept_choice, got_choice]), jnp.stack([got_choice, kept_choice])
    )
    length = lax.dynamic_index_in_dim(lengths, core, 0, keepdims=False)
    ends = jnp.stack([length[0], length[0] + length[1]])
    routes = routing(z, choice, ends)
    first = lax.dynamic_index_in_dim(tokens, core, 0, keepdims=False)
    cotan = lax.dynamic_index_in_dim(cotangent, core, 0, keepdims=False)
    zero = forward(z, 0, routes[0], first, layers[0])
    one = forward(z, 1, routes[1], zero["res"], layers[1])
    grad1, g1, ib1 = backward(z, 2, routes[1], cotan, zero["res"], layers[1], one)
    grad0, g0, ib0 = backward(z, 3, routes[0], grad1, first, layers[0], zero)

    def both(layer0, layer1):
        own = jnp.where(core == 0, layer0, layer1)
        other = swapped(jnp.where(core == 0, layer1, layer0))
        return jnp.where(core == 0, jnp.stack([own, other]), jnp.stack([other, own]))[None]

    def added(layer0, layer1):
        own = jnp.where(core == 0, layer0, layer1).astype(F32)
        other = swapped(jnp.where(core == 0, layer1, layer0)).astype(F32)
        return own + other

    layer_out = both(zero["res"], one["res"])
    input_grad = both(grad0, grad1)
    total = lax.psum_scatter(
        added(g0, g1).astype(BF), "seq", scatter_dimension=0, tiled=True
    ).astype(F32)
    bias = added(ib0, ib1)[0]
    bias = jnp.stack(
        [
            scale * bias[: z.pad].reshape(heads, LANES)[:, :head].reshape(inner),
            bias[z.pad :].reshape(heads, LANES)[:, head:].reshape(inner),
        ]
    )
    bias = lax.psum_scatter(bias.astype(BF), "seq", scatter_dimension=1, tiled=True).astype(F32)
    share = total.shape[0]
    c_o = 2 * z.pad
    c_u = c_o + 2 * LANES
    c_d = c_u + hidden
    c_s = c_d + hidden
    queries = total[:, : z.pad].reshape(share, heads, LANES)
    pairs = total[:, z.pad : c_o].reshape(share, heads, LANES)
    input_weight_grad = jnp.stack(
        [
            scale * queries[:, :, :head].reshape(share, inner),
            pairs[:, :, :head].reshape(share, inner),
            pairs[:, :, head:].reshape(share, inner),
        ],
        axis=1,
    )
    stats = total[:, c_s : c_s + 16].T
    return (
        layer_out,
        input_grad,
        input_weight_grad[None],
        bias[None],
        total[:, c_s + 10 : c_s + 10 + heads][None],
        total[:, c_o : c_o + inner].T[None],
        stats[0][None],
        total[:, c_u:c_d][None],
        stats[8][None],
        total[:, c_d:c_s].T[None],
        stats[9][None],
        jnp.stack([stats[3], stats[1]])[None],
        jnp.stack([stats[4], stats[2]])[None],
    )


def solution(mesh):
    return jax.shard_map(
        body,
        mesh=mesh,
        in_specs=(
            P(None, "seq", None),
            P(None, "seq", None),
            P(),
            P("section", None, "tensor", None),
            P("section", None, None, "tensor"),
            P("section", None, "tensor"),
            P("section", None, "tensor"),
            P("section", "tensor", None),
            P("section", None),
            P("section", None, "tensor"),
            P("section", "tensor"),
            P("section", "tensor", None),
            P("section", None),
            P("section", None, None),
            P("section", None, None),
        ),
        out_specs=(
            P("section", None, "seq", None),
            P("section", None, "seq", None),
            P("section", "seq", None, "tensor"),
            P("section", None, ("tensor", "seq")),
            P("section", "seq", "tensor"),
            P("section", "tensor", "seq"),
            P("section", "seq"),
            P("section", "seq", "tensor"),
            P("section", ("tensor", "seq")),
            P("section", "tensor", "seq"),
            P("section", "seq"),
            P("section", None, "seq"),
            P("section", None, "seq"),
        ),
        check_vma=False,
    )
```

```python
import functools
import math

import jax
import jax.numpy as jnp
from jax import lax
from jax.experimental import pallas as pl
from jax.experimental.pallas import tpu as pltpu
from jax.sharding import PartitionSpec as P

TILE = 64
LANES = 128
MASKED = -1e30
EPSILON = 1e-05
FAR = -(1 << 20)
MESH = pl.DeviceIdType.MESH
BF = jnp.bfloat16
F32 = jnp.float32
GELU_A = 0.044715
GELU_K = math.sqrt(2.0 / math.pi)
LIMIT = 60 * 1024 * 1024


class Sizes:
    def __init__(self, mesh_tensor, mesh_seq, rows, width, heads, hidden):
        self.T, self.S = mesh_tensor, mesh_seq
        self.rows, self.width, self.heads, self.hidden = rows, width, heads, hidden
        self.tiles = rows // TILE
        self.slots = heads * self.tiles
        self.cap = -(-self.slots // (mesh_seq - 1))
        self.capg = -(-self.cap // 8) * 8
        self.n = mesh_seq * self.cap
        self.block = rows // mesh_tensor
        self.pad = heads * LANES
        self.share = width // mesh_seq
        self.padded = -(-self.share // 16) * 16
        self.pieces = (hidden, LANES, self.pad)


SEND, INV, ORD, CONT, ARR, POS, LAST, ENDS = range(8)
WEIGHTS = ("vec", "w1", "swt", "wo", "wup", "wdn")
KEPT = ("n1", "q", "kvt", "st", "p", "ckv", "o", "mid", "n2", "u", "act")


def nn(a, b):
    return jnp.dot(a, b, preferred_element_type=F32)


def nt(a, b):
    return lax.dot_general(a, b, (((1,), (1,)), ((), ())), preferred_element_type=F32)


def tn(a, b):
    return lax.dot_general(a, b, (((0,), (0,)), ((), ())), preferred_element_type=F32)


def normed(x):
    centred = x - jnp.mean(x, axis=-1, keepdims=True)
    spread = lax.rsqrt(jnp.mean(centred * centred, axis=-1, keepdims=True) + EPSILON)
    return centred * spread, spread


def norm_back(grad, gain, y, spread):
    scaled = grad * gain
    return spread * (
        scaled
        - jnp.mean(scaled, axis=-1, keepdims=True)
        - y * jnp.mean(scaled * y, axis=-1, keepdims=True)
    )


def partner(me, step):
    return (me // 2 + step // 2) % 2 * 2 + (me % 2 + step % 2) % 2


def column_sum(x):
    return jnp.sum(x, axis=0, keepdims=True)


def smem():
    return pl.BlockSpec(memory_space=pltpu.SMEM)


def vmem():
    return pl.BlockSpec(memory_space=pltpu.VMEM)


def anywhere():
    return pl.BlockSpec(memory_space=pl.ANY)


def grid_of(shape, axis):
    return lax.broadcasted_iota(jnp.int32, shape, axis)


def prepare_kernel(
    z,
    ends_ref,
    sel_ref,
    win_ref,
    bin_ref,
    sw_ref,
    wout_ref,
    bout_ref,
    bup_ref,
    bdn_ref,
    gain_ref,
    shift_ref,
    vec_ref,
    w1_ref,
    swt_ref,
    wo_ref,
    rt0_ref,
    rt1_ref,
):
    inner, head = win_ref.shape[2], win_ref.shape[2] // z.heads
    row, col = grid_of((inner, z.pad), 0), grid_of((inner, z.pad), 1)
    lane_of = row // head * LANES + row % head
    first = (col == lane_of).astype(F32)
    second = (col == lane_of + head).astype(F32)
    low, high = first.astype(BF), second.astype(BF)
    scaled = (first * head**-0.5).astype(BF)
    w1_ref[:, : z.pad] = nn(win_ref[0], scaled).astype(BF)
    w1_ref[:, z.pad :] = (nn(win_ref[1], low) + nn(win_ref[2], high)).astype(BF)
    vec_ref[0:1, :] = gain_ref[...].astype(F32)[0:1]
    vec_ref[1:2, :] = shift_ref[...].astype(F32)[0:1]
    vec_ref[2:3, : z.pad] = nn(bin_ref[...], scaled)[0:1]
    vec_ref[2:3, z.pad :] = nn(bin_ref[...], high)[1:2]
    vec_ref[3:4, :] = bout_ref[...].astype(F32)
    vec_ref[4:5, :] = gain_ref[...].astype(F32)[1:2]
    vec_ref[5:6, :] = shift_ref[...].astype(F32)[1:2]
    vec_ref[6:7, :] = bup_ref[...].astype(F32)
    vec_ref[7:8, :] = bdn_ref[...].astype(F32)
    unit = (grid_of((16, z.heads), 0) == grid_of((16, z.heads), 1)).astype(F32).astype(BF)
    swt_ref[...] = nt(unit, sw_ref[...]).astype(BF)
    wo_ref[0:inner, :] = wout_ref[...]
    wo_ref[inner:, :] = jnp.zeros((2 * LANES - inner, z.width), BF)

    at = lax.axis_index("seq")
    n, slots, cap = z.n, z.slots, z.cap
    shift = z.tiles.bit_length() - 1
    near = 1e-3

    def total(mask, value, axis):
        return jnp.sum(jnp.where(mask, value, 0.0), axis=axis, keepdims=True)

    def whole(x):
        return (x + near).astype(jnp.int32)

    for layer, rt in enumerate((rt0_ref, rt1_ref)):
        rt[...] = jnp.zeros((8, LANES), jnp.int32)
        chosen = sel_ref[layer]
        owner = lax.shift_right_arithmetic(chosen, shift)
        sub, lan = grid_of((slots, n), 0), grid_of((slots, n), 1)
        wide = jnp.zeros((slots, n), jnp.int32)
        for d in range(z.S):
            column = jnp.sum(
                jnp.where(
                    grid_of((slots, slots), 0) == grid_of((slots, slots), 1),
                    chosen[d : d + 1].astype(F32) + 1.0,
                    0.0,
                ),
                axis=1,
                keepdims=True,
            )
            wide = jnp.where(lan // cap == d, whole(column) - 1, wide)
        mine = lax.shift_right_arithmetic(wide, shift) == at
        order = nn(
            (grid_of((slots, slots), 0) > grid_of((slots, slots), 1)).astype(F32), mine.astype(F32)
        )
        taken = mine & (whole(order) == lan % cap)
        head_of = sub // z.tiles
        inner_tile = wide - at * z.tiles
        rt[SEND : SEND + 1, :n] = whole(
            total(taken, (head_of * (z.tiles + 1) + inner_tile).astype(F32), 0)
        ) + 1
        present = jnp.sum(taken.astype(F32), axis=0, keepdims=True)
        key = total(taken, (head_of * z.tiles + inner_tile - slots).astype(F32), 0) + slots
        own = jnp.sum(
            jnp.where(grid_of((z.S, slots), 0) == at, chosen.astype(F32) + 1.0, 0.0), axis=0, keepdims=True
        )
        square_row, square_col = grid_of((slots, slots), 0), grid_of((slots, slots), 1)
        own_column = total(square_row == square_col, own, 1)
        own_row = whole(own) - 1
        own_col = whole(own_column) - 1
        owner_row = lax.shift_right_arithmetic(own_row, shift)
        owner_col = lax.shift_right_arithmetic(own_col, shift)
        same = owner_row == owner_col
        place_row = whole(jnp.sum((same & (square_row < square_col)).astype(F32), axis=0, keepdims=True))
        place_col = whole(jnp.sum((same & (square_col < square_row)).astype(F32), axis=1, keepdims=True))
        live = own_row >= 0
        rt[ARR : ARR + 1, :slots] = jnp.where(live, owner_row * cap + place_row, at * cap)
        rt[POS : POS + 1, :slots] = jnp.where(live, own_row * TILE, FAR)
        matched = (owner_col == lan // cap) & (place_col == lan % cap)
        rt[INV : INV + 1, :n] = whole(total(matched, sub.astype(F32), 0))
        big_row, big_col = grid_of((n, n), 0), grid_of((n, n), 1)
        key_col = total(big_row == big_col, key, 1)
        rank = jnp.sum(
            ((key < key_col) | ((key == key_col) & (big_col < big_row))).astype(F32), axis=1, keepdims=True
        )
        at_rank = whole(rank) == big_col
        rt[ORD : ORD + 1, :n] = whole(total(at_rank, big_row.astype(F32), 0))
        sorted_key = total(at_rank, key_col, 0)
        before = total(whole(rank) + 1 == big_col, key_col + 1.0, 0) - 1.0
        rt[CONT : CONT + 1, :n] = (sorted_key == before).astype(jnp.int32)
        tile = grid_of((n, slots), 1).astype(F32)
        upto = jnp.sum((key_col <= tile).astype(F32), axis=0, keepdims=True)
        has = jnp.sum((key_col == tile).astype(F32), axis=0, keepdims=True)
        rt[LAST : LAST + 1, :slots] = whole(jnp.where(has > 0.5, upto - 1.0, n * 1.0))
        rt[ENDS : ENDS + 1, :] = jnp.where(grid_of((1, LANES), 1) == 0, ends_ref[0], ends_ref[1])


def prepare(z, ends, sel, win, bin_, sw, wout, bout, bup, bdn, gain, shift):
    table = jax.ShapeDtypeStruct((8, LANES), jnp.int32)
    outs = pl.pallas_call(
        functools.partial(prepare_kernel, z),
        out_shape=(
            jax.ShapeDtypeStruct((8, z.width), F32),
            jax.ShapeDtypeStruct((z.width, 2 * z.pad), BF),
            jax.ShapeDtypeStruct((16, z.width), BF),
            jax.ShapeDtypeStruct((2 * LANES, z.width), BF),
            table,
            table,
        ),
        in_specs=[smem()] + [vmem()] * 10,
        out_specs=tuple(vmem() for _ in range(6)),
        name="prepare",
    )(ends, sel, win, bin_, sw, wout, bout, bup, bdn, gain, shift)
    return dict(zip(WEIGHTS[:4], outs)), outs[4:]


def to_tensor(step, me):
    return {"tensor": partner(me, step)}


def remote(src, dst, send, recv, target):
    return pltpu.make_async_remote_copy(
        src_ref=src, dst_ref=dst, send_sem=send, recv_sem=recv, device_id=target, device_id_type=MESH
    )


def signal(target, barrier):
    pl.semaphore_signal(barrier, inc=1, device_id=target, device_id_type=MESH)


class Saver:
    def __init__(self, sems):
        self.sems, self.copies = sems, []

    def save(self, src, dst):
        copy = pltpu.make_async_copy(src, dst, self.sems.at[len(self.copies)])
        copy.start()
        self.copies.append(copy)

    def finish(self):
        for copy in self.copies:
            copy.wait()


FORWARD_OUTS = KEPT + ("res",)
FORWARD_SCRATCH = (
    "gt", "gate", "edge", "edge_gate", "send_kv", "send_gate", "got_gate", "far_gate", "wo_all", "o_all",
    "part_send", "part_got", "own_part", "kv_ss", "kv_rs", "gate_ss", "gate_rs", "edge_ss", "edge_rs",
    "wo_ss", "wo_rs", "o_ss", "o_rs", "part_ss", "part_rs", "res_ss", "res_rs", "swap_ss", "swap_rs", "load", "saved",
)


class Refs:
    def __init__(self, names, refs):
        assert len(names) == len(refs), (len(names), len(refs))
        for name, ref in zip(names, refs):
            setattr(self, name, ref)


def forward_kernel(z, layer, *refs):
    count = len(WEIGHTS)
    rt, r_ref = refs[:2]
    own = dict(zip(WEIGHTS, refs[2 : 2 + count]))
    refs = refs[2 + count :]
    theirs = None
    if layer == 1:
        theirs, refs = dict(zip(WEIGHTS, refs[:count])), refs[count:]
    outs, refs = dict(zip(FORWARD_OUTS, refs)), refs[len(FORWARD_OUTS) :]
    if layer == 0:
        theirs, refs = dict(zip(WEIGHTS, refs[:count])), refs[count:]
    held, refs = Refs(FORWARD_OUTS, refs[: len(FORWARD_OUTS)]), refs[len(FORWARD_OUTS) :]
    used, refs = dict(zip(WEIGHTS, refs[:count])), refs[count:]
    s = Refs(FORWARD_SCRATCH, refs)
    me, at, core = lax.axis_index("tensor"), lax.axis_index("seq"), lax.axis_index("section")
    last = z.S - 1
    first_row = at * z.rows
    vec = used["vec"]

    def load(i, source):
        name = WEIGHTS[i]
        return pltpu.make_async_copy(source[name], used[name], s.load.at[i])

    def swap(i):
        name = WEIGHTS[i]
        return remote(own[name], theirs[name], s.swap_ss.at[i], s.swap_rs.at[i], {"section": 1 - core})

    @pl.when(core == layer)
    def _():
        for i in range(count):
            load(i, own).start()

    if layer == 1:

        @pl.when(core != layer)
        def _():
            for i in range(count):
                load(i, theirs).start()

    def ready(*wanted):
        if layer == 0:

            @pl.when(core != layer)
            def _():
                for i in wanted:
                    swap(i).wait_recv()
                    load(i, theirs).start()

        for i in wanted:
            load(i, own).wait()

    held.ckv[at * z.cap] = jnp.zeros((TILE, LANES), BF)
    barrier = pltpu.get_barrier_semaphore()
    for step in range(1, z.T):
        signal(to_tensor(step, me), barrier)
    if layer == 0:
        signal({"section": 1 - core}, barrier)

    def greet(d, _):
        signal({"seq": d}, barrier)
        return 0

    lax.fori_loop(0, at, greet, 0)
    pl.semaphore_wait(barrier, z.T - 1 + last - at + (layer == 0))
    if layer == 0:
        for i in range(count):
            swap(i).start()
    saver = Saver(s.saved)
    per_block = z.block // TILE
    ready(0)

    def norm_in(b, _):
        rows = pl.ds(b * z.block, z.block)
        y, _ = normed(r_ref[rows, :].astype(F32))
        held.n1[rows, :] = (y * vec[0:1, :] + vec[1:2, :]).astype(BF)
        return 0

    lax.fori_loop(0, z.T, norm_in, 0)
    saver.save(held.n1, outs["n1"])
    ready(1, 2)

    def project(b, _):
        rows = pl.ds(b * z.block, z.block)
        qkv = (nn(held.n1[rows, :], used["w1"][...]) + vec[2:3, :]).astype(BF)
        held.q[rows, :] = qkv[:, : z.pad]
        for h in range(z.heads):
            pairs = qkv[:, z.pad + h * LANES : z.pad + (h + 1) * LANES]
            held.kvt[pl.ds(h * (z.tiles + 1) + 1 + b * per_block, per_block)] = pairs.reshape(
                per_block, TILE, LANES
            )
        return 0

    lax.fori_loop(0, z.T, project, 0)
    score = nt(used["swt"][...], held.n1[...])[0:8]
    held.st[...] = score
    gate = jnp.minimum(score, 0.0) - jnp.log1p(jnp.exp(-jnp.abs(score)))
    s.gt[:, 0:LANES] = jnp.zeros((8, LANES), F32)
    s.gt[:, LANES : LANES + z.rows] = gate.astype(BF).astype(F32)
    s.gt[:, LANES + z.rows :] = jnp.zeros((8, LANES), F32)
    for t in range(z.tiles + 1):
        for h in range(z.heads):
            s.gate[h * (z.tiles + 1) + t, 0:1, :] = s.gt[
                h : h + 1, TILE + t * TILE : TILE + t * TILE + LANES
            ]

    def edge_copies():
        after = {"seq": jnp.minimum(at + 1, last)}
        return [
            remote(
                held.kvt.at[h * (z.tiles + 1) + z.tiles],
                s.edge.at[h],
                s.edge_ss.at[h],
                s.edge_rs.at[h],
                after,
            )
            for h in range(z.heads)
        ] + [
            remote(
                s.gt.at[:, pl.ds(z.rows, LANES)],
                s.edge_gate,
                s.edge_ss.at[z.heads],
                s.edge_rs.at[z.heads],
                after,
            )
        ]

    @pl.when(at < last)
    def _():
        for copy in edge_copies():
            copy.start()

    def tile_copies(d, source):
        return (
            remote(
                s.send_kv.at[d],
                held.ckv.at[pl.ds(source * z.cap, z.cap)],
                s.kv_ss.at[d],
                s.kv_rs.at[source],
                {"seq": d},
            ),
            remote(
                s.send_gate.at[d], s.got_gate.at[source], s.gate_ss.at[d], s.gate_rs.at[source], {"seq": d}
            ),
        )

    def pack(k, _):
        d = z.S - 1 - k

        def slot(i, _):
            u = rt[SEND, d * z.cap + i]
            s.send_kv[d, i] = held.kvt[u]
            s.send_gate[d, pl.ds(i, 1), :] = s.gate[u][0:1]
            return 0

        lax.fori_loop(0, z.cap, slot, 0)
        for copy in tile_copies(d, at):
            copy.start()
        return 0

    lax.fori_loop(0, last - at, pack, 0)
    ready(3)

    def wo_copy(step):
        return remote(
            used["wo"], s.wo_all.at[me], s.wo_ss.at[step], s.wo_rs.at[step], to_tensor(step, me)
        )

    for step in range(1, z.T):
        wo_copy(step).start()
    s.wo_all[me] = used["wo"][...]
    saver.save(held.q, outs["q"])
    saver.save(held.st, outs["st"])

    def landed(source, _):
        for copy in tile_copies(last, source):
            copy.wait_recv()
        for i in range(z.cap):
            s.far_gate[source * z.cap + i, 0:1, :] = s.got_gate[source, i : i + 1, :]
        return 0

    lax.fori_loop(0, at, landed, 0)
    lane = grid_of((TILE, LANES), 1)
    row = grid_of((TILE, LANES), 0)
    for h in range(z.heads):
        held.kvt[h * (z.tiles + 1)] = jnp.zeros((TILE, LANES), BF)

    @pl.when(at > 0)
    def _():
        for copy in edge_copies():
            copy.wait_recv()
        for h in range(z.heads):
            held.kvt[h * (z.tiles + 1)] = s.edge[h]
            s.gate[h * (z.tiles + 1), 0:1, :] = jnp.where(
                lane[0:1] < TILE,
                pltpu.roll(s.edge_gate[...], TILE, 1)[h : h + 1],
                s.gate[h * (z.tiles + 1), 0:1, :],
            )

    saver.save(held.kvt, outs["kvt"])
    saver.save(held.ckv, outs["ckv"])

    def attend(t):
        base = pl.multiple_of(t * TILE, TILE)
        query = first_row + base + row
        begin = jnp.where(
            query >= rt[ENDS, 1],
            rt[ENDS, 1],
            jnp.where(query >= rt[ENDS, 0], rt[ENDS, 0], 0),
        )
        key = first_row + base - TILE + lane
        near_ok = (key <= query) & (key > query - TILE) & (key >= begin)
        mixed = []
        for h in range(z.heads):
            cols = slice(h * LANES, (h + 1) * LANES)
            u = h * z.tiles + t
            arrived = rt[ARR, u]
            query_tile = held.q[pl.ds(base, TILE), cols]
            near = held.kvt[pl.ds(h * (z.tiles + 1) + t, 2)].reshape(2 * TILE, LANES)
            far = held.ckv[arrived]
            near_score = nt(query_tile, near) + s.gate[h * (z.tiles + 1) + t, 0:1, :]
            far_score = nt(query_tile, jnp.concatenate([far, far], axis=0)) + s.far_gate[arrived][0:1]
            far_ok = (rt[POS, u] + lane >= begin) & (lane < TILE)
            near_score = jnp.where(near_ok, near_score, MASKED)
            far_score = jnp.where(far_ok, far_score, MASKED)
            top = jnp.max(jnp.maximum(near_score, far_score), axis=-1, keepdims=True)
            near_exp = jnp.exp(near_score - top)
            far_exp = jnp.exp(far_score - top)
            scale = 1.0 / jnp.sum(near_exp + far_exp, axis=-1, keepdims=True)
            near_p = (near_exp * scale).astype(BF)
            far_p = (far_exp * scale).astype(BF)
            held.p[t * z.heads + h, :, 0:LANES] = near_p
            held.p[t * z.heads + h, :, LANES:] = far_p
            mixed.append(nn(near_p, near) + nn(far_p[:, :TILE], far))
        pair = jnp.where(lane < TILE, pltpu.roll(mixed[0], TILE, 1), mixed[1]).astype(BF)
        single = pltpu.roll(mixed[2], TILE, 1).astype(BF)
        held.o[pl.ds(base, TILE), 0:LANES] = pair
        held.o[pl.ds(base, TILE), LANES:] = single

    def o_copy(step, b):
        rows = pl.ds(b * z.block, z.block)
        return remote(
            held.o.at[rows, :],
            s.o_all.at[me, rows, :],
            s.o_ss.at[step * z.T + b],
            s.o_rs.at[step * z.T + b],
            to_tensor(step, me),
        )

    def attend_block(b, _):
        def pair(i, _):
            attend(b * per_block + 2 * i)
            attend(b * per_block + 2 * i + 1)
            return 0

        lax.fori_loop(0, per_block // 2, pair, 0)
        for step in range(1, z.T):
            o_copy(step, b).start()
        rows = pl.ds(b * z.block, z.block)
        s.o_all[me, rows, :] = held.o[rows, :]
        return 0

    lax.fori_loop(0, z.T, attend_block, 0)
    saver.save(held.p, outs["p"])
    saver.save(held.o, outs["o"])
    ready(4, 5)
    for step in range(1, z.T):
        wo_copy(step).wait()

    def part_copy(step):
        return remote(
            s.part_send.at[step - 1],
            s.part_got.at[step - 1],
            s.part_ss.at[step - 1],
            s.part_rs.at[step - 1],
            to_tensor(step, me),
        )

    def feed(k, _):
        step = (k + 1) % z.T
        block = partner(me, step)
        rows = pl.ds(pl.multiple_of(block * z.block, z.block), z.block)
        for other in range(1, z.T):
            o_copy(other, block).wait_recv()
        mixed = nn(s.o_all[0, rows, :], s.wo_all[0])
        for other in range(1, z.T):
            mixed += nn(s.o_all[other, rows, :], s.wo_all[other])
        middle = r_ref[rows, :].astype(F32) + mixed + vec[3:4, :]
        held.mid[...] = middle
        y, _ = normed(middle)
        n2 = (y * vec[4:5, :] + vec[5:6, :]).astype(BF)
        held.n2[rows, :] = n2
        u = nn(n2, used["wup"][...]) + vec[6:7, :]
        held.u[rows, :] = u.astype(BF)
        act = (0.5 * u * (1.0 + jnp.tanh(GELU_K * (u + GELU_A * u * u * u)))).astype(BF)
        held.act[rows, :] = act
        s.own_part[...] = nn(act, used["wdn"][...])

        @pl.when(step > 0)
        def _():
            s.part_send[step - 1] = s.own_part[...].astype(BF)
            part_copy(step).start()

        return 0

    lax.fori_loop(0, z.T, feed, 0)
    for name in ("mid", "n2", "u", "act"):
        saver.save(getattr(held, name), outs[name])
    total = held.mid[...] + s.own_part[...] + vec[7:8, :]
    for step in range(1, z.T):
        part_copy(step).wait_recv()
        total += s.part_got[step - 1].astype(F32)
    own_rows = pl.ds(pl.multiple_of(me * z.block, z.block), z.block)
    held.res[own_rows, :] = total.astype(BF)

    def res_copy(step):
        return remote(
            held.res.at[own_rows, :],
            held.res.at[own_rows, :],
            s.res_ss.at[step],
            s.res_rs.at[step],
            to_tensor(step, me),
        )

    for step in range(1, z.T):
        res_copy(step).start()
    for step in range(1, z.T):
        part_copy(step).wait_send()
        for b in range(z.T):
            o_copy(step, b).wait_send()

    def sent(d, _):
        for copy in tile_copies(d, at):
            copy.wait_send()
        return 0

    lax.fori_loop(at + 1, z.S, sent, 0)

    @pl.when(at < last)
    def _():
        for copy in edge_copies():
            copy.wait_send()

    if layer == 0:

        @pl.when(core == layer)
        def _():
            for i in range(count):
                swap(i).wait_recv()

        for i in range(count):
            swap(i).wait_send()
    for step in range(1, z.T):
        res_copy(step).wait()
    saver.save(held.res, outs["res"])
    saver.finish()


def forward(z, layer, route, r, own, theirs):
    rows, width, heads = z.rows, z.width, z.heads
    shapes = dict(
        n1=((rows, width), BF),
        q=((rows, z.pad), BF),
        kvt=((heads * (z.tiles + 1), TILE, LANES), BF),
        st=((8, rows), F32),
        p=((z.slots, TILE, 2 * LANES), BF),
        ckv=((z.n, TILE, LANES), BF),
        o=((rows, 2 * LANES), BF),
        mid=((z.block, width), F32),
        n2=((rows, width), BF),
        u=((rows, z.hidden), BF),
        act=((rows, z.hidden), BF),
        res=((rows, width), BF),
    )
    dma = pltpu.SemaphoreType.DMA
    shaped = [jax.ShapeDtypeStruct(*shapes[name]) for name in FORWARD_OUTS]
    mine = [own[name] for name in WEIGHTS]
    if layer == 0:
        shaped += [jax.ShapeDtypeStruct(value.shape, value.dtype) for value in mine]
        inputs = [route, r, *mine]
    else:
        inputs = [route, r, *mine, *(theirs[name] for name in WEIGHTS)]
    outs = pl.pallas_call(
        functools.partial(forward_kernel, z, layer),
        out_shape=tuple(shaped),
        in_specs=[smem(), vmem()] + [anywhere()] * (len(inputs) - 2),
        out_specs=tuple(anywhere() for _ in shaped),
        scratch_shapes=[
            *(pltpu.VMEM(*shapes[name]) for name in FORWARD_OUTS),
            *(pltpu.VMEM(value.shape, value.dtype) for value in mine),
            pltpu.VMEM((8, rows + 2 * LANES), F32),
            pltpu.VMEM((heads * (z.tiles + 1), 8, LANES), F32),
            pltpu.VMEM((heads, TILE, LANES), BF),
            pltpu.VMEM((8, LANES), F32),
            pltpu.VMEM((z.S, z.cap, TILE, LANES), BF),
            pltpu.VMEM((z.S, z.capg, LANES), F32),
            pltpu.VMEM((z.S, z.capg, LANES), F32),
            pltpu.VMEM((z.n, 8, LANES), F32),
            pltpu.VMEM((z.T, 2 * LANES, width), BF),
            pltpu.VMEM((z.T, rows, 2 * LANES), BF),
            pltpu.VMEM((z.T - 1, z.block, width), BF),
            pltpu.VMEM((z.T - 1, z.block, width), BF),
            pltpu.VMEM((z.block, width), F32),
            dma((z.S,)),
            dma((z.S,)),
            dma((z.S,)),
            dma((z.S,)),
            dma((heads + 1,)),
            dma((heads + 1,)),
            dma((z.T,)),
            dma((z.T,)),
            dma((z.T * z.T,)),
            dma((z.T * z.T,)),
            dma((z.T,)),
            dma((z.T,)),
            dma((z.T,)),
            dma((z.T,)),
            dma((len(WEIGHTS),)),
            dma((len(WEIGHTS),)),
            dma((len(WEIGHTS),)),
            dma((len(FORWARD_OUTS),)),
        ],
        compiler_params=pltpu.CompilerParams(
            collective_id=layer, has_side_effects=True, vmem_limit_bytes=LIMIT
        ),
        name=f"forward{layer}",
    )(*inputs)
    kept = dict(zip(FORWARD_OUTS, outs))
    return (kept, dict(zip(WEIGHTS, outs[len(FORWARD_OUTS) :]))) if layer == 0 else (kept, theirs)


BACKWARD_SCRATCH = (
    "du", "part_send", "part_got", "own_part", "dr2", "ob", "dout", "dqkv", "dkv", "dgate", "far", "far_gate",
    "send_kv", "send_gate", "got_kv", "got_gate", "got_gate_row", "edge_send", "edge_got", "edge_gate_got", "sum",
    "gate_sum", "tile_gate", "ds", "stat", "stat_got", "grad",
    "pa", "pb", "pc", "xa", "xb", "xc", "sa", "sb", "sc", "ta", "tb", "tc", "ha", "hb", "hc",
    "kv_ss", "kv_rs", "gate_ss", "gate_rs", "edge_ss", "edge_rs", "part_ss", "part_rs", "ob_ss", "ob_rs",
    "grad_ss", "grad_rs", "stat_ss", "stat_rs", "give_ss", "give_rs", "cross_ss", "cross_rs", "hand_ss", "hand_rs",
    "move_ss", "move_rs", "load", "saved",
)


def backward_kernel(z, layer, *refs):
    count = len(WEIGHTS)
    rt = refs[0]
    c_any, r_any, first_any, second_any = refs[1:5]
    refs = refs[5:]
    own, refs = dict(zip(WEIGHTS, refs[:count])), refs[count:]
    theirs, refs = dict(zip(WEIGHTS, refs[:count])), refs[count:]
    kept, refs = dict(zip(KEPT, refs[: len(KEPT)])), refs[len(KEPT) :]
    grad_out, both_out, g_out = refs[:3]
    refs = refs[3:]
    c_ref, r_ref, refs = refs[0], refs[1], refs[2:]
    used, refs = dict(zip(WEIGHTS, refs[:count])), refs[count:]
    k, refs = Refs(KEPT, refs[: len(KEPT)]), refs[len(KEPT) :]
    s = Refs(BACKWARD_SCRATCH, refs)
    me, at, core = lax.axis_index("tensor"), lax.axis_index("seq"), lax.axis_index("section")
    last = z.S - 1
    vec = used["vec"]
    own_rows = pl.ds(pl.multiple_of(me * z.block, z.block), z.block)
    W = z.width
    sources = {"c": (c_any, c_ref)}
    sources |= {name: (kept[name], getattr(k, name)) for name in KEPT}
    sources["r"] = (r_any.at[own_rows, :], r_ref)
    order = ("c", "wdn", "u", "wup", "act", "n2", "vec", "mid", "wo", "p", "q", "kvt", "ckv", "o", "st", "w1", "swt", "n1", "r")

    def loads(name, which):
        i = order.index(name)
        if name in WEIGHTS:
            return pltpu.make_async_copy(which[name], used[name], s.load.at[i])
        return pltpu.make_async_copy(*sources[name], s.load.at[i])

    for name in order:
        if name in WEIGHTS:

            @pl.when(core == layer)
            def _(name=name):
                loads(name, own).start()

            @pl.when(core != layer)
            def _(name=name):
                loads(name, theirs).start()
        else:
            loads(name, None).start()

    def ready(*names):
        for name in names:
            loads(name, own).wait()

    barrier = pltpu.get_barrier_semaphore()
    for step in range(1, z.T):
        signal(to_tensor(step, me), barrier)
    signal({"section": 1 - core}, barrier)

    def greet(i, _):
        signal({"seq": (at + i) % z.S}, barrier)
        return 0

    lax.fori_loop(1, z.S, greet, 0)
    pl.semaphore_wait(barrier, z.T - 1 + 1 + last)
    saver = Saver(s.saved)
    across = {"section": 1 - core}

    def move(src, i, part):
        return remote(src.at[part], both_out.at[core].at[part], s.move_ss.at[i], s.move_rs.at[i], across)

    def keep(src, part):
        return pltpu.make_async_copy(src.at[part], both_out.at[core].at[part], s.saved.at[3])

    everything = pl.ds(0, z.rows)

    @pl.when(core == 0)
    def _():
        move(second_any, 0, everything).start()

    if layer == 1:

        @pl.when(core == 0)
        def _():
            keep(first_any, everything).start()

        @pl.when(core == 1)
        def _():
            move(first_any, 0, everything).start()
            keep(second_any, everything).start()

    else:

        @pl.when(core == 1)
        def _():
            keep(second_any, everything).start()

    def part_copy(step, phase):
        return remote(
            s.part_send.at[phase, step - 1],
            s.part_got.at[phase, step - 1],
            s.part_ss.at[phase, step],
            s.part_rs.at[phase, step],
            to_tensor(step, me),
        )

    ready("c", "wdn", "u", "wup")

    def ff_back(i, _):
        step = (i + 1) % z.T
        rows = pl.ds(pl.multiple_of(partner(me, step) * z.block, z.block), z.block)
        u = k.u[rows, :].astype(F32)
        squared = u * u
        bent = jnp.tanh(GELU_K * (u + GELU_A * squared * u))
        slope = 0.5 * (1.0 + bent) + 0.5 * u * (1.0 - bent * bent) * (
            GELU_K * (1.0 + 3.0 * GELU_A * squared)
        )
        du = (nt(c_ref[rows, :], used["wdn"][...]) * slope).astype(BF)
        s.du[rows, :] = du
        s.own_part[...] = nt(du, used["wup"][...])

        @pl.when(step > 0)
        def _():
            s.part_send[0, step - 1] = s.own_part[...].astype(BF)
            part_copy(step, 0).start()

        return 0

    lax.fori_loop(0, z.T, ff_back, 0)
    ones = jnp.ones((16, z.rows), BF)
    s.stat[...] = jnp.zeros((24, W), F32)

    mine = {0: s.pa, 1: s.pb, 2: s.pc}
    theirs_part = {0: s.xa, 1: s.xb, 2: s.xc}
    summed = {0: s.sa, 1: s.sb, 2: s.sc}
    crossed = {0: s.ta, 1: s.tb, 2: s.tc}
    handed = {0: s.ha, 1: s.hb, 2: s.hc}

    def give(piece):
        return remote(
            mine[piece].at[1 - core], theirs_part[piece], s.give_ss.at[piece], s.give_rs.at[piece], across
        )

    def cross(piece, d, source):
        return remote(
            summed[piece].at[d],
            crossed[piece].at[source],
            s.cross_ss.at[piece, d],
            s.cross_rs.at[piece, source],
            {"seq": d},
        )

    def hand(piece):
        return remote(
            summed[piece].at[at], handed[piece], s.hand_ss.at[piece], s.hand_rs.at[piece], across
        )

    span = math.lcm(z.share, 16)

    def add_up(piece):
        give(piece).wait_recv()

        def chunk(i, _):
            rows = pl.ds(pl.multiple_of(i * span, span), span)
            value = mine[piece][core, rows, :].astype(F32) + theirs_part[piece][rows, :].astype(F32)
            for j in range(span // z.share):
                d = i * (span // z.share) + j
                rows_of = value[j * z.share : (j + 1) * z.share]
                if z.padded > z.share:
                    rows_of = jnp.concatenate(
                        [rows_of, jnp.zeros((z.padded - z.share, value.shape[1]), F32)], axis=0
                    )
                summed[piece][d] = rows_of.astype(BF)

                @pl.when(d != at)
                def _():
                    cross(piece, d, at).start()

            return 0

        lax.fori_loop(0, W // span, chunk, 0)

    offsets = (0, z.pieces[0], z.pieces[0] + z.pieces[1])

    def reduce(piece):
        def wait(i, _):
            d = (at + i) % z.S
            cross(piece, d, d).wait_recv()
            return 0

        lax.fori_loop(1, z.S, wait, 0)

        def add(i, running):
            return running + crossed[piece][(at + i) % z.S].astype(F32)

        total = lax.fori_loop(1, z.S, add, summed[piece][at].astype(F32))
        cols = slice(offsets[piece], offsets[piece] + z.pieces[piece])
        g_out[core, :, cols] = total[: z.share]

        @pl.when(core != layer)
        def _():
            summed[piece][at] = total.astype(BF)
            hand(piece).start()

    def take(piece):
        cols = slice(offsets[piece], offsets[piece] + z.pieces[piece])

        @pl.when(core == layer)
        def _():
            hand(piece).wait_recv()
            g_out[1 - core, :, cols] = handed[piece][...].astype(F32)[: z.share]

    ready("act", "n2")
    s.pa[0] = tn(c_ref[...], k.act[...]).astype(BF)
    s.pa[1] = tn(k.n2[...], s.du[...]).astype(BF)
    give(0).start()
    s.stat[8:9, :] = nn(ones, s.du[...])[0:1]
    s.stat[9:10, :] = nn(ones, c_ref[...])[0:1]
    ready("vec", "mid", "wo")
    grad = s.own_part[...]
    for step in range(1, z.T):
        part_copy(step, 0).wait_recv()
        grad += s.part_got[0, step - 1].astype(F32)
    y, spread = normed(k.mid[...])
    dr2 = c_ref[own_rows, :].astype(F32) + norm_back(grad, vec[4:5, :], y, spread)
    s.dr2[...] = dr2
    s.ob[own_rows, :] = dr2.astype(BF)

    def rows_copy(ref, sends, recvs, step):
        return remote(
            ref.at[own_rows, :], ref.at[own_rows, :], sends.at[step], recvs.at[step], to_tensor(step, me)
        )

    for step in range(1, z.T):
        rows_copy(s.ob, s.ob_ss, s.ob_rs, step).start()
    s.stat[0:1, :] = column_sum(dr2)
    s.stat[1:2, :] = column_sum(grad * y)
    s.stat[2:3, :] = column_sum(grad)
    s.dkv[...] = jnp.zeros((z.rows + TILE, z.pad), F32)
    add_up(0)
    lane_wide = grid_of((z.block, LANES), 1)

    def out_back(step, _):
        @pl.when(step > 0)
        def _():
            rows_copy(s.ob, s.ob_ss, s.ob_rs, step).wait_recv()

        rows = pl.ds(pl.multiple_of(partner(me, step) * z.block, z.block), z.block)
        dout = nt(s.ob[rows, :], used["wo"][...])
        pair, single = dout[:, :LANES], dout[:, LANES:]
        for h, value in enumerate((pltpu.roll(pair, TILE, 1), pair, pltpu.roll(single, TILE, 1))):
            s.dout[rows, h * LANES : (h + 1) * LANES] = jnp.where(lane_wide < TILE, 0.0, value).astype(BF)
        return 0

    lax.fori_loop(0, z.T, out_back, 0)
    ready("p", "q", "kvt", "ckv")

    def attend_back(t):
        base = pl.multiple_of(t * TILE, TILE)
        for h in range(z.heads):
            cols = slice(h * LANES, (h + 1) * LANES)
            u = h * z.tiles + t
            arrived = rt[ARR, u]
            near = k.kvt[pl.ds(h * (z.tiles + 1) + t, 2)].reshape(2 * TILE, LANES)
            far = k.ckv[arrived]
            query = k.q[pl.ds(base, TILE), cols]
            dout = s.dout[pl.ds(base, TILE), cols]
            near_p = k.p[t * z.heads + h, :, 0:LANES]
            far_p = k.p[t * z.heads + h, :, LANES : LANES + TILE]
            near_pf, far_pf = near_p.astype(F32), far_p.astype(F32)
            near_dp, far_dp = nt(dout, near), nt(dout, far)
            total = jnp.sum(near_pf * near_dp, axis=-1, keepdims=True) + jnp.sum(
                far_pf * far_dp, axis=-1, keepdims=True
            )
            near_dz = (near_pf * (near_dp - total)).astype(BF)
            far_dz = (far_pf * (far_dp - total)).astype(BF)
            s.dqkv[pl.ds(base, TILE), cols] = (nn(near_dz, near) + nn(far_dz, far)).astype(BF)
            s.dkv[pl.ds(base, 2 * TILE), cols] += tn(near_dz, query) + tn(near_p, dout)
            s.far[u] = (tn(far_dz, query) + tn(far_p, dout)).astype(BF)
            s.dgate[t, h : h + 1, :] = column_sum(near_dz.astype(F32))
            s.far_gate[u, 0:1, 0:TILE] = column_sum(far_dz.astype(F32))

    def attend_back_pair(i, _):
        attend_back(2 * i)
        attend_back(2 * i + 1)
        return 0

    lax.fori_loop(0, z.tiles // 2, attend_back_pair, 0)
    s.dgate[z.tiles] = jnp.zeros((8, LANES), F32)

    def edge_copies():
        behind = {"seq": jnp.maximum(at - 1, 0)}
        return (
            remote(s.edge_send, s.edge_got, s.edge_ss.at[0], s.edge_rs.at[0], behind),
            remote(s.dgate.at[0], s.edge_gate_got, s.edge_ss.at[1], s.edge_rs.at[1], behind),
        )

    @pl.when(at > 0)
    def _():
        s.edge_send[...] = s.dkv[0:TILE, :].astype(BF)
        for copy in edge_copies():
            copy.start()

    def tile_copies(d, source):
        return (
            remote(
                s.send_kv.at[d],
                s.got_kv.at[pl.ds(source * z.cap, z.cap)],
                s.kv_ss.at[d],
                s.kv_rs.at[source],
                {"seq": d},
            ),
            remote(
                s.send_gate.at[d], s.got_gate.at[source], s.gate_ss.at[d], s.gate_rs.at[source], {"seq": d}
            ),
        )

    def pack(d, _):
        def slot(i, _):
            u = rt[INV, d * z.cap + i]
            s.send_kv[d, i] = s.far[u]
            s.send_gate[d, pl.ds(i, 1), :] = s.far_gate[u][0:1]
            return 0

        lax.fori_loop(0, z.cap, slot, 0)
        for copy in tile_copies(d, at):
            copy.start()
        return 0

    lax.fori_loop(0, at, pack, 0)
    ready("o")
    out_grad = tn(s.ob[...], k.o[...]).astype(BF)
    s.pb[0] = out_grad[:, :LANES]
    s.pb[1] = out_grad[:, LANES:]
    give(1).start()
    s.sum[z.n] = jnp.zeros((TILE, LANES), F32)
    s.gate_sum[z.n] = jnp.zeros((8, LANES), F32)
    ready("st", "w1", "swt", "n1", "r")
    add_up(1)

    @pl.when(at < last)
    def _():
        for copy in edge_copies():
            copy.wait_recv()
        s.dkv[pl.ds(z.rows, TILE), :] += s.edge_got[...].astype(F32)
        s.dgate[z.tiles] = s.edge_gate_got[...]

    def landed(source, _):
        for copy in tile_copies(0, source):
            copy.wait_recv()
        for i in range(z.cap):
            s.got_gate_row[source * z.cap + i, 0:1, :] = s.got_gate[source, i : i + 1, :]
        return 0

    lax.fori_loop(at + 1, z.S, landed, 0)

    def gather(i, carry):
        running, gates = carry
        index = rt[ORD, i]
        joined = rt[CONT, i].astype(F32)
        running = running * joined + s.got_kv[index].astype(F32)
        gates = gates * joined + s.got_gate_row[index]
        s.sum[i] = running
        s.gate_sum[i] = gates
        return running, gates

    lax.fori_loop(0, z.n, gather, (jnp.zeros((TILE, LANES), F32), jnp.zeros((8, LANES), F32)))

    def settle(t, _):
        base = pl.multiple_of((t + 1) * TILE, TILE)
        rows = pl.ds(pl.multiple_of(t * TILE, TILE), TILE)
        for h in range(z.heads):
            cols = slice(h * LANES, (h + 1) * LANES)
            index = rt[LAST, h * z.tiles + t]
            s.dqkv[rows, z.pad + h * LANES : z.pad + (h + 1) * LANES] = (
                s.dkv[pl.ds(base, TILE), cols] + s.sum[index]
            ).astype(BF)
            s.tile_gate[t, h : h + 1, :] = s.gate_sum[index][0:1]
        return 0

    lax.fori_loop(0, z.tiles, settle, 0)
    lane = grid_of((8, LANES), 1)
    head_row = grid_of((8, LANES), 0)
    for i in range(z.tiles // 2):
        halves = []
        for t in (2 * i, 2 * i + 1):
            halves.append(pltpu.roll(s.dgate[t], TILE, 1) + s.dgate[t + 1] + s.tile_gate[t])
        joint = jnp.where(lane < TILE, halves[0], pltpu.roll(halves[1], TILE, 1))
        score = k.st[:, i * LANES : (i + 1) * LANES]
        grads = jnp.where(head_row < z.heads, joint / (1.0 + jnp.exp(score)), 0.0)
        s.ds[0:8, i * LANES : (i + 1) * LANES] = grads
        s.ds[8:16, i * LANES : (i + 1) * LANES] = jnp.zeros((8, LANES), F32)

    def in_back(i, _):
        step = (i + 1) % z.T
        rows = pl.ds(pl.multiple_of(partner(me, step) * z.block, z.block), z.block)
        s.own_part[...] = nt(s.dqkv[rows, :], used["w1"][...]) + tn(
            s.ds[:, rows].astype(BF), used["swt"][...]
        )

        @pl.when(step > 0)
        def _():
            s.part_send[1, step - 1] = s.own_part[...].astype(BF)
            part_copy(step, 1).start()

        return 0

    lax.fori_loop(0, z.T, in_back, 0)
    s.pc[0] = tn(k.n1[...], s.dqkv[:, z.pad :]).astype(BF)
    queries = tn(k.n1[...], s.dqkv[:, : z.pad])
    lane_full = grid_of((W, LANES), 1)
    s.pc[1, :, :LANES] = jnp.where(
        lane_full < TILE, queries[:, :LANES], pltpu.roll(queries[:, LANES : 2 * LANES], TILE, 1)
    ).astype(BF)
    s.pc[1, :, LANES : 2 * LANES] = queries[:, 2 * LANES :].astype(BF)
    s.stat[10:13, :] = nn(s.ds[...].astype(BF), k.n1[...])[0:3]
    source, target = grid_of((W, W), 0), grid_of((W, W), 1)
    is_value = source >= z.pad
    index = jnp.where(is_value, source - z.pad, source)
    index = index // LANES * TILE + index % TILE
    each = z.heads * TILE // z.S
    wanted = index // each * z.share + index % each + jnp.where(is_value, each, 0)
    filled = (source % LANES >= TILE) == is_value
    spread_out = jnp.where(
        (wanted == target) & filled, jnp.where(is_value, 1.0, TILE**-0.5), 0.0
    ).astype(BF)
    s.stat[13:14, :] = nn(nn(ones, s.dqkv[...]).astype(BF), spread_out)[0:1]
    grad = s.own_part[...]
    for step in range(1, z.T):
        part_copy(step, 1).wait_recv()
        grad += s.part_got[1, step - 1].astype(F32)
    y, spread = normed(r_ref[...].astype(F32))
    dr = s.dr2[...] + norm_back(grad, vec[0:1, :], y, spread)
    s.grad[own_rows, :] = dr.astype(BF)
    for step in range(1, z.T):
        rows_copy(s.grad, s.grad_ss, s.grad_rs, step).start()
    s.stat[3:4, :] = column_sum(grad * y)
    s.stat[4:5, :] = column_sum(grad)

    def stat_copy(step):
        return remote(
            s.stat.at[pl.ds(0, 8), :],
            s.stat_got.at[step - 1],
            s.stat_ss.at[step],
            s.stat_rs.at[step],
            to_tensor(step, me),
        )

    for step in range(1, z.T):
        stat_copy(step).start()
    shared = s.stat[0:8, :]
    for step in range(1, z.T):
        stat_copy(step).wait()
        shared += s.stat_got[step - 1]
    stats = jnp.concatenate([shared, s.stat[8:16, :]], axis=0).astype(BF)
    unit = (grid_of((16, LANES), 0) == grid_of((16, LANES), 1)).astype(F32).astype(BF)
    s.pc[1, :, 2 * LANES :] = tn(stats, unit).astype(BF)
    give(2).start()

    reduce(0)
    reduce(1)
    add_up(2)
    take(0)
    take(1)

    def block_of(step):
        return pl.ds(pl.multiple_of(partner(me, step) * z.block, z.block), z.block)

    for step in range(z.T):
        if step > 0:
            rows_copy(s.grad, s.grad_ss, s.grad_rs, step).wait_recv()
        if layer == 0:

            @pl.when(core == 1)
            def _(step=step):
                move(s.grad, step, block_of(step)).start()

    saver.save(s.grad, grad_out)
    reduce(2)
    take(2)
    for piece in range(3):
        give(piece).wait_send()

        @pl.when(core != layer)
        def _(piece=piece):
            hand(piece).wait_send()

        def crossed_over(i, _, piece=piece):
            cross(piece, (at + i) % z.S, at).wait_send()
            return 0

        lax.fori_loop(1, z.S, crossed_over, 0)
    for step in range(1, z.T):
        for phase in range(2):
            part_copy(step, phase).wait_send()
        rows_copy(s.ob, s.ob_ss, s.ob_rs, step).wait_send()
        rows_copy(s.grad, s.grad_ss, s.grad_rs, step).wait_send()

    def sent(d, _):
        for copy in tile_copies(d, at):
            copy.wait_send()
        return 0

    lax.fori_loop(0, at, sent, 0)

    @pl.when(at > 0)
    def _():
        for copy in edge_copies():
            copy.wait_send()

    if layer == 1:
        move(first_any, 0, everything).wait()
        keep(first_any, everything).wait()
    else:

        @pl.when(core == 0)
        def _():
            keep(s.grad, everything).start()
            move(second_any, 0, everything).wait_send()
            for step in range(z.T):
                move(s.grad, step, block_of(step)).wait_recv()

        @pl.when(core == 1)
        def _():
            move(second_any, 0, everything).wait_recv()
            for step in range(z.T):
                move(s.grad, step, block_of(step)).wait_send()

        keep(s.grad, everything).wait()
    saver.finish()


def backward(z, layer, route, c, r, first, second, own, theirs, kept):
    rows, width = z.rows, z.width
    dma = pltpu.SemaphoreType.DMA
    wide = sum(z.pieces)
    weights = [own[name] for name in WEIGHTS]
    saved = [kept[name] for name in KEPT]
    inputs = [route, c, r, first, second, *weights, *(theirs[name] for name in WEIGHTS), *saved]
    parts = [(w,) for w in z.pieces]
    return pl.pallas_call(
        functools.partial(backward_kernel, z, layer),
        out_shape=(
            jax.ShapeDtypeStruct((rows, width), BF),
            jax.ShapeDtypeStruct((2, rows, width), BF),
            jax.ShapeDtypeStruct((2, z.share, wide), F32),
        ),
        in_specs=[smem()] + [anywhere()] * (len(inputs) - 1),
        out_specs=(anywhere(), anywhere(), vmem()),
        scratch_shapes=[
            pltpu.VMEM((rows, width), BF),
            pltpu.VMEM((z.block, width), BF),
            *(pltpu.VMEM(value.shape, value.dtype) for value in weights),
            *(pltpu.VMEM(value.shape, value.dtype) for value in saved),
            pltpu.VMEM((rows, z.hidden), BF),
            pltpu.VMEM((2, z.T - 1, z.block, width), BF),
            pltpu.VMEM((2, z.T - 1, z.block, width), BF),
            pltpu.VMEM((z.block, width), F32),
            pltpu.VMEM((z.block, width), F32),
            pltpu.VMEM((rows, width), BF),
            pltpu.VMEM((rows, z.pad), BF),
            pltpu.VMEM((rows, 2 * z.pad), BF),
            pltpu.VMEM((rows + TILE, z.pad), F32),
            pltpu.VMEM((z.tiles + 1, 8, LANES), F32),
            pltpu.VMEM((z.slots, TILE, LANES), BF),
            pltpu.VMEM((z.slots, 8, LANES), F32),
            pltpu.VMEM((z.S, z.cap, TILE, LANES), BF),
            pltpu.VMEM((z.S, z.capg, LANES), F32),
            pltpu.VMEM((z.n, TILE, LANES), BF),
            pltpu.VMEM((z.S, z.capg, LANES), F32),
            pltpu.VMEM((z.n, 8, LANES), F32),
            pltpu.VMEM((TILE, z.pad), BF),
            pltpu.VMEM((TILE, z.pad), BF),
            pltpu.VMEM((8, LANES), F32),
            pltpu.VMEM((z.n + 1, TILE, LANES), F32),
            pltpu.VMEM((z.n + 1, 8, LANES), F32),
            pltpu.VMEM((z.tiles, 8, LANES), F32),
            pltpu.VMEM((16, rows), F32),
            pltpu.VMEM((24, width), F32),
            pltpu.VMEM((z.T - 1, 8, width), F32),
            pltpu.VMEM((rows, width), BF),
            *(pltpu.VMEM((2, width, w), BF) for w in z.pieces),
            *(pltpu.VMEM((width, w), BF) for w in z.pieces),
            *(pltpu.VMEM((z.S, z.padded, w), BF) for w in z.pieces),
            *(pltpu.VMEM((z.S, z.padded, w), BF) for w in z.pieces),
            *(pltpu.VMEM((z.padded, w), BF) for w in z.pieces),
            dma((z.S,)),
            dma((z.S,)),
            dma((z.S,)),
            dma((z.S,)),
            dma((2,)),
            dma((2,)),
            dma((2, z.T)),
            dma((2, z.T)),
            dma((z.T,)),
            dma((z.T,)),
            dma((z.T,)),
            dma((z.T,)),
            dma((z.T,)),
            dma((z.T,)),
            dma((3,)),
            dma((3,)),
            dma((3, z.S)),
            dma((3, z.S)),
            dma((3,)),
            dma((3,)),
            dma((z.T,)),
            dma((z.T,)),
            dma((2 + len(WEIGHTS) + len(KEPT),)),
            dma((4,)),
        ],
        compiler_params=pltpu.CompilerParams(
            collective_id=2 + layer, has_side_effects=True, vmem_limit_bytes=LIMIT
        ),
        name=f"backward{layer}",
    )(*inputs)


def swapped(value):
    return lax.ppermute(value, "section", [(0, 1), (1, 0)])


def body(
    tokens,
    cotangent,
    lengths,
    selected,
    input_weight,
    input_bias,
    score_weight,
    output_weight,
    output_bias,
    up_weight,
    up_bias,
    down_weight,
    down_bias,
    norm_gain,
    norm_bias,
):
    core = lax.axis_index("section")
    _, rows, width = tokens.shape
    heads, hidden = score_weight.shape[2], up_weight.shape[2]
    head = input_weight.shape[3] // heads
    inner = heads * head
    z = Sizes(lax.axis_size("tensor"), lax.axis_size("seq"), rows, width, heads, hidden)
    scale = head**-0.5
    grouped = (
        selected[0].reshape(2, heads, z.S, z.tiles).transpose(0, 2, 1, 3).reshape(2, z.S, z.slots)
    )
    kept_choice = lax.dynamic_index_in_dim(grouped, core, 0, keepdims=False)
    got_choice = swapped(lax.dynamic_index_in_dim(grouped, 1 - core, 0, keepdims=False))
    choice = jnp.where(
        core == 0, jnp.stack([kept_choice, got_choice]), jnp.stack([got_choice, kept_choice])
    )
    length = lax.dynamic_index_in_dim(lengths, core, 0, keepdims=False)
    ends = jnp.stack([length[0], length[0] + length[1]])
    own, routes = prepare(
        z,
        ends,
        choice,
        input_weight[0].transpose(1, 0, 2),
        input_bias[0],
        score_weight[0],
        output_weight[0],
        output_bias,
        up_bias,
        down_bias,
        norm_gain[0],
        norm_bias[0],
    )
    own |= dict(wup=up_weight[0], wdn=down_weight[0])
    first = lax.dynamic_index_in_dim(tokens, core, 0, keepdims=False)
    cotan = lax.dynamic_index_in_dim(cotangent, core, 0, keepdims=False)
    zero, theirs = forward(z, 0, routes[0], first, own, None)
    one, _ = forward(z, 1, routes[1], zero["res"], own, theirs)
    grad1, layer_out, g1 = backward(
        z, 1, routes[1], cotan, zero["res"], zero["res"], one["res"], own, theirs, one
    )
    grad0, input_grad, g0 = backward(
        z, 0, routes[0], grad1, first, grad1, grad1, own, theirs, zero
    )
    total = jnp.where(core == 0, g0, g1)
    share = z.share
    c_o, c_i = hidden, hidden + LANES
    pairs = total[0, :, c_i:].reshape(share, heads, LANES)
    input_weight_grad = jnp.stack(
        [
            scale * total[1, :, c_i : c_i + inner],
            pairs[:, :, :head].reshape(share, inner),
            pairs[:, :, head:].reshape(share, inner),
        ],
        axis=1,
    )
    out_grad = jnp.concatenate([total[0, :, c_o:c_i], total[1, :, c_o:c_i]], axis=1)[:, :inner]
    c_s = c_i + 2 * LANES
    stats = total[1, :, c_s : c_s + 16].T
    each = inner // z.S
    return (
        layer_out[None],
        input_grad[None],
        input_weight_grad[None],
        jnp.stack([stats[13, :each], stats[13, each : 2 * each]])[None],
        total[1, :, c_s + 10 : c_s + 10 + heads][None],
        out_grad.T[None],
        stats[0][None],
        total[1, :, :hidden][None],
        stats[8][None],
        total[0, :, :hidden].T[None],
        stats[9][None],
        jnp.stack([stats[3], stats[1]])[None],
        jnp.stack([stats[4], stats[2]])[None],
    )


def solution(mesh):
    return jax.shard_map(
        body,
        mesh=mesh,
        in_specs=(
            P(None, "seq", None),
            P(None, "seq", None),
            P(),
            P("section", None, "tensor", None),
            P("section", None, None, "tensor"),
            P("section", None, "tensor"),
            P("section", None, "tensor"),
            P("section", "tensor", None),
            P("section", None),
            P("section", None, "tensor"),
            P("section", "tensor"),
            P("section", "tensor", None),
            P("section", None),
            P("section", None, None),
            P("section", None, None),
        ),
        out_specs=(
            P("section", None, "seq", None),
            P("section", None, "seq", None),
            P("section", "seq", None, "tensor"),
            P("section", None, ("tensor", "seq")),
            P("section", "seq", "tensor"),
            P("section", "tensor", "seq"),
            P("section", "seq"),
            P("section", "seq", "tensor"),
            P("section", ("tensor", "seq")),
            P("section", "tensor", "seq"),
            P("section", "seq"),
            P("section", None, "seq"),
            P("section", None, "seq"),
        ),
        check_vma=False,
    )
```

```python
import functools
import math

import jax
import jax.numpy as jnp
from jax import lax
from jax.experimental import pallas as pl
from jax.experimental.pallas import tpu as pltpu
from jax.sharding import PartitionSpec as P

TILE = 64
LANES = 128
MASKED = -1e30
EPSILON = 1e-05
FAR = -(1 << 20)
MESH = pl.DeviceIdType.MESH
BF = jnp.bfloat16
F32 = jnp.float32
GELU_A = 0.044715
GELU_K = math.sqrt(2.0 / math.pi)
LIMIT = 60 * 1024 * 1024


class Sizes:
    def __init__(self, mesh_tensor, mesh_seq, rows, width, heads, hidden):
        self.T, self.S = mesh_tensor, mesh_seq
        self.rows, self.width, self.heads, self.hidden = rows, width, heads, hidden
        self.tiles = rows // TILE
        self.slots = heads * self.tiles
        self.cap = -(-self.slots // (mesh_seq - 1))
        self.capg = -(-self.cap // 8) * 8
        self.n = mesh_seq * self.cap
        self.block = rows // mesh_tensor
        self.pad = heads * LANES
        self.share = width // mesh_seq
        self.padded = -(-self.share // 16) * 16
        self.pieces = (hidden, LANES, self.pad, LANES)


SEND, INV, ORD, CONT, ARR, POS, LAST, ENDS = range(8)
WEIGHTS = ("vec", "w1", "swt", "wo", "wup", "wdn")
KEPT = ("n1", "q", "kvt", "st", "p", "ckv", "o", "mid", "n2", "u", "act")


def nn(a, b):
    return jnp.dot(a, b, preferred_element_type=F32)


def nt(a, b):
    return lax.dot_general(a, b, (((1,), (1,)), ((), ())), preferred_element_type=F32)


def tn(a, b):
    return lax.dot_general(a, b, (((0,), (0,)), ((), ())), preferred_element_type=F32)


def normed(x):
    centred = x - jnp.mean(x, axis=-1, keepdims=True)
    spread = lax.rsqrt(jnp.mean(centred * centred, axis=-1, keepdims=True) + EPSILON)
    return centred * spread, spread


def norm_back(grad, gain, y, spread):
    scaled = grad * gain
    return spread * (
        scaled
        - jnp.mean(scaled, axis=-1, keepdims=True)
        - y * jnp.mean(scaled * y, axis=-1, keepdims=True)
    )


def partner(me, step):
    return (me // 2 + step // 2) % 2 * 2 + (me % 2 + step % 2) % 2


def column_sum(x):
    return jnp.sum(x, axis=0, keepdims=True)


def smem():
    return pl.BlockSpec(memory_space=pltpu.SMEM)


def vmem():
    return pl.BlockSpec(memory_space=pltpu.VMEM)


def anywhere():
    return pl.BlockSpec(memory_space=pl.ANY)


def grid_of(shape, axis):
    return lax.broadcasted_iota(jnp.int32, shape, axis)


def prepare_kernel(
    z,
    ends_ref,
    sel_ref,
    win_ref,
    bin_ref,
    sw_ref,
    wout_ref,
    bout_ref,
    bup_ref,
    bdn_ref,
    gain_ref,
    shift_ref,
    vec_ref,
    w1_ref,
    swt_ref,
    wo_ref,
    rt0_ref,
    rt1_ref,
):
    inner, head = win_ref.shape[2], win_ref.shape[2] // z.heads
    row, col = grid_of((inner, z.pad), 0), grid_of((inner, z.pad), 1)
    lane_of = row // head * LANES + row % head
    first = (col == lane_of).astype(F32)
    second = (col == lane_of + head).astype(F32)
    low, high = first.astype(BF), second.astype(BF)
    scaled = (first * head**-0.5).astype(BF)
    w1_ref[:, : z.pad] = nn(win_ref[0], scaled).astype(BF)
    w1_ref[:, z.pad :] = (nn(win_ref[1], low) + nn(win_ref[2], high)).astype(BF)
    vec_ref[0:1, :] = gain_ref[...].astype(F32)[0:1]
    vec_ref[1:2, :] = shift_ref[...].astype(F32)[0:1]
    vec_ref[2:3, : z.pad] = nn(bin_ref[...], scaled)[0:1]
    vec_ref[2:3, z.pad :] = nn(bin_ref[...], high)[1:2]
    vec_ref[3:4, :] = bout_ref[...].astype(F32)
    vec_ref[4:5, :] = gain_ref[...].astype(F32)[1:2]
    vec_ref[5:6, :] = shift_ref[...].astype(F32)[1:2]
    vec_ref[6:7, :] = bup_ref[...].astype(F32)
    vec_ref[7:8, :] = bdn_ref[...].astype(F32)
    unit = (grid_of((16, z.heads), 0) == grid_of((16, z.heads), 1)).astype(F32).astype(BF)
    swt_ref[...] = nt(unit, sw_ref[...]).astype(BF)
    wo_ref[0:inner, :] = wout_ref[...]
    wo_ref[inner:, :] = jnp.zeros((2 * LANES - inner, z.width), BF)

    at = lax.axis_index("seq")
    n, slots, cap = z.n, z.slots, z.cap
    shift = z.tiles.bit_length() - 1
    near = 1e-3

    def total(mask, value, axis):
        return jnp.sum(jnp.where(mask, value, 0.0), axis=axis, keepdims=True)

    def whole(x):
        return (x + near).astype(jnp.int32)

    for layer, rt in enumerate((rt0_ref, rt1_ref)):
        rt[...] = jnp.zeros((8, LANES), jnp.int32)
        chosen = sel_ref[layer]
        owner = lax.shift_right_arithmetic(chosen, shift)
        sub, lan = grid_of((slots, n), 0), grid_of((slots, n), 1)
        wide = jnp.zeros((slots, n), jnp.int32)
        for d in range(z.S):
            column = jnp.sum(
                jnp.where(
                    grid_of((slots, slots), 0) == grid_of((slots, slots), 1),
                    chosen[d : d + 1].astype(F32) + 1.0,
                    0.0,
                ),
                axis=1,
                keepdims=True,
            )
            wide = jnp.where(lan // cap == d, whole(column) - 1, wide)
        mine = lax.shift_right_arithmetic(wide, shift) == at
        order = nn(
            (grid_of((slots, slots), 0) > grid_of((slots, slots), 1)).astype(F32), mine.astype(F32)
        )
        taken = mine & (whole(order) == lan % cap)
        head_of = sub // z.tiles
        inner_tile = wide - at * z.tiles
        rt[SEND : SEND + 1, :n] = whole(
            total(taken, (head_of * (z.tiles + 1) + inner_tile).astype(F32), 0)
        ) + 1
        present = jnp.sum(taken.astype(F32), axis=0, keepdims=True)
        key = total(taken, (head_of * z.tiles + inner_tile - slots).astype(F32), 0) + slots
        own = jnp.sum(
            jnp.where(grid_of((z.S, slots), 0) == at, chosen.astype(F32) + 1.0, 0.0), axis=0, keepdims=True
        )
        square_row, square_col = grid_of((slots, slots), 0), grid_of((slots, slots), 1)
        own_column = total(square_row == square_col, own, 1)
        own_row = whole(own) - 1
        own_col = whole(own_column) - 1
        owner_row = lax.shift_right_arithmetic(own_row, shift)
        owner_col = lax.shift_right_arithmetic(own_col, shift)
        same = owner_row == owner_col
        place_row = whole(jnp.sum((same & (square_row < square_col)).astype(F32), axis=0, keepdims=True))
        place_col = whole(jnp.sum((same & (square_col < square_row)).astype(F32), axis=1, keepdims=True))
        live = own_row >= 0
        rt[ARR : ARR + 1, :slots] = jnp.where(live, owner_row * cap + place_row, at * cap)
        rt[POS : POS + 1, :slots] = jnp.where(live, own_row * TILE, FAR)
        matched = (owner_col == lan // cap) & (place_col == lan % cap)
        rt[INV : INV + 1, :n] = whole(total(matched, sub.astype(F32), 0))
        big_row, big_col = grid_of((n, n), 0), grid_of((n, n), 1)
        key_col = total(big_row == big_col, key, 1)
        rank = jnp.sum(
            ((key < key_col) | ((key == key_col) & (big_col < big_row))).astype(F32), axis=1, keepdims=True
        )
        at_rank = whole(rank) == big_col
        rt[ORD : ORD + 1, :n] = whole(total(at_rank, big_row.astype(F32), 0))
        sorted_key = total(at_rank, key_col, 0)
        before = total(whole(rank) + 1 == big_col, key_col + 1.0, 0) - 1.0
        rt[CONT : CONT + 1, :n] = (sorted_key == before).astype(jnp.int32)
        tile = grid_of((n, slots), 1).astype(F32)
        upto = jnp.sum((key_col <= tile).astype(F32), axis=0, keepdims=True)
        has = jnp.sum((key_col == tile).astype(F32), axis=0, keepdims=True)
        rt[LAST : LAST + 1, :slots] = whole(jnp.where(has > 0.5, upto - 1.0, n * 1.0))
        rt[ENDS : ENDS + 1, :] = jnp.where(grid_of((1, LANES), 1) == 0, ends_ref[0], ends_ref[1])


def prepare(z, ends, sel, win, bin_, sw, wout, bout, bup, bdn, gain, shift):
    table = jax.ShapeDtypeStruct((8, LANES), jnp.int32)
    outs = pl.pallas_call(
        functools.partial(prepare_kernel, z),
        out_shape=(
            jax.ShapeDtypeStruct((8, z.width), F32),
            jax.ShapeDtypeStruct((z.width, 2 * z.pad), BF),
            jax.ShapeDtypeStruct((16, z.width), BF),
            jax.ShapeDtypeStruct((2 * LANES, z.width), BF),
            table,
            table,
        ),
        in_specs=[smem()] + [vmem()] * 10,
        out_specs=tuple(vmem() for _ in range(6)),
        name="prepare",
    )(ends, sel, win, bin_, sw, wout, bout, bup, bdn, gain, shift)
    return dict(zip(WEIGHTS[:4], outs)), outs[4:]


def to_tensor(step, me):
    return {"tensor": partner(me, step)}


def remote(src, dst, send, recv, target):
    return pltpu.make_async_remote_copy(
        src_ref=src, dst_ref=dst, send_sem=send, recv_sem=recv, device_id=target, device_id_type=MESH
    )


def signal(target, barrier):
    pl.semaphore_signal(barrier, inc=1, device_id=target, device_id_type=MESH)


class Spread:
    def __init__(self, me, view, sends, recvs):
        self.me, self.view, self.sends, self.recvs = me, view, sends, recvs

    def copy(self, i):
        me, x, y = self.me, partner(self.me, 1), partner(self.me, 2)
        owner, half, step = ((me, 0, 1), (me, 1, 2), (me, 1, 1), (me, 0, 2), (x, 0, 2), (y, 1, 1))[i]
        ref = self.view(owner, half)
        return remote(ref, ref, self.sends(i), self.recvs(i), to_tensor(step, me))

    def start(self):
        for i in range(4):
            self.copy(i).start()

    def forward(self):
        for i in range(2):
            self.copy(i).wait_recv()
            self.copy(4 + i).start()

    def wait(self, step):
        for i in ((), (2,), (3,), (4, 5))[step]:
            self.copy(i).wait_recv()

    def finish(self):
        for i in range(6):
            self.copy(i).wait_send()


class Collect:
    def __init__(self, z, me, send, got, via, sends, recvs):
        self.me, self.send, self.got, self.via, self.sends, self.recvs = me, send, got, via, sends, recvs
        half = z.block // 2
        self.halves = (pl.ds(0, half), pl.ds(half, half))

    def copy(self, i):
        top, bottom = self.halves
        block, rows, target, step = (
            (2, top, self.via.at[0], 1),
            (2, bottom, self.via.at[1], 2),
            (0, top, self.got.at[0, top, :], 1),
            (1, bottom, self.got.at[1, bottom, :], 2),
            (0, bottom, self.got.at[0, bottom, :], 1),
            (1, top, self.got.at[1, top, :], 2),
        )[i]
        return remote(
            self.send.at[block, rows, :], target, self.sends(i), self.recvs(i), to_tensor(step, self.me)
        )

    def put(self, step, value):
        for wanted, copies in ((3, (0, 1)), (1, (2,)), (2, (3,))):

            @pl.when(step == wanted)
            def _(wanted=wanted, copies=copies):
                self.send[wanted - 1] = value().astype(BF)
                for i in copies:
                    self.copy(i).start()

    def join(self):
        top, bottom = self.halves
        for i, block, rows in ((1, 0, bottom), (0, 1, top)):
            self.copy(i).wait_recv()
            joined = self.send[block, rows, :].astype(F32) + self.via[i].astype(F32)
            self.send[block, rows, :] = joined.astype(BF)
            self.copy(5 - i).start()

    def total(self, own):
        for i in range(2, 6):
            self.copy(i).wait_recv()
        return own + self.got[0].astype(F32) + self.got[1].astype(F32)

    def finish(self):
        for i in range(6):
            self.copy(i).wait_send()


def visiting(k):
    return jnp.where(k == 0, 3, jnp.where(k == 3, 0, k))


class Saver:
    def __init__(self, sems):
        self.sems, self.copies = sems, []

    def save(self, src, dst):
        copy = pltpu.make_async_copy(src, dst, self.sems.at[len(self.copies)])
        copy.start()
        self.copies.append(copy)

    def finish(self):
        for copy in self.copies:
            copy.wait()


FORWARD_OUTS = KEPT + ("res",)
FORWARD_SCRATCH = (
    "gt", "gate", "edge", "edge_gate", "send_kv", "send_gate", "got_gate", "far_gate", "wo_all", "wo_high",
    "pair_all", "single_all", "part_send", "part_got", "part_via", "own_part", "kv_ss", "kv_rs", "gate_ss", "gate_rs", "edge_ss", "edge_rs",
    "wo_ss", "wo_rs", "o_ss", "o_rs", "part_ss", "part_rs", "res_ss", "res_rs", "swap_ss", "swap_rs", "load", "saved",
)


class Refs:
    def __init__(self, names, refs):
        assert len(names) == len(refs), (len(names), len(refs))
        for name, ref in zip(names, refs):
            setattr(self, name, ref)


def forward_kernel(z, layer, *refs):
    count = len(WEIGHTS)
    rt, r_ref = refs[:2]
    own = dict(zip(WEIGHTS, refs[2 : 2 + count]))
    refs = refs[2 + count :]
    theirs = None
    if layer == 1:
        theirs, refs = dict(zip(WEIGHTS, refs[:count])), refs[count:]
    outs, refs = dict(zip(FORWARD_OUTS, refs)), refs[len(FORWARD_OUTS) :]
    if layer == 0:
        theirs, refs = dict(zip(WEIGHTS, refs[:count])), refs[count:]
    held, refs = Refs(FORWARD_OUTS, refs[: len(FORWARD_OUTS)]), refs[len(FORWARD_OUTS) :]
    used, refs = dict(zip(WEIGHTS, refs[:count])), refs[count:]
    s = Refs(FORWARD_SCRATCH, refs)
    me, at, core = lax.axis_index("tensor"), lax.axis_index("seq"), lax.axis_index("section")
    last = z.S - 1
    first_row = at * z.rows
    vec = used["vec"]

    def load(i, source):
        name = WEIGHTS[i]
        return pltpu.make_async_copy(source[name], used[name], s.load.at[i])

    def swap(i):
        name = WEIGHTS[i]
        return remote(own[name], theirs[name], s.swap_ss.at[i], s.swap_rs.at[i], {"section": 1 - core})

    @pl.when(core == layer)
    def _():
        for i in range(count):
            load(i, own).start()

    if layer == 1:

        @pl.when(core != layer)
        def _():
            for i in range(count):
                load(i, theirs).start()

    def ready(*wanted):
        if layer == 0:

            @pl.when(core != layer)
            def _():
                for i in wanted:
                    swap(i).wait_recv()
                    load(i, theirs).start()

        for i in wanted:
            load(i, own).wait()

    held.ckv[at * z.cap] = jnp.zeros((TILE, LANES), BF)
    barrier = pltpu.get_barrier_semaphore()
    for step in range(1, z.T):
        signal(to_tensor(step, me), barrier)
    if layer == 0:
        signal({"section": 1 - core}, barrier)

    def greet(d, _):
        signal({"seq": d}, barrier)
        return 0

    lax.fori_loop(0, at, greet, 0)
    pl.semaphore_wait(barrier, z.T - 1 + last - at + (layer == 0))
    if layer == 0:
        for i in range(count):
            swap(i).start()
    saver = Saver(s.saved)
    per_block = z.block // TILE
    ready(0)

    def norm_in(b, _):
        rows = pl.ds(b * z.block, z.block)
        y, _ = normed(r_ref[rows, :].astype(F32))
        held.n1[rows, :] = (y * vec[0:1, :] + vec[1:2, :]).astype(BF)
        return 0

    lax.fori_loop(0, z.T, norm_in, 0)
    saver.save(held.n1, outs["n1"])
    ready(1, 2)

    def project(b, _):
        rows = pl.ds(b * z.block, z.block)
        qkv = (nn(held.n1[rows, :], used["w1"][...]) + vec[2:3, :]).astype(BF)
        held.q[rows, :] = qkv[:, : z.pad]
        for h in range(z.heads):
            pairs = qkv[:, z.pad + h * LANES : z.pad + (h + 1) * LANES]
            held.kvt[pl.ds(h * (z.tiles + 1) + 1 + b * per_block, per_block)] = pairs.reshape(
                per_block, TILE, LANES
            )
        return 0

    lax.fori_loop(0, z.T, project, 0)
    score = nt(used["swt"][...], held.n1[...])[0:8]
    held.st[...] = score
    gate = jnp.minimum(score, 0.0) - jnp.log1p(jnp.exp(-jnp.abs(score)))
    s.gt[:, 0:LANES] = jnp.zeros((8, LANES), F32)
    s.gt[:, LANES : LANES + z.rows] = gate.astype(BF).astype(F32)
    s.gt[:, LANES + z.rows :] = jnp.zeros((8, LANES), F32)
    for t in range(z.tiles + 1):
        for h in range(z.heads):
            s.gate[h * (z.tiles + 1) + t, 0:1, :] = s.gt[
                h : h + 1, TILE + t * TILE : TILE + t * TILE + LANES
            ]

    def edge_copies():
        after = {"seq": jnp.minimum(at + 1, last)}
        return [
            remote(
                held.kvt.at[h * (z.tiles + 1) + z.tiles],
                s.edge.at[h],
                s.edge_ss.at[h],
                s.edge_rs.at[h],
                after,
            )
            for h in range(z.heads)
        ] + [
            remote(
                s.gt.at[:, pl.ds(z.rows, LANES)],
                s.edge_gate,
                s.edge_ss.at[z.heads],
                s.edge_rs.at[z.heads],
                after,
            )
        ]

    @pl.when(at < last)
    def _():
        for copy in edge_copies():
            copy.start()

    def tile_copies(d, source):
        return (
            remote(
                s.send_kv.at[d],
                held.ckv.at[pl.ds(source * z.cap, z.cap)],
                s.kv_ss.at[d],
                s.kv_rs.at[source],
                {"seq": d},
            ),
            remote(
                s.send_gate.at[d], s.got_gate.at[source], s.gate_ss.at[d], s.gate_rs.at[source], {"seq": d}
            ),
        )

    def pack(k, _):
        d = z.S - 1 - k

        def slot(i, _):
            u = rt[SEND, d * z.cap + i]
            s.send_kv[d, i] = held.kvt[u]
            s.send_gate[d, pl.ds(i, 1), :] = s.gate[u][0:1]
            return 0

        lax.fori_loop(0, z.cap, slot, 0)
        for copy in tile_copies(d, at):
            copy.start()
        return 0

    lax.fori_loop(0, last - at, pack, 0)
    ready(3)

    def wo_copy(step):
        return remote(
            used["wo"], s.wo_all.at[me], s.wo_ss.at[step], s.wo_rs.at[step], to_tensor(step, me)
        )

    for step in range(1, z.T):
        wo_copy(step).start()
    s.wo_all[me] = used["wo"][...]
    saver.save(held.q, outs["q"])
    saver.save(held.st, outs["st"])

    def landed(source, _):
        for copy in tile_copies(last, source):
            copy.wait_recv()
        for i in range(z.cap):
            s.far_gate[source * z.cap + i, 0:1, :] = s.got_gate[source, i : i + 1, :]
        return 0

    lax.fori_loop(0, at, landed, 0)
    lane = grid_of((TILE, LANES), 1)
    row = grid_of((TILE, LANES), 0)
    for h in range(z.heads):
        held.kvt[h * (z.tiles + 1)] = jnp.zeros((TILE, LANES), BF)

    @pl.when(at > 0)
    def _():
        for copy in edge_copies():
            copy.wait_recv()
        for h in range(z.heads):
            held.kvt[h * (z.tiles + 1)] = s.edge[h]
            s.gate[h * (z.tiles + 1), 0:1, :] = jnp.where(
                lane[0:1] < TILE,
                pltpu.roll(s.edge_gate[...], TILE, 1)[h : h + 1],
                s.gate[h * (z.tiles + 1), 0:1, :],
            )

    saver.save(held.kvt, outs["kvt"])
    saver.save(held.ckv, outs["ckv"])

    def attend(t):
        base = pl.multiple_of(t * TILE, TILE)
        query = first_row + base + row
        begin = jnp.where(
            query >= rt[ENDS, 1],
            rt[ENDS, 1],
            jnp.where(query >= rt[ENDS, 0], rt[ENDS, 0], 0),
        )
        key = first_row + base - TILE + lane
        near_ok = (key <= query) & (key > query - TILE) & (key >= begin)
        mixed = []
        for h in range(z.heads):
            cols = slice(h * LANES, (h + 1) * LANES)
            u = h * z.tiles + t
            arrived = rt[ARR, u]
            far = held.ckv[arrived]
            near = held.kvt[pl.ds(h * (z.tiles + 1) + t, 2)].reshape(2 * TILE, LANES)
            keys = jnp.concatenate([near, far, far], axis=0)
            gates = jnp.concatenate(
                [s.gate[h * (z.tiles + 1) + t, 0:1, :], s.far_gate[arrived][0:1]], axis=1
            )
            far_ok = (rt[POS, u] + lane >= begin) & (lane < TILE)
            score = jnp.where(
                jnp.concatenate([near_ok, far_ok], axis=1),
                nt(held.q[pl.ds(base, TILE), cols], keys) + gates,
                MASKED,
            )
            raised = jnp.exp(score - jnp.max(score, axis=-1, keepdims=True))
            p = (raised * (1.0 / jnp.sum(raised, axis=-1, keepdims=True))).astype(BF)
            held.p[t * z.heads + h] = p
            mixed.append(nn(p, keys))
        pair = jnp.where(lane < TILE, pltpu.roll(mixed[0], TILE, 1), mixed[1]).astype(BF)
        single = pltpu.roll(mixed[2], TILE, 1)
        held.o[pl.ds(base, TILE), 0:LANES] = pair
        held.o[pl.ds(base, TILE), LANES:] = single.astype(BF)
        s.pair_all[me, pl.ds(base, TILE), :] = pair
        return single, mixed[2]

    half_rows = z.block // 2

    def pair_spread(b):
        return Spread(
            me,
            lambda owner, half: s.pair_all.at[owner, pl.ds(b * z.block + half * half_rows, half_rows), :],
            lambda i: s.o_ss.at[b * 12 + i],
            lambda i: s.o_rs.at[b * 12 + i],
        )

    def single_spread(b):
        return Spread(
            me,
            lambda owner, half: s.single_all.at[
                owner, pl.ds(b * half_rows + half * (half_rows // 2), half_rows // 2), :
            ],
            lambda i: s.o_ss.at[b * 12 + 6 + i],
            lambda i: s.o_rs.at[b * 12 + 6 + i],
        )

    def attend_block(b, _):
        def two(i, _):
            t = b * per_block + 2 * i
            even, _ = attend(t)
            _, odd = attend(t + 1)
            s.single_all[me, pl.ds(pl.multiple_of(b * half_rows + i * TILE, TILE), TILE), :] = jnp.where(
                lane < TILE, even, odd
            ).astype(BF)
            return 0

        lax.fori_loop(0, per_block // 2, two, 0)
        pair_spread(b).start()
        single_spread(b).start()

        @pl.when(b > 0)
        def _():
            pair_spread(b - 1).forward()
            single_spread(b - 1).forward()

        return 0

    lax.fori_loop(0, z.T, attend_block, 0)
    pair_spread(z.T - 1).forward()
    single_spread(z.T - 1).forward()
    saver.save(held.p, outs["p"])
    saver.save(held.o, outs["o"])
    ready(4, 5)
    for step in range(1, z.T):
        wo_copy(step).wait()
    for t in range(z.T):
        s.wo_high[t, 0:TILE, :] = jnp.zeros((TILE, z.width), BF)
        s.wo_high[t, TILE:, :] = s.wo_all[t, LANES : LANES + TILE, :]
    collect = Collect(
        z, me, s.part_send, s.part_got, s.part_via, lambda i: s.part_ss.at[i], lambda i: s.part_rs.at[i]
    )

    def feed(k, _):
        step = visiting(k)
        block = partner(me, step)
        rows = pl.ds(pl.multiple_of(block * z.block, z.block), z.block)
        few = pl.ds(pl.multiple_of(block * half_rows, half_rows), half_rows)
        for other in range(1, z.T):
            pair_spread(block).wait(other)
            single_spread(block).wait(other)
        mixed = nn(s.pair_all[0, rows, :], s.wo_all[0, 0:LANES, :])
        even = nn(s.single_all[0, few, :], s.wo_all[0, LANES:, :])
        odd = nn(s.single_all[0, few, :], s.wo_high[0])
        for other in range(1, z.T):
            mixed += nn(s.pair_all[other, rows, :], s.wo_all[other, 0:LANES, :])
            even += nn(s.single_all[other, few, :], s.wo_all[other, LANES:, :])
            odd += nn(s.single_all[other, few, :], s.wo_high[other])
        turns = []
        for i in range(per_block // 2):
            turns += [even[i * TILE : (i + 1) * TILE], odd[i * TILE : (i + 1) * TILE]]
        mixed += jnp.concatenate(turns, axis=0)
        middle = r_ref[rows, :].astype(F32) + mixed + vec[3:4, :]
        held.mid[...] = middle
        y, _ = normed(middle)
        n2 = (y * vec[4:5, :] + vec[5:6, :]).astype(BF)
        held.n2[rows, :] = n2
        u = nn(n2, used["wup"][...]) + vec[6:7, :]
        held.u[rows, :] = u.astype(BF)
        act = (0.5 * u * (1.0 + jnp.tanh(GELU_K * (u + GELU_A * u * u * u)))).astype(BF)
        held.act[rows, :] = act
        s.own_part[...] = nn(act, used["wdn"][...])

        collect.put(step, lambda: s.own_part[...])
        return 0

    lax.fori_loop(0, z.T, feed, 0)
    collect.join()
    for name in ("mid", "n2", "u", "act"):
        saver.save(getattr(held, name), outs[name])
    total = collect.total(held.mid[...] + s.own_part[...] + vec[7:8, :])
    own_rows = pl.ds(pl.multiple_of(me * z.block, z.block), z.block)
    held.res[own_rows, :] = total.astype(BF)
    spread = Spread(
        me,
        lambda owner, half: held.res.at[
            pl.ds(pl.multiple_of(owner * z.block + half * half_rows, half_rows), half_rows), :
        ],
        lambda i: s.res_ss.at[i],
        lambda i: s.res_rs.at[i],
    )
    spread.start()
    collect.finish()

    def finish_block(b, _):
        pair_spread(b).finish()
        single_spread(b).finish()
        return 0

    lax.fori_loop(0, z.T, finish_block, 0)

    def sent(d, _):
        for copy in tile_copies(d, at):
            copy.wait_send()
        return 0

    lax.fori_loop(at + 1, z.S, sent, 0)

    @pl.when(at < last)
    def _():
        for copy in edge_copies():
            copy.wait_send()

    if layer == 0:

        @pl.when(core == layer)
        def _():
            for i in range(count):
                swap(i).wait_recv()

        for i in range(count):
            swap(i).wait_send()
    spread.forward()
    for step in range(1, z.T):
        spread.wait(step)
    spread.finish()
    saver.save(held.res, outs["res"])
    saver.finish()


def forward(z, layer, route, r, own, theirs):
    rows, width, heads = z.rows, z.width, z.heads
    shapes = dict(
        n1=((rows, width), BF),
        q=((rows, z.pad), BF),
        kvt=((heads * (z.tiles + 1), TILE, LANES), BF),
        st=((8, rows), F32),
        p=((z.slots, TILE, 2 * LANES), BF),
        ckv=((z.n, TILE, LANES), BF),
        o=((rows, 2 * LANES), BF),
        mid=((z.block, width), F32),
        n2=((rows, width), BF),
        u=((rows, z.hidden), BF),
        act=((rows, z.hidden), BF),
        res=((rows, width), BF),
    )
    dma = pltpu.SemaphoreType.DMA
    shaped = [jax.ShapeDtypeStruct(*shapes[name]) for name in FORWARD_OUTS]
    mine = [own[name] for name in WEIGHTS]
    if layer == 0:
        shaped += [jax.ShapeDtypeStruct(value.shape, value.dtype) for value in mine]
        inputs = [route, r, *mine]
    else:
        inputs = [route, r, *mine, *(theirs[name] for name in WEIGHTS)]
    outs = pl.pallas_call(
        functools.partial(forward_kernel, z, layer),
        out_shape=tuple(shaped),
        in_specs=[smem(), vmem()] + [anywhere()] * (len(inputs) - 2),
        out_specs=tuple(anywhere() for _ in shaped),
        scratch_shapes=[
            *(pltpu.VMEM(*shapes[name]) for name in FORWARD_OUTS),
            *(pltpu.VMEM(value.shape, value.dtype) for value in mine),
            pltpu.VMEM((8, rows + 2 * LANES), F32),
            pltpu.VMEM((heads * (z.tiles + 1), 8, LANES), F32),
            pltpu.VMEM((heads, TILE, LANES), BF),
            pltpu.VMEM((8, LANES), F32),
            pltpu.VMEM((z.S, z.cap, TILE, LANES), BF),
            pltpu.VMEM((z.S, z.capg, LANES), F32),
            pltpu.VMEM((z.S, z.capg, LANES), F32),
            pltpu.VMEM((z.n, 8, LANES), F32),
            pltpu.VMEM((z.T, 2 * LANES, width), BF),
            pltpu.VMEM((z.T, LANES, width), BF),
            pltpu.VMEM((z.T, rows, LANES), BF),
            pltpu.VMEM((z.T, rows // 2, LANES), BF),
            pltpu.VMEM((z.T - 1, z.block, width), BF),
            pltpu.VMEM((2, z.block, width), BF),
            pltpu.VMEM((2, z.block // 2, width), BF),
            pltpu.VMEM((z.block, width), F32),
            dma((z.S,)),
            dma((z.S,)),
            dma((z.S,)),
            dma((z.S,)),
            dma((heads + 1,)),
            dma((heads + 1,)),
            dma((z.T,)),
            dma((z.T,)),
            dma((z.T * 12,)),
            dma((z.T * 12,)),
            dma((6,)),
            dma((6,)),
            dma((6,)),
            dma((6,)),
            dma((len(WEIGHTS),)),
            dma((len(WEIGHTS),)),
            dma((len(WEIGHTS),)),
            dma((len(FORWARD_OUTS),)),
        ],
        compiler_params=pltpu.CompilerParams(
            collective_id=layer, has_side_effects=True, vmem_limit_bytes=LIMIT
        ),
        name=f"forward{layer}",
    )(*inputs)
    kept = dict(zip(FORWARD_OUTS, outs))
    return (kept, dict(zip(WEIGHTS, outs[len(FORWARD_OUTS) :]))) if layer == 0 else (kept, theirs)


BACKWARD_SCRATCH = (
    "du", "part_send", "part_got", "part_via", "own_part", "dr2", "ob", "dout", "dqkv", "dkv", "dgate", "far", "far_gate",
    "send_kv", "send_gate", "got_kv", "got_gate", "got_gate_row", "edge_send", "edge_got", "edge_gate_got", "sum",
    "gate_sum", "tile_gate", "ds", "stat", "stat_got", "grad", "bounce",
    "pa", "pb", "pc", "pd", "xa", "xb", "xc", "xd", "sa", "sb", "sc", "sd", "ta", "tb", "tc", "td", "ha", "hb", "hc",
    "kv_ss", "kv_rs", "gate_ss", "gate_rs", "edge_ss", "edge_rs", "part_ss", "part_rs", "ob_ss", "ob_rs",
    "grad_ss", "grad_rs", "stat_ss", "stat_rs", "give_ss", "give_rs", "cross_ss", "cross_rs", "hand_ss", "hand_rs",
    "move_ss", "move_rs", "load", "saved",
)


def backward_kernel(z, layer, *refs):
    count = len(WEIGHTS)
    rt = refs[0]
    c_any, r_any, first_any, second_any = refs[1:5]
    refs = refs[5:]
    own, refs = dict(zip(WEIGHTS, refs[:count])), refs[count:]
    theirs, refs = dict(zip(WEIGHTS, refs[:count])), refs[count:]
    kept, refs = dict(zip(KEPT, refs[: len(KEPT)])), refs[len(KEPT) :]
    grad_out, both_out, g_out = refs[:3]
    refs = refs[3:]
    c_ref, r_ref, refs = refs[0], refs[1], refs[2:]
    used, refs = dict(zip(WEIGHTS, refs[:count])), refs[count:]
    k, refs = Refs(KEPT, refs[: len(KEPT)]), refs[len(KEPT) :]
    s = Refs(BACKWARD_SCRATCH, refs)
    me, at, core = lax.axis_index("tensor"), lax.axis_index("seq"), lax.axis_index("section")
    last = z.S - 1
    vec = used["vec"]
    own_rows = pl.ds(pl.multiple_of(me * z.block, z.block), z.block)
    W = z.width
    sources = {"c": (c_any, c_ref)}
    sources |= {name: (kept[name], getattr(k, name)) for name in KEPT}
    sources["r"] = (r_any.at[own_rows, :], r_ref)
    order = ("c", "wdn", "u", "wup", "act", "n2", "vec", "mid", "wo", "p", "q", "kvt", "ckv", "o", "st", "w1", "swt", "n1", "r")

    def loads(name, which):
        i = order.index(name)
        if name in WEIGHTS:
            return pltpu.make_async_copy(which[name], used[name], s.load.at[i])
        return pltpu.make_async_copy(*sources[name], s.load.at[i])

    for name in order:
        if name in WEIGHTS:

            @pl.when(core == layer)
            def _(name=name):
                loads(name, own).start()

            @pl.when(core != layer)
            def _(name=name):
                loads(name, theirs).start()
        else:
            loads(name, None).start()

    def ready(*names):
        for name in names:
            loads(name, own).wait()

    barrier = pltpu.get_barrier_semaphore()
    for step in range(1, z.T):
        signal(to_tensor(step, me), barrier)
    signal({"section": 1 - core}, barrier)

    def greet(i, _):
        signal({"seq": (at + i) % z.S}, barrier)
        return 0

    lax.fori_loop(1, z.S, greet, 0)
    pl.semaphore_wait(barrier, z.T - 1 + 1 + last)
    saver = Saver(s.saved)
    across = {"section": 1 - core}

    def move(src, i, part):
        return remote(src.at[part], both_out.at[core].at[part], s.move_ss.at[i], s.move_rs.at[i], across)

    def keep(src, part):
        return pltpu.make_async_copy(src.at[part], both_out.at[core].at[part], s.saved.at[3])

    def fetch(src, i):
        return pltpu.make_async_copy(src, s.bounce.at[i], s.saved.at[1 + i])

    everything = pl.ds(0, z.rows)
    stay, leave = s.bounce.at[0], s.bounce.at[1]

    @pl.when(core == 0)
    def _():
        fetch(second_any, 1).start()
        if layer == 1:
            fetch(first_any, 0).start()

    @pl.when(core == 1)
    def _():
        fetch(second_any, 0).start()
        if layer == 1:
            fetch(first_any, 1).start()

    def forward_rows():
        def leaving():
            fetch(second_any, 1).wait()
            move(leave, 0, everything).start()

        def staying():
            fetch(second_any, 0).wait()
            keep(stay, everything).start()

        if layer == 1:
            leaving()
            staying()
        else:
            pl.when(core == 0)(leaving)
            pl.when(core == 1)(staying)

    collects = [
        Collect(
            z,
            me,
            s.part_send.at[phase],
            s.part_got.at[phase],
            s.part_via.at[phase],
            lambda i, phase=phase: s.part_ss.at[phase, i],
            lambda i, phase=phase: s.part_rs.at[phase, i],
        )
        for phase in range(2)
    ]
    half_rows = z.block // 2

    def rows_spread(ref, sends, recvs):
        return Spread(
            me,
            lambda owner, half: ref.at[
                pl.ds(pl.multiple_of(owner * z.block + half * half_rows, half_rows), half_rows), :
            ],
            lambda i: sends.at[i],
            lambda i: recvs.at[i],
        )

    ready("c", "wdn", "u", "wup")

    def ff_back(i, _):
        step = visiting(i)
        rows = pl.ds(pl.multiple_of(partner(me, step) * z.block, z.block), z.block)
        u = k.u[rows, :].astype(F32)
        squared = u * u
        bent = jnp.tanh(GELU_K * (u + GELU_A * squared * u))
        slope = 0.5 * (1.0 + bent) + 0.5 * u * (1.0 - bent * bent) * (
            GELU_K * (1.0 + 3.0 * GELU_A * squared)
        )
        du = (nt(c_ref[rows, :], used["wdn"][...]) * slope).astype(BF)
        s.du[rows, :] = du
        s.own_part[...] = nt(du, used["wup"][...])

        collects[0].put(step, lambda: s.own_part[...])
        return 0

    lax.fori_loop(0, z.T, ff_back, 0)
    collects[0].join()
    ones = jnp.ones((16, z.rows), BF)
    s.stat[...] = jnp.zeros((24, W), F32)

    mine = (s.pa, s.pb, s.pc, s.pd)
    theirs_part = (s.xa, s.xb, s.xc, s.xd)
    summed = (s.sa, s.sb, s.sc, s.sd)
    crossed = (s.ta, s.tb, s.tc, s.td)
    handed = (s.ha, s.hb, s.hc)

    def give(piece):
        return remote(
            mine[piece].at[1 - core], theirs_part[piece], s.give_ss.at[piece], s.give_rs.at[piece], across
        )

    def cross(piece, d, source):
        return remote(
            summed[piece].at[d],
            crossed[piece].at[source],
            s.cross_ss.at[piece, d],
            s.cross_rs.at[piece, source],
            {"seq": d},
        )

    def hand(piece):
        return remote(
            summed[piece].at[at], handed[piece], s.hand_ss.at[piece], s.hand_rs.at[piece], across
        )

    span = math.lcm(z.share, 16)

    def add_up(piece):
        give(piece).wait_recv()

        def chunk(i, _):
            rows = pl.ds(pl.multiple_of(i * span, span), span)
            value = mine[piece][core, rows, :].astype(F32) + theirs_part[piece][rows, :].astype(F32)
            for j in range(span // z.share):
                d = i * (span // z.share) + j
                rows_of = value[j * z.share : (j + 1) * z.share]
                if z.padded > z.share:
                    rows_of = jnp.concatenate(
                        [rows_of, jnp.zeros((z.padded - z.share, value.shape[1]), F32)], axis=0
                    )
                summed[piece][d] = rows_of.astype(BF)

                @pl.when(d != at)
                def _():
                    cross(piece, d, at).start()

            return 0

        lax.fori_loop(0, W // span, chunk, 0)

    offsets = [sum(z.pieces[:piece]) for piece in range(len(z.pieces))]

    def reduce(piece):
        def wait(i, _):
            d = (at + i) % z.S
            cross(piece, d, d).wait_recv()
            return 0

        lax.fori_loop(1, z.S, wait, 0)

        def add(i, running):
            return running + crossed[piece][(at + i) % z.S].astype(F32)

        total = lax.fori_loop(1, z.S, add, summed[piece][at].astype(F32))
        cols = slice(offsets[piece], offsets[piece] + z.pieces[piece])
        g_out[core, :, cols] = total[: z.share]

        @pl.when(core != layer)
        def _():
            if piece < len(handed):
                summed[piece][at] = total.astype(BF)
                hand(piece).start()

    def take(piece):
        cols = slice(offsets[piece], offsets[piece] + z.pieces[piece])

        @pl.when(core == layer)
        def _():
            hand(piece).wait_recv()
            g_out[1 - core, :, cols] = handed[piece][...].astype(F32)[: z.share]

    forward_rows()
    ready("act", "n2")
    s.pa[0] = tn(c_ref[...], k.act[...]).astype(BF)
    s.pa[1] = tn(k.n2[...], s.du[...]).astype(BF)
    give(0).start()
    s.stat[8:9, :] = nn(ones, s.du[...])[0:1]
    s.stat[9:10, :] = nn(ones, c_ref[...])[0:1]
    ready("vec", "mid", "wo")
    grad = collects[0].total(s.own_part[...])
    y, spread = normed(k.mid[...])
    dr2 = c_ref[own_rows, :].astype(F32) + norm_back(grad, vec[4:5, :], y, spread)
    s.dr2[...] = dr2
    s.ob[own_rows, :] = dr2.astype(BF)

    ob_spread = rows_spread(s.ob, s.ob_ss, s.ob_rs)
    ob_spread.start()
    s.stat[0:1, :] = column_sum(dr2)
    s.stat[1:2, :] = column_sum(grad * y)
    s.stat[2:3, :] = column_sum(grad)
    s.dkv[...] = jnp.zeros((z.rows + TILE, z.pad), F32)
    ob_spread.forward()
    add_up(0)
    lane_wide = grid_of((z.block, LANES), 1)

    def out_back(step, _):
        for wanted in range(1, z.T):

            @pl.when(step == wanted)
            def _(wanted=wanted):
                ob_spread.wait(wanted)

        rows = pl.ds(pl.multiple_of(partner(me, step) * z.block, z.block), z.block)
        dout = nt(s.ob[rows, :], used["wo"][...])
        pair, single = dout[:, :LANES], dout[:, LANES:]
        for h, value in enumerate((pltpu.roll(pair, TILE, 1), pair, pltpu.roll(single, TILE, 1))):
            s.dout[rows, h * LANES : (h + 1) * LANES] = jnp.where(lane_wide < TILE, 0.0, value).astype(BF)
        return 0

    lax.fori_loop(0, z.T, out_back, 0)
    ready("p", "q", "kvt", "ckv")

    def attend_back(t):
        base = pl.multiple_of(t * TILE, TILE)
        for h in range(z.heads):
            cols = slice(h * LANES, (h + 1) * LANES)
            u = h * z.tiles + t
            arrived = rt[ARR, u]
            near = k.kvt[pl.ds(h * (z.tiles + 1) + t, 2)].reshape(2 * TILE, LANES)
            far = k.ckv[arrived]
            keys = jnp.concatenate([near, far, far], axis=0)
            query = k.q[pl.ds(base, TILE), cols]
            dout = s.dout[pl.ds(base, TILE), cols]
            p = k.p[t * z.heads + h]
            weight = p.astype(F32)
            dp = nt(dout, keys)
            dz = (weight * (dp - jnp.sum(weight * dp, axis=-1, keepdims=True))).astype(BF)
            s.dqkv[pl.ds(base, TILE), cols] = nn(dz, keys).astype(BF)
            dkeys = tn(jnp.concatenate([dz, p], axis=0), jnp.concatenate([query, dout], axis=0))
            s.dkv[pl.ds(base, 2 * TILE), cols] += dkeys[: 2 * TILE]
            s.far[u] = dkeys[2 * TILE : 3 * TILE].astype(BF)
            gates = column_sum(dz.astype(F32))
            s.dgate[t, h : h + 1, :] = gates[:, :LANES]
            s.far_gate[u, 0:1, :] = gates[:, LANES:]

    def attend_back_pair(i, _):
        attend_back(2 * i)
        attend_back(2 * i + 1)
        return 0

    lax.fori_loop(0, z.tiles // 2, attend_back_pair, 0)
    s.dgate[z.tiles] = jnp.zeros((8, LANES), F32)

    def edge_copies():
        behind = {"seq": jnp.maximum(at - 1, 0)}
        return (
            remote(s.edge_send, s.edge_got, s.edge_ss.at[0], s.edge_rs.at[0], behind),
            remote(s.dgate.at[0], s.edge_gate_got, s.edge_ss.at[1], s.edge_rs.at[1], behind),
        )

    @pl.when(at > 0)
    def _():
        s.edge_send[...] = s.dkv[0:TILE, :].astype(BF)
        for copy in edge_copies():
            copy.start()

    def tile_copies(d, source):
        return (
            remote(
                s.send_kv.at[d],
                s.got_kv.at[pl.ds(source * z.cap, z.cap)],
                s.kv_ss.at[d],
                s.kv_rs.at[source],
                {"seq": d},
            ),
            remote(
                s.send_gate.at[d], s.got_gate.at[source], s.gate_ss.at[d], s.gate_rs.at[source], {"seq": d}
            ),
        )

    def pack(d, _):
        def slot(i, _):
            u = rt[INV, d * z.cap + i]
            s.send_kv[d, i] = s.far[u]
            s.send_gate[d, pl.ds(i, 1), :] = s.far_gate[u][0:1]
            return 0

        lax.fori_loop(0, z.cap, slot, 0)
        for copy in tile_copies(d, at):
            copy.start()
        return 0

    lax.fori_loop(0, at, pack, 0)
    ready("o")
    out_grad = tn(s.ob[...], k.o[...]).astype(BF)
    s.pb[0] = out_grad[:, :LANES]
    s.pb[1] = out_grad[:, LANES:]
    give(1).start()
    s.sum[z.n] = jnp.zeros((TILE, LANES), F32)
    s.gate_sum[z.n] = jnp.zeros((8, LANES), F32)
    ready("st", "w1", "swt", "n1", "r")
    add_up(1)

    @pl.when(at < last)
    def _():
        for copy in edge_copies():
            copy.wait_recv()
        s.dkv[pl.ds(z.rows, TILE), :] += s.edge_got[...].astype(F32)
        s.dgate[z.tiles] = s.edge_gate_got[...]

    def landed(source, _):
        for copy in tile_copies(0, source):
            copy.wait_recv()
        for i in range(z.cap):
            s.got_gate_row[source * z.cap + i, 0:1, :] = s.got_gate[source, i : i + 1, :]
        return 0

    lax.fori_loop(at + 1, z.S, landed, 0)

    def gather(i, carry):
        running, gates = carry
        index = rt[ORD, i]
        joined = rt[CONT, i].astype(F32)
        running = running * joined + s.got_kv[index].astype(F32)
        gates = gates * joined + s.got_gate_row[index]
        s.sum[i] = running
        s.gate_sum[i] = gates
        return running, gates

    lax.fori_loop(0, z.n, gather, (jnp.zeros((TILE, LANES), F32), jnp.zeros((8, LANES), F32)))

    def settle(t, _):
        base = pl.multiple_of((t + 1) * TILE, TILE)
        rows = pl.ds(pl.multiple_of(t * TILE, TILE), TILE)
        for h in range(z.heads):
            cols = slice(h * LANES, (h + 1) * LANES)
            index = rt[LAST, h * z.tiles + t]
            s.dqkv[rows, z.pad + h * LANES : z.pad + (h + 1) * LANES] = (
                s.dkv[pl.ds(base, TILE), cols] + s.sum[index]
            ).astype(BF)
            s.tile_gate[t, h : h + 1, :] = s.gate_sum[index][0:1]
        return 0

    lax.fori_loop(0, z.tiles, settle, 0)
    lane = grid_of((8, LANES), 1)
    head_row = grid_of((8, LANES), 0)
    for i in range(z.tiles // 2):
        halves = []
        for t in (2 * i, 2 * i + 1):
            halves.append(pltpu.roll(s.dgate[t], TILE, 1) + s.dgate[t + 1] + s.tile_gate[t])
        joint = jnp.where(lane < TILE, halves[0], pltpu.roll(halves[1], TILE, 1))
        score = k.st[:, i * LANES : (i + 1) * LANES]
        grads = jnp.where(head_row < z.heads, joint / (1.0 + jnp.exp(score)), 0.0)
        s.ds[0:8, i * LANES : (i + 1) * LANES] = grads
        s.ds[8:16, i * LANES : (i + 1) * LANES] = jnp.zeros((8, LANES), F32)

    def in_back(i, _):
        step = visiting(i)
        rows = pl.ds(pl.multiple_of(partner(me, step) * z.block, z.block), z.block)
        s.own_part[...] = nt(s.dqkv[rows, :], used["w1"][...]) + tn(
            s.ds[:, rows].astype(BF), used["swt"][...]
        )

        collects[1].put(step, lambda: s.own_part[...])
        return 0

    lax.fori_loop(0, z.T, in_back, 0)
    collects[1].join()
    s.pc[0] = tn(k.n1[...], s.dqkv[:, z.pad :]).astype(BF)
    queries = tn(k.n1[...], s.dqkv[:, : z.pad])
    lane_full = grid_of((W, LANES), 1)
    s.pc[1, :, :LANES] = jnp.where(
        lane_full < TILE, queries[:, :LANES], pltpu.roll(queries[:, LANES : 2 * LANES], TILE, 1)
    ).astype(BF)
    s.pc[1, :, LANES : 2 * LANES] = queries[:, 2 * LANES :].astype(BF)
    s.pc[1, :, 2 * LANES :] = jnp.zeros((W, z.pad - 2 * LANES), BF)
    give(2).start()
    s.stat[10:13, :] = nn(s.ds[...].astype(BF), k.n1[...])[0:3]
    source, target = grid_of((W, W), 0), grid_of((W, W), 1)
    is_value = source >= z.pad
    index = jnp.where(is_value, source - z.pad, source)
    index = index // LANES * TILE + index % TILE
    each = z.heads * TILE // z.S
    wanted = index // each * z.share + index % each + jnp.where(is_value, each, 0)
    filled = (source % LANES >= TILE) == is_value
    spread_out = jnp.where(
        (wanted == target) & filled, jnp.where(is_value, 1.0, TILE**-0.5), 0.0
    ).astype(BF)
    s.stat[13:14, :] = nn(nn(ones, s.dqkv[...]).astype(BF), spread_out)[0:1]
    grad = collects[1].total(s.own_part[...])
    y, spread = normed(r_ref[...].astype(F32))
    dr = s.dr2[...] + norm_back(grad, vec[0:1, :], y, spread)
    s.grad[own_rows, :] = dr.astype(BF)
    grad_spread = rows_spread(s.grad, s.grad_ss, s.grad_rs)
    grad_spread.start()
    s.stat[3:4, :] = column_sum(grad * y)
    s.stat[4:5, :] = column_sum(grad)

    def stat_copy(step):
        return remote(
            s.stat.at[pl.ds(0, 8), :],
            s.stat_got.at[step - 1],
            s.stat_ss.at[step],
            s.stat_rs.at[step],
            to_tensor(step, me),
        )

    for step in range(1, z.T):
        stat_copy(step).start()
    shared = s.stat[0:8, :]
    for step in range(1, z.T):
        stat_copy(step).wait()
        shared += s.stat_got[step - 1]
    stats = jnp.concatenate([shared, s.stat[8:16, :]], axis=0).astype(BF)
    unit = (grid_of((16, LANES), 0) == grid_of((16, LANES), 1)).astype(F32).astype(BF)
    s.pd[core] = tn(stats, unit).astype(BF)
    s.pd[1 - core] = s.pd[core]

    @pl.when(core != layer)
    def _():
        give(3).start()

    grad_spread.forward()
    add_up(2)

    @pl.when(core == layer)
    def _():
        add_up(3)

    reduce(0)
    reduce(1)
    take(0)
    take(1)

    def block_of(step):
        return pl.ds(pl.multiple_of(partner(me, step) * z.block, z.block), z.block)

    for step in range(z.T):
        grad_spread.wait(step)
        if layer == 0:

            @pl.when(core == 1)
            def _(step=step):
                move(s.grad, step, block_of(step)).start()

    saver.save(s.grad, grad_out)
    reduce(2)
    take(2)

    @pl.when(core == layer)
    def _():
        reduce(3)

    def last_sent(i, _):
        cross(3, (at + i) % z.S, at).wait_send()
        return 0

    @pl.when(core == layer)
    def _():
        lax.fori_loop(1, z.S, last_sent, 0)

    @pl.when(core != layer)
    def _():
        give(3).wait_send()

    for piece in range(3):
        give(piece).wait_send()

        @pl.when(core != layer)
        def _(piece=piece):
            hand(piece).wait_send()

        def crossed_over(i, _, piece=piece):
            cross(piece, (at + i) % z.S, at).wait_send()
            return 0

        lax.fori_loop(1, z.S, crossed_over, 0)
    for collect in collects:
        collect.finish()
    ob_spread.finish()
    grad_spread.finish()

    def sent(d, _):
        for copy in tile_copies(d, at):
            copy.wait_send()
        return 0

    lax.fori_loop(0, at, sent, 0)

    @pl.when(at > 0)
    def _():
        for copy in edge_copies():
            copy.wait_send()

    if layer == 1:
        move(leave, 0, everything).wait()
        keep(stay, everything).wait()
    else:

        @pl.when(core == 0)
        def _():
            keep(s.grad, everything).start()
            move(leave, 0, everything).wait_send()
            for step in range(z.T):
                move(s.grad, step, block_of(step)).wait_recv()

        @pl.when(core == 1)
        def _():
            move(leave, 0, everything).wait_recv()
            for step in range(z.T):
                move(s.grad, step, block_of(step)).wait_send()

        keep(s.grad, everything).wait()
    saver.finish()


def backward(z, layer, route, c, r, first, second, own, theirs, kept):
    rows, width = z.rows, z.width
    dma = pltpu.SemaphoreType.DMA
    wide = sum(z.pieces)
    weights = [own[name] for name in WEIGHTS]
    saved = [kept[name] for name in KEPT]
    inputs = [route, c, r, first, second, *weights, *(theirs[name] for name in WEIGHTS), *saved]
    parts = [(w,) for w in z.pieces]
    return pl.pallas_call(
        functools.partial(backward_kernel, z, layer),
        out_shape=(
            jax.ShapeDtypeStruct((rows, width), BF),
            jax.ShapeDtypeStruct((2, rows, width), BF),
            jax.ShapeDtypeStruct((2, z.share, wide), F32),
        ),
        in_specs=[smem()] + [anywhere()] * (len(inputs) - 1),
        out_specs=(anywhere(), anywhere(), vmem()),
        scratch_shapes=[
            pltpu.VMEM((rows, width), BF),
            pltpu.VMEM((z.block, width), BF),
            *(pltpu.VMEM(value.shape, value.dtype) for value in weights),
            *(pltpu.VMEM(value.shape, value.dtype) for value in saved),
            pltpu.VMEM((rows, z.hidden), BF),
            pltpu.VMEM((2, z.T - 1, z.block, width), BF),
            pltpu.VMEM((2, 2, z.block, width), BF),
            pltpu.VMEM((2, 2, z.block // 2, width), BF),
            pltpu.VMEM((z.block, width), F32),
            pltpu.VMEM((z.block, width), F32),
            pltpu.VMEM((rows, width), BF),
            pltpu.VMEM((rows, z.pad), BF),
            pltpu.VMEM((rows, 2 * z.pad), BF),
            pltpu.VMEM((rows + TILE, z.pad), F32),
            pltpu.VMEM((z.tiles + 1, 8, LANES), F32),
            pltpu.VMEM((z.slots, TILE, LANES), BF),
            pltpu.VMEM((z.slots, 8, LANES), F32),
            pltpu.VMEM((z.S, z.cap, TILE, LANES), BF),
            pltpu.VMEM((z.S, z.capg, LANES), F32),
            pltpu.VMEM((z.n, TILE, LANES), BF),
            pltpu.VMEM((z.S, z.capg, LANES), F32),
            pltpu.VMEM((z.n, 8, LANES), F32),
            pltpu.VMEM((TILE, z.pad), BF),
            pltpu.VMEM((TILE, z.pad), BF),
            pltpu.VMEM((8, LANES), F32),
            pltpu.VMEM((z.n + 1, TILE, LANES), F32),
            pltpu.VMEM((z.n + 1, 8, LANES), F32),
            pltpu.VMEM((z.tiles, 8, LANES), F32),
            pltpu.VMEM((16, rows), F32),
            pltpu.VMEM((24, width), F32),
            pltpu.VMEM((z.T - 1, 8, width), F32),
            pltpu.VMEM((rows, width), BF),
            pltpu.VMEM((2, rows, width), BF),
            *(pltpu.VMEM((2, width, w), BF) for w in z.pieces),
            *(pltpu.VMEM((width, w), BF) for w in z.pieces),
            *(pltpu.VMEM((z.S, z.padded, w), BF) for w in z.pieces),
            *(pltpu.VMEM((z.S, z.padded, w), BF) for w in z.pieces),
            *(pltpu.VMEM((z.padded, w), BF) for w in z.pieces[:3]),
            dma((z.S,)),
            dma((z.S,)),
            dma((z.S,)),
            dma((z.S,)),
            dma((2,)),
            dma((2,)),
            dma((2, 6)),
            dma((2, 6)),
            dma((6,)),
            dma((6,)),
            dma((6,)),
            dma((6,)),
            dma((z.T,)),
            dma((z.T,)),
            dma((4,)),
            dma((4,)),
            dma((4, z.S)),
            dma((4, z.S)),
            dma((3,)),
            dma((3,)),
            dma((z.T,)),
            dma((z.T,)),
            dma((2 + len(WEIGHTS) + len(KEPT),)),
            dma((4,)),
        ],
        compiler_params=pltpu.CompilerParams(
            collective_id=2 + layer, has_side_effects=True, vmem_limit_bytes=LIMIT
        ),
        name=f"backward{layer}",
    )(*inputs)


def swapped(value):
    return lax.ppermute(value, "section", [(0, 1), (1, 0)])


def body(
    tokens,
    cotangent,
    lengths,
    selected,
    input_weight,
    input_bias,
    score_weight,
    output_weight,
    output_bias,
    up_weight,
    up_bias,
    down_weight,
    down_bias,
    norm_gain,
    norm_bias,
):
    core = lax.axis_index("section")
    _, rows, width = tokens.shape
    heads, hidden = score_weight.shape[2], up_weight.shape[2]
    head = input_weight.shape[3] // heads
    inner = heads * head
    z = Sizes(lax.axis_size("tensor"), lax.axis_size("seq"), rows, width, heads, hidden)
    scale = head**-0.5
    grouped = (
        selected[0].reshape(2, heads, z.S, z.tiles).transpose(0, 2, 1, 3).reshape(2, z.S, z.slots)
    )
    kept_choice = lax.dynamic_index_in_dim(grouped, core, 0, keepdims=False)
    got_choice = swapped(lax.dynamic_index_in_dim(grouped, 1 - core, 0, keepdims=False))
    choice = jnp.where(
        core == 0, jnp.stack([kept_choice, got_choice]), jnp.stack([got_choice, kept_choice])
    )
    length = lax.dynamic_index_in_dim(lengths, core, 0, keepdims=False)
    ends = jnp.stack([length[0], length[0] + length[1]])
    own, routes = prepare(
        z,
        ends,
        choice,
        input_weight[0].transpose(1, 0, 2),
        input_bias[0],
        score_weight[0],
        output_weight[0],
        output_bias,
        up_bias,
        down_bias,
        norm_gain[0],
        norm_bias[0],
    )
    own |= dict(wup=up_weight[0], wdn=down_weight[0])
    first = lax.dynamic_index_in_dim(tokens, core, 0, keepdims=False)
    cotan = lax.dynamic_index_in_dim(cotangent, core, 0, keepdims=False)
    zero, theirs = forward(z, 0, routes[0], first, own, None)
    one, _ = forward(z, 1, routes[1], zero["res"], own, theirs)
    grad1, layer_out, g1 = backward(
        z, 1, routes[1], cotan, zero["res"], zero["res"], one["res"], own, theirs, one
    )
    grad0, input_grad, g0 = backward(
        z, 0, routes[0], grad1, first, grad1, grad1, own, theirs, zero
    )
    total = jnp.where(core == 0, g0, g1)
    share = z.share
    c_o, c_i = hidden, hidden + LANES
    pairs = total[0, :, c_i : c_i + z.pad].reshape(share, heads, LANES)
    input_weight_grad = jnp.stack(
        [
            scale * total[1, :, c_i : c_i + inner],
            pairs[:, :, :head].reshape(share, inner),
            pairs[:, :, head:].reshape(share, inner),
        ],
        axis=1,
    )
    out_grad = jnp.concatenate([total[0, :, c_o:c_i], total[1, :, c_o:c_i]], axis=1)[:, :inner]
    c_s = c_i + z.pad
    kept_stats = jnp.where(core == 0, g0[0, :, c_s : c_s + 16], g1[1, :, c_s : c_s + 16])
    stats = kept_stats.T
    each = inner // z.S
    return (
        layer_out[None],
        input_grad[None],
        input_weight_grad[None],
        jnp.stack([stats[13, :each], stats[13, each : 2 * each]])[None],
        kept_stats[:, 10 : 10 + heads][None],
        out_grad.T[None],
        stats[0][None],
        total[1, :, :hidden][None],
        stats[8][None],
        total[0, :, :hidden].T[None],
        stats[9][None],
        jnp.stack([stats[3], stats[1]])[None],
        jnp.stack([stats[4], stats[2]])[None],
    )


def solution(mesh):
    return jax.shard_map(
        body,
        mesh=mesh,
        in_specs=(
            P(None, "seq", None),
            P(None, "seq", None),
            P(),
            P("section", None, "tensor", None),
            P("section", None, None, "tensor"),
            P("section", None, "tensor"),
            P("section", None, "tensor"),
            P("section", "tensor", None),
            P("section", None),
            P("section", None, "tensor"),
            P("section", "tensor"),
            P("section", "tensor", None),
            P("section", None),
            P("section", None, None),
            P("section", None, None),
        ),
        out_specs=(
            P("section", None, "seq", None),
            P("section", None, "seq", None),
            P("section", "seq", None, "tensor"),
            P("section", None, ("tensor", "seq")),
            P("section", "seq", "tensor"),
            P("section", "tensor", "seq"),
            P("section", "seq"),
            P("section", "seq", "tensor"),
            P("section", ("tensor", "seq")),
            P("section", "tensor", "seq"),
            P("section", "seq"),
            P("section", None, "seq"),
            P("section", None, "seq"),
        ),
        check_vma=False,
    )
```

```python
import functools
import math

import jax
import jax.numpy as jnp
from jax import lax
from jax.experimental import pallas as pl
from jax.experimental.pallas import tpu as pltpu
from jax.sharding import PartitionSpec as P

TILE = 64
LANES = 128
MASKED = -1e30
EPSILON = 1e-05
FAR = -(1 << 20)
MESH = pl.DeviceIdType.MESH
BF = jnp.bfloat16
F32 = jnp.float32
GELU_A = 0.044715
GELU_K = math.sqrt(2.0 / math.pi)
LIMIT = 62 * 1024 * 1024


class Sizes:
    def __init__(self, mesh_tensor, mesh_seq, rows, width, heads, hidden):
        self.T, self.S = mesh_tensor, mesh_seq
        self.rows, self.width, self.heads, self.hidden = rows, width, heads, hidden
        self.tiles = rows // TILE
        self.slots = heads * self.tiles
        self.cap = -(-self.slots // (mesh_seq - 1))
        self.capg = -(-self.cap // 8) * 8
        self.n = mesh_seq * self.cap
        self.block = rows // mesh_tensor
        self.pad = heads * LANES
        self.share = width // mesh_seq
        self.padded = -(-self.share // 16) * 16
        self.pieces = (hidden, LANES, self.pad, LANES)


SEND, INV, ORD, CONT, ARR, POS, LAST, ENDS = range(8)
WEIGHTS = ("vec", "w1", "swt", "wo", "wup", "wdn")
KEPT = ("n1", "q", "kvt", "st", "p", "ckv", "o", "mid", "n2", "u", "act")


def nn(a, b):
    return jnp.dot(a, b, preferred_element_type=F32)


def nt(a, b):
    return lax.dot_general(a, b, (((1,), (1,)), ((), ())), preferred_element_type=F32)


def tn(a, b):
    return lax.dot_general(a, b, (((0,), (0,)), ((), ())), preferred_element_type=F32)


def normed(x):
    centred = x - jnp.mean(x, axis=-1, keepdims=True)
    spread = lax.rsqrt(jnp.mean(centred * centred, axis=-1, keepdims=True) + EPSILON)
    return centred * spread, spread


def norm_back(grad, gain, y, spread):
    scaled = grad * gain
    return spread * (
        scaled
        - jnp.mean(scaled, axis=-1, keepdims=True)
        - y * jnp.mean(scaled * y, axis=-1, keepdims=True)
    )


def partner(me, step):
    return (me // 2 + step // 2) % 2 * 2 + (me % 2 + step % 2) % 2


def column_sum(x):
    return jnp.sum(x, axis=0, keepdims=True)


def smem():
    return pl.BlockSpec(memory_space=pltpu.SMEM)


def vmem():
    return pl.BlockSpec(memory_space=pltpu.VMEM)


def anywhere():
    return pl.BlockSpec(memory_space=pl.ANY)


def grid_of(shape, axis):
    return lax.broadcasted_iota(jnp.int32, shape, axis)


def prepare_kernel(
    z,
    ends_ref,
    sel_ref,
    win_ref,
    bin_ref,
    sw_ref,
    wout_ref,
    bout_ref,
    bup_ref,
    bdn_ref,
    gain_ref,
    shift_ref,
    vec_ref,
    w1_ref,
    swt_ref,
    wo_ref,
    rt0_ref,
    rt1_ref,
):
    inner, head = win_ref.shape[2], win_ref.shape[2] // z.heads
    row, col = grid_of((inner, z.pad), 0), grid_of((inner, z.pad), 1)
    lane_of = row // head * LANES + row % head
    first = (col == lane_of).astype(F32)
    second = (col == lane_of + head).astype(F32)
    low, high = first.astype(BF), second.astype(BF)
    scaled = (first * head**-0.5).astype(BF)
    w1_ref[:, : z.pad] = nn(win_ref[0], scaled).astype(BF)
    w1_ref[:, z.pad :] = (nn(win_ref[1], low) + nn(win_ref[2], high)).astype(BF)
    vec_ref[0:1, :] = gain_ref[...].astype(F32)[0:1]
    vec_ref[1:2, :] = shift_ref[...].astype(F32)[0:1]
    vec_ref[2:3, : z.pad] = nn(bin_ref[...], scaled)[0:1]
    vec_ref[2:3, z.pad :] = nn(bin_ref[...], high)[1:2]
    vec_ref[3:4, :] = bout_ref[...].astype(F32)
    vec_ref[4:5, :] = gain_ref[...].astype(F32)[1:2]
    vec_ref[5:6, :] = shift_ref[...].astype(F32)[1:2]
    vec_ref[6:7, :] = bup_ref[...].astype(F32)
    vec_ref[7:8, :] = bdn_ref[...].astype(F32)
    unit = (grid_of((16, z.heads), 0) == grid_of((16, z.heads), 1)).astype(F32).astype(BF)
    swt_ref[...] = nt(unit, sw_ref[...]).astype(BF)
    wo_ref[0:inner, :] = wout_ref[...]
    wo_ref[inner:, :] = jnp.zeros((2 * LANES - inner, z.width), BF)

    at = lax.axis_index("seq")
    n, slots, cap = z.n, z.slots, z.cap
    shift = z.tiles.bit_length() - 1
    near = 1e-3

    def total(mask, value, axis):
        return jnp.sum(jnp.where(mask, value, 0.0), axis=axis, keepdims=True)

    def whole(x):
        return (x + near).astype(jnp.int32)

    for layer, rt in enumerate((rt0_ref, rt1_ref)):
        rt[...] = jnp.zeros((8, LANES), jnp.int32)
        chosen = sel_ref[layer]
        owner = lax.shift_right_arithmetic(chosen, shift)
        sub, lan = grid_of((slots, n), 0), grid_of((slots, n), 1)
        wide = jnp.zeros((slots, n), jnp.int32)
        for d in range(z.S):
            column = jnp.sum(
                jnp.where(
                    grid_of((slots, slots), 0) == grid_of((slots, slots), 1),
                    chosen[d : d + 1].astype(F32) + 1.0,
                    0.0,
                ),
                axis=1,
                keepdims=True,
            )
            wide = jnp.where(lan // cap == d, whole(column) - 1, wide)
        mine = lax.shift_right_arithmetic(wide, shift) == at
        order = nn(
            (grid_of((slots, slots), 0) > grid_of((slots, slots), 1)).astype(F32), mine.astype(F32)
        )
        taken = mine & (whole(order) == lan % cap)
        head_of = sub // z.tiles
        inner_tile = wide - at * z.tiles
        rt[SEND : SEND + 1, :n] = whole(
            total(taken, (head_of * (z.tiles + 1) + inner_tile).astype(F32), 0)
        ) + 1
        present = jnp.sum(taken.astype(F32), axis=0, keepdims=True)
        key = total(taken, (head_of * z.tiles + inner_tile - slots).astype(F32), 0) + slots
        own = jnp.sum(
            jnp.where(grid_of((z.S, slots), 0) == at, chosen.astype(F32) + 1.0, 0.0), axis=0, keepdims=True
        )
        square_row, square_col = grid_of((slots, slots), 0), grid_of((slots, slots), 1)
        own_column = total(square_row == square_col, own, 1)
        own_row = whole(own) - 1
        own_col = whole(own_column) - 1
        owner_row = lax.shift_right_arithmetic(own_row, shift)
        owner_col = lax.shift_right_arithmetic(own_col, shift)
        same = owner_row == owner_col
        place_row = whole(jnp.sum((same & (square_row < square_col)).astype(F32), axis=0, keepdims=True))
        place_col = whole(jnp.sum((same & (square_col < square_row)).astype(F32), axis=1, keepdims=True))
        live = own_row >= 0
        rt[ARR : ARR + 1, :slots] = jnp.where(live, owner_row * cap + place_row, at * cap)
        rt[POS : POS + 1, :slots] = jnp.where(live, own_row * TILE, FAR)
        matched = (owner_col == lan // cap) & (place_col == lan % cap)
        rt[INV : INV + 1, :n] = whole(total(matched, sub.astype(F32), 0))
        big_row, big_col = grid_of((n, n), 0), grid_of((n, n), 1)
        key_col = total(big_row == big_col, key, 1)
        rank = jnp.sum(
            ((key < key_col) | ((key == key_col) & (big_col < big_row))).astype(F32), axis=1, keepdims=True
        )
        at_rank = whole(rank) == big_col
        rt[ORD : ORD + 1, :n] = whole(total(at_rank, big_row.astype(F32), 0))
        sorted_key = total(at_rank, key_col, 0)
        before = total(whole(rank) + 1 == big_col, key_col + 1.0, 0) - 1.0
        rt[CONT : CONT + 1, :n] = (sorted_key == before).astype(jnp.int32)
        tile = grid_of((n, slots), 1).astype(F32)
        upto = jnp.sum((key_col <= tile).astype(F32), axis=0, keepdims=True)
        has = jnp.sum((key_col == tile).astype(F32), axis=0, keepdims=True)
        rt[LAST : LAST + 1, :slots] = whole(jnp.where(has > 0.5, upto - 1.0, n * 1.0))
        rt[ENDS : ENDS + 1, :] = jnp.where(grid_of((1, LANES), 1) == 0, ends_ref[0], ends_ref[1])


def prepare(z, ends, sel, win, bin_, sw, wout, bout, bup, bdn, gain, shift):
    table = jax.ShapeDtypeStruct((8, LANES), jnp.int32)
    outs = pl.pallas_call(
        functools.partial(prepare_kernel, z),
        out_shape=(
            jax.ShapeDtypeStruct((8, z.width), F32),
            jax.ShapeDtypeStruct((z.width, 2 * z.pad), BF),
            jax.ShapeDtypeStruct((16, z.width), BF),
            jax.ShapeDtypeStruct((2 * LANES, z.width), BF),
            table,
            table,
        ),
        in_specs=[smem()] + [vmem()] * 10,
        out_specs=tuple(vmem() for _ in range(6)),
        name="prepare",
    )(ends, sel, win, bin_, sw, wout, bout, bup, bdn, gain, shift)
    return dict(zip(WEIGHTS[:4], outs)), outs[4:]


def to_tensor(step, me):
    return {"tensor": partner(me, step)}


def remote(src, dst, send, recv, target):
    return pltpu.make_async_remote_copy(
        src_ref=src, dst_ref=dst, send_sem=send, recv_sem=recv, device_id=target, device_id_type=MESH
    )


def signal(target, barrier):
    pl.semaphore_signal(barrier, inc=1, device_id=target, device_id_type=MESH)


class Spread:
    def __init__(self, me, view, sends, recvs):
        self.me, self.view, self.sends, self.recvs = me, view, sends, recvs

    def copy(self, i):
        me, x, y = self.me, partner(self.me, 1), partner(self.me, 2)
        owner, half, step = ((me, 0, 1), (me, 1, 2), (me, 1, 1), (me, 0, 2), (x, 0, 2), (y, 1, 1))[i]
        ref = self.view(owner, half)
        return remote(ref, ref, self.sends(i), self.recvs(i), to_tensor(step, me))

    def start(self):
        for i in range(4):
            self.copy(i).start()

    def forward(self):
        for i in range(2):
            self.copy(i).wait_recv()
            self.copy(4 + i).start()

    def wait(self, step):
        for i in ((), (2,), (3,), (4, 5))[step]:
            self.copy(i).wait_recv()

    def finish(self):
        for i in range(6):
            self.copy(i).wait_send()


class Collect:
    def __init__(self, z, me, send, got, via, sends, recvs):
        self.me, self.send, self.got, self.via, self.sends, self.recvs = me, send, got, via, sends, recvs
        half = z.block // 2
        self.halves = (pl.ds(0, half), pl.ds(half, half))

    def copy(self, i):
        top, bottom = self.halves
        block, rows, target, step = (
            (2, top, self.via.at[0], 1),
            (2, bottom, self.via.at[1], 2),
            (0, top, self.got.at[0, top, :], 1),
            (1, bottom, self.got.at[1, bottom, :], 2),
            (0, bottom, self.got.at[0, bottom, :], 1),
            (1, top, self.got.at[1, top, :], 2),
        )[i]
        return remote(
            self.send.at[block, rows, :], target, self.sends(i), self.recvs(i), to_tensor(step, self.me)
        )

    def put(self, step, value):
        for wanted, copies in ((3, (0, 1)), (1, (2,)), (2, (3,))):

            @pl.when(step == wanted)
            def _(wanted=wanted, copies=copies):
                self.send[wanted - 1] = value().astype(BF)
                for i in copies:
                    self.copy(i).start()

    def join(self):
        top, bottom = self.halves
        for i, block, rows in ((1, 0, bottom), (0, 1, top)):
            self.copy(i).wait_recv()
            joined = self.send[block, rows, :].astype(F32) + self.via[i].astype(F32)
            self.send[block, rows, :] = joined.astype(BF)
            self.copy(5 - i).start()

    def total(self, own):
        for i in range(2, 6):
            self.copy(i).wait_recv()
        return own + self.got[0].astype(F32) + self.got[1].astype(F32)

    def finish(self):
        for i in range(6):
            self.copy(i).wait_send()


def visiting(k):
    return jnp.where(k == 0, 3, jnp.where(k == 3, 0, k))


class Saver:
    def __init__(self, sems):
        self.sems, self.copies = sems, []

    def save(self, src, dst):
        copy = pltpu.make_async_copy(src, dst, self.sems.at[len(self.copies)])
        copy.start()
        self.copies.append(copy)

    def finish(self):
        for copy in self.copies:
            copy.wait()


class Refs:
    def __init__(self, names, refs):
        assert len(names) == len(refs), (len(names), len(refs))
        for name, ref in zip(names, refs):
            setattr(self, name, ref)


def forward_part(z, layer, e):
    rt, r_ref, res_ref = e.routes[layer], (e.rows, e.middle)[layer], (e.middle, e.rows)[layer]
    used, s, me, at, core, load = e.used, e.s, e.me, e.at, e.core, e.load
    held = e.held(layer)
    last = z.S - 1
    first_row = at * z.rows
    vec = e.vec(layer)
    edge_ss, edge_rs = s.edge_ss.at[layer], s.edge_rs.at[layer]
    kv_ss, kv_rs, gate_ss, gate_rs = (
        sems.at[layer] for sems in (s.kv_ss, s.kv_rs, s.gate_ss, s.gate_rs)
    )
    edge, edge_gate, got_gate = s.edge.at[layer], s.edge_gate.at[layer], s.got_gate.at[layer]
    held.ckv[at * z.cap] = jnp.zeros((TILE, LANES), BF)
    outs = e.store

    def ready(*wanted):
        for i in wanted:
            e.weight_ready(layer, i)

    if layer == 0:
        e.input_load.wait()
    saver = Saver(s.saved) if layer == 0 else Unsaved()
    per_block = z.block // TILE
    ready(0)

    def norm_in(b, _):
        rows = pl.ds(b * z.block, z.block)
        y, _ = normed(r_ref[rows, :].astype(F32))
        held.n1[rows, :] = (y * vec[0:1, :] + vec[1:2, :]).astype(BF)
        return 0

    lax.fori_loop(0, z.T, norm_in, 0)
    saver.save(held.n1, outs["n1"])
    ready(1, 2)

    def project(b, _):
        rows = pl.ds(b * z.block, z.block)
        qkv = (nn(held.n1[rows, :], used["w1"][...]) + vec[2:3, :]).astype(BF)
        held.q[rows, :] = qkv[:, : z.pad]
        for h in range(z.heads):
            pairs = qkv[:, z.pad + h * LANES : z.pad + (h + 1) * LANES]
            held.kvt[pl.ds(h * (z.tiles + 1) + 1 + b * per_block, per_block)] = pairs.reshape(
                per_block, TILE, LANES
            )
        return 0

    lax.fori_loop(0, z.T, project, 0)
    score = nt(used["swt"][...], held.n1[...])[0:8]
    held.st[...] = score
    gate = jnp.minimum(score, 0.0) - jnp.log1p(jnp.exp(-jnp.abs(score)))
    s.gt[:, 0:LANES] = jnp.zeros((8, LANES), F32)
    s.gt[:, LANES : LANES + z.rows] = gate.astype(BF).astype(F32)
    s.gt[:, LANES + z.rows :] = jnp.zeros((8, LANES), F32)
    for t in range(z.tiles + 1):
        for h in range(z.heads):
            s.gate[h * (z.tiles + 1) + t, 0:1, :] = s.gt[
                h : h + 1, TILE + t * TILE : TILE + t * TILE + LANES
            ]

    def edge_copies():
        after = {"seq": jnp.minimum(at + 1, last)}
        return [
            remote(
                held.kvt.at[h * (z.tiles + 1) + z.tiles],
                edge.at[h],
                edge_ss.at[h],
                edge_rs.at[h],
                after,
            )
            for h in range(z.heads)
        ] + [
            remote(
                s.gt.at[:, pl.ds(z.rows, LANES)],
                edge_gate,
                edge_ss.at[z.heads],
                edge_rs.at[z.heads],
                after,
            )
        ]

    @pl.when(at < last)
    def _():
        for copy in edge_copies():
            copy.start()

    def tile_copies(d, source):
        return (
            remote(
                s.send_kv.at[d],
                held.ckv.at[pl.ds(source * z.cap, z.cap)],
                kv_ss.at[d],
                kv_rs.at[source],
                {"seq": d},
            ),
            remote(
                s.send_gate.at[d], got_gate.at[source], gate_ss.at[d], gate_rs.at[source], {"seq": d}
            ),
        )

    def pack(k, _):
        d = z.S - 1 - k

        def slot(i, _):
            u = rt[SEND, d * z.cap + i]
            s.send_kv[d, i] = held.kvt[u]
            s.send_gate[d, pl.ds(i, 1), :] = s.gate[u][0:1]
            return 0

        lax.fori_loop(0, z.cap, slot, 0)
        for copy in tile_copies(d, at):
            copy.start()
        return 0

    e.turn(layer, "pack")
    lax.fori_loop(0, last - at, pack, 0)
    ready(3)

    def wo_copy(step):
        return remote(
            used["wo"], s.wo_all.at[me], s.wo_ss.at[step], s.wo_rs.at[step], to_tensor(step, me)
        )

    for step in range(1, z.T):
        wo_copy(step).start()
    s.wo_all[me] = used["wo"][...]
    saver.save(held.q, outs["q"])
    saver.save(held.st, outs["st"])

    def landed(source, _):
        for copy in tile_copies(last, source):
            copy.wait_recv()
        for i in range(z.cap):
            s.far_gate[source * z.cap + i, 0:1, :] = got_gate[source, i : i + 1, :]
        return 0

    lax.fori_loop(0, at, landed, 0)
    lane = grid_of((TILE, LANES), 1)
    row = grid_of((TILE, LANES), 0)
    for h in range(z.heads):
        held.kvt[h * (z.tiles + 1)] = jnp.zeros((TILE, LANES), BF)

    @pl.when(at > 0)
    def _():
        for copy in edge_copies():
            copy.wait_recv()
        for h in range(z.heads):
            held.kvt[h * (z.tiles + 1)] = edge[h]
            s.gate[h * (z.tiles + 1), 0:1, :] = jnp.where(
                lane[0:1] < TILE,
                pltpu.roll(edge_gate[...], TILE, 1)[h : h + 1],
                s.gate[h * (z.tiles + 1), 0:1, :],
            )

    saver.save(held.kvt, outs["kvt"])
    saver.save(held.ckv, outs["ckv"])

    def attend(tiles):
        units = [(g, h) for g in range(len(tiles)) for h in range(z.heads)]
        keys, scores = {}, {}
        for g, t in enumerate(tiles):
            base = pl.multiple_of(t * TILE, TILE)
            query = first_row + base + row
            begin = jnp.where(
                query >= rt[ENDS, 1],
                rt[ENDS, 1],
                jnp.where(query >= rt[ENDS, 0], rt[ENDS, 0], 0),
            )
            key = first_row + base - TILE + lane
            near_ok = (key <= query) & (key > query - TILE) & (key >= begin)
            for h in range(z.heads):
                u = h * z.tiles + t
                arrived = rt[ARR, u]
                far = held.ckv[arrived]
                near = held.kvt[pl.ds(h * (z.tiles + 1) + t, 2)].reshape(2 * TILE, LANES)
                keys[g, h] = jnp.concatenate([near, far, far], axis=0)
                gates = jnp.concatenate(
                    [s.gate[h * (z.tiles + 1) + t, 0:1, :], s.far_gate[arrived][0:1]], axis=1
                )
                far_ok = (rt[POS, u] + lane >= begin) & (lane < TILE)
                query_tile = held.q[pl.ds(base, TILE), h * LANES : (h + 1) * LANES]
                scores[g, h] = jnp.where(
                    jnp.concatenate([near_ok, far_ok], axis=1), nt(query_tile, keys[g, h]) + gates, MASKED
                )
        tops = {u: jnp.max(scores[u], axis=-1, keepdims=True) for u in units}
        raised = {u: jnp.exp(scores[u] - tops[u]) for u in units}
        sums = {u: jnp.sum(raised[u], axis=-1, keepdims=True) for u in units}
        probs = {u: (raised[u] * (1.0 / sums[u])).astype(BF) for u in units}
        mixed = {u: nn(probs[u], keys[u]) for u in units}
        for g, t in enumerate(tiles):
            base = pl.multiple_of(t * TILE, TILE)
            for h in range(z.heads):
                held.p[t * z.heads + h] = probs[g, h]
            pair = jnp.where(lane < TILE, pltpu.roll(mixed[g, 0], TILE, 1), mixed[g, 1]).astype(BF)
            single = pltpu.roll(mixed[g, 2], TILE, 1)
            held.o[pl.ds(base, TILE), 0:LANES] = pair
            held.o[pl.ds(base, TILE), LANES:] = single.astype(BF)
            s.pair_all[me, pl.ds(base, TILE), :] = pair
            if g % 2 == 0:
                even = single
            else:
                couple = pl.ds(pl.multiple_of((t - 1) * (TILE // 2), TILE), TILE)
                s.single_all[me, couple, :] = jnp.where(lane < TILE, even, mixed[g, 2]).astype(BF)

    e.turn(layer, "attend")
    half_rows = z.block // 2

    def pair_spread(b):
        return Spread(
            me,
            lambda owner, half: s.pair_all.at[owner, pl.ds(b * z.block + half * half_rows, half_rows), :],
            lambda i: s.o_ss.at[b * 12 + i],
            lambda i: s.o_rs.at[b * 12 + i],
        )

    def single_spread(b):
        return Spread(
            me,
            lambda owner, half: s.single_all.at[
                owner, pl.ds(b * half_rows + half * (half_rows // 2), half_rows // 2), :
            ],
            lambda i: s.o_ss.at[b * 12 + 6 + i],
            lambda i: s.o_rs.at[b * 12 + 6 + i],
        )

    def attend_block(b, _):
        attend([b * per_block + g for g in range(per_block)])
        pair_spread(b).start()
        single_spread(b).start()

        @pl.when(b > 0)
        def _():
            pair_spread(b - 1).forward()
            single_spread(b - 1).forward()

        return 0

    lax.fori_loop(0, z.T, attend_block, 0)
    pair_spread(z.T - 1).forward()
    single_spread(z.T - 1).forward()
    saver.save(held.p, outs["p"])
    saver.save(held.o, outs["o"])
    ready(4, 5)
    for step in range(1, z.T):
        wo_copy(step).wait()
    for t in range(z.T):
        s.wo_high[t, 0:TILE, :] = jnp.zeros((TILE, z.width), BF)
        s.wo_high[t, TILE:, :] = s.wo_all[t, LANES : LANES + TILE, :]
    collect = e.collect(0)

    def feed(k, _):
        step = visiting(k)
        block = partner(me, step)
        rows = pl.ds(pl.multiple_of(block * z.block, z.block), z.block)
        few = pl.ds(pl.multiple_of(block * half_rows, half_rows), half_rows)
        for other in range(1, z.T):
            pair_spread(block).wait(other)
            single_spread(block).wait(other)
        mixed = nn(s.pair_all[0, rows, :], s.wo_all[0, 0:LANES, :])
        even = nn(s.single_all[0, few, :], s.wo_all[0, LANES:, :])
        odd = nn(s.single_all[0, few, :], s.wo_high[0])
        for other in range(1, z.T):
            mixed += nn(s.pair_all[other, rows, :], s.wo_all[other, 0:LANES, :])
            even += nn(s.single_all[other, few, :], s.wo_all[other, LANES:, :])
            odd += nn(s.single_all[other, few, :], s.wo_high[other])
        turns = []
        for i in range(per_block // 2):
            turns += [even[i * TILE : (i + 1) * TILE], odd[i * TILE : (i + 1) * TILE]]
        mixed += jnp.concatenate(turns, axis=0)
        middle = r_ref[rows, :].astype(F32) + mixed + vec[3:4, :]
        held.mid[...] = middle
        y, _ = normed(middle)
        n2 = (y * vec[4:5, :] + vec[5:6, :]).astype(BF)
        held.n2[rows, :] = n2
        u = nn(n2, used["wup"][...]) + vec[6:7, :]
        held.u[rows, :] = u.astype(BF)
        act = (0.5 * u * (1.0 + jnp.tanh(GELU_K * (u + GELU_A * u * u * u)))).astype(BF)
        held.act[rows, :] = act
        s.own_part[...] = nn(act, used["wdn"][...])

        collect.put(step, lambda: s.own_part[...])
        return 0

    lax.fori_loop(0, z.T, feed, 0)
    collect.join()
    if layer == 0:
        e.next_weights()
    e.turn(layer, "feed")
    for name in ("mid", "n2", "u", "act"):
        saver.save(getattr(held, name), outs[name])
    total = collect.total(held.mid[...] + s.own_part[...] + vec[7:8, :])
    own_rows = pl.ds(pl.multiple_of(me * z.block, z.block), z.block)
    res_ref[own_rows, :] = total.astype(BF)
    spread = Spread(
        me,
        lambda owner, half: res_ref.at[
            pl.ds(pl.multiple_of(owner * z.block + half * half_rows, half_rows), half_rows), :
        ],
        lambda i: s.res_ss.at[i],
        lambda i: s.res_rs.at[i],
    )
    spread.start()
    collect.finish()

    def finish_block(b, _):
        pair_spread(b).finish()
        single_spread(b).finish()
        return 0

    lax.fori_loop(0, z.T, finish_block, 0)

    def sent(d, _):
        for copy in tile_copies(d, at):
            copy.wait_send()
        return 0

    lax.fori_loop(at + 1, z.S, sent, 0)

    @pl.when(at < last)
    def _():
        for copy in edge_copies():
            copy.wait_send()

    spread.forward()
    for step in range(1, z.T):
        spread.wait(step)
    spread.finish()
    e.deliver(layer, res_ref, e.layer_out)
    saver.finish()


def backward_part(z, layer, e):
    rt, used, s, me, at, core = e.routes[layer], e.used, e.s, e.me, e.at, e.core
    c_ref, grad_ref = (e.grad, e.cotan) if layer == 0 else (e.cotan, e.grad)
    k = e.held(layer)
    last = z.S - 1
    vec = e.vec(layer)
    own_rows = pl.ds(pl.multiple_of(me * z.block, z.block), z.block)
    W = z.width
    g_out = e.g_out
    across = {"section": 1 - core}

    def ready(*names):
        for name in names:
            if name in WEIGHTS:
                e.weight_ready(layer, WEIGHTS.index(name))
            else:
                e.kept_ready(layer, name)

    def done(*names):
        if layer == 1:
            for name in names:
                if name in WEIGHTS:
                    e.weight_again(WEIGHTS.index(name))
                else:
                    e.kept_again(name)

    collects = (e.collect(0), e.collect(1))
    half_rows = z.block // 2

    def rows_spread(ref, sends, recvs):
        return Spread(
            me,
            lambda owner, half: ref.at[
                pl.ds(pl.multiple_of(owner * z.block + half * half_rows, half_rows), half_rows), :
            ],
            lambda i: sends.at[i],
            lambda i: recvs.at[i],
        )

    if layer == 1:
        e.cotan_load.wait()
    ready("wdn", "u", "wup")

    def ff_back(i, _):
        step = visiting(i)
        rows = pl.ds(pl.multiple_of(partner(me, step) * z.block, z.block), z.block)
        u = k.u[rows, :].astype(F32)
        squared = u * u
        bent = jnp.tanh(GELU_K * (u + GELU_A * squared * u))
        slope = 0.5 * (1.0 + bent) + 0.5 * u * (1.0 - bent * bent) * (
            GELU_K * (1.0 + 3.0 * GELU_A * squared)
        )
        du = (nt(c_ref[rows, :], used["wdn"][...]) * slope).astype(BF)
        s.du[rows, :] = du
        s.own_part[...] = nt(du, used["wup"][...])

        collects[0].put(step, lambda: s.own_part[...])
        return 0

    lax.fori_loop(0, z.T, ff_back, 0)
    ones = jnp.ones((16, z.rows), BF)
    s.stat[...] = jnp.zeros((24, W), F32)

    mine = (s.pa, s.pb, s.pc, s.pd)
    theirs_part = (s.xa, s.xb, s.xc, s.xd)
    summed = (s.sa, s.sb, s.sc, s.sd)
    crossed = (s.ta, s.tb, s.tc, s.td)
    handed = (s.ha, s.hb, s.hc)

    def give(piece):
        return remote(
            mine[piece].at[1 - core if piece < 3 else 0], theirs_part[piece], s.give_ss.at[piece], s.give_rs.at[piece], across
        )

    def cross(piece, d, source):
        return remote(
            summed[piece].at[d],
            crossed[piece].at[source],
            s.cross_ss.at[piece, d],
            s.cross_rs.at[piece, source],
            {"seq": d},
        )

    def hand(piece):
        return remote(
            summed[piece].at[at], handed[piece], s.hand_ss.at[piece], s.hand_rs.at[piece], across
        )

    span = math.lcm(z.share, 16)

    def add_up(piece):
        give(piece).wait_recv()

        def chunk(i, _):
            rows = pl.ds(pl.multiple_of(i * span, span), span)
            value = mine[piece][core if piece < 3 else 0, rows, :].astype(F32) + theirs_part[piece][rows, :].astype(F32)
            for j in range(span // z.share):
                d = i * (span // z.share) + j
                rows_of = value[j * z.share : (j + 1) * z.share]
                if z.padded > z.share:
                    rows_of = jnp.concatenate(
                        [rows_of, jnp.zeros((z.padded - z.share, value.shape[1]), F32)], axis=0
                    )
                summed[piece][d] = rows_of.astype(BF)

                @pl.when(d != at)
                def _():
                    cross(piece, d, at).start()

            return 0

        lax.fori_loop(0, W // span, chunk, 0)

    offsets = [sum(z.pieces[:piece]) for piece in range(len(z.pieces))]

    def reduce(piece):
        def wait(i, _):
            d = (at + i) % z.S
            cross(piece, d, d).wait_recv()
            return 0

        lax.fori_loop(1, z.S, wait, 0)

        def add(i, running):
            return running + crossed[piece][(at + i) % z.S].astype(F32)

        total = lax.fori_loop(1, z.S, add, summed[piece][at].astype(F32))
        cols = slice(offsets[piece], offsets[piece] + z.pieces[piece])

        @pl.when(core == layer)
        def _():
            g_out[core, :, cols] = total[: z.share]

        @pl.when(core != layer)
        def _():
            if piece < len(handed):
                summed[piece][at] = total.astype(BF)
                hand(piece).start()

    def take(piece):
        cols = slice(offsets[piece], offsets[piece] + z.pieces[piece])

        @pl.when(core == layer)
        def _():
            hand(piece).wait_recv()
            g_out[1 - core, :, cols] = handed[piece][...].astype(F32)[: z.share]

    ready("act", "n2")
    wide = z.hidden // 2
    for cols in (slice(0, wide), slice(wide, z.hidden)):
        s.pa[0, :, cols] = tn(c_ref[...], k.act[:, cols]).astype(BF)
    collects[0].join()
    for cols in (slice(0, wide), slice(wide, z.hidden)):
        s.pa[1, :, cols] = tn(k.n2[...], s.du[:, cols]).astype(BF)
    give(0).start()
    done("wdn", "wup", "u", "act", "n2")
    s.stat[8:9, :] = nn(ones, s.du[...])[0:1]
    s.stat[9:10, :] = nn(ones, c_ref[...])[0:1]
    ready("mid", "wo")
    add_up(0)
    grad = collects[0].total(s.own_part[...])
    y, spread = normed(k.mid[...])
    dr2 = c_ref[own_rows, :].astype(F32) + norm_back(grad, vec[4:5, :], y, spread)
    s.dr2[...] = dr2
    s.wo_all[me] = dr2.astype(BF)

    ob_spread = Spread(
        me,
        lambda owner, half: s.wo_all.at[owner, pl.ds(half * half_rows, half_rows), :],
        lambda i: s.ob_ss.at[i],
        lambda i: s.ob_rs.at[i],
    )
    ob_spread.start()
    done("mid")
    s.stat[0:1, :] = column_sum(dr2)
    s.stat[1:2, :] = column_sum(grad * y)
    s.stat[2:3, :] = column_sum(grad)
    s.dkv[...] = jnp.zeros((z.rows + TILE, z.pad), F32)
    ob_spread.forward()
    lane_wide = grid_of((z.block, LANES), 1)

    def out_back(step, _):
        for wanted in range(1, z.T):

            @pl.when(step == wanted)
            def _(wanted=wanted):
                ob_spread.wait(wanted)

        rows = pl.ds(pl.multiple_of(partner(me, step) * z.block, z.block), z.block)
        dout = nt(s.wo_all[partner(me, step)], used["wo"][...])
        pair, single = dout[:, :LANES], dout[:, LANES:]
        for h, value in enumerate((pltpu.roll(pair, TILE, 1), pair, pltpu.roll(single, TILE, 1))):
            s.pair_all[h, rows, :] = jnp.where(lane_wide < TILE, 0.0, value).astype(BF)
        return 0

    lax.fori_loop(0, z.T, out_back, 0)
    done("wo")
    collects[0].finish()
    ready("p", "q", "kvt", "ckv")

    ones_row = jnp.ones((16, TILE), BF)

    def attend_back(i, _):
        tiles = [i * group + g for g in range(group)]
        units = [(g, h) for g in range(group) for h in range(z.heads)]
        keys, query, dout, prob, dprob = {}, {}, {}, {}, {}
        for g, t in enumerate(tiles):
            base = pl.multiple_of(t * TILE, TILE)
            for h in range(z.heads):
                cols = slice(h * LANES, (h + 1) * LANES)
                far = k.ckv[rt[ARR, h * z.tiles + t]]
                near = k.kvt[pl.ds(h * (z.tiles + 1) + t, 2)].reshape(2 * TILE, LANES)
                keys[g, h] = jnp.concatenate([near, far, far], axis=0)
                query[g, h] = k.q[pl.ds(base, TILE), cols]
                dout[g, h] = s.pair_all[h, pl.ds(base, TILE), :]
                prob[g, h] = k.p[t * z.heads + h]
                dprob[g, h] = nt(dout[g, h], keys[g, h])
        totals = {u: jnp.sum(prob[u].astype(F32) * dprob[u], axis=-1, keepdims=True) for u in units}
        dz = {u: (prob[u].astype(F32) * (dprob[u] - totals[u])).astype(BF) for u in units}
        for g, t in enumerate(tiles):
            base = pl.multiple_of(t * TILE, TILE)
            for h in range(z.heads):
                cols = slice(h * LANES, (h + 1) * LANES)
                u = h * z.tiles + t
                s.dqkv[pl.ds(base, TILE), cols] = nn(dz[g, h], keys[g, h]).astype(BF)
                dkeys = tn(
                    jnp.concatenate([dz[g, h], prob[g, h]], axis=0),
                    jnp.concatenate([query[g, h], dout[g, h]], axis=0),
                )
                s.dkv[pl.ds(base, 2 * TILE), cols] += dkeys[: 2 * TILE]
                s.far[u] = dkeys[2 * TILE : 3 * TILE].astype(BF)
                gates = nn(ones_row, dz[g, h])[0:1]
                s.dgate[t, h : h + 1, :] = gates[:, :LANES]
                s.far_gate[u, 0:1, :] = gates[:, LANES:]
        return 0

    group = 4
    lax.fori_loop(0, z.tiles // group, attend_back, 0)
    done("p", "q", "kvt", "ckv")
    s.dgate[z.tiles] = jnp.zeros((8, LANES), F32)

    def edge_copies():
        behind = {"seq": jnp.maximum(at - 1, 0)}
        return (
            remote(s.edge_send, s.edge_got, s.back_edge_ss.at[0], s.back_edge_rs.at[0], behind),
            remote(s.dgate.at[0], s.edge_gate_got, s.back_edge_ss.at[1], s.back_edge_rs.at[1], behind),
        )

    @pl.when(at > 0)
    def _():
        s.edge_send[...] = s.dkv[0:TILE, :].astype(BF)
        for copy in edge_copies():
            copy.start()

    def tile_copies(d, source):
        return (
            remote(
                s.send_kv.at[d],
                s.got_kv.at[pl.ds(source * z.cap, z.cap)],
                s.back_kv_ss.at[d],
                s.back_kv_rs.at[source],
                {"seq": d},
            ),
            remote(
                s.back_send_gate.at[d], s.back_got_gate.at[source], s.back_gate_ss.at[d], s.back_gate_rs.at[source], {"seq": d}
            ),
        )

    def pack(d, _):
        def slot(i, _):
            u = rt[INV, d * z.cap + i]
            s.send_kv[d, i] = s.far[u]
            s.back_send_gate[d, pl.ds(i, 1), :] = s.far_gate[u][0:1]
            return 0

        lax.fori_loop(0, z.cap, slot, 0)
        for copy in tile_copies(d, at):
            copy.start()
        return 0

    lax.fori_loop(0, at, pack, 0)
    ready("o")
    out_grad = tn(s.wo_all[...].reshape(z.rows, W), k.o[...]).astype(BF)
    done("o")
    s.pb[0] = out_grad[:, :LANES]
    s.pb[1] = out_grad[:, LANES:]
    give(1).start()
    s.sum[z.n] = jnp.zeros((TILE, LANES), F32)
    s.gate_sum[z.n] = jnp.zeros((8, LANES), F32)
    ready("st", "w1", "swt", "n1")

    @pl.when(at < last)
    def _():
        for copy in edge_copies():
            copy.wait_recv()
        s.dkv[pl.ds(z.rows, TILE), :] += s.edge_got[...].astype(F32)
        s.dgate[z.tiles] = s.edge_gate_got[...]

    def landed(source, _):
        for copy in tile_copies(0, source):
            copy.wait_recv()
        for i in range(z.cap):
            s.got_gate_row[source * z.cap + i, 0:1, :] = s.back_got_gate[source, i : i + 1, :]
        return 0

    lax.fori_loop(at + 1, z.S, landed, 0)

    def gather(i, carry):
        running, gates = carry
        index = rt[ORD, i]
        joined = rt[CONT, i].astype(F32)
        running = running * joined + s.got_kv[index].astype(F32)
        gates = gates * joined + s.got_gate_row[index]
        s.sum[i] = running
        s.gate_sum[i] = gates
        return running, gates

    lax.fori_loop(0, z.n, gather, (jnp.zeros((TILE, LANES), F32), jnp.zeros((8, LANES), F32)))

    def settle(t, _):
        base = pl.multiple_of((t + 1) * TILE, TILE)
        rows = pl.ds(pl.multiple_of(t * TILE, TILE), TILE)
        for h in range(z.heads):
            cols = slice(h * LANES, (h + 1) * LANES)
            index = rt[LAST, h * z.tiles + t]
            s.dqkv[rows, z.pad + h * LANES : z.pad + (h + 1) * LANES] = (
                s.dkv[pl.ds(base, TILE), cols] + s.sum[index]
            ).astype(BF)
            s.tile_gate[t, h : h + 1, :] = s.gate_sum[index][0:1]
        return 0

    lax.fori_loop(0, z.tiles, settle, 0)
    lane = grid_of((8, LANES), 1)
    head_row = grid_of((8, LANES), 0)
    for i in range(z.tiles // 2):
        halves = []
        for t in (2 * i, 2 * i + 1):
            halves.append(pltpu.roll(s.dgate[t], TILE, 1) + s.dgate[t + 1] + s.tile_gate[t])
        joint = jnp.where(lane < TILE, halves[0], pltpu.roll(halves[1], TILE, 1))
        score = k.st[:, i * LANES : (i + 1) * LANES]
        grads = jnp.where(head_row < z.heads, joint / (1.0 + jnp.exp(score)), 0.0)
        s.ds[0:8, i * LANES : (i + 1) * LANES] = grads
        s.ds[8:16, i * LANES : (i + 1) * LANES] = jnp.zeros((8, LANES), F32)

    def in_back(i, _):
        step = visiting(i)
        rows = pl.ds(pl.multiple_of(partner(me, step) * z.block, z.block), z.block)
        s.own_part[...] = nt(s.dqkv[rows, :], used["w1"][...]) + tn(
            s.ds[:, rows].astype(BF), used["swt"][...]
        )

        collects[1].put(step, lambda: s.own_part[...])
        return 0

    lax.fori_loop(0, z.T, in_back, 0)
    done("st", "w1", "swt")
    collects[1].join()
    s.pc[0] = tn(k.n1[...], s.dqkv[:, z.pad :]).astype(BF)
    queries = tn(k.n1[...], s.dqkv[:, : z.pad])
    lane_full = grid_of((W, LANES), 1)
    s.pc[1, :, :LANES] = jnp.where(
        lane_full < TILE, queries[:, :LANES], pltpu.roll(queries[:, LANES : 2 * LANES], TILE, 1)
    ).astype(BF)
    s.pc[1, :, LANES : 2 * LANES] = queries[:, 2 * LANES :].astype(BF)
    s.pc[1, :, 2 * LANES :] = jnp.zeros((W, z.pad - 2 * LANES), BF)
    give(2).start()
    s.stat[10:13, :] = nn(s.ds[...].astype(BF), k.n1[...])[0:3]
    done("n1")
    source, target = grid_of((W, 1), 0), grid_of((1, W), 1)
    is_value = source >= z.pad
    index = jnp.where(is_value, source - z.pad, source)
    index = index // LANES * TILE + index % TILE
    each = z.heads * TILE // z.S
    wanted = index // each * z.share + index % each + jnp.where(is_value, each, 0)
    filled = (source % LANES >= TILE) == is_value
    wanted = jnp.where(filled, wanted, -1)
    spread_out = jnp.where(wanted == target, jnp.where(is_value, 1.0, TILE**-0.5), 0.0).astype(BF)
    s.stat[13:14, :] = nn(nn(ones, s.dqkv[...]).astype(BF), spread_out)[0:1]
    reduce(0)
    add_up(1)
    add_up(2)
    grad = collects[1].total(s.own_part[...])
    if layer == 1:
        entry = e.middle[own_rows, :]
    else:
        e.entry_load.wait()
        entry = s.entry[...]
    y, spread = normed(entry.astype(F32))
    dr = s.dr2[...] + norm_back(grad, vec[0:1, :], y, spread)
    grad_ref[own_rows, :] = dr.astype(BF)
    grad_spread = rows_spread(grad_ref, s.grad_ss, s.grad_rs)
    s.stat[3:4, :] = column_sum(grad * y)
    s.stat[4:5, :] = column_sum(grad)

    def stat_copy(step):
        return remote(
            s.stat.at[pl.ds(0, 8), :],
            s.stat_got.at[step - 1],
            s.stat_ss.at[step],
            s.stat_rs.at[step],
            to_tensor(step, me),
        )

    for step in range(1, z.T):
        stat_copy(step).start()
    grad_spread.start()
    shared = s.stat[0:8, :]
    for step in range(1, z.T):
        stat_copy(step).wait()
        shared += s.stat_got[step - 1]
    stats = jnp.concatenate([shared, s.stat[8:16, :]], axis=0).astype(BF)
    unit = (grid_of((16, LANES), 0) == grid_of((16, LANES), 1)).astype(F32).astype(BF)
    s.pd[0] = tn(stats, unit).astype(BF)

    @pl.when(core != layer)
    def _():
        give(3).start()

    grad_spread.forward()

    @pl.when(core == layer)
    def _():
        add_up(3)

    reduce(1)
    take(0)
    take(1)

    for step in range(z.T):
        grad_spread.wait(step)
        if layer == 0:
            e.deliver_block(grad_ref, step)

    if layer == 1:
        e.deliver(1, grad_ref, e.input_grad)
    reduce(2)
    take(2)

    @pl.when(core == layer)
    def _():
        reduce(3)

    def last_sent(i, _):
        cross(3, (at + i) % z.S, at).wait_send()
        return 0

    @pl.when(core == layer)
    def _():
        lax.fori_loop(1, z.S, last_sent, 0)

    @pl.when(core != layer)
    def _():
        give(3).wait_send()

    for piece in range(3):
        give(piece).wait_send()

        @pl.when(core != layer)
        def _(piece=piece):
            hand(piece).wait_send()

        def crossed_over(i, _, piece=piece):
            cross(piece, (at + i) % z.S, at).wait_send()
            return 0

        lax.fori_loop(1, z.S, crossed_over, 0)
    collects[1].finish()
    ob_spread.finish()
    grad_spread.finish()

    def sent(d, _):
        for copy in tile_copies(d, at):
            copy.wait_send()
        return 0

    lax.fori_loop(0, at, sent, 0)

    @pl.when(at > 0)
    def _():
        for copy in edge_copies():
            copy.wait_send()


class Unsaved:
    def save(self, src, dst):
        pass

    def finish(self):
        pass


class Env:
    pass


def layers_kernel(z, names, *refs):
    count = len(WEIGHTS)
    e = Env()
    e.routes, refs = refs[:2], refs[2:]
    tokens, cotangent, refs = refs[0], refs[1], refs[2:]
    own, refs = dict(zip(WEIGHTS, refs[:count])), refs[count:]
    e.layer_out, e.input_grad, e.g_out, refs = refs[0], refs[1], refs[2], refs[3:]
    theirs, refs = dict(zip(WEIGHTS, refs[:count])), refs[count:]
    e.store, refs = dict(zip(KEPT, refs[: len(KEPT)])), refs[len(KEPT) :]
    e.used, refs = dict(zip(WEIGHTS, refs[:count])), refs[count:]
    held, refs = dict(zip(KEPT, refs[: len(KEPT)])), refs[len(KEPT) :]
    s = e.s = Refs(names, refs)
    e.rows, e.middle, e.cotan, e.grad = s.rows, s.middle, s.cotan, s.grad
    me, at, core = e.me, e.at, e.core = lax.axis_index("tensor"), lax.axis_index("seq"), lax.axis_index("section")
    across = {"section": 1 - core}
    own_rows = pl.ds(pl.multiple_of(me * z.block, z.block), z.block)
    e.input_load = pltpu.make_async_copy(tokens, s.rows, s.load.at[0])
    e.cotan_load = pltpu.make_async_copy(cotangent, s.cotan, s.load.at[1])
    e.entry_load = pltpu.make_async_copy(tokens.at[own_rows, :], s.entry, s.load.at[2])
    e.input_load.start()

    def vec(layer):
        return e.used["vec"].at[layer]

    def chosen_keys(layer):
        return s.ckv_next if layer == 1 else held["ckv"]

    def held_in(layer):
        return Refs(KEPT, [chosen_keys(layer) if name == "ckv" else held[name] for name in KEPT])

    e.vec, e.held = vec, held_in

    def load(layer, i, source):
        name = WEIGHTS[i]
        target = e.used[name].at[layer] if name == "vec" else e.used[name]
        return pltpu.make_async_copy(source[name], target, s.weight_load.at[i])

    e.load = load

    def swap(i):
        name = WEIGHTS[i]
        return remote(own[name], theirs[name], s.swap_ss.at[i], s.swap_rs.at[i], across)

    def start_weight(layer, i):
        @pl.when(core == layer)
        def _():
            load(layer, i, own).start()

        @pl.when(core != layer)
        def _():
            load(layer, i, theirs).start()

    loaded = {0: set(), 1: set()}
    pending = {}

    def weight_ready(layer, i):
        if layer == 0 and i not in loaded[0]:

            @pl.when(core != layer)
            def _():
                swap(i).wait_recv()
                load(layer, i, theirs).start()

            loaded[0].add(i)
            load(layer, i, own).wait()
        elif pending.pop((layer, i), False):
            load(layer, i, own).wait()

    def next_weights():
        @pl.when(core == 0)
        def _():
            for i in range(count):
                swap(i).wait_recv()

        for i in range(count):
            start_weight(1, i)
            pending[1, i] = True

    def weight_again(i):
        if WEIGHTS[i] != "vec":
            start_weight(0, i)
            pending[0, i] = True

    e.weight_ready, e.next_weights, e.weight_again = weight_ready, next_weights, weight_again
    kept_pending = {}

    def kept_load(name):
        return pltpu.make_async_copy(e.store[name], held[name], s.kept_load.at[KEPT.index(name)])

    def kept_again(name):
        if name != "ckv":
            kept_load(name).start()
            kept_pending[name] = True

    def kept_ready(layer, name):
        if kept_pending.pop(name, False):
            kept_load(name).wait()

    e.kept_again, e.kept_ready = kept_again, kept_ready

    def collect(phase):
        return Collect(
            z,
            me,
            s.part_send,
            s.part_got,
            s.part_via,
            lambda i: s.part_ss.at[phase, i],
            lambda i: s.part_rs.at[phase, i],
        )

    e.collect = collect
    delivered = []

    def rows_to(ref, target, slot, part):
        local = pltpu.make_async_copy(ref.at[part, :], target.at[core].at[part, :], s.keep.at[slot])
        return local, remote(
            ref.at[part, :], target.at[core].at[part, :], s.move_ss.at[slot], s.move_rs.at[slot], across
        )

    everything = pl.ds(0, z.rows)

    def deliver(layer, ref, target):
        slot = len(delivered)
        local, away = rows_to(ref, target, slot, everything)

        @pl.when(core == layer)
        def _():
            local.start()

        @pl.when(core != layer)
        def _():
            away.start()

        delivered.append((layer, local, away))

    def deliver_block(ref, step):
        slot = len(delivered)
        part = pl.ds(pl.multiple_of(partner(me, step) * z.block, z.block), z.block)
        local, away = rows_to(ref, target=e.input_grad, slot=slot, part=part)

        @pl.when(core == 0)
        def _():
            local.start()

        @pl.when(core == 1)
        def _():
            away.start()

        delivered.append((0, local, away))

    e.deliver, e.deliver_block = deliver, deliver_block

    def turn(layer, where):
        if (layer, where) == TURN_FROM:

            @pl.when(core == 0)
            def _():
                pl.semaphore_signal(s.turn, inc=1, device_id=across, device_id_type=MESH)

        if (layer, where) == TURN_TO:

            @pl.when(core == 1)
            def _():
                pl.semaphore_wait(s.turn, 1)

    e.turn = turn

    @pl.when(core == 0)
    def _():
        for i in range(count):
            load(0, i, own).start()

    barrier = pltpu.get_barrier_semaphore()
    for step in range(1, z.T):
        signal(to_tensor(step, me), barrier)
    signal(across, barrier)

    def greet(i, _):
        signal({"seq": (at + i) % z.S}, barrier)
        return 0

    lax.fori_loop(1, z.S, greet, 0)
    pl.semaphore_wait(barrier, z.T - 1 + 1 + z.S - 1)
    for i in range(count):
        swap(i).start()
    e.cotan_load.start()
    e.entry_load.start()
    forward_part(z, 0, e)
    forward_part(z, 1, e)
    backward_part(z, 1, e)
    backward_part(z, 0, e)
    for i in range(count):
        swap(i).wait_send()
    for layer, local, away in delivered:

        @pl.when(core == layer)
        def _(local=local, away=away):
            local.wait()
            away.wait_recv()

        @pl.when(core != layer)
        def _(away=away):
            away.wait_send()


TURN_FROM, TURN_TO = (0, "attend"), (0, "pack")


def layers(z, routes, tokens, cotangent, own):
    rows, width, heads = z.rows, z.width, z.heads
    half = z.block // 2
    kept = dict(
        n1=((rows, width), BF),
        q=((rows, z.pad), BF),
        kvt=((heads * (z.tiles + 1), TILE, LANES), BF),
        st=((8, rows), F32),
        p=((z.slots, TILE, 2 * LANES), BF),
        ckv=((z.n, TILE, LANES), BF),
        o=((rows, 2 * LANES), BF),
        mid=((z.block, width), F32),
        n2=((rows, width), BF),
        u=((rows, z.hidden), BF),
        act=((rows, z.hidden), BF),
    )
    weights = [own[name] for name in WEIGHTS]
    vmem_of, dma = pltpu.VMEM, pltpu.SemaphoreType.DMA
    scratch = dict(
        rows=vmem_of((rows, width), BF),
        middle=vmem_of((rows, width), BF),
        cotan=vmem_of((rows, width), BF),
        grad=vmem_of((rows, width), BF),
        entry=vmem_of((z.block, width), BF),
        ckv_next=vmem_of((z.n, TILE, LANES), BF),
        gt=vmem_of((8, rows + 2 * LANES), F32),
        gate=vmem_of((heads * (z.tiles + 1), 8, LANES), F32),
        edge=vmem_of((2, heads, TILE, LANES), BF),
        edge_gate=vmem_of((2, 8, LANES), F32),
        send_kv=vmem_of((z.S, z.cap, TILE, LANES), BF),
        send_gate=vmem_of((z.S, z.capg, LANES), F32),
        got_gate=vmem_of((2, z.S, z.capg, LANES), F32),
        far_gate=vmem_of((max(z.n, z.slots), 8, LANES), F32),
        wo_all=vmem_of((z.T, max(2 * LANES, z.block), width), BF),
        wo_high=vmem_of((z.T, LANES, width), BF),
        pair_all=vmem_of((z.T, rows, LANES), BF),
        single_all=vmem_of((z.T, rows // 2, LANES), BF),
        part_send=vmem_of((z.T - 1, z.block, width), BF),
        part_got=vmem_of((2, z.block, width), BF),
        part_via=vmem_of((2, half, width), BF),
        own_part=vmem_of((z.block, width), F32),
        du=vmem_of((rows, z.hidden), BF),
        dr2=vmem_of((z.block, width), F32),
        dqkv=vmem_of((rows, 2 * z.pad), BF),
        dkv=vmem_of((rows + TILE, z.pad), F32),
        dgate=vmem_of((z.tiles + 1, 8, LANES), F32),
        far=vmem_of((z.slots, TILE, LANES), BF),
        back_send_gate=vmem_of((z.S, z.capg, LANES), F32),
        got_kv=vmem_of((z.n, TILE, LANES), BF),
        back_got_gate=vmem_of((z.S, z.capg, LANES), F32),
        got_gate_row=vmem_of((z.n, 8, LANES), F32),
        edge_send=vmem_of((TILE, z.pad), BF),
        edge_got=vmem_of((TILE, z.pad), BF),
        edge_gate_got=vmem_of((8, LANES), F32),
        sum=vmem_of((z.n + 1, TILE, LANES), F32),
        gate_sum=vmem_of((z.n + 1, 8, LANES), F32),
        tile_gate=vmem_of((z.tiles, 8, LANES), F32),
        ds=vmem_of((16, rows), F32),
        stat=vmem_of((24, width), F32),
        stat_got=vmem_of((z.T - 1, 8, width), F32),
    )
    for name, w in zip("abcd", z.pieces):
        scratch["p" + name] = vmem_of((1 if name == "d" else 2, width, w), BF)
        scratch["x" + name] = vmem_of((width, w), BF)
        scratch["s" + name] = vmem_of((z.S, z.padded, w), BF)
        scratch["t" + name] = vmem_of((z.S, z.padded, w), BF)
        if name != "d":
            scratch["h" + name] = vmem_of((z.padded, w), BF)
    pairs = dict(
        kv=(2, z.S), gate=(2, z.S), edge=(2, heads + 1), wo=(z.T,), o=(z.T * 12,), part=(2, 6), res=(6,),
        swap=(len(WEIGHTS),), move=(3 + z.T,), back_kv=(z.S,), back_gate=(z.S,), back_edge=(2,), ob=(6,),
        grad=(6,), stat=(z.T,), give=(4,), cross=(4, z.S), hand=(3,),
    )
    for name, shape in pairs.items():
        scratch[name + "_ss"] = dma(shape)
        scratch[name + "_rs"] = dma(shape)
    scratch |= dict(
        load=dma((3,)),
        weight_load=dma((len(WEIGHTS),)),
        kept_load=dma((len(KEPT),)),
        saved=dma((len(KEPT),)),
        keep=dma((3 + z.T,)),
        turn=pltpu.SemaphoreType.REGULAR,
    )
    doubled = {"vec"}

    def room(name, shape, kind):
        return vmem_of((2, *shape) if name in doubled else shape, kind)

    shaped = (
        jax.ShapeDtypeStruct((2, rows, width), BF),
        jax.ShapeDtypeStruct((2, rows, width), BF),
        jax.ShapeDtypeStruct((2, z.share, sum(z.pieces)), F32),
        *(jax.ShapeDtypeStruct(value.shape, value.dtype) for value in weights),
        *(jax.ShapeDtypeStruct(*kept[name]) for name in KEPT),
    )
    outs = pl.pallas_call(
        functools.partial(layers_kernel, z, tuple(scratch)),
        out_shape=shaped,
        in_specs=[smem(), smem()] + [anywhere()] * (2 + len(weights)),
        out_specs=tuple(vmem() if i == 2 else anywhere() for i in range(len(shaped))),
        scratch_shapes=[
            *(room(name, value.shape, value.dtype) for name, value in zip(WEIGHTS, weights)),
            *(room(name, *kept[name]) for name in KEPT),
            *scratch.values(),
        ],
        compiler_params=pltpu.CompilerParams(
            collective_id=0, has_side_effects=True, vmem_limit_bytes=LIMIT
        ),
        name="layers",
    )(*routes, tokens, cotangent, *weights)
    return outs[:3]


def swapped(value):
    return lax.ppermute(value, "section", [(0, 1), (1, 0)])


def body(
    tokens,
    cotangent,
    lengths,
    selected,
    input_weight,
    input_bias,
    score_weight,
    output_weight,
    output_bias,
    up_weight,
    up_bias,
    down_weight,
    down_bias,
    norm_gain,
    norm_bias,
):
    core = lax.axis_index("section")
    _, rows, width = tokens.shape
    heads, hidden = score_weight.shape[2], up_weight.shape[2]
    head = input_weight.shape[3] // heads
    inner = heads * head
    z = Sizes(lax.axis_size("tensor"), lax.axis_size("seq"), rows, width, heads, hidden)
    scale = head**-0.5
    grouped = (
        selected[0].reshape(2, heads, z.S, z.tiles).transpose(0, 2, 1, 3).reshape(2, z.S, z.slots)
    )
    kept_choice = lax.dynamic_index_in_dim(grouped, core, 0, keepdims=False)
    got_choice = swapped(lax.dynamic_index_in_dim(grouped, 1 - core, 0, keepdims=False))
    choice = jnp.where(
        core == 0, jnp.stack([kept_choice, got_choice]), jnp.stack([got_choice, kept_choice])
    )
    length = lax.dynamic_index_in_dim(lengths, core, 0, keepdims=False)
    ends = jnp.stack([length[0], length[0] + length[1]])
    own, routes = prepare(
        z,
        ends,
        choice,
        input_weight[0].transpose(1, 0, 2),
        input_bias[0],
        score_weight[0],
        output_weight[0],
        output_bias,
        up_bias,
        down_bias,
        norm_gain[0],
        norm_bias[0],
    )
    own |= dict(wup=up_weight[0], wdn=down_weight[0])
    first = lax.dynamic_index_in_dim(tokens, core, 0, keepdims=False)
    cotan = lax.dynamic_index_in_dim(cotangent, core, 0, keepdims=False)
    layer_out, input_grad, total = layers(z, routes, first, cotan, own)
    share = z.share
    c_o, c_i = hidden, hidden + LANES
    pairs = total[0, :, c_i : c_i + z.pad].reshape(share, heads, LANES)
    input_weight_grad = jnp.stack(
        [
            scale * total[1, :, c_i : c_i + inner],
            pairs[:, :, :head].reshape(share, inner),
            pairs[:, :, head:].reshape(share, inner),
        ],
        axis=1,
    )
    out_grad = jnp.concatenate([total[0, :, c_o:c_i], total[1, :, c_o:c_i]], axis=1)[:, :inner]
    c_s = c_i + z.pad
    kept_stats = lax.dynamic_index_in_dim(total, core, 0, keepdims=False)[:, c_s : c_s + 16]
    stats = kept_stats.T
    each = inner // z.S
    return (
        layer_out[None],
        input_grad[None],
        input_weight_grad[None],
        jnp.stack([stats[13, :each], stats[13, each : 2 * each]])[None],
        kept_stats[:, 10 : 10 + heads][None],
        out_grad.T[None],
        stats[0][None],
        total[1, :, :hidden][None],
        stats[8][None],
        total[0, :, :hidden].T[None],
        stats[9][None],
        jnp.stack([stats[3], stats[1]])[None],
        jnp.stack([stats[4], stats[2]])[None],
    )


def solution(mesh):
    return jax.shard_map(
        body,
        mesh=mesh,
        in_specs=(
            P(None, "seq", None),
            P(None, "seq", None),
            P(),
            P("section", None, "tensor", None),
            P("section", None, None, "tensor"),
            P("section", None, "tensor"),
            P("section", None, "tensor"),
            P("section", "tensor", None),
            P("section", None),
            P("section", None, "tensor"),
            P("section", "tensor"),
            P("section", "tensor", None),
            P("section", None),
            P("section", None, None),
            P("section", None, None),
        ),
        out_specs=(
            P("section", None, "seq", None),
            P("section", None, "seq", None),
            P("section", "seq", None, "tensor"),
            P("section", None, ("tensor", "seq")),
            P("section", "seq", "tensor"),
            P("section", "tensor", "seq"),
            P("section", "seq"),
            P("section", "seq", "tensor"),
            P("section", ("tensor", "seq")),
            P("section", "tensor", "seq"),
            P("section", "seq"),
            P("section", None, "seq"),
            P("section", None, "seq"),
        ),
        check_vma=False,
    )
```

```python
import functools
import math

import jax
import jax.numpy as jnp
from jax import lax
from jax.experimental import pallas as pl
from jax.experimental.pallas import tpu as pltpu
from jax.sharding import PartitionSpec as P

TILE = 64
LANES = 128
MASKED = -1e30
EPSILON = 1e-05
FAR = -(1 << 20)
MESH = pl.DeviceIdType.MESH
BF = jnp.bfloat16
F32 = jnp.float32
GELU_A = 0.044715
GELU_K = math.sqrt(2.0 / math.pi)
LIMIT = 62 * 1024 * 1024


class Sizes:
    def __init__(self, mesh_tensor, mesh_seq, rows, width, heads, hidden):
        self.T, self.S = mesh_tensor, mesh_seq
        self.rows, self.width, self.heads, self.hidden = rows, width, heads, hidden
        self.tiles = rows // TILE
        self.slots = heads * self.tiles
        self.cap = -(-self.slots // (mesh_seq - 1))
        self.capg = -(-self.cap // 8) * 8
        self.n = mesh_seq * self.cap
        self.block = rows // mesh_tensor
        self.pad = heads * LANES
        self.share = width // mesh_seq
        self.padded = -(-self.share // 16) * 16
        self.pieces = (hidden, LANES, self.pad, LANES)


SEND, INV, ORD, CONT, ARR, POS, LAST, ENDS = range(8)
WEIGHTS = ("vec", "w1", "swt", "wo", "wup", "wdn")
KEPT = ("n1", "q", "kvt", "st", "p", "ckv", "o", "mid", "n2", "u", "act")


def nn(a, b):
    return jnp.dot(a, b, preferred_element_type=F32)


def nt(a, b):
    return lax.dot_general(a, b, (((1,), (1,)), ((), ())), preferred_element_type=F32)


def tn(a, b):
    return lax.dot_general(a, b, (((0,), (0,)), ((), ())), preferred_element_type=F32)


def normed(x):
    centred = x - jnp.mean(x, axis=-1, keepdims=True)
    spread = lax.rsqrt(jnp.mean(centred * centred, axis=-1, keepdims=True) + EPSILON)
    return centred * spread, spread


def norm_back(grad, gain, y, spread):
    scaled = grad * gain
    return spread * (
        scaled
        - jnp.mean(scaled, axis=-1, keepdims=True)
        - y * jnp.mean(scaled * y, axis=-1, keepdims=True)
    )


def partner(me, step):
    return (me // 2 + step // 2) % 2 * 2 + (me % 2 + step % 2) % 2


def column_sum(x):
    return jnp.sum(x, axis=0, keepdims=True)


def smem():
    return pl.BlockSpec(memory_space=pltpu.SMEM)


def vmem():
    return pl.BlockSpec(memory_space=pltpu.VMEM)


def anywhere():
    return pl.BlockSpec(memory_space=pl.ANY)


def grid_of(shape, axis):
    return lax.broadcasted_iota(jnp.int32, shape, axis)


def prepare_kernel(
    z,
    length_ref,
    kept_ref,
    got_ref,
    win_ref,
    bin_ref,
    sw_ref,
    wout_ref,
    bout_ref,
    bup_ref,
    bdn_ref,
    gain_ref,
    shift_ref,
    vec_ref,
    w1_ref,
    swt_ref,
    wo_ref,
    rt0_ref,
    rt1_ref,
):
    inner, head = win_ref.shape[2], win_ref.shape[2] // z.heads
    row, col = grid_of((inner, z.pad), 0), grid_of((inner, z.pad), 1)
    lane_of = row // head * LANES + row % head
    first = (col == lane_of).astype(F32)
    second = (col == lane_of + head).astype(F32)
    low, high = first.astype(BF), second.astype(BF)
    scaled = (first * head**-0.5).astype(BF)
    w1_ref[:, : z.pad] = nn(win_ref[0], scaled).astype(BF)
    w1_ref[:, z.pad :] = (nn(win_ref[1], low) + nn(win_ref[2], high)).astype(BF)
    vec_ref[0:1, :] = gain_ref[...].astype(F32)[0:1]
    vec_ref[1:2, :] = shift_ref[...].astype(F32)[0:1]
    vec_ref[2:3, : z.pad] = nn(bin_ref[...], scaled)[0:1]
    vec_ref[2:3, z.pad :] = nn(bin_ref[...], high)[1:2]
    vec_ref[3:4, :] = bout_ref[...].astype(F32)
    vec_ref[4:5, :] = gain_ref[...].astype(F32)[1:2]
    vec_ref[5:6, :] = shift_ref[...].astype(F32)[1:2]
    vec_ref[6:7, :] = bup_ref[...].astype(F32)
    vec_ref[7:8, :] = bdn_ref[...].astype(F32)
    unit = (grid_of((16, z.heads), 0) == grid_of((16, z.heads), 1)).astype(F32).astype(BF)
    swt_ref[...] = nt(unit, sw_ref[...]).astype(BF)
    wo_ref[0:inner, :] = wout_ref[...]
    wo_ref[inner:, :] = jnp.zeros((2 * LANES - inner, z.width), BF)

    at, core = lax.axis_index("seq"), lax.axis_index("section")
    n, slots, cap = z.n, z.slots, z.cap
    first_end = length_ref[core, 0]
    second_end = first_end + length_ref[core, 1]
    shift = z.tiles.bit_length() - 1
    near = 1e-3

    def total(mask, value, axis):
        return jnp.sum(jnp.where(mask, value, 0.0), axis=axis, keepdims=True)

    def whole(x):
        return (x + near).astype(jnp.int32)

    for layer, rt in enumerate((rt0_ref, rt1_ref)):
        rt[...] = jnp.zeros((8, LANES), jnp.int32)
        chosen = jnp.where(core == layer, kept_ref[...], got_ref[...])
        owner = lax.shift_right_arithmetic(chosen, shift)
        sub, lan = grid_of((slots, n), 0), grid_of((slots, n), 1)
        wide = jnp.zeros((slots, n), jnp.int32)
        for d in range(z.S):
            column = jnp.sum(
                jnp.where(
                    grid_of((slots, slots), 0) == grid_of((slots, slots), 1),
                    chosen[d : d + 1].astype(F32) + 1.0,
                    0.0,
                ),
                axis=1,
                keepdims=True,
            )
            wide = jnp.where(lan // cap == d, whole(column) - 1, wide)
        mine = lax.shift_right_arithmetic(wide, shift) == at
        order = nn(
            (grid_of((slots, slots), 0) > grid_of((slots, slots), 1)).astype(F32), mine.astype(F32)
        )
        taken = mine & (whole(order) == lan % cap)
        head_of = sub // z.tiles
        inner_tile = wide - at * z.tiles
        rt[SEND : SEND + 1, :n] = whole(
            total(taken, (head_of * (z.tiles + 1) + inner_tile).astype(F32), 0)
        ) + 1
        present = jnp.sum(taken.astype(F32), axis=0, keepdims=True)
        key = total(taken, (head_of * z.tiles + inner_tile - slots).astype(F32), 0) + slots
        own = jnp.sum(
            jnp.where(grid_of((z.S, slots), 0) == at, chosen.astype(F32) + 1.0, 0.0), axis=0, keepdims=True
        )
        square_row, square_col = grid_of((slots, slots), 0), grid_of((slots, slots), 1)
        own_column = total(square_row == square_col, own, 1)
        own_row = whole(own) - 1
        own_col = whole(own_column) - 1
        owner_row = lax.shift_right_arithmetic(own_row, shift)
        owner_col = lax.shift_right_arithmetic(own_col, shift)
        same = owner_row == owner_col
        place_row = whole(jnp.sum((same & (square_row < square_col)).astype(F32), axis=0, keepdims=True))
        place_col = whole(jnp.sum((same & (square_col < square_row)).astype(F32), axis=1, keepdims=True))
        live = own_row >= 0
        rt[ARR : ARR + 1, :slots] = jnp.where(live, owner_row * cap + place_row, at * cap)
        rt[POS : POS + 1, :slots] = jnp.where(live, own_row * TILE, FAR)
        matched = (owner_col == lan // cap) & (place_col == lan % cap)
        rt[INV : INV + 1, :n] = whole(total(matched, sub.astype(F32), 0))
        big_row, big_col = grid_of((n, n), 0), grid_of((n, n), 1)
        key_col = total(big_row == big_col, key, 1)
        rank = jnp.sum(
            ((key < key_col) | ((key == key_col) & (big_col < big_row))).astype(F32), axis=1, keepdims=True
        )
        at_rank = whole(rank) == big_col
        rt[ORD : ORD + 1, :n] = whole(total(at_rank, big_row.astype(F32), 0))
        sorted_key = total(at_rank, key_col, 0)
        before = total(whole(rank) + 1 == big_col, key_col + 1.0, 0) - 1.0
        rt[CONT : CONT + 1, :n] = (sorted_key == before).astype(jnp.int32)
        tile = grid_of((n, slots), 1).astype(F32)
        upto = jnp.sum((key_col <= tile).astype(F32), axis=0, keepdims=True)
        has = jnp.sum((key_col == tile).astype(F32), axis=0, keepdims=True)
        rt[LAST : LAST + 1, :slots] = whole(jnp.where(has > 0.5, upto - 1.0, n * 1.0))
        rt[ENDS : ENDS + 1, :] = jnp.where(grid_of((1, LANES), 1) == 0, first_end, second_end)


def prepare(z, lengths, kept, got, win, bin_, sw, wout, bout, bup, bdn, gain, shift):
    table = jax.ShapeDtypeStruct((8, LANES), jnp.int32)
    outs = pl.pallas_call(
        functools.partial(prepare_kernel, z),
        out_shape=(
            jax.ShapeDtypeStruct((8, z.width), F32),
            jax.ShapeDtypeStruct((z.width, 2 * z.pad), BF),
            jax.ShapeDtypeStruct((16, z.width), BF),
            jax.ShapeDtypeStruct((2 * LANES, z.width), BF),
            table,
            table,
        ),
        in_specs=[smem()] + [vmem()] * 11,
        out_specs=tuple(vmem() for _ in range(6)),
        name="prepare",
    )(lengths, kept, got, win, bin_, sw, wout, bout, bup, bdn, gain, shift)
    return dict(zip(WEIGHTS[:4], outs)), outs[4:]


def to_tensor(step, me):
    return {"tensor": partner(me, step)}


def remote(src, dst, send, recv, target):
    return pltpu.make_async_remote_copy(
        src_ref=src, dst_ref=dst, send_sem=send, recv_sem=recv, device_id=target, device_id_type=MESH
    )


def signal(target, barrier):
    pl.semaphore_signal(barrier, inc=1, device_id=target, device_id_type=MESH)


class Spread:
    def __init__(self, me, view, sends, recvs):
        self.me, self.view, self.sends, self.recvs = me, view, sends, recvs

    def copy(self, i):
        me, x, y = self.me, partner(self.me, 1), partner(self.me, 2)
        owner, half, step = ((me, 0, 1), (me, 1, 2), (me, 1, 1), (me, 0, 2), (x, 0, 2), (y, 1, 1))[i]
        ref = self.view(owner, half)
        return remote(ref, ref, self.sends(i), self.recvs(i), to_tensor(step, me))

    def start(self):
        for i in range(4):
            self.copy(i).start()

    def forward(self):
        for i in range(2):
            self.copy(i).wait_recv()
            self.copy(4 + i).start()

    def wait(self, step):
        for i in ((), (2,), (3,), (4, 5))[step]:
            self.copy(i).wait_recv()

    def finish(self):
        for i in range(6):
            self.copy(i).wait_send()


class Collect:
    def __init__(self, z, me, send, got, via, sends, recvs):
        self.me, self.send, self.got, self.via, self.sends, self.recvs = me, send, got, via, sends, recvs
        half = z.block // 2
        self.halves = (pl.ds(0, half), pl.ds(half, half))

    def copy(self, i):
        top, bottom = self.halves
        block, rows, target, step = (
            (2, top, self.via.at[0], 1),
            (2, bottom, self.via.at[1], 2),
            (0, top, self.got.at[0, top, :], 1),
            (1, bottom, self.got.at[1, bottom, :], 2),
            (0, bottom, self.got.at[0, bottom, :], 1),
            (1, top, self.got.at[1, top, :], 2),
        )[i]
        return remote(
            self.send.at[block, rows, :], target, self.sends(i), self.recvs(i), to_tensor(step, self.me)
        )

    def put(self, step, value):
        for wanted, copies in ((3, (0, 1)), (1, (2,)), (2, (3,))):

            @pl.when(step == wanted)
            def _(wanted=wanted, copies=copies):
                self.send[wanted - 1] = value().astype(BF)
                for i in copies:
                    self.copy(i).start()

    def join(self):
        top, bottom = self.halves
        for i, block, rows in ((1, 0, bottom), (0, 1, top)):
            self.copy(i).wait_recv()
            joined = self.send[block, rows, :].astype(F32) + self.via[i].astype(F32)
            self.send[block, rows, :] = joined.astype(BF)
            self.copy(5 - i).start()

    def total(self, own):
        for i in range(2, 6):
            self.copy(i).wait_recv()
        return own + self.got[0].astype(F32) + self.got[1].astype(F32)

    def finish(self):
        for i in range(6):
            self.copy(i).wait_send()


def visiting(k):
    return jnp.where(k == 0, 3, jnp.where(k == 3, 0, k))


class Saver:
    def __init__(self, sems):
        self.sems, self.copies = sems, []

    def save(self, src, dst):
        copy = pltpu.make_async_copy(src, dst, self.sems.at[len(self.copies)])
        copy.start()
        self.copies.append(copy)

    def finish(self):
        for copy in self.copies:
            copy.wait()


class Refs:
    def __init__(self, names, refs):
        assert len(names) == len(refs), (len(names), len(refs))
        for name, ref in zip(names, refs):
            setattr(self, name, ref)


def forward_part(z, layer, e):
    rt, r_ref, res_ref = e.routes[layer], (e.rows, e.middle)[layer], (e.middle, e.rows)[layer]
    used, s, me, at, core, load = e.used, e.s, e.me, e.at, e.core, e.load
    held = e.held(layer)
    last = z.S - 1
    first_row = at * z.rows
    vec = e.vec(layer)
    edge_ss, edge_rs = s.edge_ss.at[layer], s.edge_rs.at[layer]
    kv_ss, kv_rs, gate_ss, gate_rs = (
        sems.at[layer] for sems in (s.kv_ss, s.kv_rs, s.gate_ss, s.gate_rs)
    )
    edge, edge_gate, got_gate = s.edge.at[layer], s.edge_gate.at[layer], s.got_gate.at[layer]
    held.ckv[at * z.cap] = jnp.zeros((TILE, LANES), BF)
    outs = e.store

    def ready(*wanted):
        for i in wanted:
            e.weight_ready(layer, i)

    if layer == 0:
        e.input_load.wait()
    saver = Saver(s.saved) if layer == 0 else Unsaved()
    per_block = z.block // TILE
    ready(0)

    def norm_in(b):
        rows = pl.ds(pl.multiple_of(b * z.block, z.block), z.block)
        y, _ = normed(r_ref[rows, :].astype(F32))
        held.n1[rows, :] = (y * vec[0:1, :] + vec[1:2, :]).astype(BF)

    def project(b):
        rows = pl.ds(pl.multiple_of(b * z.block, z.block), z.block)
        qkv = (nn(held.n1[rows, :], used["w1"][...]) + vec[2:3, :]).astype(BF)
        held.q[rows, :] = qkv[:, : z.pad]
        for h in range(z.heads):
            pairs = qkv[:, z.pad + h * LANES : z.pad + (h + 1) * LANES]
            held.kvt[pl.ds(h * (z.tiles + 1) + 1 + b * per_block, per_block)] = pairs.reshape(
                per_block, TILE, LANES
            )

    def each_norm(b, _):
        norm_in(b)
        return 0

    def each_project(b, _):
        project(b)
        return 0

    def arrived_block(step, _):
        for wanted in range(1, z.T):

            @pl.when(step == wanted)
            def _(wanted=wanted):
                e.arriving.wait(wanted)

        norm_in(partner(me, step))
        project(partner(me, step))
        return 0

    if layer == 0:
        lax.fori_loop(0, z.T, each_norm, 0)
        saver.save(held.n1, outs["n1"])
        ready(1, 2)
        lax.fori_loop(0, z.T, each_project, 0)
    else:
        ready(1, 2)
        arrived_block(0, 0)
        e.arriving.forward()
        lax.fori_loop(1, z.T, arrived_block, 0)
        e.arriving.finish()
        e.deliver(0, r_ref, e.layer_out)
    score = nt(used["swt"][...], held.n1[...])[0:8]
    held.st[...] = score
    gate = jnp.minimum(score, 0.0) - jnp.log1p(jnp.exp(-jnp.abs(score)))
    s.gt[:, 0:LANES] = jnp.zeros((8, LANES), F32)
    s.gt[:, LANES : LANES + z.rows] = gate.astype(BF).astype(F32)
    s.gt[:, LANES + z.rows :] = jnp.zeros((8, LANES), F32)
    for t in range(z.tiles + 1):
        for h in range(z.heads):
            s.gate[h * (z.tiles + 1) + t, 0:1, :] = s.gt[
                h : h + 1, TILE + t * TILE : TILE + t * TILE + LANES
            ]

    def edge_copies():
        after = {"seq": jnp.minimum(at + 1, last)}
        return [
            remote(
                held.kvt.at[h * (z.tiles + 1) + z.tiles],
                edge.at[h],
                edge_ss.at[h],
                edge_rs.at[h],
                after,
            )
            for h in range(z.heads)
        ] + [
            remote(
                s.gt.at[:, pl.ds(z.rows, LANES)],
                edge_gate,
                edge_ss.at[z.heads],
                edge_rs.at[z.heads],
                after,
            )
        ]

    @pl.when(at < last)
    def _():
        for copy in edge_copies():
            copy.start()

    def tile_copies(d, source):
        return (
            remote(
                s.send_kv.at[d],
                held.ckv.at[pl.ds(source * z.cap, z.cap)],
                kv_ss.at[d],
                kv_rs.at[source],
                {"seq": d},
            ),
            remote(
                s.send_gate.at[d], got_gate.at[source], gate_ss.at[d], gate_rs.at[source], {"seq": d}
            ),
        )

    def pack(k, _):
        d = z.S - 1 - k

        def slot(i, _):
            u = rt[SEND, d * z.cap + i]
            s.send_kv[d, i] = held.kvt[u]
            s.send_gate[d, pl.ds(i, 1), :] = s.gate[u][0:1]
            return 0

        lax.fori_loop(0, z.cap, slot, 0)
        for copy in tile_copies(d, at):
            copy.start()
        return 0

    e.turn(layer, "pack")
    lax.fori_loop(0, last - at, pack, 0)
    ready(3)

    def wo_copy(step):
        return remote(
            used["wo"], s.wo_all.at[me], s.wo_ss.at[step], s.wo_rs.at[step], to_tensor(step, me)
        )

    for step in range(1, z.T):
        wo_copy(step).start()
    s.wo_all[me] = used["wo"][...]
    saver.save(held.q, outs["q"])
    saver.save(held.st, outs["st"])

    def landed(source, _):
        for copy in tile_copies(last, source):
            copy.wait_recv()
        for i in range(z.cap):
            s.far_gate[source * z.cap + i, 0:1, :] = got_gate[source, i : i + 1, :]
        return 0

    lax.fori_loop(0, at, landed, 0)
    lane = grid_of((TILE, LANES), 1)
    row = grid_of((TILE, LANES), 0)
    for h in range(z.heads):
        held.kvt[h * (z.tiles + 1)] = jnp.zeros((TILE, LANES), BF)

    @pl.when(at > 0)
    def _():
        for copy in edge_copies():
            copy.wait_recv()
        for h in range(z.heads):
            held.kvt[h * (z.tiles + 1)] = edge[h]
            s.gate[h * (z.tiles + 1), 0:1, :] = jnp.where(
                lane[0:1] < TILE,
                pltpu.roll(edge_gate[...], TILE, 1)[h : h + 1],
                s.gate[h * (z.tiles + 1), 0:1, :],
            )

    saver.save(held.kvt, outs["kvt"])
    saver.save(held.ckv, outs["ckv"])

    def attend(tiles):
        units = [(g, h) for g in range(len(tiles)) for h in range(z.heads)]
        keys, scores = {}, {}
        for g, t in enumerate(tiles):
            base = pl.multiple_of(t * TILE, TILE)
            query = first_row + base + row
            begin = jnp.where(
                query >= rt[ENDS, 1],
                rt[ENDS, 1],
                jnp.where(query >= rt[ENDS, 0], rt[ENDS, 0], 0),
            )
            key = first_row + base - TILE + lane
            near_ok = (key <= query) & (key > query - TILE) & (key >= begin)
            for h in range(z.heads):
                u = h * z.tiles + t
                arrived = rt[ARR, u]
                far = held.ckv[arrived]
                near = held.kvt[pl.ds(h * (z.tiles + 1) + t, 2)].reshape(2 * TILE, LANES)
                keys[g, h] = jnp.concatenate([near, far, far], axis=0)
                gates = jnp.concatenate(
                    [s.gate[h * (z.tiles + 1) + t, 0:1, :], s.far_gate[arrived][0:1]], axis=1
                )
                far_ok = (rt[POS, u] + lane >= begin) & (lane < TILE)
                query_tile = held.q[pl.ds(base, TILE), h * LANES : (h + 1) * LANES]
                scores[g, h] = jnp.where(
                    jnp.concatenate([near_ok, far_ok], axis=1), nt(query_tile, keys[g, h]) + gates, MASKED
                )
        tops = {u: jnp.max(scores[u], axis=-1, keepdims=True) for u in units}
        raised = {u: jnp.exp(scores[u] - tops[u]) for u in units}
        sums = {u: jnp.sum(raised[u], axis=-1, keepdims=True) for u in units}
        probs = {u: (raised[u] * (1.0 / sums[u])).astype(BF) for u in units}
        mixed = {u: nn(probs[u], keys[u]) for u in units}
        for g, t in enumerate(tiles):
            base = pl.multiple_of(t * TILE, TILE)
            for h in range(z.heads):
                held.p[t * z.heads + h] = probs[g, h]
            pair = jnp.where(lane < TILE, pltpu.roll(mixed[g, 0], TILE, 1), mixed[g, 1]).astype(BF)
            single = pltpu.roll(mixed[g, 2], TILE, 1)
            held.o[pl.ds(base, TILE), 0:LANES] = pair
            held.o[pl.ds(base, TILE), LANES:] = single.astype(BF)
            s.pair_all[me, pl.ds(base, TILE), :] = pair
            if g % 2 == 0:
                even = single
            else:
                couple = pl.ds(pl.multiple_of((t - 1) * (TILE // 2), TILE), TILE)
                s.single_all[me, couple, :] = jnp.where(lane < TILE, even, mixed[g, 2]).astype(BF)

    e.turn(layer, "attend")
    half_rows = z.block // 2

    def pair_spread(b):
        return Spread(
            me,
            lambda owner, half: s.pair_all.at[owner, pl.ds(b * z.block + half * half_rows, half_rows), :],
            lambda i: s.o_ss.at[b * 12 + i],
            lambda i: s.o_rs.at[b * 12 + i],
        )

    def single_spread(b):
        return Spread(
            me,
            lambda owner, half: s.single_all.at[
                owner, pl.ds(b * half_rows + half * (half_rows // 2), half_rows // 2), :
            ],
            lambda i: s.o_ss.at[b * 12 + 6 + i],
            lambda i: s.o_rs.at[b * 12 + 6 + i],
        )

    def attend_block(b, _):
        attend([b * per_block + g for g in range(per_block)])
        pair_spread(b).start()
        single_spread(b).start()

        @pl.when(b > 0)
        def _():
            pair_spread(b - 1).forward()
            single_spread(b - 1).forward()

        return 0

    lax.fori_loop(0, z.T, attend_block, 0)
    pair_spread(z.T - 1).forward()
    single_spread(z.T - 1).forward()
    saver.save(held.p, outs["p"])
    saver.save(held.o, outs["o"])
    ready(4, 5)
    for step in range(1, z.T):
        wo_copy(step).wait()
    for t in range(z.T):
        s.wo_high[t, 0:TILE, :] = jnp.zeros((TILE, z.width), BF)
        s.wo_high[t, TILE:, :] = s.wo_all[t, LANES : LANES + TILE, :]
    collect = e.collect(0)

    def feed(k, _):
        step = visiting(k)
        block = partner(me, step)
        rows = pl.ds(pl.multiple_of(block * z.block, z.block), z.block)
        few = pl.ds(pl.multiple_of(block * half_rows, half_rows), half_rows)
        for other in range(1, z.T):
            pair_spread(block).wait(other)
            single_spread(block).wait(other)
        def joined(value, weight):
            return sum(
                nn(
                    jnp.concatenate([value(t), value(t + 1)], axis=1),
                    jnp.concatenate([weight(t), weight(t + 1)], axis=0),
                )
                for t in range(0, z.T, 2)
            )

        mixed = joined(lambda t: s.pair_all[t, rows, :], lambda t: s.wo_all[t, 0:LANES, :])
        even = joined(lambda t: s.single_all[t, few, :], lambda t: s.wo_all[t, LANES : 2 * LANES, :])
        odd = joined(lambda t: s.single_all[t, few, :], lambda t: s.wo_high[t])
        turns = []
        for i in range(per_block // 2):
            turns += [even[i * TILE : (i + 1) * TILE], odd[i * TILE : (i + 1) * TILE]]
        mixed += jnp.concatenate(turns, axis=0)
        middle = r_ref[rows, :].astype(F32) + mixed + vec[3:4, :]
        held.mid[...] = middle
        y, _ = normed(middle)
        n2 = (y * vec[4:5, :] + vec[5:6, :]).astype(BF)
        held.n2[rows, :] = n2
        u = nn(n2, used["wup"][...]) + vec[6:7, :]
        held.u[rows, :] = u.astype(BF)
        act = (0.5 * u * (1.0 + jnp.tanh(GELU_K * (u + GELU_A * u * u * u)))).astype(BF)
        held.act[rows, :] = act
        s.own_part[...] = nn(act, used["wdn"][...])

        collect.put(step, lambda: s.own_part[...])
        return 0

    lax.fori_loop(0, z.T, feed, 0)
    collect.join()
    if layer == 0:
        e.next_weights()
    e.turn(layer, "feed")
    for name in ("mid", "n2", "u", "act"):
        saver.save(getattr(held, name), outs[name])
    total = collect.total(held.mid[...] + s.own_part[...] + vec[7:8, :])
    own_rows = pl.ds(pl.multiple_of(me * z.block, z.block), z.block)
    res_ref[own_rows, :] = total.astype(BF)
    spread = Spread(
        me,
        lambda owner, half: res_ref.at[
            pl.ds(pl.multiple_of(owner * z.block + half * half_rows, half_rows), half_rows), :
        ],
        lambda i: s.res_ss.at[i],
        lambda i: s.res_rs.at[i],
    )
    e.arriving = spread
    if layer == 0:
        spread.start()
    collect.finish()

    def finish_block(b, _):
        pair_spread(b).finish()
        single_spread(b).finish()
        return 0

    lax.fori_loop(0, z.T, finish_block, 0)

    def sent(d, _):
        for copy in tile_copies(d, at):
            copy.wait_send()
        return 0

    lax.fori_loop(at + 1, z.S, sent, 0)

    @pl.when(at < last)
    def _():
        for copy in edge_copies():
            copy.wait_send()

    saver.finish()


def backward_part(z, layer, e):
    rt, used, s, me, at, core = e.routes[layer], e.used, e.s, e.me, e.at, e.core
    c_ref, grad_ref = (e.grad, e.cotan) if layer == 0 else (e.cotan, e.grad)
    k = e.held(layer)
    last = z.S - 1
    vec = e.vec(layer)
    own_rows = pl.ds(pl.multiple_of(me * z.block, z.block), z.block)
    W = z.width
    g_out = e.g_out
    across = {"section": 1 - core}

    def ready(*names):
        for name in names:
            if name in WEIGHTS:
                e.weight_ready(layer, WEIGHTS.index(name))
            else:
                e.kept_ready(layer, name)

    def done(*names):
        if layer == 1:
            for name in names:
                if name in WEIGHTS:
                    e.weight_again(WEIGHTS.index(name))
                else:
                    e.kept_again(name)

    collects = (e.collect(1), e.collect(2))
    half_rows = z.block // 2

    def rows_spread(ref, sends, recvs):
        return Spread(
            me,
            lambda owner, half: ref.at[
                pl.ds(pl.multiple_of(owner * z.block + half * half_rows, half_rows), half_rows), :
            ],
            lambda i: sends.at[i],
            lambda i: recvs.at[i],
        )

    if layer == 1:
        e.cotan_load.wait()
    ready("wdn", "u", "wup")

    def ff_back(i, _):
        step = visiting(i)
        rows = pl.ds(pl.multiple_of(partner(me, step) * z.block, z.block), z.block)
        u = k.u[rows, :].astype(F32)
        squared = u * u
        bent = jnp.tanh(GELU_K * (u + GELU_A * squared * u))
        slope = 0.5 * (1.0 + bent) + 0.5 * u * (1.0 - bent * bent) * (
            GELU_K * (1.0 + 3.0 * GELU_A * squared)
        )
        du = (nt(c_ref[rows, :], used["wdn"][...]) * slope).astype(BF)
        s.du[rows, :] = du
        s.own_part[...] = nt(du, used["wup"][...])

        collects[0].put(step, lambda: s.own_part[...])
        return 0

    lax.fori_loop(0, z.T, ff_back, 0)
    ones = jnp.ones((16, z.rows), BF)
    s.stat[...] = jnp.zeros((24, W), F32)

    mine = (s.pa, s.pb, s.pc, s.pd)
    theirs_part = (s.xa, s.xb, s.xc, s.xd)
    summed = (s.sa, s.sb, s.sc, s.sd)
    crossed = (s.ta, s.tb, s.tc, s.td)
    handed = (s.ha, s.hb, s.hc)

    def give(piece):
        return remote(
            mine[piece].at[1 - core if piece < 3 else 0], theirs_part[piece], s.give_ss.at[piece], s.give_rs.at[piece], across
        )

    def cross(piece, d, source):
        return remote(
            summed[piece].at[d],
            crossed[piece].at[source],
            s.cross_ss.at[piece, d],
            s.cross_rs.at[piece, source],
            {"seq": d},
        )

    def hand(piece):
        return remote(
            summed[piece].at[at], handed[piece], s.hand_ss.at[piece], s.hand_rs.at[piece], across
        )

    span = math.lcm(z.share, 16)

    def add_up(piece):
        give(piece).wait_recv()

        def chunk(i, _):
            rows = pl.ds(pl.multiple_of(i * span, span), span)
            value = mine[piece][core if piece < 3 else 0, rows, :].astype(F32) + theirs_part[piece][rows, :].astype(F32)
            for j in range(span // z.share):
                d = i * (span // z.share) + j
                rows_of = value[j * z.share : (j + 1) * z.share]
                if z.padded > z.share:
                    rows_of = jnp.concatenate(
                        [rows_of, jnp.zeros((z.padded - z.share, value.shape[1]), F32)], axis=0
                    )
                summed[piece][d] = rows_of.astype(BF)

                @pl.when(d != at)
                def _():
                    cross(piece, d, at).start()

            return 0

        lax.fori_loop(0, W // span, chunk, 0)

    offsets = [sum(z.pieces[:piece]) for piece in range(len(z.pieces))]

    def reduce(piece):
        def wait(i, _):
            d = (at + i) % z.S
            cross(piece, d, d).wait_recv()
            return 0

        lax.fori_loop(1, z.S, wait, 0)

        def add(i, running):
            return running + crossed[piece][(at + i) % z.S].astype(F32)

        total = lax.fori_loop(1, z.S, add, summed[piece][at].astype(F32))
        cols = slice(offsets[piece], offsets[piece] + z.pieces[piece])

        @pl.when(core == layer)
        def _():
            g_out[core, :, cols] = total[: z.share]

        @pl.when(core != layer)
        def _():
            if piece < len(handed):
                summed[piece][at] = total.astype(BF)
                hand(piece).start()

    def take(piece):
        cols = slice(offsets[piece], offsets[piece] + z.pieces[piece])

        @pl.when(core == layer)
        def _():
            hand(piece).wait_recv()
            g_out[1 - core, :, cols] = handed[piece][...].astype(F32)[: z.share]

    ready("act", "n2")
    wide = z.hidden // 2
    for cols in (slice(0, wide), slice(wide, z.hidden)):
        s.pa[0, :, cols] = tn(c_ref[...], k.act[:, cols]).astype(BF)
    collects[0].join()
    for cols in (slice(0, wide), slice(wide, z.hidden)):
        s.pa[1, :, cols] = tn(k.n2[...], s.du[:, cols]).astype(BF)
    give(0).start()
    done("wdn", "wup", "u", "act", "n2")
    s.stat[8:9, :] = nn(ones, s.du[...])[0:1]
    s.stat[9:10, :] = nn(ones, c_ref[...])[0:1]
    ready("mid", "wo")
    add_up(0)
    grad = collects[0].total(s.own_part[...])
    y, spread = normed(k.mid[...])
    dr2 = c_ref[own_rows, :].astype(F32) + norm_back(grad, vec[4:5, :], y, spread)
    s.dr2[...] = dr2
    s.wo_all[me] = dr2.astype(BF)

    ob_spread = Spread(
        me,
        lambda owner, half: s.wo_all.at[owner, pl.ds(half * half_rows, half_rows), :],
        lambda i: s.ob_ss.at[i],
        lambda i: s.ob_rs.at[i],
    )
    ob_spread.start()
    done("mid")
    s.stat[0:1, :] = column_sum(dr2)
    s.stat[1:2, :] = column_sum(grad * y)
    s.stat[2:3, :] = column_sum(grad)
    s.dkv[...] = jnp.zeros((z.rows + TILE, z.pad), F32)
    ob_spread.forward()
    lane_wide = grid_of((z.block, LANES), 1)

    def out_back(step, _):
        for wanted in range(1, z.T):

            @pl.when(step == wanted)
            def _(wanted=wanted):
                ob_spread.wait(wanted)

        rows = pl.ds(pl.multiple_of(partner(me, step) * z.block, z.block), z.block)
        dout = nt(s.wo_all[partner(me, step)], used["wo"][...])
        pair, single = dout[:, :LANES], dout[:, LANES:]
        for h, value in enumerate((pltpu.roll(pair, TILE, 1), pair, pltpu.roll(single, TILE, 1))):
            s.pair_all[h, rows, :] = jnp.where(lane_wide < TILE, 0.0, value).astype(BF)
        return 0

    lax.fori_loop(0, z.T, out_back, 0)
    done("wo")
    collects[0].finish()
    if layer == 1:
        e.arriving.start()
    ready("p", "q", "kvt", "ckv")

    ones_row = jnp.ones((16, TILE), BF)

    def attend_back(i, _):
        tiles = [i * group + g for g in range(group)]
        units = [(g, h) for g in range(group) for h in range(z.heads)]
        keys, query, dout, prob, dprob = {}, {}, {}, {}, {}
        for g, t in enumerate(tiles):
            base = pl.multiple_of(t * TILE, TILE)
            for h in range(z.heads):
                cols = slice(h * LANES, (h + 1) * LANES)
                far = k.ckv[rt[ARR, h * z.tiles + t]]
                near = k.kvt[pl.ds(h * (z.tiles + 1) + t, 2)].reshape(2 * TILE, LANES)
                keys[g, h] = jnp.concatenate([near, far, far], axis=0)
                query[g, h] = k.q[pl.ds(base, TILE), cols]
                dout[g, h] = s.pair_all[h, pl.ds(base, TILE), :]
                prob[g, h] = k.p[t * z.heads + h]
                dprob[g, h] = nt(dout[g, h], keys[g, h])
        totals = {u: jnp.sum(prob[u].astype(F32) * dprob[u], axis=-1, keepdims=True) for u in units}
        dz = {u: (prob[u].astype(F32) * (dprob[u] - totals[u])).astype(BF) for u in units}
        for g, t in enumerate(tiles):
            base = pl.multiple_of(t * TILE, TILE)
            for h in range(z.heads):
                cols = slice(h * LANES, (h + 1) * LANES)
                u = h * z.tiles + t
                s.dqkv[pl.ds(base, TILE), cols] = nn(dz[g, h], keys[g, h]).astype(BF)
                dkeys = tn(
                    jnp.concatenate([dz[g, h], prob[g, h]], axis=0),
                    jnp.concatenate([query[g, h], dout[g, h]], axis=0),
                )
                s.dkv[pl.ds(base, 2 * TILE), cols] += dkeys[: 2 * TILE]
                s.far[u] = dkeys[2 * TILE : 3 * TILE].astype(BF)
                gates = nn(ones_row, dz[g, h])[0:1]
                s.dgate[t, h : h + 1, :] = gates[:, :LANES]
                s.far_gate[u, 0:1, :] = gates[:, LANES:]
        return 0

    group = 4
    lax.fori_loop(0, z.tiles // group, attend_back, 0)
    done("p", "q", "kvt", "ckv")
    s.dgate[z.tiles] = jnp.zeros((8, LANES), F32)

    def edge_copies():
        behind = {"seq": jnp.maximum(at - 1, 0)}
        return (
            remote(s.edge_send, s.edge_got, s.back_edge_ss.at[0], s.back_edge_rs.at[0], behind),
            remote(s.dgate.at[0], s.edge_gate_got, s.back_edge_ss.at[1], s.back_edge_rs.at[1], behind),
        )

    @pl.when(at > 0)
    def _():
        s.edge_send[...] = s.dkv[0:TILE, :].astype(BF)
        for copy in edge_copies():
            copy.start()

    def tile_copies(d, source):
        return (
            remote(
                s.send_kv.at[d],
                s.got_kv.at[pl.ds(source * z.cap, z.cap)],
                s.back_kv_ss.at[d],
                s.back_kv_rs.at[source],
                {"seq": d},
            ),
            remote(
                s.back_send_gate.at[d], s.back_got_gate.at[source], s.back_gate_ss.at[d], s.back_gate_rs.at[source], {"seq": d}
            ),
        )

    def pack(d, _):
        def slot(i, _):
            u = rt[INV, d * z.cap + i]
            s.send_kv[d, i] = s.far[u]
            s.back_send_gate[d, pl.ds(i, 1), :] = s.far_gate[u][0:1]
            return 0

        lax.fori_loop(0, z.cap, slot, 0)
        for copy in tile_copies(d, at):
            copy.start()
        return 0

    lax.fori_loop(0, at, pack, 0)
    if layer == 1:
        e.arriving.forward()
    ready("o")
    out_grad = tn(s.wo_all[...].reshape(z.rows, W), k.o[...]).astype(BF)
    done("o")
    s.pb[0] = out_grad[:, :LANES]
    s.pb[1] = out_grad[:, LANES:]
    give(1).start()
    s.sum[z.n] = jnp.zeros((TILE, LANES), F32)
    s.gate_sum[z.n] = jnp.zeros((8, LANES), F32)
    ready("st", "w1", "swt", "n1")

    @pl.when(at < last)
    def _():
        for copy in edge_copies():
            copy.wait_recv()
        s.dkv[pl.ds(z.rows, TILE), :] += s.edge_got[...].astype(F32)
        s.dgate[z.tiles] = s.edge_gate_got[...]

    def landed(source, _):
        for copy in tile_copies(0, source):
            copy.wait_recv()
        for i in range(z.cap):
            s.got_gate_row[source * z.cap + i, 0:1, :] = s.back_got_gate[source, i : i + 1, :]
        return 0

    lax.fori_loop(at + 1, z.S, landed, 0)

    def gather(i, carry):
        running, gates = carry
        index = rt[ORD, i]
        joined = rt[CONT, i].astype(F32)
        running = running * joined + s.got_kv[index].astype(F32)
        gates = gates * joined + s.got_gate_row[index]
        s.sum[i] = running
        s.gate_sum[i] = gates
        return running, gates

    lax.fori_loop(0, z.n, gather, (jnp.zeros((TILE, LANES), F32), jnp.zeros((8, LANES), F32)))

    def settle(t, _):
        base = pl.multiple_of((t + 1) * TILE, TILE)
        rows = pl.ds(pl.multiple_of(t * TILE, TILE), TILE)
        for h in range(z.heads):
            cols = slice(h * LANES, (h + 1) * LANES)
            index = rt[LAST, h * z.tiles + t]
            s.dqkv[rows, z.pad + h * LANES : z.pad + (h + 1) * LANES] = (
                s.dkv[pl.ds(base, TILE), cols] + s.sum[index]
            ).astype(BF)
            s.tile_gate[t, h : h + 1, :] = s.gate_sum[index][0:1]
        return 0

    lax.fori_loop(0, z.tiles, settle, 0)
    if layer == 1:
        for step in range(1, z.T):
            e.arriving.wait(step)
        e.arriving.finish()
        e.deliver(1, e.rows, e.layer_out)
    lane = grid_of((8, LANES), 1)
    head_row = grid_of((8, LANES), 0)
    for i in range(z.tiles // 2):
        halves = []
        for t in (2 * i, 2 * i + 1):
            halves.append(pltpu.roll(s.dgate[t], TILE, 1) + s.dgate[t + 1] + s.tile_gate[t])
        joint = jnp.where(lane < TILE, halves[0], pltpu.roll(halves[1], TILE, 1))
        score = k.st[:, i * LANES : (i + 1) * LANES]
        grads = jnp.where(head_row < z.heads, joint / (1.0 + jnp.exp(score)), 0.0)
        s.ds[0:8, i * LANES : (i + 1) * LANES] = grads
        s.ds[8:16, i * LANES : (i + 1) * LANES] = jnp.zeros((8, LANES), F32)

    def in_back(i, _):
        step = visiting(i)
        rows = pl.ds(pl.multiple_of(partner(me, step) * z.block, z.block), z.block)
        s.own_part[...] = nt(s.dqkv[rows, :], used["w1"][...]) + tn(
            s.ds[:, rows].astype(BF), used["swt"][...]
        )

        collects[1].put(step, lambda: s.own_part[...])
        return 0

    lax.fori_loop(0, z.T, in_back, 0)
    done("st", "w1", "swt")
    collects[1].join()
    s.pc[0] = tn(k.n1[...], s.dqkv[:, z.pad :]).astype(BF)
    queries = tn(k.n1[...], s.dqkv[:, : z.pad])
    lane_full = grid_of((W, LANES), 1)
    s.pc[1, :, :LANES] = jnp.where(
        lane_full < TILE, queries[:, :LANES], pltpu.roll(queries[:, LANES : 2 * LANES], TILE, 1)
    ).astype(BF)
    s.pc[1, :, LANES : 2 * LANES] = queries[:, 2 * LANES :].astype(BF)
    s.pc[1, :, 2 * LANES :] = jnp.zeros((W, z.pad - 2 * LANES), BF)
    give(2).start()
    s.stat[10:13, :] = nn(s.ds[...].astype(BF), k.n1[...])[0:3]
    done("n1")
    source, target = grid_of((W, 1), 0), grid_of((1, W), 1)
    is_value = source >= z.pad
    index = jnp.where(is_value, source - z.pad, source)
    index = index // LANES * TILE + index % TILE
    each = z.heads * TILE // z.S
    wanted = index // each * z.share + index % each + jnp.where(is_value, each, 0)
    filled = (source % LANES >= TILE) == is_value
    wanted = jnp.where(filled, wanted, -1)
    spread_out = jnp.where(wanted == target, jnp.where(is_value, 1.0, TILE**-0.5), 0.0).astype(BF)
    s.stat[13:14, :] = nn(nn(ones, s.dqkv[...]).astype(BF), spread_out)[0:1]
    reduce(0)
    add_up(1)
    add_up(2)
    grad = collects[1].total(s.own_part[...])
    if layer == 1:
        entry = e.middle[own_rows, :]
    else:
        e.entry_load.wait()
        entry = s.entry[...]
    y, spread = normed(entry.astype(F32))
    dr = s.dr2[...] + norm_back(grad, vec[0:1, :], y, spread)
    grad_ref[own_rows, :] = dr.astype(BF)
    grad_spread = rows_spread(grad_ref, s.grad_ss, s.grad_rs)
    s.stat[3:4, :] = column_sum(grad * y)
    s.stat[4:5, :] = column_sum(grad)

    def stat_copy(step):
        return remote(
            s.stat.at[pl.ds(0, 8), :],
            s.stat_got.at[step - 1],
            s.stat_ss.at[step],
            s.stat_rs.at[step],
            to_tensor(step, me),
        )

    for step in range(1, z.T):
        stat_copy(step).start()
    grad_spread.start()
    shared = s.stat[0:8, :]
    for step in range(1, z.T):
        stat_copy(step).wait()
        shared += s.stat_got[step - 1]
    stats = jnp.concatenate([shared, s.stat[8:16, :]], axis=0).astype(BF)
    unit = (grid_of((16, LANES), 0) == grid_of((16, LANES), 1)).astype(F32).astype(BF)
    s.pd[0] = tn(stats, unit).astype(BF)

    @pl.when(core != layer)
    def _():
        give(3).start()

    grad_spread.forward()

    @pl.when(core == layer)
    def _():
        add_up(3)

    reduce(1)
    take(0)
    take(1)

    for step in range(z.T):
        grad_spread.wait(step)
        if layer == 0:
            e.deliver_block(grad_ref, step)

    if layer == 1:
        e.deliver(1, grad_ref, e.input_grad)
    reduce(2)
    take(2)

    @pl.when(core == layer)
    def _():
        reduce(3)

    def last_sent(i, _):
        cross(3, (at + i) % z.S, at).wait_send()
        return 0

    @pl.when(core == layer)
    def _():
        lax.fori_loop(1, z.S, last_sent, 0)

    @pl.when(core != layer)
    def _():
        give(3).wait_send()

    for piece in range(3):
        give(piece).wait_send()

        @pl.when(core != layer)
        def _(piece=piece):
            hand(piece).wait_send()

        def crossed_over(i, _, piece=piece):
            cross(piece, (at + i) % z.S, at).wait_send()
            return 0

        lax.fori_loop(1, z.S, crossed_over, 0)
    collects[1].finish()
    ob_spread.finish()
    grad_spread.finish()

    def sent(d, _):
        for copy in tile_copies(d, at):
            copy.wait_send()
        return 0

    lax.fori_loop(0, at, sent, 0)

    @pl.when(at > 0)
    def _():
        for copy in edge_copies():
            copy.wait_send()


class Unsaved:
    def save(self, src, dst):
        pass

    def finish(self):
        pass


class Env:
    pass


def layers_kernel(z, names, *refs):
    count = len(WEIGHTS)
    e = Env()
    e.routes, refs = refs[:2], refs[2:]
    tokens, cotangent, refs = refs[0], refs[1], refs[2:]
    own, refs = dict(zip(WEIGHTS, refs[:count])), refs[count:]
    e.layer_out, e.input_grad, e.g_out, refs = refs[0], refs[1], refs[2], refs[3:]
    theirs, refs = dict(zip(WEIGHTS, refs[:count])), refs[count:]
    e.store, refs = dict(zip(KEPT, refs[: len(KEPT)])), refs[len(KEPT) :]
    e.used, refs = dict(zip(WEIGHTS, refs[:count])), refs[count:]
    held, refs = dict(zip(KEPT, refs[: len(KEPT)])), refs[len(KEPT) :]
    s = e.s = Refs(names, refs)
    e.rows, e.middle, e.cotan, e.grad = s.rows, s.middle, s.cotan, s.grad
    me, at, core = e.me, e.at, e.core = lax.axis_index("tensor"), lax.axis_index("seq"), lax.axis_index("section")
    across = {"section": 1 - core}
    own_rows = pl.ds(pl.multiple_of(me * z.block, z.block), z.block)
    e.input_load = pltpu.make_async_copy(tokens.at[core], s.rows, s.load.at[0])
    e.cotan_load = pltpu.make_async_copy(cotangent.at[core], s.cotan, s.load.at[1])
    e.entry_load = pltpu.make_async_copy(tokens.at[core].at[own_rows, :], s.entry, s.load.at[2])
    e.input_load.start()

    def vec(layer):
        return e.used["vec"].at[layer]

    def chosen_keys(layer):
        return s.ckv_next if layer == 1 else held["ckv"]

    def held_in(layer):
        return Refs(KEPT, [chosen_keys(layer) if name == "ckv" else held[name] for name in KEPT])

    e.vec, e.held = vec, held_in

    def load(layer, i, source):
        name = WEIGHTS[i]
        target = e.used[name].at[layer] if name == "vec" else e.used[name]
        return pltpu.make_async_copy(source[name], target, s.weight_load.at[i])

    e.load = load

    def swap(i):
        name = WEIGHTS[i]
        return remote(own[name], theirs[name], s.swap_ss.at[i], s.swap_rs.at[i], across)

    def start_weight(layer, i):
        @pl.when(core == layer)
        def _():
            load(layer, i, own).start()

        @pl.when(core != layer)
        def _():
            load(layer, i, theirs).start()

    loaded = {0: set(), 1: set()}
    pending = {}

    def weight_ready(layer, i):
        if layer == 0 and i not in loaded[0]:

            @pl.when(core != layer)
            def _():
                swap(i).wait_recv()
                load(layer, i, theirs).start()

            loaded[0].add(i)
            load(layer, i, own).wait()
        elif pending.pop((layer, i), False):
            load(layer, i, own).wait()

    def next_weights():
        @pl.when(core == 0)
        def _():
            for i in range(count):
                swap(i).wait_recv()

        for i in range(count):
            start_weight(1, i)
            pending[1, i] = True

    def weight_again(i):
        if WEIGHTS[i] != "vec":
            start_weight(0, i)
            pending[0, i] = True

    e.weight_ready, e.next_weights, e.weight_again = weight_ready, next_weights, weight_again
    kept_pending = {}

    def kept_load(name):
        return pltpu.make_async_copy(e.store[name], held[name], s.kept_load.at[KEPT.index(name)])

    def kept_again(name):
        if name != "ckv":
            kept_load(name).start()
            kept_pending[name] = True

    def kept_ready(layer, name):
        if kept_pending.pop(name, False):
            kept_load(name).wait()

    e.kept_again, e.kept_ready = kept_again, kept_ready

    def collect(phase):
        return Collect(
            z,
            me,
            s.part_send,
            s.part_got.at[phase % 2],
            s.part_via.at[phase % 2],
            lambda i: s.part_ss.at[phase, i],
            lambda i: s.part_rs.at[phase, i],
        )

    e.collect = collect
    delivered = []

    def rows_to(ref, target, slot, part):
        local = pltpu.make_async_copy(ref.at[part, :], target.at[core].at[part, :], s.keep.at[slot])
        return local, remote(
            ref.at[part, :], target.at[core].at[part, :], s.move_ss.at[slot], s.move_rs.at[slot], across
        )

    everything = pl.ds(0, z.rows)

    def deliver(layer, ref, target):
        slot = len(delivered)
        local, away = rows_to(ref, target, slot, everything)

        @pl.when(core == layer)
        def _():
            local.start()

        @pl.when(core != layer)
        def _():
            away.start()

        delivered.append((layer, local, away))

    def deliver_block(ref, step):
        slot = len(delivered)
        part = pl.ds(pl.multiple_of(partner(me, step) * z.block, z.block), z.block)
        local, away = rows_to(ref, target=e.input_grad, slot=slot, part=part)

        @pl.when(core == 0)
        def _():
            local.start()

        @pl.when(core == 1)
        def _():
            away.start()

        delivered.append((0, local, away))

    e.deliver, e.deliver_block = deliver, deliver_block

    def turn(layer, where):
        if (layer, where) == TURN_FROM:

            @pl.when(core == 0)
            def _():
                pl.semaphore_signal(s.turn, inc=1, device_id=across, device_id_type=MESH)

        if (layer, where) == TURN_TO:

            @pl.when(core == 1)
            def _():
                pl.semaphore_wait(s.turn, 1)

    e.turn = turn

    @pl.when(core == 0)
    def _():
        for i in range(count):
            load(0, i, own).start()

    barrier = pltpu.get_barrier_semaphore()
    for step in range(1, z.T):
        signal(to_tensor(step, me), barrier)
    signal(across, barrier)

    def greet(i, _):
        signal({"seq": (at + i) % z.S}, barrier)
        return 0

    lax.fori_loop(1, z.S, greet, 0)
    pl.semaphore_wait(barrier, z.T - 1 + 1 + z.S - 1)
    for i in range(count):
        swap(i).start()
    e.cotan_load.start()
    e.entry_load.start()
    forward_part(z, 0, e)
    forward_part(z, 1, e)
    backward_part(z, 1, e)
    backward_part(z, 0, e)
    for i in range(count):
        swap(i).wait_send()
    for layer, local, away in delivered:

        @pl.when(core == layer)
        def _(local=local, away=away):
            local.wait()
            away.wait_recv()

        @pl.when(core != layer)
        def _(away=away):
            away.wait_send()


TURN_FROM, TURN_TO = (0, "attend"), (0, "pack")


def layers(z, routes, tokens, cotangent, own):
    rows, width, heads = z.rows, z.width, z.heads
    half = z.block // 2
    kept = dict(
        n1=((rows, width), BF),
        q=((rows, z.pad), BF),
        kvt=((heads * (z.tiles + 1), TILE, LANES), BF),
        st=((8, rows), F32),
        p=((z.slots, TILE, 2 * LANES), BF),
        ckv=((z.n, TILE, LANES), BF),
        o=((rows, 2 * LANES), BF),
        mid=((z.block, width), F32),
        n2=((rows, width), BF),
        u=((rows, z.hidden), BF),
        act=((rows, z.hidden), BF),
    )
    weights = [own[name] for name in WEIGHTS]
    vmem_of, dma = pltpu.VMEM, pltpu.SemaphoreType.DMA
    scratch = dict(
        rows=vmem_of((rows, width), BF),
        middle=vmem_of((rows, width), BF),
        cotan=vmem_of((rows, width), BF),
        grad=vmem_of((rows, width), BF),
        entry=vmem_of((z.block, width), BF),
        ckv_next=vmem_of((z.n, TILE, LANES), BF),
        gt=vmem_of((8, rows + 2 * LANES), F32),
        gate=vmem_of((heads * (z.tiles + 1), 8, LANES), F32),
        edge=vmem_of((2, heads, TILE, LANES), BF),
        edge_gate=vmem_of((2, 8, LANES), F32),
        send_kv=vmem_of((z.S, z.cap, TILE, LANES), BF),
        send_gate=vmem_of((z.S, z.capg, LANES), F32),
        got_gate=vmem_of((2, z.S, z.capg, LANES), F32),
        far_gate=vmem_of((max(z.n, z.slots), 8, LANES), F32),
        wo_all=vmem_of((z.T, max(2 * LANES, z.block), width), BF),
        wo_high=vmem_of((z.T, LANES, width), BF),
        pair_all=vmem_of((z.T, rows, LANES), BF),
        single_all=vmem_of((z.T, rows // 2, LANES), BF),
        part_send=vmem_of((z.T - 1, z.block, width), BF),
        part_got=vmem_of((2, 2, z.block, width), BF),
        part_via=vmem_of((2, 2, half, width), BF),
        own_part=vmem_of((z.block, width), F32),
        du=vmem_of((rows, z.hidden), BF),
        dr2=vmem_of((z.block, width), F32),
        dqkv=vmem_of((rows, 2 * z.pad), BF),
        dkv=vmem_of((rows + TILE, z.pad), F32),
        dgate=vmem_of((z.tiles + 1, 8, LANES), F32),
        far=vmem_of((z.slots, TILE, LANES), BF),
        back_send_gate=vmem_of((z.S, z.capg, LANES), F32),
        got_kv=vmem_of((z.n, TILE, LANES), BF),
        back_got_gate=vmem_of((z.S, z.capg, LANES), F32),
        got_gate_row=vmem_of((z.n, 8, LANES), F32),
        edge_send=vmem_of((TILE, z.pad), BF),
        edge_got=vmem_of((TILE, z.pad), BF),
        edge_gate_got=vmem_of((8, LANES), F32),
        sum=vmem_of((z.n + 1, TILE, LANES), F32),
        gate_sum=vmem_of((z.n + 1, 8, LANES), F32),
        tile_gate=vmem_of((z.tiles, 8, LANES), F32),
        ds=vmem_of((16, rows), F32),
        stat=vmem_of((24, width), F32),
        stat_got=vmem_of((z.T - 1, 8, width), F32),
    )
    for name, w in zip("abcd", z.pieces):
        scratch["p" + name] = vmem_of((1 if name == "d" else 2, width, w), BF)
        scratch["x" + name] = vmem_of((width, w), BF)
        scratch["s" + name] = vmem_of((z.S, z.padded, w), BF)
        scratch["t" + name] = vmem_of((z.S, z.padded, w), BF)
        if name != "d":
            scratch["h" + name] = vmem_of((z.padded, w), BF)
    pairs = dict(
        kv=(2, z.S), gate=(2, z.S), edge=(2, heads + 1), wo=(z.T,), o=(z.T * 12,), part=(3, 6), res=(6,),
        swap=(len(WEIGHTS),), move=(3 + z.T,), back_kv=(z.S,), back_gate=(z.S,), back_edge=(2,), ob=(6,),
        grad=(6,), stat=(z.T,), give=(4,), cross=(4, z.S), hand=(3,),
    )
    for name, shape in pairs.items():
        scratch[name + "_ss"] = dma(shape)
        scratch[name + "_rs"] = dma(shape)
    scratch |= dict(
        load=dma((3,)),
        weight_load=dma((len(WEIGHTS),)),
        kept_load=dma((len(KEPT),)),
        saved=dma((len(KEPT),)),
        keep=dma((3 + z.T,)),
        turn=pltpu.SemaphoreType.REGULAR,
    )
    doubled = {"vec"}

    def room(name, shape, kind):
        return vmem_of((2, *shape) if name in doubled else shape, kind)

    shaped = (
        jax.ShapeDtypeStruct((2, rows, width), BF),
        jax.ShapeDtypeStruct((2, rows, width), BF),
        jax.ShapeDtypeStruct((2, z.share, sum(z.pieces)), F32),
        *(jax.ShapeDtypeStruct(value.shape, value.dtype) for value in weights),
        *(jax.ShapeDtypeStruct(*kept[name]) for name in KEPT),
    )
    outs = pl.pallas_call(
        functools.partial(layers_kernel, z, tuple(scratch)),
        out_shape=shaped,
        in_specs=[smem(), smem()] + [anywhere()] * (2 + len(weights)),
        out_specs=tuple(vmem() if i == 2 else anywhere() for i in range(len(shaped))),
        scratch_shapes=[
            *(room(name, value.shape, value.dtype) for name, value in zip(WEIGHTS, weights)),
            *(room(name, *kept[name]) for name in KEPT),
            *scratch.values(),
        ],
        compiler_params=pltpu.CompilerParams(
            collective_id=0, has_side_effects=True, vmem_limit_bytes=LIMIT
        ),
        name="layers",
    )(*routes, tokens, cotangent, *weights)
    return outs[:3]


UNPACKED = (
    "input_weight", "input_bias", "score", "out", "out_bias", "up", "up_bias", "down", "down_bias", "gain", "shift",
)


def unpack_kernel(z, head, total_ref, *refs):
    out = Refs(UNPACKED, refs)
    core = lax.axis_index("section")
    inner, hidden, share = z.heads * head, z.hidden, z.share
    c_o, c_i = hidden, hidden + LANES
    c_s = c_i + z.pad
    out.up[...] = total_ref[1, :, :hidden]
    out.down[...] = total_ref[0, :, :hidden].T
    first, second = total_ref[0, :, c_o:c_i].T, total_ref[1, :, c_o:c_i].T
    out.out[0:LANES, :] = first
    out.out[LANES:inner, :] = second[: inner - LANES]
    out.input_weight[0] = head**-0.5 * total_ref[1, :, c_i : c_i + inner]
    lane = grid_of((share, LANES), 1)
    pairs = [total_ref[0, :, c_i + h * LANES : c_i + (h + 1) * LANES] for h in range(z.heads)]
    turned = [pltpu.roll(pair, LANES // 2, 1) for pair in pairs]
    out.input_weight[1, :, 0:LANES] = jnp.where(lane < head, pairs[0], turned[1])
    out.input_weight[1, :, LANES:inner] = pairs[2][:, :head]
    out.input_weight[2, :, 0:LANES] = jnp.where(lane < head, turned[0], pairs[1])
    out.input_weight[2, :, LANES:inner] = turned[2][:, :head]
    stats = total_ref[core, :, c_s : c_s + LANES]
    rows = stats.T
    out.score[...] = pltpu.roll(stats, LANES - 10, 1)[:, : z.heads]
    each = inner // z.S
    out.input_bias[0:1, :] = rows[13:14, :each]
    out.input_bias[1:2, :] = pltpu.roll(rows[8:16], share - each, 1)[5:6, :each]
    out.out_bias[...] = rows[0:1]
    out.up_bias[...] = rows[8:9]
    out.down_bias[...] = rows[9:10]
    out.gain[0:1, :] = rows[3:4]
    out.gain[1:2, :] = rows[1:2]
    out.shift[0:1, :] = rows[4:5]
    out.shift[1:2, :] = rows[2:3]


def unpack(z, head, total):
    inner, hidden, share = z.heads * head, z.hidden, z.share
    shapes = (
        (3, share, inner), (2, inner // z.S), (share, z.heads), (inner, share), (1, share), (share, hidden), (1, share),
        (hidden, share), (1, share), (2, share), (2, share),
    )
    outs = pl.pallas_call(
        functools.partial(unpack_kernel, z, head),
        out_shape=tuple(jax.ShapeDtypeStruct(shape, F32) for shape in shapes),
        in_specs=[vmem()],
        out_specs=tuple(vmem() for _ in shapes),
        compiler_params=pltpu.CompilerParams(vmem_limit_bytes=LIMIT // 2),
        name="unpack",
    )(total)
    return dict(zip(UNPACKED, outs))


def swapped(value):
    return lax.ppermute(value, "section", [(0, 1), (1, 0)])


def body(
    tokens,
    cotangent,
    lengths,
    selected,
    input_weight,
    input_bias,
    score_weight,
    output_weight,
    output_bias,
    up_weight,
    up_bias,
    down_weight,
    down_bias,
    norm_gain,
    norm_bias,
):
    core = lax.axis_index("section")
    _, rows, width = tokens.shape
    heads, hidden = score_weight.shape[2], up_weight.shape[2]
    head = input_weight.shape[3] // heads
    inner = heads * head
    z = Sizes(lax.axis_size("tensor"), lax.axis_size("seq"), rows, width, heads, hidden)
    scale = head**-0.5
    grouped = (
        selected[0].reshape(2, heads, z.S, z.tiles).transpose(0, 2, 1, 3).reshape(2, z.S, z.slots)
    )
    kept_choice = lax.dynamic_index_in_dim(grouped, core, 0, keepdims=False)
    got_choice = swapped(lax.dynamic_index_in_dim(grouped, 1 - core, 0, keepdims=False))
    own, routes = prepare(
        z,
        lengths,
        kept_choice,
        got_choice,
        input_weight[0].transpose(1, 0, 2),
        input_bias[0],
        score_weight[0],
        output_weight[0],
        output_bias,
        up_bias,
        down_bias,
        norm_gain[0],
        norm_bias[0],
    )
    own |= dict(wup=up_weight[0], wdn=down_weight[0])
    layer_out, input_grad, total = layers(z, routes, tokens, cotangent, own)
    parts = unpack(z, head, total)
    parts["input_weight"] = parts["input_weight"].transpose(1, 0, 2)
    return (layer_out[None], input_grad[None], *(part.reshape(1, *shape) for part, shape in (
        (parts["input_weight"], (z.share, 3, inner)),
        (parts["input_bias"], (2, inner // z.S)),
        (parts["score"], (z.share, heads)),
        (parts["out"], (inner, z.share)),
        (parts["out_bias"], (z.share,)),
        (parts["up"], (z.share, hidden)),
        (parts["up_bias"], (z.share,)),
        (parts["down"], (hidden, z.share)),
        (parts["down_bias"], (z.share,)),
        (parts["gain"], (2, z.share)),
        (parts["shift"], (2, z.share)),
    )))


def solution(mesh):
    return jax.shard_map(
        body,
        mesh=mesh,
        in_specs=(
            P(None, "seq", None),
            P(None, "seq", None),
            P(),
            P("section", None, "tensor", None),
            P("section", None, None, "tensor"),
            P("section", None, "tensor"),
            P("section", None, "tensor"),
            P("section", "tensor", None),
            P("section", None),
            P("section", None, "tensor"),
            P("section", "tensor"),
            P("section", "tensor", None),
            P("section", None),
            P("section", None, None),
            P("section", None, None),
        ),
        out_specs=(
            P("section", None, "seq", None),
            P("section", None, "seq", None),
            P("section", "seq", None, "tensor"),
            P("section", None, ("tensor", "seq")),
            P("section", "seq", "tensor"),
            P("section", "tensor", "seq"),
            P("section", "seq"),
            P("section", "seq", "tensor"),
            P("section", ("tensor", "seq")),
            P("section", "tensor", "seq"),
            P("section", "seq"),
            P("section", None, "seq"),
            P("section", None, "seq"),
        ),
        check_vma=False,
    )
```

```python
import functools
import math

import jax
import jax.numpy as jnp
from jax import lax
from jax.experimental import pallas as pl
from jax.experimental.pallas import tpu as pltpu
from jax.sharding import PartitionSpec as P

TILE = 64
LANES = 128
MASKED = -1e30
EPSILON = 1e-05
FAR = -(1 << 20)
MESH = pl.DeviceIdType.MESH
BF = jnp.bfloat16
F32 = jnp.float32
GELU_A = 0.044715
GELU_K = math.sqrt(2.0 / math.pi)
LIMIT = 62 * 1024 * 1024


class Sizes:
    def __init__(self, mesh_tensor, mesh_seq, rows, width, heads, hidden):
        self.T, self.S = mesh_tensor, mesh_seq
        self.rows, self.width, self.heads, self.hidden = rows, width, heads, hidden
        self.tiles = rows // TILE
        self.slots = heads * self.tiles
        self.cap = -(-self.slots // (mesh_seq - 1))
        self.capg = -(-self.cap // 8) * 8
        self.n = mesh_seq * self.cap
        self.block = rows // mesh_tensor
        self.pad = heads * LANES
        self.share = width // mesh_seq
        self.padded = -(-self.share // 16) * 16
        self.pieces = (hidden, LANES, self.pad, LANES)


SEND, INV, ORD, CONT, ARR, POS, LAST, ENDS = range(8)
WEIGHTS = ("vec", "w1", "swt", "wo", "wup", "wdn")
KEPT = ("n1", "q", "kvt", "st", "p", "ckv", "o", "mid", "n2", "u", "act")


def nn(a, b):
    return jnp.dot(a, b, preferred_element_type=F32)


def nt(a, b):
    return lax.dot_general(a, b, (((1,), (1,)), ((), ())), preferred_element_type=F32)


def tn(a, b):
    return lax.dot_general(a, b, (((0,), (0,)), ((), ())), preferred_element_type=F32)


def normed(x):
    centred = x - jnp.mean(x, axis=-1, keepdims=True)
    spread = lax.rsqrt(jnp.mean(centred * centred, axis=-1, keepdims=True) + EPSILON)
    return centred * spread, spread


def norm_back(grad, gain, y, spread):
    scaled = grad * gain
    return spread * (
        scaled
        - jnp.mean(scaled, axis=-1, keepdims=True)
        - y * jnp.mean(scaled * y, axis=-1, keepdims=True)
    )


def partner(me, step):
    return (me // 2 + step // 2) % 2 * 2 + (me % 2 + step % 2) % 2


def column_sum(x):
    return jnp.sum(x, axis=0, keepdims=True)


def smem():
    return pl.BlockSpec(memory_space=pltpu.SMEM)


def vmem():
    return pl.BlockSpec(memory_space=pltpu.VMEM)


def anywhere():
    return pl.BlockSpec(memory_space=pl.ANY)


def grid_of(shape, axis):
    return lax.broadcasted_iota(jnp.int32, shape, axis)


def prepare_kernel(
    z,
    length_ref,
    kept_ref,
    got_ref,
    win_ref,
    bin_ref,
    sw_ref,
    wout_ref,
    bout_ref,
    bup_ref,
    bdn_ref,
    gain_ref,
    shift_ref,
    vec_ref,
    w1_ref,
    swt_ref,
    wo_ref,
    rt0_ref,
    rt1_ref,
):
    inner, head = win_ref.shape[2], win_ref.shape[2] // z.heads
    row, col = grid_of((inner, z.pad), 0), grid_of((inner, z.pad), 1)
    lane_of = row // head * LANES + row % head
    first = (col == lane_of).astype(F32)
    second = (col == lane_of + head).astype(F32)
    low, high = first.astype(BF), second.astype(BF)
    scaled = (first * head**-0.5).astype(BF)
    w1_ref[:, : z.pad] = nn(win_ref[0], scaled).astype(BF)
    w1_ref[:, z.pad :] = (nn(win_ref[1], low) + nn(win_ref[2], high)).astype(BF)
    vec_ref[0:1, :] = gain_ref[...].astype(F32)[0:1]
    vec_ref[1:2, :] = shift_ref[...].astype(F32)[0:1]
    vec_ref[2:3, : z.pad] = nn(bin_ref[...], scaled)[0:1]
    vec_ref[2:3, z.pad :] = nn(bin_ref[...], high)[1:2]
    vec_ref[3:4, :] = bout_ref[...].astype(F32)
    vec_ref[4:5, :] = gain_ref[...].astype(F32)[1:2]
    vec_ref[5:6, :] = shift_ref[...].astype(F32)[1:2]
    vec_ref[6:7, :] = bup_ref[...].astype(F32)
    vec_ref[7:8, :] = bdn_ref[...].astype(F32)
    unit = (grid_of((16, z.heads), 0) == grid_of((16, z.heads), 1)).astype(F32).astype(BF)
    swt_ref[...] = nt(unit, sw_ref[...]).astype(BF)
    wo_ref[0:inner, :] = wout_ref[...]
    wo_ref[inner:, :] = jnp.zeros((2 * LANES - inner, z.width), BF)

    at, core = lax.axis_index("seq"), lax.axis_index("section")
    n, slots, cap = z.n, z.slots, z.cap
    first_end = length_ref[core, 0]
    second_end = first_end + length_ref[core, 1]
    shift = z.tiles.bit_length() - 1
    near = 1e-3

    def total(mask, value, axis):
        return jnp.sum(jnp.where(mask, value, 0.0), axis=axis, keepdims=True)

    def whole(x):
        return (x + near).astype(jnp.int32)

    for layer, rt in enumerate((rt0_ref, rt1_ref)):
        rt[...] = jnp.zeros((8, LANES), jnp.int32)
        chosen = jnp.where(core == layer, kept_ref[...], got_ref[...])
        owner = lax.shift_right_arithmetic(chosen, shift)
        sub, lan = grid_of((slots, n), 0), grid_of((slots, n), 1)
        wide = jnp.zeros((slots, n), jnp.int32)
        for d in range(z.S):
            column = jnp.sum(
                jnp.where(
                    grid_of((slots, slots), 0) == grid_of((slots, slots), 1),
                    chosen[d : d + 1].astype(F32) + 1.0,
                    0.0,
                ),
                axis=1,
                keepdims=True,
            )
            wide = jnp.where(lan // cap == d, whole(column) - 1, wide)
        mine = lax.shift_right_arithmetic(wide, shift) == at
        order = nn(
            (grid_of((slots, slots), 0) > grid_of((slots, slots), 1)).astype(F32), mine.astype(F32)
        )
        taken = mine & (whole(order) == lan % cap)
        head_of = sub // z.tiles
        inner_tile = wide - at * z.tiles
        rt[SEND : SEND + 1, :n] = whole(
            total(taken, (head_of * (z.tiles + 1) + inner_tile).astype(F32), 0)
        ) + 1
        present = jnp.sum(taken.astype(F32), axis=0, keepdims=True)
        key = total(taken, (head_of * z.tiles + inner_tile - slots).astype(F32), 0) + slots
        own = jnp.sum(
            jnp.where(grid_of((z.S, slots), 0) == at, chosen.astype(F32) + 1.0, 0.0), axis=0, keepdims=True
        )
        square_row, square_col = grid_of((slots, slots), 0), grid_of((slots, slots), 1)
        own_column = total(square_row == square_col, own, 1)
        own_row = whole(own) - 1
        own_col = whole(own_column) - 1
        owner_row = lax.shift_right_arithmetic(own_row, shift)
        owner_col = lax.shift_right_arithmetic(own_col, shift)
        same = owner_row == owner_col
        place_row = whole(jnp.sum((same & (square_row < square_col)).astype(F32), axis=0, keepdims=True))
        place_col = whole(jnp.sum((same & (square_col < square_row)).astype(F32), axis=1, keepdims=True))
        live = own_row >= 0
        rt[ARR : ARR + 1, :slots] = jnp.where(live, owner_row * cap + place_row, at * cap)
        rt[POS : POS + 1, :slots] = jnp.where(live, own_row * TILE, FAR)
        matched = (owner_col == lan // cap) & (place_col == lan % cap)
        rt[INV : INV + 1, :n] = whole(total(matched, sub.astype(F32), 0))
        big_row, big_col = grid_of((n, n), 0), grid_of((n, n), 1)
        key_col = total(big_row == big_col, key, 1)
        rank = jnp.sum(
            ((key < key_col) | ((key == key_col) & (big_col < big_row))).astype(F32), axis=1, keepdims=True
        )
        at_rank = whole(rank) == big_col
        rt[ORD : ORD + 1, :n] = whole(total(at_rank, big_row.astype(F32), 0))
        sorted_key = total(at_rank, key_col, 0)
        before = total(whole(rank) + 1 == big_col, key_col + 1.0, 0) - 1.0
        rt[CONT : CONT + 1, :n] = (sorted_key == before).astype(jnp.int32)
        tile = grid_of((n, slots), 1).astype(F32)
        upto = jnp.sum((key_col <= tile).astype(F32), axis=0, keepdims=True)
        has = jnp.sum((key_col == tile).astype(F32), axis=0, keepdims=True)
        rt[LAST : LAST + 1, :slots] = whole(jnp.where(has > 0.5, upto - 1.0, n * 1.0))
        rt[ENDS : ENDS + 1, :] = jnp.where(grid_of((1, LANES), 1) == 0, first_end, second_end)


def prepare(z, lengths, kept, got, win, bin_, sw, wout, bout, bup, bdn, gain, shift):
    table = jax.ShapeDtypeStruct((8, LANES), jnp.int32)
    outs = pl.pallas_call(
        functools.partial(prepare_kernel, z),
        out_shape=(
            jax.ShapeDtypeStruct((8, z.width), F32),
            jax.ShapeDtypeStruct((z.width, 2 * z.pad), BF),
            jax.ShapeDtypeStruct((16, z.width), BF),
            jax.ShapeDtypeStruct((2 * LANES, z.width), BF),
            table,
            table,
        ),
        in_specs=[smem()] + [vmem()] * 11,
        out_specs=tuple(vmem() for _ in range(6)),
        name="prepare",
    )(lengths, kept, got, win, bin_, sw, wout, bout, bup, bdn, gain, shift)
    return dict(zip(WEIGHTS[:4], outs)), outs[4:]


def to_tensor(step, me):
    return {"tensor": partner(me, step)}


def remote(src, dst, send, recv, target):
    return pltpu.make_async_remote_copy(
        src_ref=src, dst_ref=dst, send_sem=send, recv_sem=recv, device_id=target, device_id_type=MESH
    )


def signal(target, barrier):
    pl.semaphore_signal(barrier, inc=1, device_id=target, device_id_type=MESH)


class Spread:
    def __init__(self, me, view, sends, recvs):
        self.me, self.view, self.sends, self.recvs = me, view, sends, recvs

    def copy(self, i):
        me, x, y = self.me, partner(self.me, 1), partner(self.me, 2)
        owner, half, step = ((me, 0, 1), (me, 1, 2), (me, 1, 1), (me, 0, 2), (x, 0, 2), (y, 1, 1))[i]
        ref = self.view(owner, half)
        return remote(ref, ref, self.sends(i), self.recvs(i), to_tensor(step, me))

    def start(self):
        for i in range(4):
            self.copy(i).start()

    def forward(self):
        for i in range(2):
            self.copy(i).wait_recv()
            self.copy(4 + i).start()

    def wait(self, step):
        for i in ((), (2,), (3,), (4, 5))[step]:
            self.copy(i).wait_recv()

    def finish(self):
        for i in range(6):
            self.copy(i).wait_send()


class Collect:
    def __init__(self, z, me, send, got, via, sends, recvs):
        self.me, self.send, self.got, self.via, self.sends, self.recvs = me, send, got, via, sends, recvs
        half = z.block // 2
        self.halves = (pl.ds(0, half), pl.ds(half, half))

    def copy(self, i):
        top, bottom = self.halves
        block, rows, target, step = (
            (2, top, self.via.at[0], 1),
            (2, bottom, self.via.at[1], 2),
            (0, top, self.got.at[0, top, :], 1),
            (1, bottom, self.got.at[1, bottom, :], 2),
            (0, bottom, self.got.at[0, bottom, :], 1),
            (1, top, self.got.at[1, top, :], 2),
        )[i]
        return remote(
            self.send.at[block, rows, :], target, self.sends(i), self.recvs(i), to_tensor(step, self.me)
        )

    def put(self, step, value):
        for wanted, copies in ((3, (0, 1)), (1, (2,)), (2, (3,))):

            @pl.when(step == wanted)
            def _(wanted=wanted, copies=copies):
                self.send[wanted - 1] = value().astype(BF)
                for i in copies:
                    self.copy(i).start()

    def join(self):
        top, bottom = self.halves
        for i, block, rows in ((1, 0, bottom), (0, 1, top)):
            self.copy(i).wait_recv()
            joined = self.send[block, rows, :].astype(F32) + self.via[i].astype(F32)
            self.send[block, rows, :] = joined.astype(BF)
            self.copy(5 - i).start()

    def total(self, own):
        for i in range(2, 6):
            self.copy(i).wait_recv()
        return own + self.got[0].astype(F32) + self.got[1].astype(F32)

    def finish(self):
        for i in range(6):
            self.copy(i).wait_send()


def visiting(k):
    return jnp.where(k == 0, 3, jnp.where(k == 3, 0, k))


class Saver:
    def __init__(self, sems):
        self.sems, self.copies = sems, []

    def save(self, src, dst):
        copy = pltpu.make_async_copy(src, dst, self.sems.at[len(self.copies)])
        copy.start()
        self.copies.append(copy)

    def finish(self):
        for copy in self.copies:
            copy.wait()


class Refs:
    def __init__(self, names, refs):
        assert len(names) == len(refs), (len(names), len(refs))
        for name, ref in zip(names, refs):
            setattr(self, name, ref)


def forward_part(z, layer, e):
    rt, r_ref, res_ref = e.routes[layer], (e.rows, e.middle)[layer], (e.middle, e.rows)[layer]
    used, s, me, at, core, load = e.used, e.s, e.me, e.at, e.core, e.load
    held = e.held(layer)
    last = z.S - 1
    first_row = at * z.rows
    vec = e.vec(layer)
    edge_ss, edge_rs = s.edge_ss.at[layer], s.edge_rs.at[layer]
    kv_ss, kv_rs, gate_ss, gate_rs = (
        sems.at[layer] for sems in (s.kv_ss, s.kv_rs, s.gate_ss, s.gate_rs)
    )
    edge, edge_gate, got_gate = s.edge.at[layer], s.edge_gate.at[layer], s.got_gate.at[layer]
    held.ckv[at * z.cap] = jnp.zeros((TILE, LANES), BF)
    outs = e.store

    def ready(*wanted):
        for i in wanted:
            e.weight_ready(layer, i)

    if layer == 0:
        e.input_load.wait()
    saver = Saver(s.saved) if layer == 0 else Unsaved()
    per_block = z.block // TILE
    ready(0)

    def norm_in(b):
        rows = pl.ds(pl.multiple_of(b * z.block, z.block), z.block)
        y, _ = normed(r_ref[rows, :].astype(F32))
        held.n1[rows, :] = (y * vec[0:1, :] + vec[1:2, :]).astype(BF)

    def project(b):
        rows = pl.ds(pl.multiple_of(b * z.block, z.block), z.block)
        qkv = (nn(held.n1[rows, :], used["w1"][...]) + vec[2:3, :]).astype(BF)
        held.q[rows, :] = qkv[:, : z.pad]
        for h in range(z.heads):
            pairs = qkv[:, z.pad + h * LANES : z.pad + (h + 1) * LANES]
            held.kvt[pl.ds(h * (z.tiles + 1) + 1 + b * per_block, per_block)] = pairs.reshape(
                per_block, TILE, LANES
            )

    def each_norm(b, _):
        norm_in(b)
        return 0

    def each_project(b, _):
        project(b)
        return 0

    def arrived_block(step, _):
        for wanted in range(1, z.T):

            @pl.when(step == wanted)
            def _(wanted=wanted):
                e.arriving.wait(wanted)

        norm_in(partner(me, step))
        project(partner(me, step))
        return 0

    if layer == 0:
        lax.fori_loop(0, z.T, each_norm, 0)
        saver.save(held.n1, outs["n1"])
        ready(1, 2)
        lax.fori_loop(0, z.T, each_project, 0)
    else:
        ready(1, 2)
        arrived_block(0, 0)
        e.arriving.forward()
        lax.fori_loop(1, z.T, arrived_block, 0)
        e.arriving.finish()
        e.deliver(0, r_ref, e.layer_out)
    score = nt(used["swt"][...], held.n1[...])[0:8]
    held.st[...] = score
    gate = jnp.minimum(score, 0.0) - jnp.log1p(jnp.exp(-jnp.abs(score)))
    s.gt[:, 0:LANES] = jnp.zeros((8, LANES), F32)
    s.gt[:, LANES : LANES + z.rows] = gate.astype(BF).astype(F32)
    s.gt[:, LANES + z.rows :] = jnp.zeros((8, LANES), F32)
    for t in range(z.tiles + 1):
        for h in range(z.heads):
            s.gate[h * (z.tiles + 1) + t, 0:1, :] = s.gt[
                h : h + 1, TILE + t * TILE : TILE + t * TILE + LANES
            ]

    def edge_copies():
        after = {"seq": jnp.minimum(at + 1, last)}
        return [
            remote(
                held.kvt.at[h * (z.tiles + 1) + z.tiles],
                edge.at[h],
                edge_ss.at[h],
                edge_rs.at[h],
                after,
            )
            for h in range(z.heads)
        ] + [
            remote(
                s.gt.at[:, pl.ds(z.rows, LANES)],
                edge_gate,
                edge_ss.at[z.heads],
                edge_rs.at[z.heads],
                after,
            )
        ]

    @pl.when(at < last)
    def _():
        for copy in edge_copies():
            copy.start()

    def tile_copies(d, source):
        return (
            remote(
                s.send_kv.at[d],
                held.ckv.at[pl.ds(source * z.cap, z.cap)],
                kv_ss.at[d],
                kv_rs.at[source],
                {"seq": d},
            ),
            remote(
                s.send_gate.at[d], got_gate.at[source], gate_ss.at[d], gate_rs.at[source], {"seq": d}
            ),
        )

    def pack(k, _):
        d = z.S - 1 - k

        def slot(i, _):
            u = rt[SEND, d * z.cap + i]
            s.send_kv[d, i] = held.kvt[u]
            s.send_gate[d, pl.ds(i, 1), :] = s.gate[u][0:1]
            return 0

        lax.fori_loop(0, z.cap, slot, 0)
        for copy in tile_copies(d, at):
            copy.start()
        return 0

    e.turn(layer, "pack")
    lax.fori_loop(0, last - at, pack, 0)
    ready(3)

    def wo_copy(step):
        return remote(
            used["wo"], s.wo_all.at[me], s.wo_ss.at[step], s.wo_rs.at[step], to_tensor(step, me)
        )

    for step in range(1, z.T):
        wo_copy(step).start()
    s.wo_all[me] = used["wo"][...]
    saver.save(held.q, outs["q"])
    saver.save(held.st, outs["st"])

    def landed(source, _):
        for copy in tile_copies(last, source):
            copy.wait_recv()
        for i in range(z.cap):
            s.far_gate[source * z.cap + i, 0:1, :] = got_gate[source, i : i + 1, :]
        return 0

    lax.fori_loop(0, at, landed, 0)
    lane = grid_of((TILE, LANES), 1)
    row = grid_of((TILE, LANES), 0)
    for h in range(z.heads):
        held.kvt[h * (z.tiles + 1)] = jnp.zeros((TILE, LANES), BF)

    @pl.when(at > 0)
    def _():
        for copy in edge_copies():
            copy.wait_recv()
        for h in range(z.heads):
            held.kvt[h * (z.tiles + 1)] = edge[h]
            s.gate[h * (z.tiles + 1), 0:1, :] = jnp.where(
                lane[0:1] < TILE,
                pltpu.roll(edge_gate[...], TILE, 1)[h : h + 1],
                s.gate[h * (z.tiles + 1), 0:1, :],
            )

    saver.save(held.kvt, outs["kvt"])
    saver.save(held.ckv, outs["ckv"])

    def attend(tiles):
        units = [(g, h) for g in range(len(tiles)) for h in range(z.heads)]
        keys, scores = {}, {}
        for g, t in enumerate(tiles):
            base = pl.multiple_of(t * TILE, TILE)
            query = first_row + base + row
            begin = jnp.where(
                query >= rt[ENDS, 1],
                rt[ENDS, 1],
                jnp.where(query >= rt[ENDS, 0], rt[ENDS, 0], 0),
            )
            key = first_row + base - TILE + lane
            near_ok = (key <= query) & (key > query - TILE) & (key >= begin)
            for h in range(z.heads):
                u = h * z.tiles + t
                arrived = rt[ARR, u]
                far = held.ckv[arrived]
                near = held.kvt[pl.ds(h * (z.tiles + 1) + t, 2)].reshape(2 * TILE, LANES)
                keys[g, h] = jnp.concatenate([near, far, far], axis=0)
                gates = jnp.concatenate(
                    [s.gate[h * (z.tiles + 1) + t, 0:1, :], s.far_gate[arrived][0:1]], axis=1
                )
                far_ok = (rt[POS, u] + lane >= begin) & (lane < TILE)
                query_tile = held.q[pl.ds(base, TILE), h * LANES : (h + 1) * LANES]
                scores[g, h] = jnp.where(
                    jnp.concatenate([near_ok, far_ok], axis=1), nt(query_tile, keys[g, h]) + gates, MASKED
                )
        tops = {u: jnp.max(scores[u], axis=-1, keepdims=True) for u in units}
        raised = {u: jnp.exp(scores[u] - tops[u]) for u in units}
        sums = {u: jnp.sum(raised[u], axis=-1, keepdims=True) for u in units}
        probs = {u: (raised[u] * (1.0 / sums[u])).astype(BF) for u in units}
        mixed = {u: nn(probs[u], keys[u]) for u in units}
        for g, t in enumerate(tiles):
            base = pl.multiple_of(t * TILE, TILE)
            for h in range(z.heads):
                held.p[t * z.heads + h] = probs[g, h]
            pair = jnp.where(lane < TILE, pltpu.roll(mixed[g, 0], TILE, 1), mixed[g, 1]).astype(BF)
            single = pltpu.roll(mixed[g, 2], TILE, 1)
            held.o[pl.ds(base, TILE), 0:LANES] = pair
            held.o[pl.ds(base, TILE), LANES:] = single.astype(BF)
            s.pair_all[me, pl.ds(base, TILE), :] = pair
            if g % 2 == 0:
                even = single
            else:
                couple = pl.ds(pl.multiple_of((t - 1) * (TILE // 2), TILE), TILE)
                s.single_all[me, couple, :] = jnp.where(lane < TILE, even, mixed[g, 2]).astype(BF)

    e.turn(layer, "attend")
    half_rows = z.block // 2

    def pair_spread(b):
        return Spread(
            me,
            lambda owner, half: s.pair_all.at[owner, pl.ds(b * z.block + half * half_rows, half_rows), :],
            lambda i: s.o_ss.at[b * 12 + i],
            lambda i: s.o_rs.at[b * 12 + i],
        )

    def single_spread(b):
        return Spread(
            me,
            lambda owner, half: s.single_all.at[
                owner, pl.ds(b * half_rows + half * (half_rows // 2), half_rows // 2), :
            ],
            lambda i: s.o_ss.at[b * 12 + 6 + i],
            lambda i: s.o_rs.at[b * 12 + 6 + i],
        )

    def attend_block(b, _):
        attend([b * per_block + g for g in range(per_block)])
        pair_spread(b).start()
        single_spread(b).start()

        @pl.when(b > 0)
        def _():
            pair_spread(b - 1).forward()
            single_spread(b - 1).forward()

        return 0

    lax.fori_loop(0, z.T, attend_block, 0)
    pair_spread(z.T - 1).forward()
    single_spread(z.T - 1).forward()
    saver.save(held.p, outs["p"])
    saver.save(held.o, outs["o"])
    ready(4, 5)
    for step in range(1, z.T):
        wo_copy(step).wait()
    for t in range(z.T):
        s.wo_high[t, 0:TILE, :] = jnp.zeros((TILE, z.width), BF)
        s.wo_high[t, TILE:, :] = s.wo_all[t, LANES : LANES + TILE, :]
    collect = e.collect(0)

    def feed(k, _):
        step = visiting(k)
        block = partner(me, step)
        rows = pl.ds(pl.multiple_of(block * z.block, z.block), z.block)
        few = pl.ds(pl.multiple_of(block * half_rows, half_rows), half_rows)
        for other in range(1, z.T):
            pair_spread(block).wait(other)
            single_spread(block).wait(other)
        def joined(value, weight):
            return sum(
                nn(
                    jnp.concatenate([value(t), value(t + 1)], axis=1),
                    jnp.concatenate([weight(t), weight(t + 1)], axis=0),
                )
                for t in range(0, z.T, 2)
            )

        mixed = joined(lambda t: s.pair_all[t, rows, :], lambda t: s.wo_all[t, 0:LANES, :])
        even = joined(lambda t: s.single_all[t, few, :], lambda t: s.wo_all[t, LANES : 2 * LANES, :])
        odd = joined(lambda t: s.single_all[t, few, :], lambda t: s.wo_high[t])
        turns = []
        for i in range(per_block // 2):
            turns += [even[i * TILE : (i + 1) * TILE], odd[i * TILE : (i + 1) * TILE]]
        mixed += jnp.concatenate(turns, axis=0)
        middle = r_ref[rows, :].astype(F32) + mixed + vec[3:4, :]
        held.mid[...] = middle
        y, _ = normed(middle)
        n2 = (y * vec[4:5, :] + vec[5:6, :]).astype(BF)
        held.n2[rows, :] = n2
        u = nn(n2, used["wup"][...]) + vec[6:7, :]
        held.u[rows, :] = u.astype(BF)
        act = (0.5 * u * (1.0 + jnp.tanh(GELU_K * (u + GELU_A * u * u * u)))).astype(BF)
        held.act[rows, :] = act
        s.own_part[...] = nn(act, used["wdn"][...])

        collect.put(step, lambda: s.own_part[...])
        return 0

    lax.fori_loop(0, z.T, feed, 0)
    collect.join()
    if layer == 0:
        e.next_weights()
    e.turn(layer, "feed")
    for name in ("mid", "n2", "u", "act"):
        saver.save(getattr(held, name), outs[name])
    total = collect.total(held.mid[...] + s.own_part[...] + vec[7:8, :])
    own_rows = pl.ds(pl.multiple_of(me * z.block, z.block), z.block)
    res_ref[own_rows, :] = total.astype(BF)
    spread = Spread(
        me,
        lambda owner, half: res_ref.at[
            pl.ds(pl.multiple_of(owner * z.block + half * half_rows, half_rows), half_rows), :
        ],
        lambda i: s.res_ss.at[i],
        lambda i: s.res_rs.at[i],
    )
    e.arriving = spread
    if layer == 0:
        spread.start()
    collect.finish()

    def finish_block(b, _):
        pair_spread(b).finish()
        single_spread(b).finish()
        return 0

    lax.fori_loop(0, z.T, finish_block, 0)

    def sent(d, _):
        for copy in tile_copies(d, at):
            copy.wait_send()
        return 0

    lax.fori_loop(at + 1, z.S, sent, 0)

    @pl.when(at < last)
    def _():
        for copy in edge_copies():
            copy.wait_send()

    saver.finish()


def backward_part(z, layer, e):
    rt, used, s, me, at, core = e.routes[layer], e.used, e.s, e.me, e.at, e.core
    c_ref, grad_ref = (e.grad, e.cotan) if layer == 0 else (e.cotan, e.grad)
    k = e.held(layer)
    last = z.S - 1
    vec = e.vec(layer)
    own_rows = pl.ds(pl.multiple_of(me * z.block, z.block), z.block)
    W = z.width
    g_out = e.g_out
    across = {"section": 1 - core}

    def ready(*names):
        for name in names:
            if name in WEIGHTS:
                e.weight_ready(layer, WEIGHTS.index(name))
            else:
                e.kept_ready(layer, name)

    def done(*names):
        if layer == 1:
            for name in names:
                if name in WEIGHTS:
                    e.weight_again(WEIGHTS.index(name))
                else:
                    e.kept_again(name)

    collects = (e.collect(1), e.collect(2))
    half_rows = z.block // 2

    def rows_spread(ref, sends, recvs):
        return Spread(
            me,
            lambda owner, half: ref.at[
                pl.ds(pl.multiple_of(owner * z.block + half * half_rows, half_rows), half_rows), :
            ],
            lambda i: sends.at[i],
            lambda i: recvs.at[i],
        )

    if layer == 1:
        e.cotan_load.wait()
    ready("wdn", "u", "wup")

    def ff_back(i, _):
        step = visiting(i)
        rows = pl.ds(pl.multiple_of(partner(me, step) * z.block, z.block), z.block)
        u = k.u[rows, :].astype(F32)
        squared = u * u
        bent = jnp.tanh(GELU_K * (u + GELU_A * squared * u))
        slope = 0.5 * (1.0 + bent) + 0.5 * u * (1.0 - bent * bent) * (
            GELU_K * (1.0 + 3.0 * GELU_A * squared)
        )
        du = (nt(c_ref[rows, :], used["wdn"][...]) * slope).astype(BF)
        s.du[rows, :] = du
        s.own_part[...] = nt(du, used["wup"][...])

        collects[0].put(step, lambda: s.own_part[...])
        return 0

    lax.fori_loop(0, z.T, ff_back, 0)
    ones = jnp.ones((16, z.rows), BF)
    s.stat[...] = jnp.zeros((24, W), F32)

    mine = (s.pa, s.pb, s.pc, s.pd)
    theirs_part = (s.xa, s.xb, s.xc, s.xd)
    summed = (s.sa, s.sb, s.sc, s.sd)
    crossed = (s.ta, s.tb, s.tc, s.td)
    handed = (s.ha, s.hb, s.hc)

    def give(piece):
        return remote(
            mine[piece].at[1 - core if piece < 3 else 0], theirs_part[piece], s.give_ss.at[piece], s.give_rs.at[piece], across
        )

    def cross(piece, d, source):
        return remote(
            summed[piece].at[d],
            crossed[piece].at[source],
            s.cross_ss.at[piece, d],
            s.cross_rs.at[piece, source],
            {"seq": d},
        )

    stepwise = z.S == 4
    near_by, far_off = at + 1 - 2 * (at % 2), (at + 2) % z.S

    def hop(piece, i):
        block, target = ((near_by, near_by), ((near_by + 2) % z.S, near_by), (far_off, far_off))[i]
        return remote(
            summed[piece].at[block],
            crossed[piece].at[i],
            s.cross_ss.at[piece, i],
            s.cross_rs.at[piece, i],
            {"seq": target},
        )

    def relay(piece):
        if stepwise:
            hop(piece, 1).wait_recv()
            summed[piece][far_off] = (
                summed[piece][far_off].astype(F32) + crossed[piece][1].astype(F32)
            ).astype(BF)
            hop(piece, 2).start()

    def hand(piece):
        return remote(
            summed[piece].at[at], handed[piece], s.hand_ss.at[piece], s.hand_rs.at[piece], across
        )

    span = math.lcm(z.share, 16)

    def add_up(piece):
        give(piece).wait_recv()

        def chunk(i, _):
            rows = pl.ds(pl.multiple_of(i * span, span), span)
            value = mine[piece][core if piece < 3 else 0, rows, :].astype(F32) + theirs_part[piece][rows, :].astype(F32)
            for j in range(span // z.share):
                d = i * (span // z.share) + j
                rows_of = value[j * z.share : (j + 1) * z.share]
                if z.padded > z.share:
                    rows_of = jnp.concatenate(
                        [rows_of, jnp.zeros((z.padded - z.share, value.shape[1]), F32)], axis=0
                    )
                summed[piece][d] = rows_of.astype(BF)

                if not stepwise:

                    @pl.when(d != at)
                    def _():
                        cross(piece, d, at).start()

            return 0

        lax.fori_loop(0, W // span, chunk, 0)
        if stepwise:
            hop(piece, 0).start()
            hop(piece, 1).start()

    offsets = [sum(z.pieces[:piece]) for piece in range(len(z.pieces))]

    def reduce(piece):
        def wait(i, _):
            d = (at + i) % z.S
            cross(piece, d, d).wait_recv()
            return 0

        def add(i, running):
            return running + crossed[piece][(at + i) % z.S].astype(F32)

        if stepwise:
            hop(piece, 0).wait_recv()
            hop(piece, 2).wait_recv()
            total = (
                summed[piece][at].astype(F32) + crossed[piece][0].astype(F32) + crossed[piece][2].astype(F32)
            )
        else:
            lax.fori_loop(1, z.S, wait, 0)
            total = lax.fori_loop(1, z.S, add, summed[piece][at].astype(F32))
        cols = slice(offsets[piece], offsets[piece] + z.pieces[piece])

        @pl.when(core == layer)
        def _():
            g_out[core, :, cols] = total[: z.share]

        @pl.when(core != layer)
        def _():
            if piece < len(handed):
                summed[piece][at] = total.astype(BF)
                hand(piece).start()

    def crossed_over(piece):
        def one(i, _):
            cross(piece, (at + i) % z.S, at).wait_send()
            return 0

        if stepwise:
            for i in range(3):
                hop(piece, i).wait_send()
        else:
            lax.fori_loop(1, z.S, one, 0)

    def take(piece):
        cols = slice(offsets[piece], offsets[piece] + z.pieces[piece])

        @pl.when(core == layer)
        def _():
            hand(piece).wait_recv()
            g_out[1 - core, :, cols] = handed[piece][...].astype(F32)[: z.share]

    ready("act", "n2")
    wide = z.hidden // 2
    for cols in (slice(0, wide), slice(wide, z.hidden)):
        s.pa[0, :, cols] = tn(c_ref[...], k.act[:, cols]).astype(BF)
    collects[0].join()
    for cols in (slice(0, wide), slice(wide, z.hidden)):
        s.pa[1, :, cols] = tn(k.n2[...], s.du[:, cols]).astype(BF)
    give(0).start()
    done("wdn", "wup", "u", "act", "n2")
    s.stat[8:9, :] = nn(ones, s.du[...])[0:1]
    s.stat[9:10, :] = nn(ones, c_ref[...])[0:1]
    ready("mid", "wo")
    if layer == 0:
        e.leftover()
    add_up(0)
    grad = collects[0].total(s.own_part[...])
    y, spread = normed(k.mid[...])
    dr2 = c_ref[own_rows, :].astype(F32) + norm_back(grad, vec[4:5, :], y, spread)
    s.dr2[...] = dr2
    s.wo_all[me] = dr2.astype(BF)

    ob_spread = Spread(
        me,
        lambda owner, half: s.wo_all.at[owner, pl.ds(half * half_rows, half_rows), :],
        lambda i: s.ob_ss.at[i],
        lambda i: s.ob_rs.at[i],
    )
    ob_spread.start()
    done("mid")
    s.stat[0:1, :] = column_sum(dr2)
    s.stat[1:2, :] = column_sum(grad * y)
    s.stat[2:3, :] = column_sum(grad)
    s.dkv[...] = jnp.zeros((z.rows + TILE, z.pad), F32)
    ob_spread.forward()
    relay(0)
    lane_wide = grid_of((z.block, LANES), 1)

    def out_back(step, _):
        for wanted in range(1, z.T):

            @pl.when(step == wanted)
            def _(wanted=wanted):
                ob_spread.wait(wanted)

        rows = pl.ds(pl.multiple_of(partner(me, step) * z.block, z.block), z.block)
        dout = nt(s.wo_all[partner(me, step)], used["wo"][...])
        pair, single = dout[:, :LANES], dout[:, LANES:]
        for h, value in enumerate((pltpu.roll(pair, TILE, 1), pair, pltpu.roll(single, TILE, 1))):
            s.pair_all[h, rows, :] = jnp.where(lane_wide < TILE, 0.0, value).astype(BF)
        return 0

    lax.fori_loop(0, z.T, out_back, 0)
    done("wo")
    collects[0].finish()
    if layer == 1:
        e.arriving.start()
    ready("p", "q", "kvt", "ckv")

    ones_row = jnp.ones((16, TILE), BF)

    def attend_back(i, _):
        tiles = [i * group + g for g in range(group)]
        units = [(g, h) for g in range(group) for h in range(z.heads)]
        keys, query, dout, prob, dprob = {}, {}, {}, {}, {}
        for g, t in enumerate(tiles):
            base = pl.multiple_of(t * TILE, TILE)
            for h in range(z.heads):
                cols = slice(h * LANES, (h + 1) * LANES)
                far = k.ckv[rt[ARR, h * z.tiles + t]]
                near = k.kvt[pl.ds(h * (z.tiles + 1) + t, 2)].reshape(2 * TILE, LANES)
                keys[g, h] = jnp.concatenate([near, far, far], axis=0)
                query[g, h] = k.q[pl.ds(base, TILE), cols]
                dout[g, h] = s.pair_all[h, pl.ds(base, TILE), :]
                prob[g, h] = k.p[t * z.heads + h]
                dprob[g, h] = nt(dout[g, h], keys[g, h])
        totals = {u: jnp.sum(prob[u].astype(F32) * dprob[u], axis=-1, keepdims=True) for u in units}
        dz = {u: (prob[u].astype(F32) * (dprob[u] - totals[u])).astype(BF) for u in units}
        for g, t in enumerate(tiles):
            base = pl.multiple_of(t * TILE, TILE)
            for h in range(z.heads):
                cols = slice(h * LANES, (h + 1) * LANES)
                u = h * z.tiles + t
                s.dqkv[pl.ds(base, TILE), cols] = nn(dz[g, h], keys[g, h]).astype(BF)
                dkeys = tn(
                    jnp.concatenate([dz[g, h], prob[g, h]], axis=0),
                    jnp.concatenate([query[g, h], dout[g, h]], axis=0),
                )
                s.dkv[pl.ds(base, 2 * TILE), cols] += dkeys[: 2 * TILE]
                s.far[u] = dkeys[2 * TILE : 3 * TILE].astype(BF)
                gates = nn(ones_row, dz[g, h])[0:1]
                s.dgate[t, h : h + 1, :] = gates[:, :LANES]
                s.far_gate[u, 0:1, :] = gates[:, LANES:]
        return 0

    group = 4
    lax.fori_loop(0, z.tiles // group, attend_back, 0)
    done("p", "q", "kvt", "ckv")
    s.dgate[z.tiles] = jnp.zeros((8, LANES), F32)

    def edge_copies():
        behind = {"seq": jnp.maximum(at - 1, 0)}
        return (
            remote(s.edge_send, s.edge_got, s.back_edge_ss.at[0], s.back_edge_rs.at[0], behind),
            remote(s.dgate.at[0], s.edge_gate_got, s.back_edge_ss.at[1], s.back_edge_rs.at[1], behind),
        )

    @pl.when(at > 0)
    def _():
        s.edge_send[...] = s.dkv[0:TILE, :].astype(BF)
        for copy in edge_copies():
            copy.start()

    def tile_copies(d, source):
        return (
            remote(
                s.send_kv.at[d],
                s.got_kv.at[pl.ds(source * z.cap, z.cap)],
                s.back_kv_ss.at[d],
                s.back_kv_rs.at[source],
                {"seq": d},
            ),
            remote(
                s.back_send_gate.at[d], s.back_got_gate.at[source], s.back_gate_ss.at[d], s.back_gate_rs.at[source], {"seq": d}
            ),
        )

    def pack(d, _):
        def slot(i, _):
            u = rt[INV, d * z.cap + i]
            s.send_kv[d, i] = s.far[u]
            s.back_send_gate[d, pl.ds(i, 1), :] = s.far_gate[u][0:1]
            return 0

        lax.fori_loop(0, z.cap, slot, 0)
        for copy in tile_copies(d, at):
            copy.start()
        return 0

    lax.fori_loop(0, at, pack, 0)
    if layer == 1:
        e.arriving.forward()
    ready("o")
    out_grad = tn(s.wo_all[...].reshape(z.rows, W), k.o[...]).astype(BF)
    done("o")
    s.pb[0] = out_grad[:, :LANES]
    s.pb[1] = out_grad[:, LANES:]
    give(1).start()
    s.sum[z.n] = jnp.zeros((TILE, LANES), F32)
    s.gate_sum[z.n] = jnp.zeros((8, LANES), F32)
    ready("st", "w1", "swt", "n1")

    @pl.when(at < last)
    def _():
        for copy in edge_copies():
            copy.wait_recv()
        s.dkv[pl.ds(z.rows, TILE), :] += s.edge_got[...].astype(F32)
        s.dgate[z.tiles] = s.edge_gate_got[...]

    def landed(source, _):
        for copy in tile_copies(0, source):
            copy.wait_recv()
        for i in range(z.cap):
            s.got_gate_row[source * z.cap + i, 0:1, :] = s.back_got_gate[source, i : i + 1, :]
        return 0

    lax.fori_loop(at + 1, z.S, landed, 0)

    def gather(i, carry):
        running, gates = carry
        index = rt[ORD, i]
        joined = rt[CONT, i].astype(F32)
        running = running * joined + s.got_kv[index].astype(F32)
        gates = gates * joined + s.got_gate_row[index]
        s.sum[i] = running
        s.gate_sum[i] = gates
        return running, gates

    lax.fori_loop(0, z.n, gather, (jnp.zeros((TILE, LANES), F32), jnp.zeros((8, LANES), F32)))

    def settle(t, _):
        base = pl.multiple_of((t + 1) * TILE, TILE)
        rows = pl.ds(pl.multiple_of(t * TILE, TILE), TILE)
        for h in range(z.heads):
            cols = slice(h * LANES, (h + 1) * LANES)
            index = rt[LAST, h * z.tiles + t]
            s.dqkv[rows, z.pad + h * LANES : z.pad + (h + 1) * LANES] = (
                s.dkv[pl.ds(base, TILE), cols] + s.sum[index]
            ).astype(BF)
            s.tile_gate[t, h : h + 1, :] = s.gate_sum[index][0:1]
        return 0

    lax.fori_loop(0, z.tiles, settle, 0)
    if layer == 1:
        for step in range(1, z.T):
            e.arriving.wait(step)
        e.arriving.finish()
        e.deliver(1, e.rows, e.layer_out)
    lane = grid_of((8, LANES), 1)
    head_row = grid_of((8, LANES), 0)
    for i in range(z.tiles // 2):
        halves = []
        for t in (2 * i, 2 * i + 1):
            halves.append(pltpu.roll(s.dgate[t], TILE, 1) + s.dgate[t + 1] + s.tile_gate[t])
        joint = jnp.where(lane < TILE, halves[0], pltpu.roll(halves[1], TILE, 1))
        score = k.st[:, i * LANES : (i + 1) * LANES]
        grads = jnp.where(head_row < z.heads, joint / (1.0 + jnp.exp(score)), 0.0)
        s.ds[0:8, i * LANES : (i + 1) * LANES] = grads
        s.ds[8:16, i * LANES : (i + 1) * LANES] = jnp.zeros((8, LANES), F32)

    def in_back(i, _):
        step = visiting(i)
        rows = pl.ds(pl.multiple_of(partner(me, step) * z.block, z.block), z.block)
        s.own_part[...] = nt(s.dqkv[rows, :], used["w1"][...]) + tn(
            s.ds[:, rows].astype(BF), used["swt"][...]
        )

        collects[1].put(step, lambda: s.own_part[...])
        return 0

    lax.fori_loop(0, z.T, in_back, 0)
    done("st", "w1", "swt")
    s.pc[0] = tn(k.n1[...], s.dqkv[:, z.pad :]).astype(BF)
    collects[1].join()
    queries = tn(k.n1[...], s.dqkv[:, : z.pad])
    lane_full = grid_of((W, LANES), 1)
    s.pc[1, :, :LANES] = jnp.where(
        lane_full < TILE, queries[:, :LANES], pltpu.roll(queries[:, LANES : 2 * LANES], TILE, 1)
    ).astype(BF)
    s.pc[1, :, LANES : 2 * LANES] = queries[:, 2 * LANES :].astype(BF)
    s.pc[1, :, 2 * LANES :] = jnp.zeros((W, z.pad - 2 * LANES), BF)
    give(2).start()
    s.stat[10:13, :] = nn(s.ds[...].astype(BF), k.n1[...])[0:3]
    done("n1")
    source, target = grid_of((W, 1), 0), grid_of((1, W), 1)
    is_value = source >= z.pad
    index = jnp.where(is_value, source - z.pad, source)
    index = index // LANES * TILE + index % TILE
    each = z.heads * TILE // z.S
    wanted = index // each * z.share + index % each + jnp.where(is_value, each, 0)
    filled = (source % LANES >= TILE) == is_value
    wanted = jnp.where(filled, wanted, -1)
    spread_out = jnp.where(wanted == target, jnp.where(is_value, 1.0, TILE**-0.5), 0.0).astype(BF)
    s.stat[13:14, :] = nn(nn(ones, s.dqkv[...]).astype(BF), spread_out)[0:1]
    reduce(0)
    add_up(1)
    add_up(2)
    grad = collects[1].total(s.own_part[...])
    if layer == 1:
        entry = e.middle[own_rows, :]
    else:
        e.entry_load.wait()
        entry = s.entry[...]
    y, spread = normed(entry.astype(F32))
    dr = s.dr2[...] + norm_back(grad, vec[0:1, :], y, spread)
    grad_ref[own_rows, :] = dr.astype(BF)
    grad_spread = rows_spread(grad_ref, s.grad_ss, s.grad_rs)
    s.stat[3:4, :] = column_sum(grad * y)
    s.stat[4:5, :] = column_sum(grad)

    def stat_copy(step):
        return remote(
            s.stat.at[pl.ds(0, 8), :],
            s.stat_got.at[step - 1],
            s.stat_ss.at[step],
            s.stat_rs.at[step],
            to_tensor(step, me),
        )

    for step in range(1, z.T):
        stat_copy(step).start()
    grad_spread.start()
    shared = s.stat[0:8, :]
    for step in range(1, z.T):
        stat_copy(step).wait()
        shared += s.stat_got[step - 1]
    stats = jnp.concatenate([shared, s.stat[8:16, :]], axis=0).astype(BF)
    unit = (grid_of((16, LANES), 0) == grid_of((16, LANES), 1)).astype(F32).astype(BF)
    s.pd[0] = tn(stats, unit).astype(BF)

    @pl.when(core != layer)
    def _():
        give(3).start()

    grad_spread.forward()
    relay(1)
    relay(2)

    @pl.when(core == layer)
    def _():
        add_up(3)

    for step in range(z.T):
        grad_spread.wait(step)
        if layer == 0:
            e.deliver_block(grad_ref, step)

    if layer == 1:
        e.deliver(1, grad_ref, e.input_grad)
    def settle_sums():
        reduce(1)
        take(0)
        take(1)

        @pl.when(core == layer)
        def _():
            relay(3)

        reduce(2)
        take(2)

        @pl.when(core == layer)
        def _():
            reduce(3)
            crossed_over(3)

        @pl.when(core != layer)
        def _():
            give(3).wait_send()
            for piece in range(3):
                hand(piece).wait_send()

        for piece in range(3):
            crossed_over(piece)

    for piece in range(3):
        give(piece).wait_send()
    if layer == 1:
        e.leftover = settle_sums
    else:
        settle_sums()
    collects[1].finish()
    ob_spread.finish()
    grad_spread.finish()

    def sent(d, _):
        for copy in tile_copies(d, at):
            copy.wait_send()
        return 0

    lax.fori_loop(0, at, sent, 0)

    @pl.when(at > 0)
    def _():
        for copy in edge_copies():
            copy.wait_send()


class Unsaved:
    def save(self, src, dst):
        pass

    def finish(self):
        pass


class Env:
    pass


def layers_kernel(z, names, *refs):
    count = len(WEIGHTS)
    e = Env()
    e.routes, refs = refs[:2], refs[2:]
    tokens, cotangent, refs = refs[0], refs[1], refs[2:]
    own, refs = dict(zip(WEIGHTS, refs[:count])), refs[count:]
    e.layer_out, e.input_grad, e.g_out, refs = refs[0], refs[1], refs[2], refs[3:]
    theirs, refs = dict(zip(WEIGHTS, refs[:count])), refs[count:]
    e.store, refs = dict(zip(KEPT, refs[: len(KEPT)])), refs[len(KEPT) :]
    e.used, refs = dict(zip(WEIGHTS, refs[:count])), refs[count:]
    held, refs = dict(zip(KEPT, refs[: len(KEPT)])), refs[len(KEPT) :]
    s = e.s = Refs(names, refs)
    e.rows, e.middle, e.cotan, e.grad = s.rows, s.middle, s.cotan, s.grad
    me, at, core = e.me, e.at, e.core = lax.axis_index("tensor"), lax.axis_index("seq"), lax.axis_index("section")
    across = {"section": 1 - core}
    own_rows = pl.ds(pl.multiple_of(me * z.block, z.block), z.block)
    e.input_load = pltpu.make_async_copy(tokens.at[core], s.rows, s.load.at[0])
    e.cotan_load = pltpu.make_async_copy(cotangent.at[core], s.cotan, s.load.at[1])
    e.entry_load = pltpu.make_async_copy(tokens.at[core].at[own_rows, :], s.entry, s.load.at[2])
    e.input_load.start()

    def vec(layer):
        return e.used["vec"].at[layer]

    def chosen_keys(layer):
        return s.ckv_next if layer == 1 else held["ckv"]

    def held_in(layer):
        return Refs(KEPT, [chosen_keys(layer) if name == "ckv" else held[name] for name in KEPT])

    e.vec, e.held = vec, held_in

    def load(layer, i, source):
        name = WEIGHTS[i]
        target = e.used[name].at[layer] if name == "vec" else e.used[name]
        return pltpu.make_async_copy(source[name], target, s.weight_load.at[i])

    e.load = load

    def swap(i):
        name = WEIGHTS[i]
        return remote(own[name], theirs[name], s.swap_ss.at[i], s.swap_rs.at[i], across)

    def start_weight(layer, i):
        @pl.when(core == layer)
        def _():
            load(layer, i, own).start()

        @pl.when(core != layer)
        def _():
            load(layer, i, theirs).start()

    loaded = {0: set(), 1: set()}
    pending = {}

    def weight_ready(layer, i):
        if layer == 0 and i not in loaded[0]:

            @pl.when(core != layer)
            def _():
                swap(i).wait_recv()
                load(layer, i, theirs).start()

            loaded[0].add(i)
            load(layer, i, own).wait()
        elif pending.pop((layer, i), False):
            load(layer, i, own).wait()

    def next_weights():
        @pl.when(core == 0)
        def _():
            for i in range(count):
                swap(i).wait_recv()

        for i in range(count):
            start_weight(1, i)
            pending[1, i] = True

    def weight_again(i):
        if WEIGHTS[i] != "vec":
            start_weight(0, i)
            pending[0, i] = True

    e.weight_ready, e.next_weights, e.weight_again = weight_ready, next_weights, weight_again
    kept_pending = {}

    def kept_load(name):
        return pltpu.make_async_copy(e.store[name], held[name], s.kept_load.at[KEPT.index(name)])

    def kept_again(name):
        if name != "ckv":
            kept_load(name).start()
            kept_pending[name] = True

    def kept_ready(layer, name):
        if kept_pending.pop(name, False):
            kept_load(name).wait()

    e.kept_again, e.kept_ready = kept_again, kept_ready

    def collect(phase):
        return Collect(
            z,
            me,
            s.part_send,
            s.part_got.at[phase % 2],
            s.part_via.at[phase % 2],
            lambda i: s.part_ss.at[phase, i],
            lambda i: s.part_rs.at[phase, i],
        )

    e.collect = collect
    delivered = []

    def rows_to(ref, target, slot, part):
        local = pltpu.make_async_copy(ref.at[part, :], target.at[core].at[part, :], s.keep.at[slot])
        return local, remote(
            ref.at[part, :], target.at[core].at[part, :], s.move_ss.at[slot], s.move_rs.at[slot], across
        )

    everything = pl.ds(0, z.rows)

    def deliver(layer, ref, target):
        slot = len(delivered)
        local, away = rows_to(ref, target, slot, everything)

        @pl.when(core == layer)
        def _():
            local.start()

        @pl.when(core != layer)
        def _():
            away.start()

        delivered.append((layer, local, away))

    def deliver_block(ref, step):
        slot = len(delivered)
        part = pl.ds(pl.multiple_of(partner(me, step) * z.block, z.block), z.block)
        local, away = rows_to(ref, target=e.input_grad, slot=slot, part=part)

        @pl.when(core == 0)
        def _():
            local.start()

        @pl.when(core == 1)
        def _():
            away.start()

        delivered.append((0, local, away))

    e.deliver, e.deliver_block = deliver, deliver_block

    def turn(layer, where):
        if (layer, where) == TURN_FROM:

            @pl.when(core == 0)
            def _():
                pl.semaphore_signal(s.turn, inc=1, device_id=across, device_id_type=MESH)

        if (layer, where) == TURN_TO:

            @pl.when(core == 1)
            def _():
                pl.semaphore_wait(s.turn, 1)

    e.turn = turn

    @pl.when(core == 0)
    def _():
        for i in range(count):
            load(0, i, own).start()

    barrier = pltpu.get_barrier_semaphore()
    for step in range(1, z.T):
        signal(to_tensor(step, me), barrier)
    signal(across, barrier)

    def greet(i, _):
        signal({"seq": (at + i) % z.S}, barrier)
        return 0

    lax.fori_loop(1, z.S, greet, 0)
    pl.semaphore_wait(barrier, z.T - 1 + 1 + z.S - 1)
    for i in range(count):
        swap(i).start()
    e.cotan_load.start()
    e.entry_load.start()
    forward_part(z, 0, e)
    forward_part(z, 1, e)
    backward_part(z, 1, e)
    backward_part(z, 0, e)
    for i in range(count):
        swap(i).wait_send()
    for layer, local, away in delivered:

        @pl.when(core == layer)
        def _(local=local, away=away):
            local.wait()
            away.wait_recv()

        @pl.when(core != layer)
        def _(away=away):
            away.wait_send()


TURN_FROM, TURN_TO = (0, "attend"), (0, "pack")


def layers(z, routes, tokens, cotangent, own):
    rows, width, heads = z.rows, z.width, z.heads
    half = z.block // 2
    kept = dict(
        n1=((rows, width), BF),
        q=((rows, z.pad), BF),
        kvt=((heads * (z.tiles + 1), TILE, LANES), BF),
        st=((8, rows), F32),
        p=((z.slots, TILE, 2 * LANES), BF),
        ckv=((z.n, TILE, LANES), BF),
        o=((rows, 2 * LANES), BF),
        mid=((z.block, width), F32),
        n2=((rows, width), BF),
        u=((rows, z.hidden), BF),
        act=((rows, z.hidden), BF),
    )
    weights = [own[name] for name in WEIGHTS]
    vmem_of, dma = pltpu.VMEM, pltpu.SemaphoreType.DMA
    scratch = dict(
        rows=vmem_of((rows, width), BF),
        middle=vmem_of((rows, width), BF),
        cotan=vmem_of((rows, width), BF),
        grad=vmem_of((rows, width), BF),
        entry=vmem_of((z.block, width), BF),
        ckv_next=vmem_of((z.n, TILE, LANES), BF),
        gt=vmem_of((8, rows + 2 * LANES), F32),
        gate=vmem_of((heads * (z.tiles + 1), 8, LANES), F32),
        edge=vmem_of((2, heads, TILE, LANES), BF),
        edge_gate=vmem_of((2, 8, LANES), F32),
        send_kv=vmem_of((z.S, z.cap, TILE, LANES), BF),
        send_gate=vmem_of((z.S, z.capg, LANES), F32),
        got_gate=vmem_of((2, z.S, z.capg, LANES), F32),
        far_gate=vmem_of((max(z.n, z.slots), 8, LANES), F32),
        wo_all=vmem_of((z.T, max(2 * LANES, z.block), width), BF),
        wo_high=vmem_of((z.T, LANES, width), BF),
        pair_all=vmem_of((z.T, rows, LANES), BF),
        single_all=vmem_of((z.T, rows // 2, LANES), BF),
        part_send=vmem_of((z.T - 1, z.block, width), BF),
        part_got=vmem_of((2, 2, z.block, width), BF),
        part_via=vmem_of((2, 2, half, width), BF),
        own_part=vmem_of((z.block, width), F32),
        du=vmem_of((rows, z.hidden), BF),
        dr2=vmem_of((z.block, width), F32),
        dqkv=vmem_of((rows, 2 * z.pad), BF),
        dkv=vmem_of((rows + TILE, z.pad), F32),
        dgate=vmem_of((z.tiles + 1, 8, LANES), F32),
        far=vmem_of((z.slots, TILE, LANES), BF),
        back_send_gate=vmem_of((z.S, z.capg, LANES), F32),
        got_kv=vmem_of((z.n, TILE, LANES), BF),
        back_got_gate=vmem_of((z.S, z.capg, LANES), F32),
        got_gate_row=vmem_of((z.n, 8, LANES), F32),
        edge_send=vmem_of((TILE, z.pad), BF),
        edge_got=vmem_of((TILE, z.pad), BF),
        edge_gate_got=vmem_of((8, LANES), F32),
        sum=vmem_of((z.n + 1, TILE, LANES), F32),
        gate_sum=vmem_of((z.n + 1, 8, LANES), F32),
        tile_gate=vmem_of((z.tiles, 8, LANES), F32),
        ds=vmem_of((16, rows), F32),
        stat=vmem_of((24, width), F32),
        stat_got=vmem_of((z.T - 1, 8, width), F32),
    )
    for name, w in zip("abcd", z.pieces):
        scratch["p" + name] = vmem_of((1 if name == "d" else 2, width, w), BF)
        scratch["x" + name] = vmem_of((width, w), BF)
        scratch["s" + name] = vmem_of((z.S, z.padded, w), BF)
        scratch["t" + name] = vmem_of((z.S, z.padded, w), BF)
        if name != "d":
            scratch["h" + name] = vmem_of((z.padded, w), BF)
    pairs = dict(
        kv=(2, z.S), gate=(2, z.S), edge=(2, heads + 1), wo=(z.T,), o=(z.T * 12,), part=(3, 6), res=(6,),
        swap=(len(WEIGHTS),), move=(3 + z.T,), back_kv=(z.S,), back_gate=(z.S,), back_edge=(2,), ob=(6,),
        grad=(6,), stat=(z.T,), give=(4,), cross=(4, z.S), hand=(3,),
    )
    for name, shape in pairs.items():
        scratch[name + "_ss"] = dma(shape)
        scratch[name + "_rs"] = dma(shape)
    scratch |= dict(
        load=dma((3,)),
        weight_load=dma((len(WEIGHTS),)),
        kept_load=dma((len(KEPT),)),
        saved=dma((len(KEPT),)),
        keep=dma((3 + z.T,)),
        turn=pltpu.SemaphoreType.REGULAR,
    )
    doubled = {"vec"}

    def room(name, shape, kind):
        return vmem_of((2, *shape) if name in doubled else shape, kind)

    shaped = (
        jax.ShapeDtypeStruct((2, rows, width), BF),
        jax.ShapeDtypeStruct((2, rows, width), BF),
        jax.ShapeDtypeStruct((2, z.share, sum(z.pieces)), F32),
        *(jax.ShapeDtypeStruct(value.shape, value.dtype) for value in weights),
        *(jax.ShapeDtypeStruct(*kept[name]) for name in KEPT),
    )
    outs = pl.pallas_call(
        functools.partial(layers_kernel, z, tuple(scratch)),
        out_shape=shaped,
        in_specs=[smem(), smem()] + [anywhere()] * (2 + len(weights)),
        out_specs=tuple(vmem() if i == 2 else anywhere() for i in range(len(shaped))),
        scratch_shapes=[
            *(room(name, value.shape, value.dtype) for name, value in zip(WEIGHTS, weights)),
            *(room(name, *kept[name]) for name in KEPT),
            *scratch.values(),
        ],
        compiler_params=pltpu.CompilerParams(
            collective_id=0, has_side_effects=True, vmem_limit_bytes=LIMIT
        ),
        name="layers",
    )(*routes, tokens, cotangent, *weights)
    return outs[:3]


UNPACKED = (
    "input_weight", "input_bias", "score", "out", "out_bias", "up", "up_bias", "down", "down_bias", "gain", "shift",
)


def unpack_kernel(z, head, total_ref, *refs):
    out = Refs(UNPACKED, refs)
    core = lax.axis_index("section")
    inner, hidden, share = z.heads * head, z.hidden, z.share
    c_o, c_i = hidden, hidden + LANES
    c_s = c_i + z.pad
    out.up[...] = total_ref[1, :, :hidden]
    out.down[...] = total_ref[0, :, :hidden].T
    first, second = total_ref[0, :, c_o:c_i].T, total_ref[1, :, c_o:c_i].T
    out.out[0:LANES, :] = first
    out.out[LANES:inner, :] = second[: inner - LANES]
    out.input_weight[0] = head**-0.5 * total_ref[1, :, c_i : c_i + inner]
    lane = grid_of((share, LANES), 1)
    pairs = [total_ref[0, :, c_i + h * LANES : c_i + (h + 1) * LANES] for h in range(z.heads)]
    turned = [pltpu.roll(pair, LANES // 2, 1) for pair in pairs]
    out.input_weight[1, :, 0:LANES] = jnp.where(lane < head, pairs[0], turned[1])
    out.input_weight[1, :, LANES:inner] = pairs[2][:, :head]
    out.input_weight[2, :, 0:LANES] = jnp.where(lane < head, turned[0], pairs[1])
    out.input_weight[2, :, LANES:inner] = turned[2][:, :head]
    stats = total_ref[core, :, c_s : c_s + LANES]
    rows = stats.T
    out.score[...] = pltpu.roll(stats, LANES - 10, 1)[:, : z.heads]
    each = inner // z.S
    out.input_bias[0:1, :] = rows[13:14, :each]
    out.input_bias[1:2, :] = pltpu.roll(rows[8:16], share - each, 1)[5:6, :each]
    out.out_bias[...] = rows[0:1]
    out.up_bias[...] = rows[8:9]
    out.down_bias[...] = rows[9:10]
    out.gain[0:1, :] = rows[3:4]
    out.gain[1:2, :] = rows[1:2]
    out.shift[0:1, :] = rows[4:5]
    out.shift[1:2, :] = rows[2:3]


def unpack(z, head, total):
    inner, hidden, share = z.heads * head, z.hidden, z.share
    shapes = (
        (3, share, inner), (2, inner // z.S), (share, z.heads), (inner, share), (1, share), (share, hidden), (1, share),
        (hidden, share), (1, share), (2, share), (2, share),
    )
    outs = pl.pallas_call(
        functools.partial(unpack_kernel, z, head),
        out_shape=tuple(jax.ShapeDtypeStruct(shape, F32) for shape in shapes),
        in_specs=[vmem()],
        out_specs=tuple(vmem() for _ in shapes),
        compiler_params=pltpu.CompilerParams(vmem_limit_bytes=LIMIT // 2),
        name="unpack",
    )(total)
    return dict(zip(UNPACKED, outs))


def swapped(value):
    return lax.ppermute(value, "section", [(0, 1), (1, 0)])


def body(
    tokens,
    cotangent,
    lengths,
    selected,
    input_weight,
    input_bias,
    score_weight,
    output_weight,
    output_bias,
    up_weight,
    up_bias,
    down_weight,
    down_bias,
    norm_gain,
    norm_bias,
):
    core = lax.axis_index("section")
    _, rows, width = tokens.shape
    heads, hidden = score_weight.shape[2], up_weight.shape[2]
    head = input_weight.shape[3] // heads
    inner = heads * head
    z = Sizes(lax.axis_size("tensor"), lax.axis_size("seq"), rows, width, heads, hidden)
    scale = head**-0.5
    grouped = (
        selected[0].reshape(2, heads, z.S, z.tiles).transpose(0, 2, 1, 3).reshape(2, z.S, z.slots)
    )
    kept_choice = lax.dynamic_index_in_dim(grouped, core, 0, keepdims=False)
    got_choice = swapped(lax.dynamic_index_in_dim(grouped, 1 - core, 0, keepdims=False))
    own, routes = prepare(
        z,
        lengths,
        kept_choice,
        got_choice,
        input_weight[0].transpose(1, 0, 2),
        input_bias[0],
        score_weight[0],
        output_weight[0],
        output_bias,
        up_bias,
        down_bias,
        norm_gain[0],
        norm_bias[0],
    )
    own |= dict(wup=up_weight[0], wdn=down_weight[0])
    layer_out, input_grad, total = layers(z, routes, tokens, cotangent, own)
    parts = unpack(z, head, total)
    parts["input_weight"] = parts["input_weight"].transpose(1, 0, 2)
    return (layer_out[None], input_grad[None], *(part.reshape(1, *shape) for part, shape in (
        (parts["input_weight"], (z.share, 3, inner)),
        (parts["input_bias"], (2, inner // z.S)),
        (parts["score"], (z.share, heads)),
        (parts["out"], (inner, z.share)),
        (parts["out_bias"], (z.share,)),
        (parts["up"], (z.share, hidden)),
        (parts["up_bias"], (z.share,)),
        (parts["down"], (hidden, z.share)),
        (parts["down_bias"], (z.share,)),
        (parts["gain"], (2, z.share)),
        (parts["shift"], (2, z.share)),
    )))


def solution(mesh):
    return jax.shard_map(
        body,
        mesh=mesh,
        in_specs=(
            P(None, "seq", None),
            P(None, "seq", None),
            P(),
            P("section", None, "tensor", None),
            P("section", None, None, "tensor"),
            P("section", None, "tensor"),
            P("section", None, "tensor"),
            P("section", "tensor", None),
            P("section", None),
            P("section", None, "tensor"),
            P("section", "tensor"),
            P("section", "tensor", None),
            P("section", None),
            P("section", None, None),
            P("section", None, None),
        ),
        out_specs=(
            P("section", None, "seq", None),
            P("section", None, "seq", None),
            P("section", "seq", None, "tensor"),
            P("section", None, ("tensor", "seq")),
            P("section", "seq", "tensor"),
            P("section", "tensor", "seq"),
            P("section", "seq"),
            P("section", "seq", "tensor"),
            P("section", ("tensor", "seq")),
            P("section", "tensor", "seq"),
            P("section", "seq"),
            P("section", None, "seq"),
            P("section", None, "seq"),
        ),
        check_vma=False,
    )
```

```python
import functools
import math

import jax
import jax.numpy as jnp
from jax import lax
from jax.experimental import pallas as pl
from jax.experimental.pallas import tpu as pltpu
from jax.sharding import PartitionSpec as P

TILE = 64
LANES = 128
MASKED = -1e30
EPSILON = 1e-05
FAR = -(1 << 20)
MESH = pl.DeviceIdType.MESH
BF = jnp.bfloat16
F32 = jnp.float32
GELU_A = 0.044715
GELU_K = math.sqrt(2.0 / math.pi)
LIMIT = 62 * 1024 * 1024


class Sizes:
    def __init__(self, mesh_tensor, mesh_seq, rows, width, heads, hidden):
        self.T, self.S = mesh_tensor, mesh_seq
        self.rows, self.width, self.heads, self.hidden = rows, width, heads, hidden
        self.tiles = rows // TILE
        self.slots = heads * self.tiles
        self.cap = -(-self.slots // (mesh_seq - 1))
        self.capg = -(-self.cap // 8) * 8
        self.n = mesh_seq * self.cap
        self.block = rows // mesh_tensor
        self.pad = heads * LANES
        self.share = width // mesh_seq
        self.padded = -(-self.share // 16) * 16
        self.pieces = (hidden, LANES, self.pad, LANES)


SEND, INV, ORD, CONT, ARR, POS, LAST, ENDS = range(8)
WEIGHTS = ("vec", "w1", "swt", "wo", "wup", "wdn")
KEPT = ("n1", "q", "kvt", "st", "p", "ckv", "o", "mid", "n2", "u", "act")


def nn(a, b):
    return jnp.dot(a, b, preferred_element_type=F32)


def nt(a, b):
    return lax.dot_general(a, b, (((1,), (1,)), ((), ())), preferred_element_type=F32)


def tn(a, b):
    return lax.dot_general(a, b, (((0,), (0,)), ((), ())), preferred_element_type=F32)


def normed(x):
    centred = x - jnp.mean(x, axis=-1, keepdims=True)
    spread = lax.rsqrt(jnp.mean(centred * centred, axis=-1, keepdims=True) + EPSILON)
    return centred * spread, spread


def norm_back(grad, gain, y, spread):
    scaled = grad * gain
    return spread * (
        scaled
        - jnp.mean(scaled, axis=-1, keepdims=True)
        - y * jnp.mean(scaled * y, axis=-1, keepdims=True)
    )


def partner(me, step):
    return (me // 2 + step // 2) % 2 * 2 + (me % 2 + step % 2) % 2


def column_sum(x):
    return jnp.sum(x, axis=0, keepdims=True)


def smem():
    return pl.BlockSpec(memory_space=pltpu.SMEM)


def vmem():
    return pl.BlockSpec(memory_space=pltpu.VMEM)


def anywhere():
    return pl.BlockSpec(memory_space=pl.ANY)


def grid_of(shape, axis):
    return lax.broadcasted_iota(jnp.int32, shape, axis)


def prepare_kernel(
    z,
    length_ref,
    kept_ref,
    got_ref,
    win_ref,
    bin_ref,
    sw_ref,
    wout_ref,
    bout_ref,
    bup_ref,
    bdn_ref,
    gain_ref,
    shift_ref,
    vec_ref,
    w1_ref,
    swt_ref,
    wo_ref,
    rt0_ref,
    rt1_ref,
):
    inner, head = win_ref.shape[2], win_ref.shape[2] // z.heads
    row, col = grid_of((inner, z.pad), 0), grid_of((inner, z.pad), 1)
    lane_of = row // head * LANES + row % head
    first = (col == lane_of).astype(F32)
    second = (col == lane_of + head).astype(F32)
    low, high = first.astype(BF), second.astype(BF)
    scaled = (first * head**-0.5).astype(BF)
    w1_ref[:, : z.pad] = nn(win_ref[0], scaled).astype(BF)
    w1_ref[:, z.pad :] = (nn(win_ref[1], low) + nn(win_ref[2], high)).astype(BF)
    vec_ref[0:1, :] = gain_ref[...].astype(F32)[0:1]
    vec_ref[1:2, :] = shift_ref[...].astype(F32)[0:1]
    vec_ref[2:3, : z.pad] = nn(bin_ref[...], scaled)[0:1]
    vec_ref[2:3, z.pad :] = nn(bin_ref[...], high)[1:2]
    vec_ref[3:4, :] = bout_ref[...].astype(F32)
    vec_ref[4:5, :] = gain_ref[...].astype(F32)[1:2]
    vec_ref[5:6, :] = shift_ref[...].astype(F32)[1:2]
    vec_ref[6:7, :] = bup_ref[...].astype(F32)
    vec_ref[7:8, :] = bdn_ref[...].astype(F32)
    unit = (grid_of((16, z.heads), 0) == grid_of((16, z.heads), 1)).astype(F32).astype(BF)
    swt_ref[...] = nn(unit, sw_ref[...]).astype(BF)
    wo_ref[0:inner, :] = wout_ref[...]
    wo_ref[inner:, :] = jnp.zeros((2 * LANES - inner, z.width), BF)

    at, core = lax.axis_index("seq"), lax.axis_index("section")
    n, slots, cap = z.n, z.slots, z.cap
    first_end = length_ref[core, 0]
    second_end = first_end + length_ref[core, 1]
    shift = z.tiles.bit_length() - 1
    near = 1e-3

    def total(mask, value, axis):
        return jnp.sum(jnp.where(mask, value, 0.0), axis=axis, keepdims=True)

    def whole(x):
        return (x + near).astype(jnp.int32)

    for layer, rt in enumerate((rt0_ref, rt1_ref)):
        rt[...] = jnp.zeros((8, LANES), jnp.int32)
        chosen = jnp.where(core == layer, kept_ref[...], got_ref[...])
        owner = lax.shift_right_arithmetic(chosen, shift)
        sub, lan = grid_of((slots, n), 0), grid_of((slots, n), 1)
        wide = jnp.zeros((slots, n), jnp.int32)
        for d in range(z.S):
            column = jnp.sum(
                jnp.where(
                    grid_of((slots, slots), 0) == grid_of((slots, slots), 1),
                    chosen[d : d + 1].astype(F32) + 1.0,
                    0.0,
                ),
                axis=1,
                keepdims=True,
            )
            wide = jnp.where(lan // cap == d, whole(column) - 1, wide)
        mine = lax.shift_right_arithmetic(wide, shift) == at
        order = nn(
            (grid_of((slots, slots), 0) > grid_of((slots, slots), 1)).astype(F32), mine.astype(F32)
        )
        taken = mine & (whole(order) == lan % cap)
        head_of = sub // z.tiles
        inner_tile = wide - at * z.tiles
        rt[SEND : SEND + 1, :n] = whole(
            total(taken, (head_of * (z.tiles + 1) + inner_tile).astype(F32), 0)
        ) + 1
        present = jnp.sum(taken.astype(F32), axis=0, keepdims=True)
        key = total(taken, (head_of * z.tiles + inner_tile - slots).astype(F32), 0) + slots
        own = jnp.sum(
            jnp.where(grid_of((z.S, slots), 0) == at, chosen.astype(F32) + 1.0, 0.0), axis=0, keepdims=True
        )
        square_row, square_col = grid_of((slots, slots), 0), grid_of((slots, slots), 1)
        own_column = total(square_row == square_col, own, 1)
        own_row = whole(own) - 1
        own_col = whole(own_column) - 1
        owner_row = lax.shift_right_arithmetic(own_row, shift)
        owner_col = lax.shift_right_arithmetic(own_col, shift)
        same = owner_row == owner_col
        place_row = whole(jnp.sum((same & (square_row < square_col)).astype(F32), axis=0, keepdims=True))
        place_col = whole(jnp.sum((same & (square_col < square_row)).astype(F32), axis=1, keepdims=True))
        live = own_row >= 0
        rt[ARR : ARR + 1, :slots] = jnp.where(live, owner_row * cap + place_row, at * cap)
        rt[POS : POS + 1, :slots] = jnp.where(live, own_row * TILE, FAR)
        matched = (owner_col == lan // cap) & (place_col == lan % cap)
        rt[INV : INV + 1, :n] = whole(total(matched, sub.astype(F32), 0))
        big_row, big_col = grid_of((n, n), 0), grid_of((n, n), 1)
        key_col = total(big_row == big_col, key, 1)
        rank = jnp.sum(
            ((key < key_col) | ((key == key_col) & (big_col < big_row))).astype(F32), axis=1, keepdims=True
        )
        at_rank = whole(rank) == big_col
        rt[ORD : ORD + 1, :n] = whole(total(at_rank, big_row.astype(F32), 0))
        sorted_key = total(at_rank, key_col, 0)
        before = total(whole(rank) + 1 == big_col, key_col + 1.0, 0) - 1.0
        rt[CONT : CONT + 1, :n] = (sorted_key == before).astype(jnp.int32)
        tile = grid_of((n, slots), 1).astype(F32)
        upto = jnp.sum((key_col <= tile).astype(F32), axis=0, keepdims=True)
        has = jnp.sum((key_col == tile).astype(F32), axis=0, keepdims=True)
        rt[LAST : LAST + 1, :slots] = whole(jnp.where(has > 0.5, upto - 1.0, n * 1.0))
        rt[ENDS : ENDS + 1, :] = jnp.where(grid_of((1, LANES), 1) == 0, first_end, second_end)


def prepare(z, lengths, kept, got, win, bin_, sw, wout, bout, bup, bdn, gain, shift):
    table = jax.ShapeDtypeStruct((8, LANES), jnp.int32)
    outs = pl.pallas_call(
        functools.partial(prepare_kernel, z),
        out_shape=(
            jax.ShapeDtypeStruct((8, z.width), F32),
            jax.ShapeDtypeStruct((z.width, 2 * z.pad), BF),
            jax.ShapeDtypeStruct((16, z.width), BF),
            jax.ShapeDtypeStruct((2 * LANES, z.width), BF),
            table,
            table,
        ),
        in_specs=[smem()] + [vmem()] * 11,
        out_specs=tuple(vmem() for _ in range(6)),
        name="prepare",
    )(lengths, kept, got, win, bin_, sw, wout, bout, bup, bdn, gain, shift)
    return dict(zip(WEIGHTS[:4], outs)), outs[4:]


def to_tensor(step, me):
    return {"tensor": partner(me, step)}


def remote(src, dst, send, recv, target):
    return pltpu.make_async_remote_copy(
        src_ref=src, dst_ref=dst, send_sem=send, recv_sem=recv, device_id=target, device_id_type=MESH
    )


def signal(target, barrier):
    pl.semaphore_signal(barrier, inc=1, device_id=target, device_id_type=MESH)


class Spread:
    def __init__(self, me, view, sends, recvs):
        self.me, self.view, self.sends, self.recvs = me, view, sends, recvs

    def copy(self, i):
        me, x, y = self.me, partner(self.me, 1), partner(self.me, 2)
        owner, half, step = ((me, 0, 1), (me, 1, 2), (me, 1, 1), (me, 0, 2), (x, 0, 2), (y, 1, 1))[i]
        ref = self.view(owner, half)
        return remote(ref, ref, self.sends(i), self.recvs(i), to_tensor(step, me))

    def start(self):
        for i in range(4):
            self.copy(i).start()

    def forward(self):
        for i in range(2):
            self.copy(i).wait_recv()
            self.copy(4 + i).start()

    def wait(self, step):
        for i in ((), (2,), (3,), (4, 5))[step]:
            self.copy(i).wait_recv()

    def finish(self):
        for i in range(6):
            self.copy(i).wait_send()


class Collect:
    def __init__(self, z, me, send, got, via, sends, recvs):
        self.me, self.send, self.got, self.via, self.sends, self.recvs = me, send, got, via, sends, recvs
        half = z.block // 2
        self.halves = (pl.ds(0, half), pl.ds(half, half))

    def copy(self, i):
        top, bottom = self.halves
        block, rows, target, step = (
            (2, top, self.via.at[0], 1),
            (2, bottom, self.via.at[1], 2),
            (0, top, self.got.at[0, top, :], 1),
            (1, bottom, self.got.at[1, bottom, :], 2),
            (0, bottom, self.got.at[0, bottom, :], 1),
            (1, top, self.got.at[1, top, :], 2),
        )[i]
        return remote(
            self.send.at[block, rows, :], target, self.sends(i), self.recvs(i), to_tensor(step, self.me)
        )

    def put(self, step, value):
        for wanted, copies in ((3, (0, 1)), (1, (2,)), (2, (3,))):

            @pl.when(step == wanted)
            def _(wanted=wanted, copies=copies):
                self.send[wanted - 1] = value().astype(BF)
                for i in copies:
                    self.copy(i).start()

    def join(self):
        top, bottom = self.halves
        for i, block, rows in ((1, 0, bottom), (0, 1, top)):
            self.copy(i).wait_recv()
            joined = self.send[block, rows, :].astype(F32) + self.via[i].astype(F32)
            self.send[block, rows, :] = joined.astype(BF)
            self.copy(5 - i).start()

    def total(self, own):
        for i in range(2, 6):
            self.copy(i).wait_recv()
        return own + self.got[0].astype(F32) + self.got[1].astype(F32)

    def finish(self):
        for i in range(6):
            self.copy(i).wait_send()


def visiting(k):
    return jnp.where(k == 0, 3, jnp.where(k == 3, 0, k))


class Saver:
    def __init__(self, sems):
        self.sems, self.copies = sems, []

    def save(self, src, dst):
        copy = pltpu.make_async_copy(src, dst, self.sems.at[len(self.copies)])
        copy.start()
        self.copies.append(copy)

    def finish(self):
        for copy in self.copies:
            copy.wait()


class Refs:
    def __init__(self, names, refs):
        assert len(names) == len(refs), (len(names), len(refs))
        for name, ref in zip(names, refs):
            setattr(self, name, ref)


def forward_part(z, layer, e):
    rt, r_ref, res_ref = e.routes[layer], (e.rows, e.middle)[layer], (e.middle, e.rows)[layer]
    used, s, me, at, core, load = e.used, e.s, e.me, e.at, e.core, e.load
    held = e.held(layer)
    last = z.S - 1
    first_row = at * z.rows
    vec = e.vec(layer)
    edge_ss, edge_rs = s.edge_ss.at[layer], s.edge_rs.at[layer]
    kv_ss, kv_rs, gate_ss, gate_rs = (
        sems.at[layer] for sems in (s.kv_ss, s.kv_rs, s.gate_ss, s.gate_rs)
    )
    edge, edge_gate, got_gate = s.edge.at[layer], s.edge_gate.at[layer], s.got_gate.at[layer]
    held.ckv[at * z.cap] = jnp.zeros((TILE, LANES), BF)
    outs = e.store

    def ready(*wanted):
        for i in wanted:
            e.weight_ready(layer, i)

    if layer == 0:
        e.input_load.wait()
    saver = Saver(s.saved) if layer == 0 else Unsaved()
    per_block = z.block // TILE
    ready(0)

    def norm_in(b):
        rows = pl.ds(pl.multiple_of(b * z.block, z.block), z.block)
        y, _ = normed(r_ref[rows, :].astype(F32))
        held.n1[rows, :] = (y * vec[0:1, :] + vec[1:2, :]).astype(BF)

    def project(b):
        rows = pl.ds(pl.multiple_of(b * z.block, z.block), z.block)
        qkv = (nn(held.n1[rows, :], used["w1"][...]) + vec[2:3, :]).astype(BF)
        held.q[rows, :] = qkv[:, : z.pad]
        for h in range(z.heads):
            pairs = qkv[:, z.pad + h * LANES : z.pad + (h + 1) * LANES]
            held.kvt[pl.ds(h * (z.tiles + 1) + 1 + b * per_block, per_block)] = pairs.reshape(
                per_block, TILE, LANES
            )

    def each_norm(b, _):
        norm_in(b)
        return 0

    def each_project(b, _):
        project(b)
        return 0

    def arrived_block(step, _):
        for wanted in range(1, z.T):

            @pl.when(step == wanted)
            def _(wanted=wanted):
                e.arriving.wait(wanted)

        norm_in(partner(me, step))
        project(partner(me, step))
        return 0

    if layer == 0:
        lax.fori_loop(0, z.T, each_norm, 0)
        saver.save(held.n1, outs["n1"])
        ready(1, 2)
        lax.fori_loop(0, z.T, each_project, 0)
    else:
        ready(1, 2)
        arrived_block(0, 0)
        e.arriving.forward()
        lax.fori_loop(1, z.T, arrived_block, 0)
        e.arriving.finish()
        e.deliver(0, r_ref, e.layer_out)
    score = nt(used["swt"][...], held.n1[...])[0:8]
    held.st[...] = score
    gate = jnp.minimum(score, 0.0) - jnp.log1p(jnp.exp(-jnp.abs(score)))
    s.gt[:, 0:LANES] = jnp.zeros((8, LANES), F32)
    s.gt[:, LANES : LANES + z.rows] = gate.astype(BF).astype(F32)
    s.gt[:, LANES + z.rows :] = jnp.zeros((8, LANES), F32)
    for t in range(z.tiles + 1):
        for h in range(z.heads):
            s.gate[h * (z.tiles + 1) + t, 0:1, :] = s.gt[
                h : h + 1, TILE + t * TILE : TILE + t * TILE + LANES
            ]

    def edge_copies():
        after = {"seq": jnp.minimum(at + 1, last)}
        return [
            remote(
                held.kvt.at[h * (z.tiles + 1) + z.tiles],
                edge.at[h],
                edge_ss.at[h],
                edge_rs.at[h],
                after,
            )
            for h in range(z.heads)
        ] + [
            remote(
                s.gt.at[:, pl.ds(z.rows, LANES)],
                edge_gate,
                edge_ss.at[z.heads],
                edge_rs.at[z.heads],
                after,
            )
        ]

    @pl.when(at < last)
    def _():
        for copy in edge_copies():
            copy.start()

    def tile_copies(d, source):
        return (
            remote(
                s.send_kv.at[d],
                held.ckv.at[pl.ds(source * z.cap, z.cap)],
                kv_ss.at[d],
                kv_rs.at[source],
                {"seq": d},
            ),
            remote(
                s.send_gate.at[d], got_gate.at[source], gate_ss.at[d], gate_rs.at[source], {"seq": d}
            ),
        )

    def pack(k, _):
        d = z.S - 1 - k

        def slot(i, _):
            u = rt[SEND, d * z.cap + i]
            s.send_kv[d, i] = held.kvt[u]
            s.send_gate[d, pl.ds(i, 1), :] = s.gate[u][0:1]
            return 0

        lax.fori_loop(0, z.cap, slot, 0)
        for copy in tile_copies(d, at):
            copy.start()
        return 0

    e.turn(layer, "pack")
    lax.fori_loop(0, last - at, pack, 0)
    ready(3)

    def wo_copy(step):
        return remote(
            used["wo"], s.wo_all.at[me], s.wo_ss.at[step], s.wo_rs.at[step], to_tensor(step, me)
        )

    for step in range(1, z.T):
        wo_copy(step).start()
    s.wo_all[me] = used["wo"][...]
    saver.save(held.q, outs["q"])
    saver.save(held.st, outs["st"])

    def landed(source, _):
        for copy in tile_copies(last, source):
            copy.wait_recv()
        for i in range(z.cap):
            s.far_gate[source * z.cap + i, 0:1, :] = got_gate[source, i : i + 1, :]
        return 0

    lax.fori_loop(0, at, landed, 0)
    lane = grid_of((TILE, LANES), 1)
    row = grid_of((TILE, LANES), 0)
    for h in range(z.heads):
        held.kvt[h * (z.tiles + 1)] = jnp.zeros((TILE, LANES), BF)

    @pl.when(at > 0)
    def _():
        for copy in edge_copies():
            copy.wait_recv()
        for h in range(z.heads):
            held.kvt[h * (z.tiles + 1)] = edge[h]
            s.gate[h * (z.tiles + 1), 0:1, :] = jnp.where(
                lane[0:1] < TILE,
                pltpu.roll(edge_gate[...], TILE, 1)[h : h + 1],
                s.gate[h * (z.tiles + 1), 0:1, :],
            )

    saver.save(held.kvt, outs["kvt"])
    saver.save(held.ckv, outs["ckv"])

    def attend(tiles):
        units = [(g, h) for g in range(len(tiles)) for h in range(z.heads)]
        keys, scores = {}, {}
        for g, t in enumerate(tiles):
            base = pl.multiple_of(t * TILE, TILE)
            query = first_row + base + row
            begin = jnp.where(
                query >= rt[ENDS, 1],
                rt[ENDS, 1],
                jnp.where(query >= rt[ENDS, 0], rt[ENDS, 0], 0),
            )
            key = first_row + base - TILE + lane
            near_ok = (key <= query) & (key > query - TILE) & (key >= begin)
            for h in range(z.heads):
                u = h * z.tiles + t
                arrived = rt[ARR, u]
                far = held.ckv[arrived]
                near = held.kvt[pl.ds(h * (z.tiles + 1) + t, 2)].reshape(2 * TILE, LANES)
                keys[g, h] = jnp.concatenate([near, far, far], axis=0)
                gates = jnp.concatenate(
                    [s.gate[h * (z.tiles + 1) + t, 0:1, :], s.far_gate[arrived][0:1]], axis=1
                )
                far_ok = (rt[POS, u] + lane >= begin) & (lane < TILE)
                query_tile = held.q[pl.ds(base, TILE), h * LANES : (h + 1) * LANES]
                scores[g, h] = jnp.where(
                    jnp.concatenate([near_ok, far_ok], axis=1), nt(query_tile, keys[g, h]) + gates, MASKED
                )
        tops = {u: jnp.max(scores[u], axis=-1, keepdims=True) for u in units}
        raised = {u: jnp.exp(scores[u] - tops[u]) for u in units}
        sums = {u: jnp.sum(raised[u], axis=-1, keepdims=True) for u in units}
        probs = {u: (raised[u] * (1.0 / sums[u])).astype(BF) for u in units}
        mixed = {u: nn(probs[u], keys[u]) for u in units}
        for g, t in enumerate(tiles):
            base = pl.multiple_of(t * TILE, TILE)
            for h in range(z.heads):
                held.p[t * z.heads + h] = probs[g, h]
            pair = jnp.where(lane < TILE, pltpu.roll(mixed[g, 0], TILE, 1), mixed[g, 1]).astype(BF)
            single = pltpu.roll(mixed[g, 2], TILE, 1)
            held.o[pl.ds(base, TILE), 0:LANES] = pair
            held.o[pl.ds(base, TILE), LANES:] = single.astype(BF)
            s.pair_all[me, pl.ds(base, TILE), :] = pair
            if g % 2 == 0:
                even = single
            else:
                couple = pl.ds(pl.multiple_of((t - 1) * (TILE // 2), TILE), TILE)
                s.single_all[me, couple, :] = jnp.where(lane < TILE, even, mixed[g, 2]).astype(BF)

    e.turn(layer, "attend")
    half_rows = z.block // 2

    def pair_spread(b):
        return Spread(
            me,
            lambda owner, half: s.pair_all.at[owner, pl.ds(b * z.block + half * half_rows, half_rows), :],
            lambda i: s.o_ss.at[b * 12 + i],
            lambda i: s.o_rs.at[b * 12 + i],
        )

    def single_spread(b):
        return Spread(
            me,
            lambda owner, half: s.single_all.at[
                owner, pl.ds(b * half_rows + half * (half_rows // 2), half_rows // 2), :
            ],
            lambda i: s.o_ss.at[b * 12 + 6 + i],
            lambda i: s.o_rs.at[b * 12 + 6 + i],
        )

    def attend_block(b, _):
        attend([b * per_block + g for g in range(per_block)])
        pair_spread(b).start()
        single_spread(b).start()

        @pl.when(b > 0)
        def _():
            pair_spread(b - 1).forward()
            single_spread(b - 1).forward()

        return 0

    lax.fori_loop(0, z.T, attend_block, 0)
    pair_spread(z.T - 1).forward()
    single_spread(z.T - 1).forward()
    saver.save(held.p, outs["p"])
    saver.save(held.o, outs["o"])
    ready(4, 5)
    for step in range(1, z.T):
        wo_copy(step).wait()
    for t in range(z.T):
        s.wo_high[t, 0:TILE, :] = jnp.zeros((TILE, z.width), BF)
        s.wo_high[t, TILE:, :] = s.wo_all[t, LANES : LANES + TILE, :]
    collect = e.collect(0)

    def feed(k, _):
        step = visiting(k)
        block = partner(me, step)
        rows = pl.ds(pl.multiple_of(block * z.block, z.block), z.block)
        few = pl.ds(pl.multiple_of(block * half_rows, half_rows), half_rows)
        for other in range(1, z.T):
            pair_spread(block).wait(other)
            single_spread(block).wait(other)
        def joined(value, weight):
            return sum(
                nn(
                    jnp.concatenate([value(t), value(t + 1)], axis=1),
                    jnp.concatenate([weight(t), weight(t + 1)], axis=0),
                )
                for t in range(0, z.T, 2)
            )

        mixed = joined(lambda t: s.pair_all[t, rows, :], lambda t: s.wo_all[t, 0:LANES, :])
        even = joined(lambda t: s.single_all[t, few, :], lambda t: s.wo_all[t, LANES : 2 * LANES, :])
        odd = joined(lambda t: s.single_all[t, few, :], lambda t: s.wo_high[t])
        turns = []
        for i in range(per_block // 2):
            turns += [even[i * TILE : (i + 1) * TILE], odd[i * TILE : (i + 1) * TILE]]
        mixed += jnp.concatenate(turns, axis=0)
        middle = r_ref[rows, :].astype(F32) + mixed + vec[3:4, :]
        held.mid[...] = middle
        y, _ = normed(middle)
        n2 = (y * vec[4:5, :] + vec[5:6, :]).astype(BF)
        held.n2[rows, :] = n2
        u = nn(n2, used["wup"][...]) + vec[6:7, :]
        held.u[rows, :] = u.astype(BF)
        act = (0.5 * u * (1.0 + jnp.tanh(GELU_K * (u + GELU_A * u * u * u)))).astype(BF)
        held.act[rows, :] = act
        s.own_part[...] = nn(act, used["wdn"][...])

        collect.put(step, lambda: s.own_part[...])
        return 0

    lax.fori_loop(0, z.T, feed, 0)
    collect.join()
    if layer == 0:
        e.next_weights()
    e.turn(layer, "feed")
    for name in ("mid", "n2", "u", "act"):
        saver.save(getattr(held, name), outs[name])
    total = collect.total(held.mid[...] + s.own_part[...] + vec[7:8, :])
    own_rows = pl.ds(pl.multiple_of(me * z.block, z.block), z.block)
    res_ref[own_rows, :] = total.astype(BF)
    spread = Spread(
        me,
        lambda owner, half: res_ref.at[
            pl.ds(pl.multiple_of(owner * z.block + half * half_rows, half_rows), half_rows), :
        ],
        lambda i: s.res_ss.at[i],
        lambda i: s.res_rs.at[i],
    )
    e.arriving = spread
    if layer == 0:
        spread.start()
    collect.finish()

    def finish_block(b, _):
        pair_spread(b).finish()
        single_spread(b).finish()
        return 0

    lax.fori_loop(0, z.T, finish_block, 0)

    def sent(d, _):
        for copy in tile_copies(d, at):
            copy.wait_send()
        return 0

    lax.fori_loop(at + 1, z.S, sent, 0)

    @pl.when(at < last)
    def _():
        for copy in edge_copies():
            copy.wait_send()

    saver.finish()


def backward_part(z, layer, e):
    rt, used, s, me, at, core = e.routes[layer], e.used, e.s, e.me, e.at, e.core
    c_ref, grad_ref = (e.grad, e.cotan) if layer == 0 else (e.cotan, e.grad)
    k = e.held(layer)
    last = z.S - 1
    vec = e.vec(layer)
    own_rows = pl.ds(pl.multiple_of(me * z.block, z.block), z.block)
    W = z.width
    g_out = e.g_out
    across = {"section": 1 - core}

    def ready(*names):
        for name in names:
            if name in WEIGHTS:
                e.weight_ready(layer, WEIGHTS.index(name))
            else:
                e.kept_ready(layer, name)

    def done(*names):
        if layer == 1:
            for name in names:
                if name in WEIGHTS:
                    e.weight_again(WEIGHTS.index(name))
                else:
                    e.kept_again(name)

    collects = (e.collect(1), e.collect(2))
    half_rows = z.block // 2

    def rows_spread(ref, sends, recvs):
        return Spread(
            me,
            lambda owner, half: ref.at[
                pl.ds(pl.multiple_of(owner * z.block + half * half_rows, half_rows), half_rows), :
            ],
            lambda i: sends.at[i],
            lambda i: recvs.at[i],
        )

    if layer == 1:
        e.cotan_load.wait()
    ready("wdn", "u", "wup")

    def ff_back(i, _):
        step = visiting(i)
        rows = pl.ds(pl.multiple_of(partner(me, step) * z.block, z.block), z.block)
        u = k.u[rows, :].astype(F32)
        squared = u * u
        bent = jnp.tanh(GELU_K * (u + GELU_A * squared * u))
        slope = 0.5 * (1.0 + bent) + 0.5 * u * (1.0 - bent * bent) * (
            GELU_K * (1.0 + 3.0 * GELU_A * squared)
        )
        du = (nt(c_ref[rows, :], used["wdn"][...]) * slope).astype(BF)
        s.du[rows, :] = du
        s.own_part[...] = nt(du, used["wup"][...])

        collects[0].put(step, lambda: s.own_part[...])
        return 0

    lax.fori_loop(0, z.T, ff_back, 0)
    ones = jnp.ones((16, z.rows), BF)
    s.stat[...] = jnp.zeros((24, W), F32)

    mine = (s.pa, s.pb, s.pc, s.pd)
    theirs_part = (s.xa, s.xb, s.xc, s.xd)
    summed = (s.sa, s.sb, s.sc, s.sd)
    crossed = (s.ta, s.tb, s.tc, s.td)
    handed = (s.ha, s.hb, s.hc)

    def give(piece):
        return remote(
            mine[piece].at[1 - core if piece < 3 else 0], theirs_part[piece], s.give_ss.at[piece], s.give_rs.at[piece], across
        )

    def cross(piece, d, source):
        return remote(
            summed[piece].at[d],
            crossed[piece].at[source],
            s.cross_ss.at[piece, d],
            s.cross_rs.at[piece, source],
            {"seq": d},
        )

    stepwise = z.S == 4
    near_by, far_off = at + 1 - 2 * (at % 2), (at + 2) % z.S

    def hop(piece, i):
        block, target = ((near_by, near_by), ((near_by + 2) % z.S, near_by), (far_off, far_off))[i]
        return remote(
            summed[piece].at[block],
            crossed[piece].at[i],
            s.cross_ss.at[piece, i],
            s.cross_rs.at[piece, i],
            {"seq": target},
        )

    def relay(piece):
        if stepwise:
            hop(piece, 1).wait_recv()
            summed[piece][far_off] = (
                summed[piece][far_off].astype(F32) + crossed[piece][1].astype(F32)
            ).astype(BF)
            hop(piece, 2).start()

    def hand(piece):
        return remote(
            summed[piece].at[at], handed[piece], s.hand_ss.at[piece], s.hand_rs.at[piece], across
        )

    span = math.lcm(z.share, 16)

    def add_up(piece):
        give(piece).wait_recv()

        def chunk(i, _):
            rows = pl.ds(pl.multiple_of(i * span, span), span)
            value = mine[piece][core if piece < 3 else 0, rows, :].astype(F32) + theirs_part[piece][rows, :].astype(F32)
            for j in range(span // z.share):
                d = i * (span // z.share) + j
                rows_of = value[j * z.share : (j + 1) * z.share]
                if z.padded > z.share:
                    rows_of = jnp.concatenate(
                        [rows_of, jnp.zeros((z.padded - z.share, value.shape[1]), F32)], axis=0
                    )
                summed[piece][d] = rows_of.astype(BF)

                if not stepwise:

                    @pl.when(d != at)
                    def _():
                        cross(piece, d, at).start()

            return 0

        lax.fori_loop(0, W // span, chunk, 0)
        if stepwise:
            hop(piece, 0).start()
            hop(piece, 1).start()

    offsets = [sum(z.pieces[:piece]) for piece in range(len(z.pieces))]

    def reduce(piece):
        def wait(i, _):
            d = (at + i) % z.S
            cross(piece, d, d).wait_recv()
            return 0

        def add(i, running):
            return running + crossed[piece][(at + i) % z.S].astype(F32)

        if stepwise:
            hop(piece, 0).wait_recv()
            hop(piece, 2).wait_recv()
            total = (
                summed[piece][at].astype(F32) + crossed[piece][0].astype(F32) + crossed[piece][2].astype(F32)
            )
        else:
            lax.fori_loop(1, z.S, wait, 0)
            total = lax.fori_loop(1, z.S, add, summed[piece][at].astype(F32))
        cols = slice(offsets[piece], offsets[piece] + z.pieces[piece])

        @pl.when(core == layer)
        def _():
            g_out[core, :, cols] = total[: z.share]

        @pl.when(core != layer)
        def _():
            if piece < len(handed):
                summed[piece][at] = total.astype(BF)
                hand(piece).start()

    def crossed_over(piece):
        def one(i, _):
            cross(piece, (at + i) % z.S, at).wait_send()
            return 0

        if stepwise:
            for i in range(3):
                hop(piece, i).wait_send()
        else:
            lax.fori_loop(1, z.S, one, 0)

    def take(piece):
        cols = slice(offsets[piece], offsets[piece] + z.pieces[piece])

        @pl.when(core == layer)
        def _():
            hand(piece).wait_recv()
            g_out[1 - core, :, cols] = handed[piece][...].astype(F32)[: z.share]

    ready("act", "n2")
    wide = z.hidden // 2
    for cols in (slice(0, wide), slice(wide, z.hidden)):
        s.pa[0, :, cols] = tn(c_ref[...], k.act[:, cols]).astype(BF)
    collects[0].join()
    for cols in (slice(0, wide), slice(wide, z.hidden)):
        s.pa[1, :, cols] = tn(k.n2[...], s.du[:, cols]).astype(BF)
    give(0).start()
    done("wdn", "wup", "u", "act", "n2")
    s.stat[8:9, :] = nn(ones, s.du[...])[0:1]
    s.stat[9:10, :] = nn(ones, c_ref[...])[0:1]
    ready("mid", "wo")
    if layer == 0:
        e.leftover()
    add_up(0)
    grad = collects[0].total(s.own_part[...])
    y, spread = normed(k.mid[...])
    dr2 = c_ref[own_rows, :].astype(F32) + norm_back(grad, vec[4:5, :], y, spread)
    s.dr2[...] = dr2
    s.wo_all[me] = dr2.astype(BF)

    ob_spread = Spread(
        me,
        lambda owner, half: s.wo_all.at[owner, pl.ds(half * half_rows, half_rows), :],
        lambda i: s.ob_ss.at[i],
        lambda i: s.ob_rs.at[i],
    )
    ob_spread.start()
    done("mid")
    s.stat[0:1, :] = column_sum(dr2)
    s.stat[1:2, :] = column_sum(grad * y)
    s.stat[2:3, :] = column_sum(grad)
    s.dkv[...] = jnp.zeros((z.rows + TILE, z.pad), F32)
    ob_spread.forward()
    relay(0)
    lane_wide = grid_of((z.block, LANES), 1)

    def out_back(step, _):
        for wanted in range(1, z.T):

            @pl.when(step == wanted)
            def _(wanted=wanted):
                ob_spread.wait(wanted)

        rows = pl.ds(pl.multiple_of(partner(me, step) * z.block, z.block), z.block)
        dout = nt(s.wo_all[partner(me, step)], used["wo"][...])
        pair, single = dout[:, :LANES], dout[:, LANES:]
        for h, value in enumerate((pltpu.roll(pair, TILE, 1), pair, pltpu.roll(single, TILE, 1))):
            s.pair_all[h, rows, :] = jnp.where(lane_wide < TILE, 0.0, value).astype(BF)
        return 0

    lax.fori_loop(0, z.T, out_back, 0)
    done("wo")
    collects[0].finish()
    if layer == 1:
        e.arriving.start()
    ready("p", "q", "kvt", "ckv")

    ones_row = jnp.ones((16, TILE), BF)

    def attend_back(i, _):
        tiles = [i * group + g for g in range(group)]
        units = [(g, h) for g in range(group) for h in range(z.heads)]
        keys, query, dout, prob, dprob = {}, {}, {}, {}, {}
        for g, t in enumerate(tiles):
            base = pl.multiple_of(t * TILE, TILE)
            for h in range(z.heads):
                cols = slice(h * LANES, (h + 1) * LANES)
                far = k.ckv[rt[ARR, h * z.tiles + t]]
                near = k.kvt[pl.ds(h * (z.tiles + 1) + t, 2)].reshape(2 * TILE, LANES)
                keys[g, h] = jnp.concatenate([near, far, far], axis=0)
                query[g, h] = k.q[pl.ds(base, TILE), cols]
                dout[g, h] = s.pair_all[h, pl.ds(base, TILE), :]
                prob[g, h] = k.p[t * z.heads + h]
                dprob[g, h] = nt(dout[g, h], keys[g, h])
        totals = {u: jnp.sum(prob[u].astype(F32) * dprob[u], axis=-1, keepdims=True) for u in units}
        dz = {u: (prob[u].astype(F32) * (dprob[u] - totals[u])).astype(BF) for u in units}
        for g, t in enumerate(tiles):
            base = pl.multiple_of(t * TILE, TILE)
            for h in range(z.heads):
                cols = slice(h * LANES, (h + 1) * LANES)
                u = h * z.tiles + t
                s.dqkv[pl.ds(base, TILE), cols] = nn(dz[g, h], keys[g, h]).astype(BF)
                dkeys = tn(
                    jnp.concatenate([dz[g, h], prob[g, h]], axis=0),
                    jnp.concatenate([query[g, h], dout[g, h]], axis=0),
                )
                s.dkv[pl.ds(base, 2 * TILE), cols] += dkeys[: 2 * TILE]
                s.far[u] = dkeys[2 * TILE : 3 * TILE].astype(BF)
                gates = nn(ones_row, dz[g, h])[0:1]
                s.dgate[t, h : h + 1, :] = gates[:, :LANES]
                s.far_gate[u, 0:1, :] = gates[:, LANES:]
        return 0

    group = 4
    lax.fori_loop(0, z.tiles // group, attend_back, 0)
    done("p", "q", "kvt", "ckv")
    s.dgate[z.tiles] = jnp.zeros((8, LANES), F32)

    def edge_copies():
        behind = {"seq": jnp.maximum(at - 1, 0)}
        return (
            remote(s.edge_send, s.edge_got, s.back_edge_ss.at[0], s.back_edge_rs.at[0], behind),
            remote(s.dgate.at[0], s.edge_gate_got, s.back_edge_ss.at[1], s.back_edge_rs.at[1], behind),
        )

    @pl.when(at > 0)
    def _():
        s.edge_send[...] = s.dkv[0:TILE, :].astype(BF)
        for copy in edge_copies():
            copy.start()

    def tile_copies(d, source):
        return (
            remote(
                s.send_kv.at[d],
                s.got_kv.at[pl.ds(source * z.cap, z.cap)],
                s.back_kv_ss.at[d],
                s.back_kv_rs.at[source],
                {"seq": d},
            ),
            remote(
                s.back_send_gate.at[d], s.back_got_gate.at[source], s.back_gate_ss.at[d], s.back_gate_rs.at[source], {"seq": d}
            ),
        )

    def pack(d, _):
        def slot(i, _):
            u = rt[INV, d * z.cap + i]
            s.send_kv[d, i] = s.far[u]
            s.back_send_gate[d, pl.ds(i, 1), :] = s.far_gate[u][0:1]
            return 0

        lax.fori_loop(0, z.cap, slot, 0)
        for copy in tile_copies(d, at):
            copy.start()
        return 0

    lax.fori_loop(0, at, pack, 0)
    if layer == 1:
        e.arriving.forward()
    ready("o")
    out_grad = tn(s.wo_all[...].reshape(z.rows, W), k.o[...]).astype(BF)
    done("o")
    s.pb[0] = out_grad[:, :LANES]
    s.pb[1] = out_grad[:, LANES:]
    give(1).start()
    s.sum[z.n] = jnp.zeros((TILE, LANES), F32)
    s.gate_sum[z.n] = jnp.zeros((8, LANES), F32)
    ready("st", "w1", "swt", "n1")

    @pl.when(at < last)
    def _():
        for copy in edge_copies():
            copy.wait_recv()
        s.dkv[pl.ds(z.rows, TILE), :] += s.edge_got[...].astype(F32)
        s.dgate[z.tiles] = s.edge_gate_got[...]

    def landed(source, _):
        for copy in tile_copies(0, source):
            copy.wait_recv()
        for i in range(z.cap):
            s.got_gate_row[source * z.cap + i, 0:1, :] = s.back_got_gate[source, i : i + 1, :]
        return 0

    lax.fori_loop(at + 1, z.S, landed, 0)

    def gather(i, carry):
        running, gates = carry
        index = rt[ORD, i]
        joined = rt[CONT, i].astype(F32)
        running = running * joined + s.got_kv[index].astype(F32)
        gates = gates * joined + s.got_gate_row[index]
        s.sum[i] = running
        s.gate_sum[i] = gates
        return running, gates

    lax.fori_loop(0, z.n, gather, (jnp.zeros((TILE, LANES), F32), jnp.zeros((8, LANES), F32)))

    def settle(t, _):
        base = pl.multiple_of((t + 1) * TILE, TILE)
        rows = pl.ds(pl.multiple_of(t * TILE, TILE), TILE)
        for h in range(z.heads):
            cols = slice(h * LANES, (h + 1) * LANES)
            index = rt[LAST, h * z.tiles + t]
            s.dqkv[rows, z.pad + h * LANES : z.pad + (h + 1) * LANES] = (
                s.dkv[pl.ds(base, TILE), cols] + s.sum[index]
            ).astype(BF)
            s.tile_gate[t, h : h + 1, :] = s.gate_sum[index][0:1]
        return 0

    lax.fori_loop(0, z.tiles, settle, 0)
    if layer == 1:
        for step in range(1, z.T):
            e.arriving.wait(step)
        e.arriving.finish()
        e.deliver(1, e.rows, e.layer_out)
    lane = grid_of((8, LANES), 1)
    head_row = grid_of((8, LANES), 0)
    for i in range(z.tiles // 2):
        halves = []
        for t in (2 * i, 2 * i + 1):
            halves.append(pltpu.roll(s.dgate[t], TILE, 1) + s.dgate[t + 1] + s.tile_gate[t])
        joint = jnp.where(lane < TILE, halves[0], pltpu.roll(halves[1], TILE, 1))
        score = k.st[:, i * LANES : (i + 1) * LANES]
        grads = jnp.where(head_row < z.heads, joint / (1.0 + jnp.exp(score)), 0.0)
        s.ds[0:8, i * LANES : (i + 1) * LANES] = grads
        s.ds[8:16, i * LANES : (i + 1) * LANES] = jnp.zeros((8, LANES), F32)

    def in_back(i, _):
        step = visiting(i)
        rows = pl.ds(pl.multiple_of(partner(me, step) * z.block, z.block), z.block)
        s.own_part[...] = nt(s.dqkv[rows, :], used["w1"][...]) + tn(
            s.ds[:, rows].astype(BF), used["swt"][...]
        )

        collects[1].put(step, lambda: s.own_part[...])
        return 0

    lax.fori_loop(0, z.T, in_back, 0)
    done("st", "w1", "swt")
    s.pc[0] = tn(k.n1[...], s.dqkv[:, z.pad :]).astype(BF)
    collects[1].join()
    queries = tn(k.n1[...], s.dqkv[:, : z.pad])
    lane_full = grid_of((W, LANES), 1)
    s.pc[1, :, :LANES] = jnp.where(
        lane_full < TILE, queries[:, :LANES], pltpu.roll(queries[:, LANES : 2 * LANES], TILE, 1)
    ).astype(BF)
    s.pc[1, :, LANES : 2 * LANES] = queries[:, 2 * LANES :].astype(BF)
    s.pc[1, :, 2 * LANES :] = jnp.zeros((W, z.pad - 2 * LANES), BF)
    give(2).start()
    s.stat[10:13, :] = nn(s.ds[...].astype(BF), k.n1[...])[0:3]
    done("n1")
    source, target = grid_of((W, 1), 0), grid_of((1, W), 1)
    is_value = source >= z.pad
    index = jnp.where(is_value, source - z.pad, source)
    index = index // LANES * TILE + index % TILE
    each = z.heads * TILE // z.S
    wanted = index // each * z.share + index % each + jnp.where(is_value, each, 0)
    filled = (source % LANES >= TILE) == is_value
    wanted = jnp.where(filled, wanted, -1)
    spread_out = jnp.where(wanted == target, jnp.where(is_value, 1.0, TILE**-0.5), 0.0).astype(BF)
    s.stat[13:14, :] = nn(nn(ones, s.dqkv[...]).astype(BF), spread_out)[0:1]
    reduce(0)
    add_up(1)
    add_up(2)
    grad = collects[1].total(s.own_part[...])
    if layer == 1:
        entry = e.middle[own_rows, :]
    else:
        e.entry_load.wait()
        entry = s.entry[...]
    y, spread = normed(entry.astype(F32))
    dr = s.dr2[...] + norm_back(grad, vec[0:1, :], y, spread)
    grad_ref[own_rows, :] = dr.astype(BF)
    grad_spread = rows_spread(grad_ref, s.grad_ss, s.grad_rs)
    s.stat[3:4, :] = column_sum(grad * y)
    s.stat[4:5, :] = column_sum(grad)

    def stat_copy(step):
        return remote(
            s.stat.at[pl.ds(0, 8), :],
            s.stat_got.at[step - 1],
            s.stat_ss.at[step],
            s.stat_rs.at[step],
            to_tensor(step, me),
        )

    for step in range(1, z.T):
        stat_copy(step).start()
    grad_spread.start()
    shared = s.stat[0:8, :]
    for step in range(1, z.T):
        stat_copy(step).wait()
        shared += s.stat_got[step - 1]
    stats = jnp.concatenate([shared, s.stat[8:16, :]], axis=0).astype(BF)
    unit = (grid_of((16, LANES), 0) == grid_of((16, LANES), 1)).astype(F32).astype(BF)
    s.pd[0] = tn(stats, unit).astype(BF)

    @pl.when(core != layer)
    def _():
        give(3).start()

    grad_spread.forward()
    relay(1)
    relay(2)

    @pl.when(core == layer)
    def _():
        add_up(3)

    for step in range(z.T):
        grad_spread.wait(step)
        if layer == 0:
            e.deliver_block(grad_ref, step)

    if layer == 1:
        e.deliver(1, grad_ref, e.input_grad)
    def settle_sums():
        reduce(1)
        take(0)
        take(1)

        @pl.when(core == layer)
        def _():
            relay(3)

        reduce(2)
        take(2)

        @pl.when(core == layer)
        def _():
            reduce(3)
            crossed_over(3)

        @pl.when(core != layer)
        def _():
            give(3).wait_send()
            for piece in range(3):
                hand(piece).wait_send()

        for piece in range(3):
            crossed_over(piece)

    for piece in range(3):
        give(piece).wait_send()
    if layer == 1:
        e.leftover = settle_sums
    else:
        settle_sums()
    collects[1].finish()
    ob_spread.finish()
    grad_spread.finish()

    def sent(d, _):
        for copy in tile_copies(d, at):
            copy.wait_send()
        return 0

    lax.fori_loop(0, at, sent, 0)

    @pl.when(at > 0)
    def _():
        for copy in edge_copies():
            copy.wait_send()


class Unsaved:
    def save(self, src, dst):
        pass

    def finish(self):
        pass


class Env:
    pass


def layers_kernel(z, names, *refs):
    count = len(WEIGHTS)
    e = Env()
    e.routes, refs = refs[:2], refs[2:]
    tokens, cotangent, refs = refs[0], refs[1], refs[2:]
    own, refs = dict(zip(WEIGHTS, refs[:count])), refs[count:]
    e.layer_out, e.input_grad, e.g_out, refs = refs[0], refs[1], refs[2], refs[3:]
    theirs, refs = dict(zip(WEIGHTS, refs[:count])), refs[count:]
    e.store, refs = dict(zip(KEPT, refs[: len(KEPT)])), refs[len(KEPT) :]
    e.used, refs = dict(zip(WEIGHTS, refs[:count])), refs[count:]
    held, refs = dict(zip(KEPT, refs[: len(KEPT)])), refs[len(KEPT) :]
    s = e.s = Refs(names, refs)
    e.rows, e.middle, e.cotan, e.grad = s.rows, s.middle, s.cotan, s.grad
    me, at, core = e.me, e.at, e.core = lax.axis_index("tensor"), lax.axis_index("seq"), lax.axis_index("section")
    across = {"section": 1 - core}
    own_rows = pl.ds(pl.multiple_of(me * z.block, z.block), z.block)
    e.input_load = pltpu.make_async_copy(tokens.at[core], s.rows, s.load.at[0])
    e.cotan_load = pltpu.make_async_copy(cotangent.at[core], s.cotan, s.load.at[1])
    e.entry_load = pltpu.make_async_copy(tokens.at[core].at[own_rows, :], s.entry, s.load.at[2])
    e.input_load.start()

    def vec(layer):
        return e.used["vec"].at[layer]

    def chosen_keys(layer):
        return s.ckv_next if layer == 1 else held["ckv"]

    def held_in(layer):
        return Refs(KEPT, [chosen_keys(layer) if name == "ckv" else held[name] for name in KEPT])

    e.vec, e.held = vec, held_in

    def load(layer, i, source):
        name = WEIGHTS[i]
        target = e.used[name].at[layer] if name == "vec" else e.used[name]
        return pltpu.make_async_copy(source[name], target, s.weight_load.at[i])

    e.load = load

    def swap(i):
        name = WEIGHTS[i]
        return remote(own[name], theirs[name], s.swap_ss.at[i], s.swap_rs.at[i], across)

    def start_weight(layer, i):
        @pl.when(core == layer)
        def _():
            load(layer, i, own).start()

        @pl.when(core != layer)
        def _():
            load(layer, i, theirs).start()

    loaded = {0: set(), 1: set()}
    pending = {}

    def weight_ready(layer, i):
        if layer == 0 and i not in loaded[0]:

            @pl.when(core != layer)
            def _():
                swap(i).wait_recv()
                load(layer, i, theirs).start()

            loaded[0].add(i)
            load(layer, i, own).wait()
        elif pending.pop((layer, i), False):
            load(layer, i, own).wait()

    def next_weights():
        @pl.when(core == 0)
        def _():
            for i in range(count):
                swap(i).wait_recv()

        for i in range(count):
            start_weight(1, i)
            pending[1, i] = True

    def weight_again(i):
        if WEIGHTS[i] != "vec":
            start_weight(0, i)
            pending[0, i] = True

    e.weight_ready, e.next_weights, e.weight_again = weight_ready, next_weights, weight_again
    kept_pending = {}

    def kept_load(name):
        return pltpu.make_async_copy(e.store[name], held[name], s.kept_load.at[KEPT.index(name)])

    def kept_again(name):
        if name != "ckv":
            kept_load(name).start()
            kept_pending[name] = True

    def kept_ready(layer, name):
        if kept_pending.pop(name, False):
            kept_load(name).wait()

    e.kept_again, e.kept_ready = kept_again, kept_ready

    def collect(phase):
        return Collect(
            z,
            me,
            s.part_send,
            s.part_got.at[phase % 2],
            s.part_via.at[phase % 2],
            lambda i: s.part_ss.at[phase, i],
            lambda i: s.part_rs.at[phase, i],
        )

    e.collect = collect
    delivered = []

    def rows_to(ref, target, slot, part):
        local = pltpu.make_async_copy(ref.at[part, :], target.at[core].at[part, :], s.keep.at[slot])
        return local, remote(
            ref.at[part, :], target.at[core].at[part, :], s.move_ss.at[slot], s.move_rs.at[slot], across
        )

    everything = pl.ds(0, z.rows)

    def deliver(layer, ref, target):
        slot = len(delivered)
        local, away = rows_to(ref, target, slot, everything)

        @pl.when(core == layer)
        def _():
            local.start()

        @pl.when(core != layer)
        def _():
            away.start()

        delivered.append((layer, local, away))

    def deliver_block(ref, step):
        slot = len(delivered)
        part = pl.ds(pl.multiple_of(partner(me, step) * z.block, z.block), z.block)
        local, away = rows_to(ref, target=e.input_grad, slot=slot, part=part)

        @pl.when(core == 0)
        def _():
            local.start()

        @pl.when(core == 1)
        def _():
            away.start()

        delivered.append((0, local, away))

    e.deliver, e.deliver_block = deliver, deliver_block

    def turn(layer, where):
        if (layer, where) == TURN_FROM:

            @pl.when(core == 0)
            def _():
                pl.semaphore_signal(s.turn, inc=1, device_id=across, device_id_type=MESH)

        if (layer, where) == TURN_TO:

            @pl.when(core == 1)
            def _():
                pl.semaphore_wait(s.turn, 1)

    e.turn = turn

    @pl.when(core == 0)
    def _():
        for i in range(count):
            load(0, i, own).start()

    barrier = pltpu.get_barrier_semaphore()
    for step in range(1, z.T):
        signal(to_tensor(step, me), barrier)
    signal(across, barrier)

    def greet(i, _):
        signal({"seq": (at + i) % z.S}, barrier)
        return 0

    lax.fori_loop(1, z.S, greet, 0)
    pl.semaphore_wait(barrier, z.T - 1 + 1 + z.S - 1)
    for i in range(count):
        swap(i).start()
    e.cotan_load.start()
    e.entry_load.start()
    forward_part(z, 0, e)
    forward_part(z, 1, e)
    backward_part(z, 1, e)
    backward_part(z, 0, e)
    for i in range(count):
        swap(i).wait_send()
    for layer, local, away in delivered:

        @pl.when(core == layer)
        def _(local=local, away=away):
            local.wait()
            away.wait_recv()

        @pl.when(core != layer)
        def _(away=away):
            away.wait_send()


TURN_FROM, TURN_TO = (0, "attend"), (0, "pack")


def layers(z, routes, tokens, cotangent, own):
    rows, width, heads = z.rows, z.width, z.heads
    half = z.block // 2
    kept = dict(
        n1=((rows, width), BF),
        q=((rows, z.pad), BF),
        kvt=((heads * (z.tiles + 1), TILE, LANES), BF),
        st=((8, rows), F32),
        p=((z.slots, TILE, 2 * LANES), BF),
        ckv=((z.n, TILE, LANES), BF),
        o=((rows, 2 * LANES), BF),
        mid=((z.block, width), F32),
        n2=((rows, width), BF),
        u=((rows, z.hidden), BF),
        act=((rows, z.hidden), BF),
    )
    weights = [own[name] for name in WEIGHTS]
    vmem_of, dma = pltpu.VMEM, pltpu.SemaphoreType.DMA
    scratch = dict(
        rows=vmem_of((rows, width), BF),
        middle=vmem_of((rows, width), BF),
        cotan=vmem_of((rows, width), BF),
        grad=vmem_of((rows, width), BF),
        entry=vmem_of((z.block, width), BF),
        ckv_next=vmem_of((z.n, TILE, LANES), BF),
        gt=vmem_of((8, rows + 2 * LANES), F32),
        gate=vmem_of((heads * (z.tiles + 1), 8, LANES), F32),
        edge=vmem_of((2, heads, TILE, LANES), BF),
        edge_gate=vmem_of((2, 8, LANES), F32),
        send_kv=vmem_of((z.S, z.cap, TILE, LANES), BF),
        send_gate=vmem_of((z.S, z.capg, LANES), F32),
        got_gate=vmem_of((2, z.S, z.capg, LANES), F32),
        far_gate=vmem_of((max(z.n, z.slots), 8, LANES), F32),
        wo_all=vmem_of((z.T, max(2 * LANES, z.block), width), BF),
        wo_high=vmem_of((z.T, LANES, width), BF),
        pair_all=vmem_of((z.T, rows, LANES), BF),
        single_all=vmem_of((z.T, rows // 2, LANES), BF),
        part_send=vmem_of((z.T - 1, z.block, width), BF),
        part_got=vmem_of((2, 2, z.block, width), BF),
        part_via=vmem_of((2, 2, half, width), BF),
        own_part=vmem_of((z.block, width), F32),
        du=vmem_of((rows, z.hidden), BF),
        dr2=vmem_of((z.block, width), F32),
        dqkv=vmem_of((rows, 2 * z.pad), BF),
        dkv=vmem_of((rows + TILE, z.pad), F32),
        dgate=vmem_of((z.tiles + 1, 8, LANES), F32),
        far=vmem_of((z.slots, TILE, LANES), BF),
        back_send_gate=vmem_of((z.S, z.capg, LANES), F32),
        got_kv=vmem_of((z.n, TILE, LANES), BF),
        back_got_gate=vmem_of((z.S, z.capg, LANES), F32),
        got_gate_row=vmem_of((z.n, 8, LANES), F32),
        edge_send=vmem_of((TILE, z.pad), BF),
        edge_got=vmem_of((TILE, z.pad), BF),
        edge_gate_got=vmem_of((8, LANES), F32),
        sum=vmem_of((z.n + 1, TILE, LANES), F32),
        gate_sum=vmem_of((z.n + 1, 8, LANES), F32),
        tile_gate=vmem_of((z.tiles, 8, LANES), F32),
        ds=vmem_of((16, rows), F32),
        stat=vmem_of((24, width), F32),
        stat_got=vmem_of((z.T - 1, 8, width), F32),
    )
    for name, w in zip("abcd", z.pieces):
        scratch["p" + name] = vmem_of((1 if name == "d" else 2, width, w), BF)
        scratch["x" + name] = vmem_of((width, w), BF)
        scratch["s" + name] = vmem_of((z.S, z.padded, w), BF)
        scratch["t" + name] = vmem_of((z.S, z.padded, w), BF)
        if name != "d":
            scratch["h" + name] = vmem_of((z.padded, w), BF)
    pairs = dict(
        kv=(2, z.S), gate=(2, z.S), edge=(2, heads + 1), wo=(z.T,), o=(z.T * 12,), part=(3, 6), res=(6,),
        swap=(len(WEIGHTS),), move=(3 + z.T,), back_kv=(z.S,), back_gate=(z.S,), back_edge=(2,), ob=(6,),
        grad=(6,), stat=(z.T,), give=(4,), cross=(4, z.S), hand=(3,),
    )
    for name, shape in pairs.items():
        scratch[name + "_ss"] = dma(shape)
        scratch[name + "_rs"] = dma(shape)
    scratch |= dict(
        load=dma((3,)),
        weight_load=dma((len(WEIGHTS),)),
        kept_load=dma((len(KEPT),)),
        saved=dma((len(KEPT),)),
        keep=dma((3 + z.T,)),
        turn=pltpu.SemaphoreType.REGULAR,
    )
    doubled = {"vec"}

    def room(name, shape, kind):
        return vmem_of((2, *shape) if name in doubled else shape, kind)

    shaped = (
        jax.ShapeDtypeStruct((2, rows, width), BF),
        jax.ShapeDtypeStruct((2, rows, width), BF),
        jax.ShapeDtypeStruct((2, z.share, sum(z.pieces)), F32),
        *(jax.ShapeDtypeStruct(value.shape, value.dtype) for value in weights),
        *(jax.ShapeDtypeStruct(*kept[name]) for name in KEPT),
    )
    outs = pl.pallas_call(
        functools.partial(layers_kernel, z, tuple(scratch)),
        out_shape=shaped,
        in_specs=[smem(), smem()] + [anywhere()] * (2 + len(weights)),
        out_specs=tuple(vmem() if i == 2 else anywhere() for i in range(len(shaped))),
        scratch_shapes=[
            *(room(name, value.shape, value.dtype) for name, value in zip(WEIGHTS, weights)),
            *(room(name, *kept[name]) for name in KEPT),
            *scratch.values(),
        ],
        compiler_params=pltpu.CompilerParams(
            collective_id=0, has_side_effects=True, vmem_limit_bytes=LIMIT
        ),
        name="layers",
    )(*routes, tokens, cotangent, *weights)
    return outs[:3]


UNPACKED = (
    "input_weight", "input_bias", "score", "out", "out_bias", "up", "up_bias", "down", "down_bias", "gain", "shift",
)


def unpack_kernel(z, head, total_ref, out_any, grad_any, *refs):
    count = len(UNPACKED)
    out, rows_out, buffers, sems = Refs(UNPACKED, refs[:count]), refs[count : count + 2], refs[count + 2 : count + 4], refs[-1]
    loads = [
        pltpu.make_async_copy(src, buffer, sems.at[i]) for i, (src, buffer) in enumerate(zip((out_any, grad_any), buffers))
    ]
    stores = [
        pltpu.make_async_copy(buffer, dst, sems.at[2 + i]) for i, (buffer, dst) in enumerate(zip(buffers, rows_out))
    ]
    for load in loads:
        load.start()
    for load, store in zip(loads, stores):
        load.wait()
        store.start()
    core = lax.axis_index("section")
    inner, hidden, share = z.heads * head, z.hidden, z.share
    c_o, c_i = hidden, hidden + LANES
    c_s = c_i + z.pad
    out.up[...] = total_ref[1, :, :hidden]
    out.down[...] = total_ref[0, :, :hidden]
    first, second = total_ref[0, :, c_o:c_i].T, total_ref[1, :, c_o:c_i].T
    out.out[0:LANES, :] = first
    out.out[LANES:inner, :] = second[: inner - LANES]
    out.input_weight[0] = head**-0.5 * total_ref[1, :, c_i : c_i + inner]
    lane = grid_of((share, LANES), 1)
    pairs = [total_ref[0, :, c_i + h * LANES : c_i + (h + 1) * LANES] for h in range(z.heads)]
    turned = [pltpu.roll(pair, LANES // 2, 1) for pair in pairs]
    out.input_weight[1, :, 0:LANES] = jnp.where(lane < head, pairs[0], turned[1])
    out.input_weight[1, :, LANES:inner] = pairs[2][:, :head]
    out.input_weight[2, :, 0:LANES] = jnp.where(lane < head, turned[0], pairs[1])
    out.input_weight[2, :, LANES:inner] = turned[2][:, :head]
    stats = total_ref[core, :, c_s : c_s + LANES]
    rows = stats.T
    out.score[...] = rows[10 : 10 + z.heads]
    each = inner // z.S
    out.input_bias[0:1, :] = rows[13:14, :each]
    out.input_bias[1:2, :] = pltpu.roll(rows[8:16], share - each, 1)[5:6, :each]
    out.out_bias[...] = rows[0:1]
    out.up_bias[...] = rows[8:9]
    out.down_bias[...] = rows[9:10]
    out.gain[0:1, :] = rows[3:4]
    out.gain[1:2, :] = rows[1:2]
    out.shift[0:1, :] = rows[4:5]
    out.shift[1:2, :] = rows[2:3]
    for store in stores:
        store.wait()


def unpack(z, head, total, layer_out, input_grad):
    inner, hidden, share = z.heads * head, z.hidden, z.share
    shapes = (
        (3, share, inner), (2, inner // z.S), (z.heads, share), (inner, share), (1, share), (share, hidden), (1, share),
        (share, hidden), (1, share), (2, share), (2, share),
    )
    outs = pl.pallas_call(
        functools.partial(unpack_kernel, z, head),
        out_shape=(
            *(jax.ShapeDtypeStruct(shape, F32) for shape in shapes),
            jax.ShapeDtypeStruct(layer_out.shape, BF),
            jax.ShapeDtypeStruct(input_grad.shape, BF),
        ),
        in_specs=[vmem(), anywhere(), anywhere()],
        out_specs=(*(vmem() for _ in shapes), anywhere(), anywhere()),
        scratch_shapes=[
            pltpu.VMEM(layer_out.shape, BF),
            pltpu.VMEM(input_grad.shape, BF),
            pltpu.SemaphoreType.DMA((4,)),
        ],
        compiler_params=pltpu.CompilerParams(vmem_limit_bytes=LIMIT),
        name="unpack",
    )(total, layer_out, input_grad)
    return dict(zip(UNPACKED, outs)), outs[-2], outs[-1]


def swapped(value):
    return lax.ppermute(value, "section", [(0, 1), (1, 0)])


def body(
    tokens,
    cotangent,
    lengths,
    selected,
    input_weight,
    input_bias,
    score_weight,
    output_weight,
    output_bias,
    up_weight,
    up_bias,
    down_weight,
    down_bias,
    norm_gain,
    norm_bias,
):
    core = lax.axis_index("section")
    _, rows, width = tokens.shape
    heads, hidden = score_weight.shape[2], up_weight.shape[2]
    head = input_weight.shape[3] // heads
    inner = heads * head
    z = Sizes(lax.axis_size("tensor"), lax.axis_size("seq"), rows, width, heads, hidden)
    scale = head**-0.5
    grouped = (
        selected[0].reshape(2, heads, z.S, z.tiles).transpose(0, 2, 1, 3).reshape(2, z.S, z.slots)
    )
    kept_choice = lax.dynamic_index_in_dim(grouped, core, 0, keepdims=False)
    got_choice = swapped(lax.dynamic_index_in_dim(grouped, 1 - core, 0, keepdims=False))
    own, routes = prepare(
        z,
        lengths,
        kept_choice,
        got_choice,
        input_weight[0].transpose(1, 0, 2),
        input_bias[0],
        score_weight[0].T,
        output_weight[0],
        output_bias,
        up_bias,
        down_bias,
        norm_gain[0],
        norm_bias[0],
    )
    own |= dict(wup=up_weight[0], wdn=down_weight[0])
    layer_out, input_grad, total = layers(z, routes, tokens, cotangent, own)
    parts, layer_out, input_grad = unpack(z, head, total, layer_out, input_grad)
    parts["down"], parts["score"] = parts["down"].T, parts["score"].T
    parts["input_weight"] = parts["input_weight"].transpose(1, 0, 2)
    return (layer_out[None], input_grad[None], *(part.reshape(1, *shape) for part, shape in (
        (parts["input_weight"], (z.share, 3, inner)),
        (parts["input_bias"], (2, inner // z.S)),
        (parts["score"], (z.share, heads)),
        (parts["out"], (inner, z.share)),
        (parts["out_bias"], (z.share,)),
        (parts["up"], (z.share, hidden)),
        (parts["up_bias"], (z.share,)),
        (parts["down"], (hidden, z.share)),
        (parts["down_bias"], (z.share,)),
        (parts["gain"], (2, z.share)),
        (parts["shift"], (2, z.share)),
    )))


def solution(mesh):
    return jax.shard_map(
        body,
        mesh=mesh,
        in_specs=(
            P(None, "seq", None),
            P(None, "seq", None),
            P(),
            P("section", None, "tensor", None),
            P("section", None, None, "tensor"),
            P("section", None, "tensor"),
            P("section", None, "tensor"),
            P("section", "tensor", None),
            P("section", None),
            P("section", None, "tensor"),
            P("section", "tensor"),
            P("section", "tensor", None),
            P("section", None),
            P("section", None, None),
            P("section", None, None),
        ),
        out_specs=(
            P("section", None, "seq", None),
            P("section", None, "seq", None),
            P("section", "seq", None, "tensor"),
            P("section", None, ("tensor", "seq")),
            P("section", "seq", "tensor"),
            P("section", "tensor", "seq"),
            P("section", "seq"),
            P("section", "seq", "tensor"),
            P("section", ("tensor", "seq")),
            P("section", "tensor", "seq"),
            P("section", "seq"),
            P("section", None, "seq"),
            P("section", None, "seq"),
        ),
        check_vma=False,
    )
```

```python
import functools
import math

import jax
import jax.numpy as jnp
from jax import lax
from jax.experimental import pallas as pl
from jax.experimental.pallas import tpu as pltpu
from jax.sharding import PartitionSpec as P

TILE = 64
LANES = 128
MASKED = -1e30
EPSILON = 1e-05
FAR = -(1 << 20)
MESH = pl.DeviceIdType.MESH
BF = jnp.bfloat16
F32 = jnp.float32
GELU_A = 0.044715
GELU_K = math.sqrt(2.0 / math.pi)
LIMIT = 62 * 1024 * 1024


class Sizes:
    def __init__(self, mesh_tensor, mesh_seq, rows, width, heads, hidden):
        self.T, self.S = mesh_tensor, mesh_seq
        self.rows, self.width, self.heads, self.hidden = rows, width, heads, hidden
        self.tiles = rows // TILE
        self.slots = heads * self.tiles
        self.cap = -(-self.slots // (mesh_seq - 1))
        self.capg = -(-self.cap // 8) * 8
        self.n = mesh_seq * self.cap
        self.block = rows // mesh_tensor
        self.pad = heads * LANES
        self.share = width // mesh_seq
        self.padded = -(-self.share // 16) * 16
        self.pieces = (hidden, LANES, self.pad, LANES)


SEND, INV, ORD, CONT, ARR, POS, LAST, ENDS = range(8)
WEIGHTS = ("vec", "w1", "swt", "wo", "wup", "wdn")
KEPT = ("n1", "q", "kvt", "st", "p", "ckv", "o", "mid", "n2", "u", "act")


def nn(a, b):
    return jnp.dot(a, b, preferred_element_type=F32)


def nt(a, b):
    return lax.dot_general(a, b, (((1,), (1,)), ((), ())), preferred_element_type=F32)


def tn(a, b):
    return lax.dot_general(a, b, (((0,), (0,)), ((), ())), preferred_element_type=F32)


def normed(x):
    centred = x - jnp.mean(x, axis=-1, keepdims=True)
    spread = lax.rsqrt(jnp.mean(centred * centred, axis=-1, keepdims=True) + EPSILON)
    return centred * spread, spread


def norm_back(grad, gain, y, spread):
    scaled = grad * gain
    return spread * (
        scaled
        - jnp.mean(scaled, axis=-1, keepdims=True)
        - y * jnp.mean(scaled * y, axis=-1, keepdims=True)
    )


def partner(me, step):
    return (me // 2 + step // 2) % 2 * 2 + (me % 2 + step % 2) % 2


def column_sum(x):
    return jnp.sum(x, axis=0, keepdims=True)


def smem():
    return pl.BlockSpec(memory_space=pltpu.SMEM)


def vmem():
    return pl.BlockSpec(memory_space=pltpu.VMEM)


def anywhere():
    return pl.BlockSpec(memory_space=pl.ANY)


def grid_of(shape, axis):
    return lax.broadcasted_iota(jnp.int32, shape, axis)


def prepare_kernel(
    z,
    length_ref,
    kept_ref,
    got_ref,
    win_ref,
    bin_ref,
    sw_ref,
    wout_ref,
    bout_ref,
    bup_ref,
    bdn_ref,
    gain_ref,
    shift_ref,
    vec_ref,
    w1_ref,
    swt_ref,
    wo_ref,
    rt0_ref,
    rt1_ref,
):
    inner, head = win_ref.shape[2], win_ref.shape[2] // z.heads
    row, col = grid_of((inner, z.pad), 0), grid_of((inner, z.pad), 1)
    lane_of = row // head * LANES + row % head
    first = (col == lane_of).astype(F32)
    second = (col == lane_of + head).astype(F32)
    low, high = first.astype(BF), second.astype(BF)
    scaled = (first * head**-0.5).astype(BF)
    w1_ref[:, : z.pad] = nn(win_ref[0], scaled).astype(BF)
    w1_ref[:, z.pad :] = (nn(win_ref[1], low) + nn(win_ref[2], high)).astype(BF)
    vec_ref[0:1, :] = gain_ref[...].astype(F32)[0:1]
    vec_ref[1:2, :] = shift_ref[...].astype(F32)[0:1]
    vec_ref[2:3, : z.pad] = nn(bin_ref[...], scaled)[0:1]
    vec_ref[2:3, z.pad :] = nn(bin_ref[...], high)[1:2]
    vec_ref[3:4, :] = bout_ref[...].astype(F32)
    vec_ref[4:5, :] = gain_ref[...].astype(F32)[1:2]
    vec_ref[5:6, :] = shift_ref[...].astype(F32)[1:2]
    vec_ref[6:7, :] = bup_ref[...].astype(F32)
    vec_ref[7:8, :] = bdn_ref[...].astype(F32)
    unit = (grid_of((16, z.heads), 0) == grid_of((16, z.heads), 1)).astype(F32).astype(BF)
    swt_ref[...] = nn(unit, sw_ref[...]).astype(BF)
    wo_ref[0:inner, :] = wout_ref[...]
    wo_ref[inner:, :] = jnp.zeros((2 * LANES - inner, z.width), BF)

    at, core = lax.axis_index("seq"), lax.axis_index("section")
    n, slots, cap = z.n, z.slots, z.cap
    first_end = length_ref[core, 0]
    second_end = first_end + length_ref[core, 1]
    shift = z.tiles.bit_length() - 1
    near = 1e-3

    def total(mask, value, axis):
        return jnp.sum(jnp.where(mask, value, 0.0), axis=axis, keepdims=True)

    def whole(x):
        return (x + near).astype(jnp.int32)

    for layer, rt in enumerate((rt0_ref, rt1_ref)):
        rt[...] = jnp.zeros((8, LANES), jnp.int32)
        chosen = jnp.where(core == layer, kept_ref[...], got_ref[...])
        owner = lax.shift_right_arithmetic(chosen, shift)
        sub, lan = grid_of((slots, n), 0), grid_of((slots, n), 1)
        wide = jnp.zeros((slots, n), jnp.int32)
        for d in range(z.S):
            column = jnp.sum(
                jnp.where(
                    grid_of((slots, slots), 0) == grid_of((slots, slots), 1),
                    chosen[d : d + 1].astype(F32) + 1.0,
                    0.0,
                ),
                axis=1,
                keepdims=True,
            )
            wide = jnp.where(lan // cap == d, whole(column) - 1, wide)
        mine = lax.shift_right_arithmetic(wide, shift) == at
        order = nn(
            (grid_of((slots, slots), 0) > grid_of((slots, slots), 1)).astype(F32), mine.astype(F32)
        )
        taken = mine & (whole(order) == lan % cap)
        head_of = sub // z.tiles
        inner_tile = wide - at * z.tiles
        rt[SEND : SEND + 1, :n] = whole(
            total(taken, (head_of * (z.tiles + 1) + inner_tile).astype(F32), 0)
        ) + 1
        present = jnp.sum(taken.astype(F32), axis=0, keepdims=True)
        key = total(taken, (head_of * z.tiles + inner_tile - slots).astype(F32), 0) + slots
        own = jnp.sum(
            jnp.where(grid_of((z.S, slots), 0) == at, chosen.astype(F32) + 1.0, 0.0), axis=0, keepdims=True
        )
        square_row, square_col = grid_of((slots, slots), 0), grid_of((slots, slots), 1)
        own_column = total(square_row == square_col, own, 1)
        own_row = whole(own) - 1
        own_col = whole(own_column) - 1
        owner_row = lax.shift_right_arithmetic(own_row, shift)
        owner_col = lax.shift_right_arithmetic(own_col, shift)
        same = owner_row == owner_col
        place_row = whole(jnp.sum((same & (square_row < square_col)).astype(F32), axis=0, keepdims=True))
        place_col = whole(jnp.sum((same & (square_col < square_row)).astype(F32), axis=1, keepdims=True))
        live = own_row >= 0
        rt[ARR : ARR + 1, :slots] = jnp.where(live, owner_row * cap + place_row, at * cap)
        rt[POS : POS + 1, :slots] = jnp.where(live, own_row * TILE, FAR)
        matched = (owner_col == lan // cap) & (place_col == lan % cap)
        rt[INV : INV + 1, :n] = whole(total(matched, sub.astype(F32), 0))
        big_row, big_col = grid_of((n, n), 0), grid_of((n, n), 1)
        key_col = total(big_row == big_col, key, 1)
        rank = jnp.sum(
            ((key < key_col) | ((key == key_col) & (big_col < big_row))).astype(F32), axis=1, keepdims=True
        )
        at_rank = whole(rank) == big_col
        rt[ORD : ORD + 1, :n] = whole(total(at_rank, big_row.astype(F32), 0))
        sorted_key = total(at_rank, key_col, 0)
        before = total(whole(rank) + 1 == big_col, key_col + 1.0, 0) - 1.0
        rt[CONT : CONT + 1, :n] = (sorted_key == before).astype(jnp.int32)
        tile = grid_of((n, slots), 1).astype(F32)
        upto = jnp.sum((key_col <= tile).astype(F32), axis=0, keepdims=True)
        has = jnp.sum((key_col == tile).astype(F32), axis=0, keepdims=True)
        rt[LAST : LAST + 1, :slots] = whole(jnp.where(has > 0.5, upto - 1.0, n * 1.0))
        rt[ENDS : ENDS + 1, :] = jnp.where(grid_of((1, LANES), 1) == 0, first_end, second_end)


def prepare(z, lengths, kept, got, win, bin_, sw, wout, bout, bup, bdn, gain, shift):
    table = jax.ShapeDtypeStruct((8, LANES), jnp.int32)
    outs = pl.pallas_call(
        functools.partial(prepare_kernel, z),
        out_shape=(
            jax.ShapeDtypeStruct((8, z.width), F32),
            jax.ShapeDtypeStruct((z.width, 2 * z.pad), BF),
            jax.ShapeDtypeStruct((16, z.width), BF),
            jax.ShapeDtypeStruct((2 * LANES, z.width), BF),
            table,
            table,
        ),
        in_specs=[smem()] + [vmem()] * 11,
        out_specs=tuple(vmem() for _ in range(6)),
        name="prepare",
    )(lengths, kept, got, win, bin_, sw, wout, bout, bup, bdn, gain, shift)
    return dict(zip(WEIGHTS[:4], outs)), outs[4:]


def to_tensor(step, me):
    return {"tensor": partner(me, step)}


def remote(src, dst, send, recv, target):
    return pltpu.make_async_remote_copy(
        src_ref=src, dst_ref=dst, send_sem=send, recv_sem=recv, device_id=target, device_id_type=MESH
    )


def signal(target, barrier):
    pl.semaphore_signal(barrier, inc=1, device_id=target, device_id_type=MESH)


class Spread:
    def __init__(self, me, view, sends, recvs):
        self.me, self.view, self.sends, self.recvs = me, view, sends, recvs

    def copy(self, i):
        me, x, y = self.me, partner(self.me, 1), partner(self.me, 2)
        owner, half, step = ((me, 0, 1), (me, 1, 2), (me, 1, 1), (me, 0, 2), (x, 0, 2), (y, 1, 1))[i]
        ref = self.view(owner, half)
        return remote(ref, ref, self.sends(i), self.recvs(i), to_tensor(step, me))

    def start(self):
        for i in range(4):
            self.copy(i).start()

    def forward(self):
        for i in range(2):
            self.copy(i).wait_recv()
            self.copy(4 + i).start()

    def wait(self, step):
        for i in ((), (2,), (3,), (4, 5))[step]:
            self.copy(i).wait_recv()

    def finish(self):
        for i in range(6):
            self.copy(i).wait_send()


class Collect:
    def __init__(self, z, me, send, got, via, sends, recvs):
        self.me, self.send, self.got, self.via, self.sends, self.recvs = me, send, got, via, sends, recvs
        half = z.block // 2
        self.halves = (pl.ds(0, half), pl.ds(half, half))

    def copy(self, i):
        top, bottom = self.halves
        block, rows, target, step = (
            (2, top, self.via.at[0], 1),
            (2, bottom, self.via.at[1], 2),
            (0, top, self.got.at[0, top, :], 1),
            (1, bottom, self.got.at[1, bottom, :], 2),
            (0, bottom, self.got.at[0, bottom, :], 1),
            (1, top, self.got.at[1, top, :], 2),
        )[i]
        return remote(
            self.send.at[block, rows, :], target, self.sends(i), self.recvs(i), to_tensor(step, self.me)
        )

    def put(self, step, value):
        for wanted, copies in ((3, (0, 1)), (1, (2,)), (2, (3,))):

            @pl.when(step == wanted)
            def _(wanted=wanted, copies=copies):
                self.send[wanted - 1] = value().astype(BF)
                for i in copies:
                    self.copy(i).start()

    def join(self):
        top, bottom = self.halves
        for i, block, rows in ((1, 0, bottom), (0, 1, top)):
            self.copy(i).wait_recv()
            joined = self.send[block, rows, :].astype(F32) + self.via[i].astype(F32)
            self.send[block, rows, :] = joined.astype(BF)
            self.copy(5 - i).start()

    def total(self, own):
        for i in range(2, 6):
            self.copy(i).wait_recv()
        return own + self.got[0].astype(F32) + self.got[1].astype(F32)

    def finish(self):
        for i in range(6):
            self.copy(i).wait_send()


def visiting(k):
    return jnp.where(k == 0, 3, jnp.where(k == 3, 0, k))


class Saver:
    def __init__(self, sems):
        self.sems, self.copies = sems, []

    def save(self, src, dst):
        copy = pltpu.make_async_copy(src, dst, self.sems.at[len(self.copies)])
        copy.start()
        self.copies.append(copy)

    def finish(self):
        for copy in self.copies:
            copy.wait()


class Refs:
    def __init__(self, names, refs):
        assert len(names) == len(refs), (len(names), len(refs))
        for name, ref in zip(names, refs):
            setattr(self, name, ref)


def forward_part(z, layer, e):
    rt, r_ref, res_ref = e.routes[layer], (e.rows, e.middle)[layer], (e.middle, e.rows)[layer]
    used, s, me, at, core, load = e.used, e.s, e.me, e.at, e.core, e.load
    held = e.held(layer)
    last = z.S - 1
    first_row = at * z.rows
    vec = e.vec(layer)
    edge_ss, edge_rs = s.edge_ss.at[layer], s.edge_rs.at[layer]
    kv_ss, kv_rs, gate_ss, gate_rs = (
        sems.at[layer] for sems in (s.kv_ss, s.kv_rs, s.gate_ss, s.gate_rs)
    )
    edge, edge_gate, got_gate = s.edge.at[layer], s.edge_gate.at[layer], s.got_gate.at[layer]
    held.ckv[at * z.cap] = jnp.zeros((TILE, LANES), BF)
    outs = e.store

    def ready(*wanted):
        for i in wanted:
            e.weight_ready(layer, i)

    if layer == 0:
        e.input_load.wait()
    saver = Saver(s.saved) if layer == 0 else Unsaved()
    per_block = z.block // TILE
    ready(0)

    def norm_in(b):
        rows = pl.ds(pl.multiple_of(b * z.block, z.block), z.block)
        y, _ = normed(r_ref[rows, :].astype(F32))
        held.n1[rows, :] = (y * vec[0:1, :] + vec[1:2, :]).astype(BF)

    def project(b):
        rows = pl.ds(pl.multiple_of(b * z.block, z.block), z.block)
        qkv = (nn(held.n1[rows, :], used["w1"][...]) + vec[2:3, :]).astype(BF)
        held.q[rows, :] = qkv[:, : z.pad]
        for h in range(z.heads):
            pairs = qkv[:, z.pad + h * LANES : z.pad + (h + 1) * LANES]
            held.kvt[pl.ds(h * (z.tiles + 1) + 1 + b * per_block, per_block)] = pairs.reshape(
                per_block, TILE, LANES
            )

    def each_norm(b, _):
        norm_in(b)
        return 0

    def each_project(b, _):
        project(b)
        return 0

    def arrived_block(step, _):
        for wanted in range(1, z.T):

            @pl.when(step == wanted)
            def _(wanted=wanted):
                e.arriving.wait(wanted)

        norm_in(partner(me, step))
        project(partner(me, step))
        return 0

    if layer == 0:
        lax.fori_loop(0, z.T, each_norm, 0)
        saver.save(held.n1, outs["n1"])
        ready(1, 2)
        lax.fori_loop(0, z.T, each_project, 0)
    else:
        ready(1, 2)
        arrived_block(0, 0)
        e.arriving.forward()
        lax.fori_loop(1, z.T, arrived_block, 0)
        e.arriving.finish()
        e.deliver(0, r_ref, e.layer_out)
    score = nt(used["swt"][...], held.n1[...])[0:8]
    held.st[...] = score
    gate = jnp.minimum(score, 0.0) - jnp.log1p(jnp.exp(-jnp.abs(score)))
    s.gt[:, 0:LANES] = jnp.zeros((8, LANES), F32)
    s.gt[:, LANES : LANES + z.rows] = gate.astype(BF).astype(F32)
    s.gt[:, LANES + z.rows :] = jnp.zeros((8, LANES), F32)
    for t in range(z.tiles + 1):
        for h in range(z.heads):
            s.gate[h * (z.tiles + 1) + t, 0:1, :] = s.gt[
                h : h + 1, TILE + t * TILE : TILE + t * TILE + LANES
            ]

    def edge_copies():
        after = {"seq": jnp.minimum(at + 1, last)}
        return [
            remote(
                held.kvt.at[h * (z.tiles + 1) + z.tiles],
                edge.at[h],
                edge_ss.at[h],
                edge_rs.at[h],
                after,
            )
            for h in range(z.heads)
        ] + [
            remote(
                s.gt.at[:, pl.ds(z.rows, LANES)],
                edge_gate,
                edge_ss.at[z.heads],
                edge_rs.at[z.heads],
                after,
            )
        ]

    @pl.when(at < last)
    def _():
        for copy in edge_copies():
            copy.start()

    def tile_copies(d, source):
        return (
            remote(
                s.send_kv.at[d],
                held.ckv.at[pl.ds(source * z.cap, z.cap)],
                kv_ss.at[d],
                kv_rs.at[source],
                {"seq": d},
            ),
            remote(
                s.send_gate.at[d], got_gate.at[source], gate_ss.at[d], gate_rs.at[source], {"seq": d}
            ),
        )

    def pack(k, _):
        d = z.S - 1 - k

        def slot(i, _):
            u = rt[SEND, d * z.cap + i]
            s.send_kv[d, i] = held.kvt[u]
            s.send_gate[d, pl.ds(i, 1), :] = s.gate[u][0:1]
            return 0

        lax.fori_loop(0, z.cap, slot, 0)
        for copy in tile_copies(d, at):
            copy.start()
        return 0

    e.turn(layer, "pack")
    lax.fori_loop(0, last - at, pack, 0)
    ready(3)

    def wo_copy(step):
        return remote(
            used["wo"], s.wo_all.at[me], s.wo_ss.at[step], s.wo_rs.at[step], to_tensor(step, me)
        )

    for step in range(1, z.T):
        wo_copy(step).start()
    s.wo_all[me] = used["wo"][...]
    saver.save(held.q, outs["q"])
    saver.save(held.st, outs["st"])

    def landed(source, _):
        for copy in tile_copies(last, source):
            copy.wait_recv()
        for i in range(z.cap):
            s.far_gate[source * z.cap + i, 0:1, :] = got_gate[source, i : i + 1, :]
        return 0

    lax.fori_loop(0, at, landed, 0)
    lane = grid_of((TILE, LANES), 1)
    row = grid_of((TILE, LANES), 0)
    for h in range(z.heads):
        held.kvt[h * (z.tiles + 1)] = jnp.zeros((TILE, LANES), BF)

    @pl.when(at > 0)
    def _():
        for copy in edge_copies():
            copy.wait_recv()
        for h in range(z.heads):
            held.kvt[h * (z.tiles + 1)] = edge[h]
            s.gate[h * (z.tiles + 1), 0:1, :] = jnp.where(
                lane[0:1] < TILE,
                pltpu.roll(edge_gate[...], TILE, 1)[h : h + 1],
                s.gate[h * (z.tiles + 1), 0:1, :],
            )

    saver.save(held.kvt, outs["kvt"])
    saver.save(held.ckv, outs["ckv"])

    def attend(tiles):
        units = [(g, h) for g in range(len(tiles)) for h in range(z.heads)]
        keys, scores = {}, {}
        for g, t in enumerate(tiles):
            base = pl.multiple_of(t * TILE, TILE)
            query = first_row + base + row
            begin = jnp.where(
                query >= rt[ENDS, 1],
                rt[ENDS, 1],
                jnp.where(query >= rt[ENDS, 0], rt[ENDS, 0], 0),
            )
            key = first_row + base - TILE + lane
            near_ok = (key <= query) & (key > query - TILE) & (key >= begin)
            for h in range(z.heads):
                u = h * z.tiles + t
                arrived = rt[ARR, u]
                far = held.ckv[arrived]
                near = held.kvt[pl.ds(h * (z.tiles + 1) + t, 2)].reshape(2 * TILE, LANES)
                keys[g, h] = jnp.concatenate([near, far, far], axis=0)
                gates = jnp.concatenate(
                    [s.gate[h * (z.tiles + 1) + t, 0:1, :], s.far_gate[arrived][0:1]], axis=1
                )
                far_ok = (rt[POS, u] + lane >= begin) & (lane < TILE)
                query_tile = held.q[pl.ds(base, TILE), h * LANES : (h + 1) * LANES]
                scores[g, h] = jnp.where(
                    jnp.concatenate([near_ok, far_ok], axis=1), nt(query_tile, keys[g, h]) + gates, MASKED
                )
        tops = {u: jnp.max(scores[u], axis=-1, keepdims=True) for u in units}
        raised = {u: jnp.exp(scores[u] - tops[u]) for u in units}
        sums = {u: jnp.sum(raised[u], axis=-1, keepdims=True) for u in units}
        probs = {u: (raised[u] * (1.0 / sums[u])).astype(BF) for u in units}
        mixed = {u: nn(probs[u], keys[u]) for u in units}
        for g, t in enumerate(tiles):
            base = pl.multiple_of(t * TILE, TILE)
            for h in range(z.heads):
                held.p[t * z.heads + h] = probs[g, h]
            pair = jnp.where(lane < TILE, pltpu.roll(mixed[g, 0], TILE, 1), mixed[g, 1]).astype(BF)
            single = pltpu.roll(mixed[g, 2], TILE, 1)
            held.o[pl.ds(base, TILE), 0:LANES] = pair
            held.o[pl.ds(base, TILE), LANES:] = single.astype(BF)
            s.pair_all[me, pl.ds(base, TILE), :] = pair
            if g % 2 == 0:
                even = single
            else:
                couple = pl.ds(pl.multiple_of((t - 1) * (TILE // 2), TILE), TILE)
                s.single_all[me, couple, :] = jnp.where(lane < TILE, even, mixed[g, 2]).astype(BF)

    e.turn(layer, "attend")
    half_rows = z.block // 2

    def pair_spread(b):
        return Spread(
            me,
            lambda owner, half: s.pair_all.at[owner, pl.ds(b * z.block + half * half_rows, half_rows), :],
            lambda i: s.o_ss.at[b * 12 + i],
            lambda i: s.o_rs.at[b * 12 + i],
        )

    def single_spread(b):
        return Spread(
            me,
            lambda owner, half: s.single_all.at[
                owner, pl.ds(b * half_rows + half * (half_rows // 2), half_rows // 2), :
            ],
            lambda i: s.o_ss.at[b * 12 + 6 + i],
            lambda i: s.o_rs.at[b * 12 + 6 + i],
        )

    def attend_block(b, _):
        attend([b * per_block + g for g in range(per_block)])
        pair_spread(b).start()
        single_spread(b).start()

        @pl.when(b > 0)
        def _():
            pair_spread(b - 1).forward()
            single_spread(b - 1).forward()

        return 0

    lax.fori_loop(0, z.T, attend_block, 0)
    pair_spread(z.T - 1).forward()
    single_spread(z.T - 1).forward()
    saver.save(held.p, outs["p"])
    saver.save(held.o, outs["o"])
    ready(4, 5)
    for step in range(1, z.T):
        wo_copy(step).wait()
    for t in range(z.T):
        s.wo_high[t, 0:TILE, :] = jnp.zeros((TILE, z.width), BF)
        s.wo_high[t, TILE:, :] = s.wo_all[t, LANES : LANES + TILE, :]
    collect = e.collect(0)

    def feed(k, _):
        step = visiting(k)
        block = partner(me, step)
        rows = pl.ds(pl.multiple_of(block * z.block, z.block), z.block)
        few = pl.ds(pl.multiple_of(block * half_rows, half_rows), half_rows)
        for other in range(1, z.T):
            pair_spread(block).wait(other)
            single_spread(block).wait(other)
        def joined(value, weight):
            return sum(
                nn(
                    jnp.concatenate([value(t), value(t + 1)], axis=1),
                    jnp.concatenate([weight(t), weight(t + 1)], axis=0),
                )
                for t in range(0, z.T, 2)
            )

        mixed = joined(lambda t: s.pair_all[t, rows, :], lambda t: s.wo_all[t, 0:LANES, :])
        even = joined(lambda t: s.single_all[t, few, :], lambda t: s.wo_all[t, LANES : 2 * LANES, :])
        odd = joined(lambda t: s.single_all[t, few, :], lambda t: s.wo_high[t])
        turns = []
        for i in range(per_block // 2):
            turns += [even[i * TILE : (i + 1) * TILE], odd[i * TILE : (i + 1) * TILE]]
        mixed += jnp.concatenate(turns, axis=0)
        middle = r_ref[rows, :].astype(F32) + mixed + vec[3:4, :]
        held.mid[...] = middle
        y, _ = normed(middle)
        n2 = (y * vec[4:5, :] + vec[5:6, :]).astype(BF)
        held.n2[rows, :] = n2
        u = nn(n2, used["wup"][...]) + vec[6:7, :]
        held.u[rows, :] = u.astype(BF)
        act = (0.5 * u * (1.0 + jnp.tanh(GELU_K * (u + GELU_A * u * u * u)))).astype(BF)
        held.act[rows, :] = act
        s.own_part[...] = nn(act, used["wdn"][...])

        collect.put(step, lambda: s.own_part[...])
        return 0

    lax.fori_loop(0, z.T, feed, 0)
    collect.join()
    if layer == 0:
        e.next_weights()
    e.turn(layer, "feed")
    for name in ("mid", "n2", "u", "act"):
        saver.save(getattr(held, name), outs[name])
    total = collect.total(held.mid[...] + s.own_part[...] + vec[7:8, :])
    own_rows = pl.ds(pl.multiple_of(me * z.block, z.block), z.block)
    res_ref[own_rows, :] = total.astype(BF)
    spread = Spread(
        me,
        lambda owner, half: res_ref.at[
            pl.ds(pl.multiple_of(owner * z.block + half * half_rows, half_rows), half_rows), :
        ],
        lambda i: s.res_ss.at[i],
        lambda i: s.res_rs.at[i],
    )
    e.arriving = spread
    if layer == 0:
        spread.start()
    collect.finish()

    def finish_block(b, _):
        pair_spread(b).finish()
        single_spread(b).finish()
        return 0

    lax.fori_loop(0, z.T, finish_block, 0)

    def sent(d, _):
        for copy in tile_copies(d, at):
            copy.wait_send()
        return 0

    lax.fori_loop(at + 1, z.S, sent, 0)

    @pl.when(at < last)
    def _():
        for copy in edge_copies():
            copy.wait_send()

    saver.finish()


def backward_part(z, layer, e):
    rt, used, s, me, at, core = e.routes[layer], e.used, e.s, e.me, e.at, e.core
    c_ref, grad_ref = (e.grad, e.cotan) if layer == 0 else (e.cotan, e.grad)
    k = e.held(layer)
    last = z.S - 1
    vec = e.vec(layer)
    own_rows = pl.ds(pl.multiple_of(me * z.block, z.block), z.block)
    W = z.width
    g_out = e.g_out
    across = {"section": 1 - core}

    def ready(*names):
        for name in names:
            if name in WEIGHTS:
                e.weight_ready(layer, WEIGHTS.index(name))
            else:
                e.kept_ready(layer, name)

    def done(*names):
        if layer == 1:
            for name in names:
                if name in WEIGHTS:
                    e.weight_again(WEIGHTS.index(name))
                else:
                    e.kept_again(name)

    collects = (e.collect(1), e.collect(2))
    half_rows = z.block // 2

    def rows_spread(ref, sends, recvs):
        return Spread(
            me,
            lambda owner, half: ref.at[
                pl.ds(pl.multiple_of(owner * z.block + half * half_rows, half_rows), half_rows), :
            ],
            lambda i: sends.at[i],
            lambda i: recvs.at[i],
        )

    if layer == 1:
        e.cotan_load.wait()
    ready("wdn", "u", "wup")

    def ff_back(i, _):
        step = visiting(i)
        rows = pl.ds(pl.multiple_of(partner(me, step) * z.block, z.block), z.block)
        u = k.u[rows, :].astype(F32)
        squared = u * u
        bent = jnp.tanh(GELU_K * (u + GELU_A * squared * u))
        slope = 0.5 * (1.0 + bent) + 0.5 * u * (1.0 - bent * bent) * (
            GELU_K * (1.0 + 3.0 * GELU_A * squared)
        )
        du = (nt(c_ref[rows, :], used["wdn"][...]) * slope).astype(BF)
        s.du[rows, :] = du
        s.own_part[...] = nt(du, used["wup"][...])

        collects[0].put(step, lambda: s.own_part[...])
        return 0

    lax.fori_loop(0, z.T, ff_back, 0)
    ones = jnp.ones((16, z.rows), BF)
    s.stat[...] = jnp.zeros((24, W), F32)

    mine = (s.pa, s.pb, s.pc, s.pd)
    theirs_part = (s.xa, s.xb, s.xc, s.xd)
    summed = (s.sa, s.sb, s.sc, s.sd)
    crossed = (s.ta, s.tb, s.tc, s.td)
    handed = (s.ha, s.hb, s.hc)

    def give(piece):
        return remote(
            mine[piece].at[1 - core if piece < 3 else 0], theirs_part[piece], s.give_ss.at[piece], s.give_rs.at[piece], across
        )

    def cross(piece, d, source):
        return remote(
            summed[piece].at[d],
            crossed[piece].at[source],
            s.cross_ss.at[piece, d],
            s.cross_rs.at[piece, source],
            {"seq": d},
        )

    stepwise = z.S == 4
    near_by, far_off = at + 1 - 2 * (at % 2), (at + 2) % z.S

    def hop(piece, i):
        block, target = ((near_by, near_by), ((near_by + 2) % z.S, near_by), (far_off, far_off))[i]
        return remote(
            summed[piece].at[block],
            crossed[piece].at[i],
            s.cross_ss.at[piece, i],
            s.cross_rs.at[piece, i],
            {"seq": target},
        )

    def relay(piece):
        if stepwise:
            hop(piece, 1).wait_recv()
            summed[piece][far_off] = (
                summed[piece][far_off].astype(F32) + crossed[piece][1].astype(F32)
            ).astype(BF)
            hop(piece, 2).start()

    def hand(piece):
        return remote(
            summed[piece].at[at], handed[piece], s.hand_ss.at[piece], s.hand_rs.at[piece], across
        )

    span = math.lcm(z.share, 16)

    def add_up(piece):
        give(piece).wait_recv()

        def chunk(i, _):
            rows = pl.ds(pl.multiple_of(i * span, span), span)
            value = mine[piece][core if piece < 3 else 0, rows, :].astype(F32) + theirs_part[piece][rows, :].astype(F32)
            for j in range(span // z.share):
                d = i * (span // z.share) + j
                rows_of = value[j * z.share : (j + 1) * z.share]
                if z.padded > z.share:
                    rows_of = jnp.concatenate(
                        [rows_of, jnp.zeros((z.padded - z.share, value.shape[1]), F32)], axis=0
                    )
                summed[piece][d] = rows_of.astype(BF)

                if not stepwise:

                    @pl.when(d != at)
                    def _():
                        cross(piece, d, at).start()

            return 0

        lax.fori_loop(0, W // span, chunk, 0)
        if stepwise:
            hop(piece, 0).start()
            hop(piece, 1).start()

    offsets = [sum(z.pieces[:piece]) for piece in range(len(z.pieces))]

    def reduce(piece):
        def wait(i, _):
            d = (at + i) % z.S
            cross(piece, d, d).wait_recv()
            return 0

        def add(i, running):
            return running + crossed[piece][(at + i) % z.S].astype(F32)

        if stepwise:
            hop(piece, 0).wait_recv()
            hop(piece, 2).wait_recv()
            total = (
                summed[piece][at].astype(F32) + crossed[piece][0].astype(F32) + crossed[piece][2].astype(F32)
            )
        else:
            lax.fori_loop(1, z.S, wait, 0)
            total = lax.fori_loop(1, z.S, add, summed[piece][at].astype(F32))
        cols = slice(offsets[piece], offsets[piece] + z.pieces[piece])

        @pl.when(core == layer)
        def _():
            g_out[core, :, cols] = total[: z.share]

        @pl.when(core != layer)
        def _():
            if piece < len(handed):
                summed[piece][at] = total.astype(BF)
                hand(piece).start()

    def crossed_over(piece):
        def one(i, _):
            cross(piece, (at + i) % z.S, at).wait_send()
            return 0

        if stepwise:
            for i in range(3):
                hop(piece, i).wait_send()
        else:
            lax.fori_loop(1, z.S, one, 0)

    def take(piece):
        cols = slice(offsets[piece], offsets[piece] + z.pieces[piece])

        @pl.when(core == layer)
        def _():
            hand(piece).wait_recv()
            g_out[1 - core, :, cols] = handed[piece][...].astype(F32)[: z.share]

    ready("act", "n2")
    wide = z.hidden // 2
    for cols in (slice(0, wide), slice(wide, z.hidden)):
        s.pa[0, :, cols] = tn(c_ref[...], k.act[:, cols]).astype(BF)
    collects[0].join()
    for cols in (slice(0, wide), slice(wide, z.hidden)):
        s.pa[1, :, cols] = tn(k.n2[...], s.du[:, cols]).astype(BF)
    give(0).start()
    done("wdn", "wup", "u", "act", "n2")
    s.stat[8:9, :] = nn(ones, s.du[...])[0:1]
    s.stat[9:10, :] = nn(ones, c_ref[...])[0:1]
    ready("mid", "wo")
    if layer == 0:
        e.leftover()
    add_up(0)
    grad = collects[0].total(s.own_part[...])
    y, spread = normed(k.mid[...])
    dr2 = c_ref[own_rows, :].astype(F32) + norm_back(grad, vec[4:5, :], y, spread)
    s.dr2[...] = dr2
    s.wo_all[me] = dr2.astype(BF)

    ob_spread = Spread(
        me,
        lambda owner, half: s.wo_all.at[owner, pl.ds(half * half_rows, half_rows), :],
        lambda i: s.ob_ss.at[i],
        lambda i: s.ob_rs.at[i],
    )
    ob_spread.start()
    done("mid")
    s.stat[0:1, :] = column_sum(dr2)
    s.stat[1:2, :] = column_sum(grad * y)
    s.stat[2:3, :] = column_sum(grad)
    s.dkv[...] = jnp.zeros((z.rows + TILE, z.pad), F32)
    ob_spread.forward()
    relay(0)
    lane_wide = grid_of((z.block, LANES), 1)

    def out_back(step, _):
        for wanted in range(1, z.T):

            @pl.when(step == wanted)
            def _(wanted=wanted):
                ob_spread.wait(wanted)

        rows = pl.ds(pl.multiple_of(partner(me, step) * z.block, z.block), z.block)
        dout = nt(s.wo_all[partner(me, step)], used["wo"][...])
        pair, single = dout[:, :LANES], dout[:, LANES:]
        for h, value in enumerate((pltpu.roll(pair, TILE, 1), pair, pltpu.roll(single, TILE, 1))):
            s.pair_all[h, rows, :] = jnp.where(lane_wide < TILE, 0.0, value).astype(BF)
        return 0

    lax.fori_loop(0, z.T, out_back, 0)
    done("wo")
    collects[0].finish()
    if layer == 1:
        e.arriving.start()
    ready("p", "q", "kvt", "ckv")

    ones_row = jnp.ones((16, TILE), BF)

    def attend_back(i, _):
        tiles = [i * group + g for g in range(group)]
        units = [(g, h) for g in range(group) for h in range(z.heads)]
        keys, query, dout, prob, dprob = {}, {}, {}, {}, {}
        for g, t in enumerate(tiles):
            base = pl.multiple_of(t * TILE, TILE)
            for h in range(z.heads):
                cols = slice(h * LANES, (h + 1) * LANES)
                far = k.ckv[rt[ARR, h * z.tiles + t]]
                near = k.kvt[pl.ds(h * (z.tiles + 1) + t, 2)].reshape(2 * TILE, LANES)
                keys[g, h] = jnp.concatenate([near, far, far], axis=0)
                query[g, h] = k.q[pl.ds(base, TILE), cols]
                dout[g, h] = s.pair_all[h, pl.ds(base, TILE), :]
                prob[g, h] = k.p[t * z.heads + h]
                dprob[g, h] = nt(dout[g, h], keys[g, h])
        totals = {u: jnp.sum(prob[u].astype(F32) * dprob[u], axis=-1, keepdims=True) for u in units}
        dz = {u: (prob[u].astype(F32) * (dprob[u] - totals[u])).astype(BF) for u in units}
        for g, t in enumerate(tiles):
            base = pl.multiple_of(t * TILE, TILE)
            for h in range(z.heads):
                cols = slice(h * LANES, (h + 1) * LANES)
                u = h * z.tiles + t
                s.dqkv[pl.ds(base, TILE), cols] = nn(dz[g, h], keys[g, h]).astype(BF)
                dkeys = tn(
                    jnp.concatenate([dz[g, h], prob[g, h]], axis=0),
                    jnp.concatenate([query[g, h], dout[g, h]], axis=0),
                )
                s.dkv[pl.ds(base, 2 * TILE), cols] += dkeys[: 2 * TILE]
                s.far[u] = dkeys[2 * TILE : 3 * TILE].astype(BF)
                gates = nn(ones_row, dz[g, h])[0:1]
                s.dgate[t, h : h + 1, :] = gates[:, :LANES]
                s.far_gate[u, 0:1, :] = gates[:, LANES:]
        return 0

    group = 4
    lax.fori_loop(0, z.tiles // group, attend_back, 0)
    done("p", "q", "kvt", "ckv")
    s.dgate[z.tiles] = jnp.zeros((8, LANES), F32)

    def edge_copies():
        behind = {"seq": jnp.maximum(at - 1, 0)}
        return (
            remote(s.edge_send, s.edge_got, s.back_edge_ss.at[0], s.back_edge_rs.at[0], behind),
            remote(s.dgate.at[0], s.edge_gate_got, s.back_edge_ss.at[1], s.back_edge_rs.at[1], behind),
        )

    @pl.when(at > 0)
    def _():
        s.edge_send[...] = s.dkv[0:TILE, :].astype(BF)
        for copy in edge_copies():
            copy.start()

    def tile_copies(d, source):
        return (
            remote(
                s.send_kv.at[d],
                s.got_kv.at[pl.ds(source * z.cap, z.cap)],
                s.back_kv_ss.at[d],
                s.back_kv_rs.at[source],
                {"seq": d},
            ),
            remote(
                s.back_send_gate.at[d], s.back_got_gate.at[source], s.back_gate_ss.at[d], s.back_gate_rs.at[source], {"seq": d}
            ),
        )

    def pack(d, _):
        def slot(i, _):
            u = rt[INV, d * z.cap + i]
            s.send_kv[d, i] = s.far[u]
            s.back_send_gate[d, pl.ds(i, 1), :] = s.far_gate[u][0:1]
            return 0

        lax.fori_loop(0, z.cap, slot, 0)
        for copy in tile_copies(d, at):
            copy.start()
        return 0

    lax.fori_loop(0, at, pack, 0)
    if layer == 1:
        e.arriving.forward()
    ready("o")
    out_grad = tn(s.wo_all[...].reshape(z.rows, W), k.o[...]).astype(BF)
    done("o")
    s.pb[0] = out_grad[:, :LANES]
    s.pb[1] = out_grad[:, LANES:]
    give(1).start()
    s.sum[z.n] = jnp.zeros((TILE, LANES), F32)
    s.gate_sum[z.n] = jnp.zeros((8, LANES), F32)
    ready("st", "w1", "swt", "n1")
    queries = tn(k.n1[...], s.dqkv[:, : z.pad])
    lane_full = grid_of((W, LANES), 1)
    s.pc[1, :, :LANES] = jnp.where(
        lane_full < TILE, queries[:, :LANES], pltpu.roll(queries[:, LANES : 2 * LANES], TILE, 1)
    ).astype(BF)
    s.pc[1, :, LANES : 2 * LANES] = queries[:, 2 * LANES :].astype(BF)
    s.pc[1, :, 2 * LANES :] = jnp.zeros((W, z.pad - 2 * LANES), BF)
    reduce(0)

    @pl.when(at < last)
    def _():
        for copy in edge_copies():
            copy.wait_recv()
        s.dkv[pl.ds(z.rows, TILE), :] += s.edge_got[...].astype(F32)
        s.dgate[z.tiles] = s.edge_gate_got[...]

    def landed(source, _):
        for copy in tile_copies(0, source):
            copy.wait_recv()
        for i in range(z.cap):
            s.got_gate_row[source * z.cap + i, 0:1, :] = s.back_got_gate[source, i : i + 1, :]
        return 0

    lax.fori_loop(at + 1, z.S, landed, 0)

    def gather(i, carry):
        running, gates = carry
        index = rt[ORD, i]
        joined = rt[CONT, i].astype(F32)
        running = running * joined + s.got_kv[index].astype(F32)
        gates = gates * joined + s.got_gate_row[index]
        s.sum[i] = running
        s.gate_sum[i] = gates
        return running, gates

    lax.fori_loop(0, z.n, gather, (jnp.zeros((TILE, LANES), F32), jnp.zeros((8, LANES), F32)))

    def settle(t, _):
        base = pl.multiple_of((t + 1) * TILE, TILE)
        rows = pl.ds(pl.multiple_of(t * TILE, TILE), TILE)
        for h in range(z.heads):
            cols = slice(h * LANES, (h + 1) * LANES)
            index = rt[LAST, h * z.tiles + t]
            s.dqkv[rows, z.pad + h * LANES : z.pad + (h + 1) * LANES] = (
                s.dkv[pl.ds(base, TILE), cols] + s.sum[index]
            ).astype(BF)
            s.tile_gate[t, h : h + 1, :] = s.gate_sum[index][0:1]
        return 0

    lax.fori_loop(0, z.tiles, settle, 0)
    if layer == 1:
        for step in range(1, z.T):
            e.arriving.wait(step)
        e.arriving.finish()
        e.deliver(1, e.rows, e.layer_out)
    lane = grid_of((8, LANES), 1)
    head_row = grid_of((8, LANES), 0)
    for i in range(z.tiles // 2):
        halves = []
        for t in (2 * i, 2 * i + 1):
            halves.append(pltpu.roll(s.dgate[t], TILE, 1) + s.dgate[t + 1] + s.tile_gate[t])
        joint = jnp.where(lane < TILE, halves[0], pltpu.roll(halves[1], TILE, 1))
        score = k.st[:, i * LANES : (i + 1) * LANES]
        grads = jnp.where(head_row < z.heads, joint / (1.0 + jnp.exp(score)), 0.0)
        s.ds[0:8, i * LANES : (i + 1) * LANES] = grads
        s.ds[8:16, i * LANES : (i + 1) * LANES] = jnp.zeros((8, LANES), F32)

    def in_back(i, _):
        step = visiting(i)
        rows = pl.ds(pl.multiple_of(partner(me, step) * z.block, z.block), z.block)
        s.own_part[...] = nt(s.dqkv[rows, :], used["w1"][...]) + tn(
            s.ds[:, rows].astype(BF), used["swt"][...]
        )

        collects[1].put(step, lambda: s.own_part[...])
        return 0

    lax.fori_loop(0, z.T, in_back, 0)
    done("st", "w1", "swt")
    s.pc[0] = tn(k.n1[...], s.dqkv[:, z.pad :]).astype(BF)
    collects[1].join()
    give(2).start()
    s.stat[10:13, :] = nn(s.ds[...].astype(BF), k.n1[...])[0:3]
    done("n1")
    add_up(1)
    add_up(2)
    source, target = grid_of((W, 1), 0), grid_of((1, W), 1)
    is_value = source >= z.pad
    index = jnp.where(is_value, source - z.pad, source)
    index = index // LANES * TILE + index % TILE
    each = z.heads * TILE // z.S
    wanted = index // each * z.share + index % each + jnp.where(is_value, each, 0)
    filled = (source % LANES >= TILE) == is_value
    wanted = jnp.where(filled, wanted, -1)
    spread_out = jnp.where(wanted == target, jnp.where(is_value, 1.0, TILE**-0.5), 0.0).astype(BF)
    s.stat[13:14, :] = nn(nn(ones, s.dqkv[...]).astype(BF), spread_out)[0:1]
    grad = collects[1].total(s.own_part[...])
    if layer == 1:
        entry = e.middle[own_rows, :]
    else:
        e.entry_load.wait()
        entry = s.entry[...]
    y, spread = normed(entry.astype(F32))
    dr = s.dr2[...] + norm_back(grad, vec[0:1, :], y, spread)
    grad_ref[own_rows, :] = dr.astype(BF)
    grad_spread = rows_spread(grad_ref, s.grad_ss, s.grad_rs)
    s.stat[3:4, :] = column_sum(grad * y)
    s.stat[4:5, :] = column_sum(grad)

    def stat_copy(step):
        return remote(
            s.stat.at[pl.ds(0, 8), :],
            s.stat_got.at[step - 1],
            s.stat_ss.at[step],
            s.stat_rs.at[step],
            to_tensor(step, me),
        )

    for step in range(1, z.T):
        stat_copy(step).start()
    grad_spread.start()
    shared = s.stat[0:8, :]
    for step in range(1, z.T):
        stat_copy(step).wait()
        shared += s.stat_got[step - 1]
    stats = jnp.concatenate([shared, s.stat[8:16, :]], axis=0).astype(BF)
    unit = (grid_of((16, LANES), 0) == grid_of((16, LANES), 1)).astype(F32).astype(BF)
    s.pd[0] = tn(stats, unit).astype(BF)

    @pl.when(core != layer)
    def _():
        give(3).start()

    grad_spread.forward()
    relay(1)
    relay(2)

    @pl.when(core == layer)
    def _():
        add_up(3)

    for step in range(z.T):
        grad_spread.wait(step)
        if layer == 0:
            e.deliver_block(grad_ref, step)

    if layer == 1:
        e.deliver(1, grad_ref, e.input_grad)
    def settle_sums():
        reduce(1)
        take(0)
        take(1)

        @pl.when(core == layer)
        def _():
            relay(3)

        reduce(2)
        take(2)

        @pl.when(core == layer)
        def _():
            reduce(3)
            crossed_over(3)

        @pl.when(core != layer)
        def _():
            give(3).wait_send()
            for piece in range(3):
                hand(piece).wait_send()

        for piece in range(3):
            crossed_over(piece)

    for piece in range(3):
        give(piece).wait_send()
    if layer == 1:
        e.leftover = settle_sums
    else:
        settle_sums()
    collects[1].finish()
    ob_spread.finish()
    grad_spread.finish()

    def sent(d, _):
        for copy in tile_copies(d, at):
            copy.wait_send()
        return 0

    lax.fori_loop(0, at, sent, 0)

    @pl.when(at > 0)
    def _():
        for copy in edge_copies():
            copy.wait_send()


class Unsaved:
    def save(self, src, dst):
        pass

    def finish(self):
        pass


class Env:
    pass


def layers_kernel(z, names, *refs):
    count = len(WEIGHTS)
    e = Env()
    e.routes, refs = refs[:2], refs[2:]
    tokens, cotangent, refs = refs[0], refs[1], refs[2:]
    own, refs = dict(zip(WEIGHTS, refs[:count])), refs[count:]
    e.layer_out, e.input_grad, e.g_out, refs = refs[0], refs[1], refs[2], refs[3:]
    theirs, refs = dict(zip(WEIGHTS, refs[:count])), refs[count:]
    e.store, refs = dict(zip(KEPT, refs[: len(KEPT)])), refs[len(KEPT) :]
    e.used, refs = dict(zip(WEIGHTS, refs[:count])), refs[count:]
    held, refs = dict(zip(KEPT, refs[: len(KEPT)])), refs[len(KEPT) :]
    s = e.s = Refs(names, refs)
    e.rows, e.middle, e.cotan, e.grad = s.rows, s.middle, s.cotan, s.grad
    me, at, core = e.me, e.at, e.core = lax.axis_index("tensor"), lax.axis_index("seq"), lax.axis_index("section")
    across = {"section": 1 - core}
    own_rows = pl.ds(pl.multiple_of(me * z.block, z.block), z.block)
    e.input_load = pltpu.make_async_copy(tokens.at[core], s.rows, s.load.at[0])
    e.cotan_load = pltpu.make_async_copy(cotangent.at[core], s.cotan, s.load.at[1])
    e.entry_load = pltpu.make_async_copy(tokens.at[core].at[own_rows, :], s.entry, s.load.at[2])
    e.input_load.start()

    def vec(layer):
        return e.used["vec"].at[layer]

    def chosen_keys(layer):
        return s.ckv_next if layer == 1 else held["ckv"]

    def held_in(layer):
        return Refs(KEPT, [chosen_keys(layer) if name == "ckv" else held[name] for name in KEPT])

    e.vec, e.held = vec, held_in

    def load(layer, i, source):
        name = WEIGHTS[i]
        target = e.used[name].at[layer] if name == "vec" else e.used[name]
        return pltpu.make_async_copy(source[name], target, s.weight_load.at[i])

    e.load = load

    def swap(i):
        name = WEIGHTS[i]
        return remote(own[name], theirs[name], s.swap_ss.at[i], s.swap_rs.at[i], across)

    def start_weight(layer, i):
        @pl.when(core == layer)
        def _():
            load(layer, i, own).start()

        @pl.when(core != layer)
        def _():
            load(layer, i, theirs).start()

    loaded = {0: set(), 1: set()}
    pending = {}

    def weight_ready(layer, i):
        if layer == 0 and i not in loaded[0]:

            @pl.when(core != layer)
            def _():
                swap(i).wait_recv()
                load(layer, i, theirs).start()

            loaded[0].add(i)
            load(layer, i, own).wait()
        elif pending.pop((layer, i), False):
            load(layer, i, own).wait()

    def next_weights():
        @pl.when(core == 0)
        def _():
            for i in range(count):
                swap(i).wait_recv()

        for i in range(count):
            start_weight(1, i)
            pending[1, i] = True

    def weight_again(i):
        if WEIGHTS[i] != "vec":
            start_weight(0, i)
            pending[0, i] = True

    e.weight_ready, e.next_weights, e.weight_again = weight_ready, next_weights, weight_again
    kept_pending = {}

    def kept_load(name):
        return pltpu.make_async_copy(e.store[name], held[name], s.kept_load.at[KEPT.index(name)])

    def kept_again(name):
        if name != "ckv":
            kept_load(name).start()
            kept_pending[name] = True

    def kept_ready(layer, name):
        if kept_pending.pop(name, False):
            kept_load(name).wait()

    e.kept_again, e.kept_ready = kept_again, kept_ready

    def collect(phase):
        return Collect(
            z,
            me,
            s.part_send,
            s.part_got.at[phase % 2],
            s.part_via.at[phase % 2],
            lambda i: s.part_ss.at[phase, i],
            lambda i: s.part_rs.at[phase, i],
        )

    e.collect = collect
    delivered = []

    def rows_to(ref, target, slot, part):
        local = pltpu.make_async_copy(ref.at[part, :], target.at[core].at[part, :], s.keep.at[slot])
        return local, remote(
            ref.at[part, :], target.at[core].at[part, :], s.move_ss.at[slot], s.move_rs.at[slot], across
        )

    everything = pl.ds(0, z.rows)

    def deliver(layer, ref, target):
        slot = len(delivered)
        local, away = rows_to(ref, target, slot, everything)

        @pl.when(core == layer)
        def _():
            local.start()

        @pl.when(core != layer)
        def _():
            away.start()

        delivered.append((layer, local, away))

    def deliver_block(ref, step):
        slot = len(delivered)
        part = pl.ds(pl.multiple_of(partner(me, step) * z.block, z.block), z.block)
        local, away = rows_to(ref, target=e.input_grad, slot=slot, part=part)

        @pl.when(core == 0)
        def _():
            local.start()

        @pl.when(core == 1)
        def _():
            away.start()

        delivered.append((0, local, away))

    e.deliver, e.deliver_block = deliver, deliver_block

    def turn(layer, where):
        if (layer, where) == TURN_FROM:

            @pl.when(core == 0)
            def _():
                pl.semaphore_signal(s.turn, inc=1, device_id=across, device_id_type=MESH)

        if (layer, where) == TURN_TO:

            @pl.when(core == 1)
            def _():
                pl.semaphore_wait(s.turn, 1)

    e.turn = turn

    @pl.when(core == 0)
    def _():
        for i in range(count):
            load(0, i, own).start()

    barrier = pltpu.get_barrier_semaphore()
    for step in range(1, z.T):
        signal(to_tensor(step, me), barrier)
    signal(across, barrier)

    def greet(i, _):
        signal({"seq": (at + i) % z.S}, barrier)
        return 0

    lax.fori_loop(1, z.S, greet, 0)
    pl.semaphore_wait(barrier, z.T - 1 + 1 + z.S - 1)
    for i in range(count):
        swap(i).start()
    e.cotan_load.start()
    e.entry_load.start()
    forward_part(z, 0, e)
    forward_part(z, 1, e)
    backward_part(z, 1, e)
    backward_part(z, 0, e)
    for i in range(count):
        swap(i).wait_send()
    for layer, local, away in delivered:

        @pl.when(core == layer)
        def _(local=local, away=away):
            local.wait()
            away.wait_recv()

        @pl.when(core != layer)
        def _(away=away):
            away.wait_send()


TURN_FROM, TURN_TO = (0, "attend"), (0, "pack")


def layers(z, routes, tokens, cotangent, own):
    rows, width, heads = z.rows, z.width, z.heads
    half = z.block // 2
    kept = dict(
        n1=((rows, width), BF),
        q=((rows, z.pad), BF),
        kvt=((heads * (z.tiles + 1), TILE, LANES), BF),
        st=((8, rows), F32),
        p=((z.slots, TILE, 2 * LANES), BF),
        ckv=((z.n, TILE, LANES), BF),
        o=((rows, 2 * LANES), BF),
        mid=((z.block, width), F32),
        n2=((rows, width), BF),
        u=((rows, z.hidden), BF),
        act=((rows, z.hidden), BF),
    )
    weights = [own[name] for name in WEIGHTS]
    vmem_of, dma = pltpu.VMEM, pltpu.SemaphoreType.DMA
    scratch = dict(
        rows=vmem_of((rows, width), BF),
        middle=vmem_of((rows, width), BF),
        cotan=vmem_of((rows, width), BF),
        grad=vmem_of((rows, width), BF),
        entry=vmem_of((z.block, width), BF),
        ckv_next=vmem_of((z.n, TILE, LANES), BF),
        gt=vmem_of((8, rows + 2 * LANES), F32),
        gate=vmem_of((heads * (z.tiles + 1), 8, LANES), F32),
        edge=vmem_of((2, heads, TILE, LANES), BF),
        edge_gate=vmem_of((2, 8, LANES), F32),
        send_kv=vmem_of((z.S, z.cap, TILE, LANES), BF),
        send_gate=vmem_of((z.S, z.capg, LANES), F32),
        got_gate=vmem_of((2, z.S, z.capg, LANES), F32),
        far_gate=vmem_of((max(z.n, z.slots), 8, LANES), F32),
        wo_all=vmem_of((z.T, max(2 * LANES, z.block), width), BF),
        wo_high=vmem_of((z.T, LANES, width), BF),
        pair_all=vmem_of((z.T, rows, LANES), BF),
        single_all=vmem_of((z.T, rows // 2, LANES), BF),
        part_send=vmem_of((z.T - 1, z.block, width), BF),
        part_got=vmem_of((2, 2, z.block, width), BF),
        part_via=vmem_of((2, 2, half, width), BF),
        own_part=vmem_of((z.block, width), F32),
        du=vmem_of((rows, z.hidden), BF),
        dr2=vmem_of((z.block, width), F32),
        dqkv=vmem_of((rows, 2 * z.pad), BF),
        dkv=vmem_of((rows + TILE, z.pad), F32),
        dgate=vmem_of((z.tiles + 1, 8, LANES), F32),
        far=vmem_of((z.slots, TILE, LANES), BF),
        back_send_gate=vmem_of((z.S, z.capg, LANES), F32),
        got_kv=vmem_of((z.n, TILE, LANES), BF),
        back_got_gate=vmem_of((z.S, z.capg, LANES), F32),
        got_gate_row=vmem_of((z.n, 8, LANES), F32),
        edge_send=vmem_of((TILE, z.pad), BF),
        edge_got=vmem_of((TILE, z.pad), BF),
        edge_gate_got=vmem_of((8, LANES), F32),
        sum=vmem_of((z.n + 1, TILE, LANES), F32),
        gate_sum=vmem_of((z.n + 1, 8, LANES), F32),
        tile_gate=vmem_of((z.tiles, 8, LANES), F32),
        ds=vmem_of((16, rows), F32),
        stat=vmem_of((24, width), F32),
        stat_got=vmem_of((z.T - 1, 8, width), F32),
    )
    for name, w in zip("abcd", z.pieces):
        scratch["p" + name] = vmem_of((1 if name == "d" else 2, width, w), BF)
        scratch["x" + name] = vmem_of((width, w), BF)
        scratch["s" + name] = vmem_of((z.S, z.padded, w), BF)
        scratch["t" + name] = vmem_of((z.S, z.padded, w), BF)
        if name != "d":
            scratch["h" + name] = vmem_of((z.padded, w), BF)
    pairs = dict(
        kv=(2, z.S), gate=(2, z.S), edge=(2, heads + 1), wo=(z.T,), o=(z.T * 12,), part=(3, 6), res=(6,),
        swap=(len(WEIGHTS),), move=(3 + z.T,), back_kv=(z.S,), back_gate=(z.S,), back_edge=(2,), ob=(6,),
        grad=(6,), stat=(z.T,), give=(4,), cross=(4, z.S), hand=(3,),
    )
    for name, shape in pairs.items():
        scratch[name + "_ss"] = dma(shape)
        scratch[name + "_rs"] = dma(shape)
    scratch |= dict(
        load=dma((3,)),
        weight_load=dma((len(WEIGHTS),)),
        kept_load=dma((len(KEPT),)),
        saved=dma((len(KEPT),)),
        keep=dma((3 + z.T,)),
        turn=pltpu.SemaphoreType.REGULAR,
    )
    doubled = {"vec"}

    def room(name, shape, kind):
        return vmem_of((2, *shape) if name in doubled else shape, kind)

    shaped = (
        jax.ShapeDtypeStruct((2, rows, width), BF),
        jax.ShapeDtypeStruct((2, rows, width), BF),
        jax.ShapeDtypeStruct((2, z.share, sum(z.pieces)), F32),
        *(jax.ShapeDtypeStruct(value.shape, value.dtype) for value in weights),
        *(jax.ShapeDtypeStruct(*kept[name]) for name in KEPT),
    )
    outs = pl.pallas_call(
        functools.partial(layers_kernel, z, tuple(scratch)),
        out_shape=shaped,
        in_specs=[smem(), smem()] + [anywhere()] * (2 + len(weights)),
        out_specs=tuple(vmem() if i == 2 else anywhere() for i in range(len(shaped))),
        scratch_shapes=[
            *(room(name, value.shape, value.dtype) for name, value in zip(WEIGHTS, weights)),
            *(room(name, *kept[name]) for name in KEPT),
            *scratch.values(),
        ],
        compiler_params=pltpu.CompilerParams(
            collective_id=0, has_side_effects=True, vmem_limit_bytes=LIMIT
        ),
        name="layers",
    )(*routes, tokens, cotangent, *weights)
    return outs[:3]


UNPACKED = (
    "input_weight", "input_bias", "score", "out", "out_bias", "up", "up_bias", "down", "down_bias", "gain", "shift",
)


def unpack_kernel(z, head, total_ref, out_any, grad_any, *refs):
    count = len(UNPACKED)
    out, rows_out, buffers, sems = Refs(UNPACKED, refs[:count]), refs[count : count + 2], refs[count + 2 : count + 4], refs[-1]
    loads = [
        pltpu.make_async_copy(src, buffer, sems.at[i]) for i, (src, buffer) in enumerate(zip((out_any, grad_any), buffers))
    ]
    stores = [
        pltpu.make_async_copy(buffer, dst, sems.at[2 + i]) for i, (buffer, dst) in enumerate(zip(buffers, rows_out))
    ]
    for load in loads:
        load.start()
    for load, store in zip(loads, stores):
        load.wait()
        store.start()
    core = lax.axis_index("section")
    inner, hidden, share = z.heads * head, z.hidden, z.share
    c_o, c_i = hidden, hidden + LANES
    c_s = c_i + z.pad
    out.up[...] = total_ref[1, :, :hidden]
    out.down[...] = total_ref[0, :, :hidden]
    first, second = total_ref[0, :, c_o:c_i].T, total_ref[1, :, c_o:c_i].T
    out.out[0:LANES, :] = first
    out.out[LANES:inner, :] = second[: inner - LANES]
    out.input_weight[0] = head**-0.5 * total_ref[1, :, c_i : c_i + inner]
    lane = grid_of((share, LANES), 1)
    pairs = [total_ref[0, :, c_i + h * LANES : c_i + (h + 1) * LANES] for h in range(z.heads)]
    turned = [pltpu.roll(pair, LANES // 2, 1) for pair in pairs]
    out.input_weight[1, :, 0:LANES] = jnp.where(lane < head, pairs[0], turned[1])
    out.input_weight[1, :, LANES:inner] = pairs[2][:, :head]
    out.input_weight[2, :, 0:LANES] = jnp.where(lane < head, turned[0], pairs[1])
    out.input_weight[2, :, LANES:inner] = turned[2][:, :head]
    stats = total_ref[core, :, c_s : c_s + LANES]
    rows = stats.T
    out.score[...] = rows[10 : 10 + z.heads]
    each = inner // z.S
    out.input_bias[0:1, :] = rows[13:14, :each]
    out.input_bias[1:2, :] = pltpu.roll(rows[8:16], share - each, 1)[5:6, :each]
    out.out_bias[...] = rows[0:1]
    out.up_bias[...] = rows[8:9]
    out.down_bias[...] = rows[9:10]
    out.gain[0:1, :] = rows[3:4]
    out.gain[1:2, :] = rows[1:2]
    out.shift[0:1, :] = rows[4:5]
    out.shift[1:2, :] = rows[2:3]
    for store in stores:
        store.wait()


def unpack(z, head, total, layer_out, input_grad):
    inner, hidden, share = z.heads * head, z.hidden, z.share
    shapes = (
        (3, share, inner), (2, inner // z.S), (z.heads, share), (inner, share), (1, share), (share, hidden), (1, share),
        (share, hidden), (1, share), (2, share), (2, share),
    )
    outs = pl.pallas_call(
        functools.partial(unpack_kernel, z, head),
        out_shape=(
            *(jax.ShapeDtypeStruct(shape, F32) for shape in shapes),
            jax.ShapeDtypeStruct(layer_out.shape, BF),
            jax.ShapeDtypeStruct(input_grad.shape, BF),
        ),
        in_specs=[vmem(), anywhere(), anywhere()],
        out_specs=(*(vmem() for _ in shapes), anywhere(), anywhere()),
        scratch_shapes=[
            pltpu.VMEM(layer_out.shape, BF),
            pltpu.VMEM(input_grad.shape, BF),
            pltpu.SemaphoreType.DMA((4,)),
        ],
        compiler_params=pltpu.CompilerParams(vmem_limit_bytes=LIMIT),
        name="unpack",
    )(total, layer_out, input_grad)
    return dict(zip(UNPACKED, outs)), outs[-2], outs[-1]


def swapped(value):
    return lax.ppermute(value, "section", [(0, 1), (1, 0)])


def body(
    tokens,
    cotangent,
    lengths,
    selected,
    input_weight,
    input_bias,
    score_weight,
    output_weight,
    output_bias,
    up_weight,
    up_bias,
    down_weight,
    down_bias,
    norm_gain,
    norm_bias,
):
    core = lax.axis_index("section")
    _, rows, width = tokens.shape
    heads, hidden = score_weight.shape[2], up_weight.shape[2]
    head = input_weight.shape[3] // heads
    inner = heads * head
    z = Sizes(lax.axis_size("tensor"), lax.axis_size("seq"), rows, width, heads, hidden)
    scale = head**-0.5
    grouped = (
        selected[0].reshape(2, heads, z.S, z.tiles).transpose(0, 2, 1, 3).reshape(2, z.S, z.slots)
    )
    kept_choice = lax.dynamic_index_in_dim(grouped, core, 0, keepdims=False)
    got_choice = swapped(lax.dynamic_index_in_dim(grouped, 1 - core, 0, keepdims=False))
    own, routes = prepare(
        z,
        lengths,
        kept_choice,
        got_choice,
        input_weight[0].transpose(1, 0, 2),
        input_bias[0],
        score_weight[0].T,
        output_weight[0],
        output_bias,
        up_bias,
        down_bias,
        norm_gain[0],
        norm_bias[0],
    )
    own |= dict(wup=up_weight[0], wdn=down_weight[0])
    layer_out, input_grad, total = layers(z, routes, tokens, cotangent, own)
    parts, layer_out, input_grad = unpack(z, head, total, layer_out, input_grad)
    parts["down"], parts["score"] = parts["down"].T, parts["score"].T
    parts["input_weight"] = parts["input_weight"].transpose(1, 0, 2)
    return (layer_out[None], input_grad[None], *(part.reshape(1, *shape) for part, shape in (
        (parts["input_weight"], (z.share, 3, inner)),
        (parts["input_bias"], (2, inner // z.S)),
        (parts["score"], (z.share, heads)),
        (parts["out"], (inner, z.share)),
        (parts["out_bias"], (z.share,)),
        (parts["up"], (z.share, hidden)),
        (parts["up_bias"], (z.share,)),
        (parts["down"], (hidden, z.share)),
        (parts["down_bias"], (z.share,)),
        (parts["gain"], (2, z.share)),
        (parts["shift"], (2, z.share)),
    )))


def solution(mesh):
    return jax.shard_map(
        body,
        mesh=mesh,
        in_specs=(
            P(None, "seq", None),
            P(None, "seq", None),
            P(),
            P("section", None, "tensor", None),
            P("section", None, None, "tensor"),
            P("section", None, "tensor"),
            P("section", None, "tensor"),
            P("section", "tensor", None),
            P("section", None),
            P("section", None, "tensor"),
            P("section", "tensor"),
            P("section", "tensor", None),
            P("section", None),
            P("section", None, None),
            P("section", None, None),
        ),
        out_specs=(
            P("section", None, "seq", None),
            P("section", None, "seq", None),
            P("section", "seq", None, "tensor"),
            P("section", None, ("tensor", "seq")),
            P("section", "seq", "tensor"),
            P("section", "tensor", "seq"),
            P("section", "seq"),
            P("section", "seq", "tensor"),
            P("section", ("tensor", "seq")),
            P("section", "tensor", "seq"),
            P("section", "seq"),
            P("section", None, "seq"),
            P("section", None, "seq"),
        ),
        check_vma=False,
    )
```
